32 devices in a mesh: narrow: 8 (over z, core), wide: 4 (over y, x).
Axes of the slice: x: 2, y: 2, z: 4, core: 2. Of those that a mesh axis runs over, the one named last changes fastest.
Arguments:
- frames_in: bfloat16 [16, 1536, 768], P('narrow', 'wide'), may hold values from -6 to 6
- lengths: int32 [16], P('narrow'), may hold values from 102 to 1536, as said below
- kernel: bfloat16 [128, 16, 48, 48], replicated, may hold values from -0.15625 to 0.15625
- conv_bias: bfloat16 [768], replicated, may hold values from -3 to 3
- w_query: bfloat16 [768, 768], replicated, may hold values from -0.21875 to 0.21875
- b_query: bfloat16 [768], replicated, may hold values from -3 to 3
- w_key: bfloat16 [768, 768], replicated, may hold values from -0.21875 to 0.21875
- w_value: bfloat16 [768, 768], replicated, may hold values from -0.21875 to 0.21875
- b_value: bfloat16 [768], replicated, may hold values from -3 to 3
- w_out: bfloat16 [768, 768], replicated, may hold values from -1.25 to 1.25
- b_out: bfloat16 [768], replicated, may hold values from -3 to 3
- gain_one: bfloat16 [768], replicated, may hold values from 0.25 to 1.75
- shift_one: bfloat16 [768], replicated, may hold values from -3 to 3
- w_up: bfloat16 [768, 3072], replicated, may hold values from -0.21875 to 0.21875
- b_up: bfloat16 [3072], replicated, may hold values from -3 to 3
- w_down: bfloat16 [3072, 768], replicated, may hold values from -0.109375 to 0.109375
- b_down: bfloat16 [768], replicated, may hold values from -3 to 3
- gain_two: bfloat16 [768], replicated, may hold values from 0.25 to 1.75
- shift_two: bfloat16 [768], replicated, may hold values from -3 to 3
- out_grad: bfloat16 [16, 1536, 768], P('narrow', 'wide'), may hold values from -6 to 6
Outputs:
- layer_out: bfloat16 [16, 1536, 768], P('narrow', 'wide')
- frames_grad: bfloat16 [16, 1536, 768], P('narrow', 'wide')
- grad_kernel: float32 [128, 16, 48, 48], P('wide')
- grad_conv_bias: float32 [768], P('wide')
- grad_w_query: float32 [768, 768], P('wide')
- grad_b_query: float32 [768], P('wide')
- grad_w_key: float32 [768, 768], P('wide')
- grad_w_value: float32 [768, 768], P('wide')
- grad_b_value: float32 [768], P('wide')
- grad_w_out: float32 [768, 768], P('wide')
- grad_b_out: float32 [768], P('wide')
- grad_gain_one: float32 [768], P('wide')
- grad_shift_one: float32 [768], P('wide')
- grad_w_up: float32 [768, 3072], P('wide')
- grad_b_up: float32 [3072], P('wide')
- grad_w_down: float32 [3072, 768], P('wide')
- grad_b_down: float32 [768], P('wide')
- grad_gain_two: float32 [768], P('wide')
- grad_shift_two: float32 [768], P('wide')
The draws below stay inside these ranges and needn't reach their ends.
Inputs may be any that keep to these rules, and one draw needn't show every extreme that they name: `lengths`: among the 2 clips of each index of narrow, one has exactly 1536 frames and another exactly 102.
All inputs are finite; a program needn't handle non-finite values.
Results may differ from the reference program's by a relative error of at most 0.025.
The reference program's roundings to bfloat16 on the way count: a program that leaves them out, or rounds other values in their place, can miss the bound.
Values may be sent and summed in bfloat16 or wider, within the bound.
A program may use at most 320 MiB of HBM per device.

```python
import jax
import jax.numpy as jnp
from jax import lax

D = 768
HEADS = 12
FF = 3072
KSIZE = 128
GROUPS = 16
CLIPS_DEV = 2
LEN = 1536
SHORTEST = 102
CLIPS = 16


def draw_lengths(key, part):
    group_count = CLIPS // CLIPS_DEV
    key_base, key_order = jax.random.split(jax.random.fold_in(key, 11))
    base_len = jax.random.randint(key_base, (group_count, CLIPS_DEV), SHORTEST, LEN + 1)
    rank_keys = jax.random.randint(key_order, (group_count, CLIPS_DEV), 0, 4096) * CLIPS_DEV
    rank_keys = rank_keys + jnp.arange(CLIPS_DEV, dtype=jnp.int32)[None, :]
    ordering = jnp.argsort(rank_keys, axis=1)
    column = jnp.arange(CLIPS_DEV, dtype=jnp.int32)[None, :]
    longest = column == ordering[:, 0:1]
    shortest = column == ordering[:, 1:2]
    drawn_len = jnp.where(longest, LEN, jnp.where(shortest, SHORTEST, base_len))
    return drawn_len.reshape(CLIPS).astype(jnp.int32)


def spiked(drawn, rng, source, target, shards_of, factor):
    owner, partner = [(jnp.arange(drawn.shape[dim]) // (drawn.shape[dim] // shards_of)).reshape([-1 if axis == dim else 1 for axis in range(drawn.ndim)]) for dim in (source, target)]
    chosen = jax.random.permutation(rng, shards_of)[partner]
    strong = (owner == chosen) | (owner == (partner + shards_of // 2) % shards_of)
    return jnp.where(strong, factor * drawn, drawn)


def steps_of(own_key, extent, pieces, low, high):
    def one(position, blocks):
        steps = jax.random.uniform(jax.random.fold_in(jax.random.fold_in(own_key, 6), position), (blocks,), jnp.float32, low / len(pieces), high / len(pieces))
        return jnp.repeat(jnp.exp(steps), extent[position] // blocks).reshape((-1,) + (1,) * (len(extent) - position - 1))

    factor_of = one(*pieces[0])
    for cut in pieces[1:]:
        factor_of = factor_of * one(*cut)
    return factor_of


def noise(own_key, shape, deviation, most, shards=(), held_as=jnp.bfloat16):
    level = steps_of(own_key, shape, shards, -0.22, 0.18) if shards else 1.0
    drawn = jax.random.normal(own_key, shape, jnp.float32) * deviation * level
    return jnp.minimum(jnp.maximum(drawn, -most), most).astype(held_as)


def gaussian_with(key, shape, deviation, reach, cuts, heavy, held_as=jnp.bfloat16):
    array = deviation * jax.random.normal(key, shape, jnp.float32)
    if cuts:
        array = array * steps_of(key, shape, cuts, -0.22, 0.18)
    return jnp.clip(spiked(array, jax.random.fold_in(key, 3), *heavy), -reach, reach).astype(held_as)


def setup_inputs(seed: int = 0) -> dict:
    seeds = jax.random.split(jax.random.key(seed), 21)
    return {
        "frames_in": noise(seeds[0], (CLIPS, LEN, D), 1.0, 6.0, ((0, 8), (1, 4))),
        "lengths": draw_lengths(jax.random.fold_in(seeds[20], 71), 0),
        "kernel": noise(seeds[2], (KSIZE, GROUPS, D // GROUPS, D // GROUPS), (KSIZE * (D // GROUPS) // 4) ** -0.5, 0.15625),
        "conv_bias": noise(seeds[3], (D,), 0.5, 3.0),
        "w_query": noise(seeds[4], (D, D), D ** -0.5, 0.21875),
        "b_query": noise(seeds[5], (D,), 0.5, 3.0),
        "w_key": noise(seeds[6], (D, D), D ** -0.5, 0.21875),
        "w_value": noise(seeds[7], (D, D), D ** -0.5, 0.21875),
        "b_value": noise(seeds[8], (D,), 0.5, 3.0),
        "w_out": noise(seeds[9], (D, D), (D // 32) ** -0.5, 1.25),
        "b_out": noise(seeds[10], (D,), 0.5, 3.0),
        "gain_one": jnp.clip(1.0 + 0.15 * jax.random.normal(seeds[11], (D,), jnp.float32), 0.25, 1.75).astype(jnp.bfloat16),
        "shift_one": noise(seeds[12], (D,), 0.5, 3.0),
        "w_up": noise(seeds[13], (D, FF), D ** -0.5, 0.21875),
        "b_up": noise(seeds[14], (FF,), 0.5, 3.0),
        "w_down": noise(seeds[15], (FF, D), FF ** -0.5, 0.109375),
        "b_down": noise(seeds[16], (D,), 0.5, 3.0),
        "gain_two": jnp.clip(1.0 + 0.15 * jax.random.normal(seeds[17], (D,), jnp.float32), 0.25, 1.75).astype(jnp.bfloat16),
        "shift_two": noise(seeds[18], (D,), 0.5, 3.0),
        "out_grad": gaussian_with(seeds[19], (CLIPS, LEN, D), 1.0, 6.0, ((0, 8), (1, 4)), (1, 2, 4, 2.0)),
    }


@jax.custom_vjp
def low(v):
    return lax.optimization_barrier(v.astype(jnp.bfloat16)).astype(jnp.float32)

@jax.custom_vjp
def low_back(v):
    return v

def low_keep(v):
    return (low(v), None)

def low_pass(kept, grad):
    return (grad,)

def back_keep(v):
    return (v, None)

def back_low(kept, grad):
    return (low(grad),)
low.defvjp(low_keep, low_pass)
low_back.defvjp(back_keep, back_low)
eps_norm = 1e-05
neg_large = -1e+30

def matmul(left, right):
    return jnp.dot(left, right, precision=lax.Precision.HIGHEST)

def layer_norm(value, gain, shift):
    center = value - lax.optimization_barrier(jnp.mean(value, axis=-1, keepdims=True))
    spread = lax.optimization_barrier(jnp.mean(center * center, axis=-1, keepdims=True))
    return center * lax.rsqrt(spread + eps_norm) * gain + shift

def gelu_exact(value):
    return jax.nn.gelu(value, approximate=False)

def clip_forward(params, clip_rows, length):
    kernel, conv_bias, w_query, b_query, w_key, w_value, b_value, w_out, b_out, gain_one, shift_one, w_up, b_up, w_down, b_down, gain_two, shift_two = params
    head_dim = D // HEADS
    score_scale = head_dim ** (-0.5)
    slots = jnp.arange(LEN, dtype=jnp.int32)
    key_mask = slots < length
    masked = low(clip_rows * key_mask.astype(clip_rows.dtype)[:, None])
    conv_rhs = jnp.transpose(kernel, (1, 3, 2, 0)).reshape(D, D // GROUPS, KSIZE)
    convolved = lax.conv_general_dilated(masked.T[None], conv_rhs, (1,), [(KSIZE // 2, KSIZE // 2)], feature_group_count=GROUPS, precision=lax.Precision.HIGHEST)
    convolved = convolved[0, :, :LEN].T
    pre_act = low_back(convolved + conv_bias)
    first_out = masked + gelu_exact(pre_act)
    first_low = low(first_out)
    query = low_back(low(matmul(first_low, w_query) + b_query))
    keys = low_back(low(matmul(first_low, w_key)))
    values = low_back(low(matmul(first_low, w_value) + b_value))
    heads_k = keys.reshape(LEN, HEADS, head_dim)
    heads_v = values.reshape(LEN, HEADS, head_dim)
    query_rows = 512 if LEN % 512 == 0 else LEN

    def attend(query_block):
        scores = low_back(jnp.einsum('qhd,khd->hqk', query_block, heads_k, precision=lax.Precision.HIGHEST) * score_scale)
        scores = jnp.where(key_mask[None, None, :], scores, neg_large)
        probs = jax.nn.softmax(scores, axis=-1)
        return jnp.einsum('hqk,khd->qhd', low(probs), heads_v, precision=lax.Precision.HIGHEST)
    blocks = query.reshape(LEN // query_rows, query_rows, HEADS, head_dim)
    mixed = lax.map(jax.checkpoint(attend), blocks).reshape(LEN, D)
    mixed = low_back(low(mixed))
    attn_out = low_back(matmul(mixed, w_out) + b_out)
    norm_one = layer_norm(first_out + attn_out, gain_one, shift_one)
    up_pre = low_back(matmul(low(norm_one), w_up) + b_up)
    down_out = low_back(matmul(low(gelu_exact(up_pre)), w_down) + b_down)
    return layer_norm(norm_one + down_out, gain_two, shift_two)

def reference(frames_in, lengths, kernel, conv_bias, w_query, b_query, w_key, w_value, b_value, w_out, b_out, gain_one, shift_one, w_up, b_up, w_down, b_down, gain_two, shift_two, out_grad):
    params = tuple((member.astype(jnp.float32) for member in (kernel, conv_bias, w_query, b_query, w_key, w_value, b_value, w_out, b_out, gain_one, shift_one, w_up, b_up, w_down, b_down, gain_two, shift_two)))
    inputs = frames_in.astype(jnp.float32)
    cotangent = out_grad.astype(jnp.float32)

    def one_clip(totals, entry):
        clip_rows, length, clip_cot = entry

        def forward(param_set, rows_in):
            return clip_forward(param_set, rows_in, length)
        result, pull = jax.vjp(forward, params, clip_rows)
        grad_params, grad_rows = pull(clip_cot)
        totals = jax.tree.map(jnp.add, totals, grad_params)
        return (totals, (result, grad_rows))
    zeros = jax.tree.map(jnp.zeros_like, params)
    totals, (results, grads) = lax.scan(one_clip, zeros, (inputs, lengths, cotangent))
    return (results.astype(jnp.bfloat16), grads.astype(jnp.bfloat16), totals[0], totals[1], totals[2], totals[3], totals[4], totals[5], totals[6], totals[7], totals[8], totals[9], totals[10], totals[11], totals[12], totals[13], totals[14], totals[15], totals[16])
```

```python
import functools

import jax
import jax.numpy as jnp
from jax import lax
from jax.experimental import pallas as pl
from jax.experimental.pallas import tpu as pltpu
from jax.sharding import PartitionSpec as P

HEADS = 12
GROUP_CH = 48
SHORT = 102
HALF = 64
UNIQUE = SHORT + HALF
FR = 384
SLOTS = 1536
SROWS = 192
TROWS = 1792
SBASE = 1600
CH = 192
eps_norm = 1e-05
neg_large = -1e30
bf16 = jnp.bfloat16
f32 = jnp.float32
VLIM = 60 * 1024 * 1024


def mm(a, b):
    return jnp.dot(a, b, preferred_element_type=f32)


def mm_nt(a, b):
    return lax.dot_general(a, b, (((1,), (1,)), ((), ())), preferred_element_type=f32)


def iota2(shape):
    return lax.broadcasted_iota(jnp.int32, shape, 0), lax.broadcasted_iota(jnp.int32, shape, 1)


def place(shape, rows_from, rows_to, cols_from):
    r, c = iota2(shape)
    hit = (c - cols_from == r - rows_from) & (r >= rows_from) & (r < rows_to)
    return hit.astype(f32).astype(bf16)


def spread(shape, lane0, start):
    r, c = iota2(shape)
    slot, inner = c >> 6, c & 63
    hit = (r == lane0 + start + slot * GROUP_CH + inner) & (inner < GROUP_CH)
    return hit.astype(f32).astype(bf16)


def gather_slots(shape, col0):
    r, c = iota2(shape)
    slot, inner = r >> 6, r & 63
    hit = (c == col0 + slot * GROUP_CH + inner) & (inner < GROUP_CH)
    return hit.astype(f32).astype(bf16)


def full(shape):
    return pl.BlockSpec(shape, lambda *_: (0,) * len(shape))


def smem():
    return pl.BlockSpec(memory_space=pltpu.SMEM)


def vmem():
    return pl.BlockSpec(memory_space=pltpu.VMEM)


def params(**kw):
    return pltpu.CompilerParams(vmem_limit_bytes=VLIM, **kw)


def gelu_parts(v):
    cdf = 0.5 * (1.0 + lax.erf(v * (2.0 ** -0.5)))
    return cdf


def density(v):
    return jnp.exp(-0.5 * v * v) * 0.3989422804014327


def pack_frames_kernel(s_ref, x_ref, *outs):
    me, li = s_ref[0], s_ref[1]
    long, short = x_ref[li], x_ref[1 - li]
    slot = me * FR + lax.broadcasted_iota(jnp.int32, (128, 768), 0)
    short = jnp.where(slot < SHORT, short[:128].astype(f32), 0.0).astype(bf16)
    top = long[:256]
    low = jnp.concatenate([long[256:], short], axis=0)
    for d in range(4):
        first = 192 * d - (64 if d % 2 else 0)
        skip = 64 if d % 2 else 0
        chunk = mm(top[:, first : first + 256], place((256, 384), skip, skip + 192, 0)) + mm(
            low[:, first : first + 256], place((256, 384), skip, skip + 192, 192)
        )
        chunk = chunk.astype(bf16)
        for r in range(4):

            @pl.when((me ^ d) == r)
            def _():
                outs[r][...] = chunk


def pack_frames(scal, frames_in):
    return pl.pallas_call(
        pack_frames_kernel,
        out_shape=[jax.ShapeDtypeStruct((256, 384), bf16)] * 4,
        in_specs=[smem(), vmem()],
        out_specs=[vmem()] * 4,
        compiler_params=params(),
        name="pack_frames",
    )(scal, frames_in)


def prep_kernel(s_ref, w_ref, wt_ref, wd_ref, z_ref):
    left, right = place((48, 128), 0, 48, 0), place((48, 128), 0, 48, 64)
    wt_ref[...] = jnp.zeros_like(wt_ref)
    z_ref[...] = jnp.zeros_like(z_ref)
    for k2 in range(8):
        taps = w_ref[16 * k2 : 16 * k2 + 16, 0]
        pairs = taps.reshape(8, 2, 48, 48)
        tile = mm(pairs[:, 0].reshape(384, 48), left) + mm(pairs[:, 1].reshape(384, 48), right)
        tile = tile.astype(bf16)
        for p in range(8):
            wt_ref[0, 64 * k2 : 64 * k2 + 48, 128 * p : 128 * p + 128] = tile[48 * p : 48 * p + 48]
    for q in range(4):
        lo, hi = w_ref[112 - 32 * q : 128 - 32 * q, 0], w_ref[96 - 32 * q : 112 - 32 * q, 0]
        tile = mm(lo.reshape(768, 48), left) + mm(hi.reshape(768, 48), right)
        for b in range(16):
            z_ref[64 * b : 64 * b + 48, :] = tile[48 * (15 - b) : 48 * (15 - b) + 48]
        wd_ref[0, 128 * q : 128 * q + 128, :] = z_ref[...].T.astype(bf16)


def prep_weights(scal, kernel):
    return pl.pallas_call(
        prep_kernel,
        grid_spec=pltpu.PrefetchScalarGridSpec(
            num_scalar_prefetch=1,
            grid=(4,),
            in_specs=[pl.BlockSpec((128, 1, 48, 48), lambda g, s: (0, 4 * s[0] + g, 0, 0))],
            out_specs=[pl.BlockSpec((1, 512, 1024), lambda g, s: (g, 0, 0))] * 2,
            scratch_shapes=[pltpu.VMEM((1024, 128), f32)],
        ),
        out_shape=[jax.ShapeDtypeStruct((4, 512, 1024), bf16)] * 2,
        compiler_params=params(),
        name="conv_weights",
    )(scal, kernel)


def pair_slots(t_ref, rows):
    wide = jnp.concatenate([t_ref[0:rows, :], t_ref[16 : rows + 16, :]], axis=1)
    r, c = iota2((256, 128))
    out = []
    for j in range(2):
        hit = ((r < 128) & (c == r - 64 * j) & (c < 64)) | ((r >= 128) & (c - 64 == r - 128 - 64 * j) & (c >= 64))
        out.append(mm(wide, hit.astype(f32).astype(bf16)).astype(bf16))
    return out


def conv_block(p_refs, w_ref, y_ref, s_ref, n0, shift):
    lane = lax.broadcasted_iota(jnp.int32, (256, 128), 1)
    parts = []
    for j in range(2):
        lhs = jnp.concatenate(
            [p_refs[j][pl.ds(pl.multiple_of(n0 + 32 * q, 16), 272), :] for q in range(4)], axis=1
        )
        y_ref[j] = mm(lhs, w_ref[j])
        total = y_ref[j, shift : shift + 257, 0:128]
        for p in range(1, 8):
            total += y_ref[j, shift + 2 * p : shift + 2 * p + 257, 128 * p : 128 * p + 128]
        s_ref[0:257, :] = total
        here, after = s_ref[0:256, :], s_ref[1:257, :]
        if j == 0:
            parts.append(here + pltpu.roll(after, 64, 1))
        else:
            parts.append(pltpu.roll(here, 64, 1) + after)
    return jnp.where(lane < 64, parts[0], parts[1])


def conv_fwd_kernel(s_ref, c0, c1, c2, c3, w_ref, b_ref, pre_ref, x_ref, packed_ref, p0, p1, y_ref, t_ref, first):
    c = pl.program_id(0)
    me = s_ref[0]
    chunks = (c0, c1, c2, c3)
    x_ref[0, 0:64, :] = jnp.zeros((64, 128), bf16)
    x_ref[0, 1600:1664, :] = jnp.zeros((64, 128), bf16)
    x_ref[0, 1792:1936, :] = jnp.zeros((144, 128), bf16)
    top_map = spread((256, 128), 0, 96 * c)
    low_map = spread((256, 128), 64, 96 * c)
    for r in range(4):
        src = me ^ r
        top = mm(chunks[r][:, 0:256], top_map).astype(bf16)
        low = mm(chunks[r][:, 128:384], low_map).astype(bf16)
        base = pl.multiple_of(64 + FR * src, 64)
        x_ref[0, pl.ds(base, 256), :] = top
        x_ref[0, pl.ds(pl.multiple_of(base + 256, 64), 128), :] = low[:128]

        @pl.when(src == 0)
        def _():
            x_ref[0, 1664:1792, :] = low[128:]

    a, b = pair_slots(x_ref.at[0], 1920)
    p0[...] = a
    p1[...] = b
    bias = b_ref[0]

    def body(j, carry):
        n0 = pl.multiple_of(256 * j, 256)
        pre = conv_block((p0, p1), w_ref, y_ref, t_ref, n0, 0) + bias
        pre_ref[0, pl.ds(n0, 256), :] = pre
        center = x_ref[0, pl.ds(pl.multiple_of(n0 + 64, 64), 256), :].astype(f32)
        first[c, pl.ds(n0, 256), :] = (center + pre * gelu_parts(pre)).astype(bf16)
        return carry

    lax.fori_loop(0, 7, body, 0)

    @pl.when(c == 1)
    def _():
        h0, h1 = gather_slots((256, 384), 0), gather_slots((256, 384), 192)

        def rows(lo, n):
            return jnp.concatenate([first[0, lo : lo + n, :], first[1, lo : lo + n, :]], axis=1)

        packed_ref[0:768, :] = (mm(rows(0, 768), h0) + mm(rows(768, 768), h1)).astype(bf16)
        packed_ref[768:864, :] = (mm(rows(SBASE, 96), h0) + mm(rows(SBASE + 96, 96), h1)).astype(bf16)


def conv_fwd(scal, chunks, wt, bias):
    return pl.pallas_call(
        conv_fwd_kernel,
        grid=(2,),
        in_specs=[smem()]
        + [full((256, 384))] * 4
        + [pl.BlockSpec((2, 512, 1024), lambda c: (c, 0, 0)), pl.BlockSpec((1, 1, 128), lambda c: (c, 0, 0))],
        out_specs=[
            pl.BlockSpec((1, TROWS, 128), lambda c: (c, 0, 0)),
            pl.BlockSpec((1, 1936, 128), lambda c: (c, 0, 0)),
            full((864, 384)),
        ],
        out_shape=[
            jax.ShapeDtypeStruct((2, TROWS, 128), f32),
            jax.ShapeDtypeStruct((2, 1936, 128), bf16),
            jax.ShapeDtypeStruct((864, 384), bf16),
        ],
        scratch_shapes=[
            pltpu.VMEM((1920, 128), bf16),
            pltpu.VMEM((1920, 128), bf16),
            pltpu.VMEM((2, 272, 1024), f32),
            pltpu.VMEM((264, 128), f32),
            pltpu.VMEM((2, TROWS, 128), bf16),
        ],
        compiler_params=params(),
        name="conv_fwd",
    )(scal, *chunks, wt, bias)


def attn_fwd_kernel(s_ref, c0, c1, c2, c3, w_ref, b_ref, qkv_ref, ot_ref, lse_ref, rows_ref, wz, vt):
    me = s_ref[0]
    chunks = (c0, c1, c2, c3)
    wz[:, 0:64, :] = jnp.zeros((4, 64, 768), bf16)
    wz[:, 256:320, :] = jnp.zeros((4, 64, 768), bf16)
    for r in range(4):
        wz[r, 64:256, :] = w_ref[pl.ds(pl.multiple_of(192 * (me ^ r), 64), 192), :]
    bias = b_ref[...]
    for half in range(2):
        row0 = 64 * (1 - half)

        def project(start, n):
            total = bias + jnp.zeros((n, 768), f32)
            for r in range(4):
                total += mm(
                    chunks[r][pl.ds(start, n), 128 * half : 128 * half + 256], wz[r, row0 : row0 + 256, :]
                )
            return total.astype(bf16)

        def body(j, carry):
            start = pl.multiple_of(256 * j, 256)
            qkv_ref[pl.ds(pl.multiple_of(768 * half + start, 256), 256), :] = project(start, 256)
            return carry

        lax.fori_loop(0, 3, body, 0)
        qkv_ref[SLOTS + 96 * half : SLOTS + 96 * half + 96, :] = project(768, 96)
    qkv_ref[SLOTS + SROWS : TROWS, :] = jnp.zeros((TROWS - SLOTS - SROWS, 768), bf16)

    half = me >> 1
    start = pl.multiple_of(FR * (me & 1), 128)
    lane0 = pl.multiple_of(128 * half, 128)
    r_i, c_i = iota2((256, 768))
    own = jnp.zeros((FR, 768), f32)
    extra0 = jnp.zeros((96, 768), f32)
    extra1 = jnp.zeros((96, 768), f32)
    for r in range(4):
        base = 192 * (me ^ r)
        inside = (c_i >= base) & (c_i < base + 192)
        sel0 = ((c_i - base == r_i) & inside).astype(f32).astype(bf16)
        sel1 = ((c_i - base == r_i - 64) & inside).astype(f32).astype(bf16)
        mid = ((c_i - base == r_i - 64 * half) & inside).astype(f32).astype(bf16)
        own += mm(chunks[r][pl.ds(start, FR), pl.ds(lane0, 256)], mid)
        extra0 += mm(chunks[r][768:864, 0:256], sel0)
        extra1 += mm(chunks[r][768:864, 128:384], sel1)
    rows_ref[0:FR, :] = own.astype(bf16)
    rows_ref[FR : FR + 96, :] = extra0.astype(bf16)
    rows_ref[FR + 96 : FR + 192, :] = extra1.astype(bf16)

    vt[...] = qkv_ref[:, 512:704].astype(f32).T.astype(bf16)
    lse_ref[...] = jnp.zeros_like(lse_ref)
    for h in range(3):
        cols = slice(64 * h, 64 * h + 64)

        def attend(q0, key0, keys, masked):
            query = (qkv_ref[pl.ds(q0, 256), 0:256][:, cols].astype(f32) * 0.125).astype(bf16)
            key = qkv_ref[key0 : key0 + keys, 256:512][:, cols]
            scores = mm_nt(key, query)
            if masked:
                slot = lax.broadcasted_iota(jnp.int32, scores.shape, 0)
                scores = jnp.where(slot < SHORT, scores, neg_large)
            top = jnp.max(scores, axis=0, keepdims=True)
            weights = jnp.exp(scores - top)
            total = jnp.sum(weights, axis=0, keepdims=True)
            out = mm(vt[cols, key0 : key0 + keys], weights.astype(bf16))
            ot_ref[cols, pl.ds(q0, 256)] = out / total
            lse_ref[h : h + 1, pl.ds(q0, 256)] = top + jnp.log(total)

        def body(j, carry):
            attend(pl.multiple_of(256 * j, 256), 0, SLOTS, False)
            return carry

        lax.fori_loop(0, 6, body, 0)
        attend(SLOTS, SLOTS, 128, True)


def attn_fwd(scal, chunks, wqkv, bqkv):
    return pl.pallas_call(
        attn_fwd_kernel,
        in_specs=[smem()] + [vmem()] * 6,
        out_specs=[vmem()] * 4,
        out_shape=[
            jax.ShapeDtypeStruct((TROWS, 768), bf16),
            jax.ShapeDtypeStruct((CH, TROWS), f32),
            jax.ShapeDtypeStruct((8, TROWS), f32),
            jax.ShapeDtypeStruct((576, 768), bf16),
        ],
        scratch_shapes=[pltpu.VMEM((4, 320, 768), bf16), pltpu.VMEM((CH, TROWS), bf16)],
        compiler_params=params(),
        name="attn_fwd",
    )(scal, *chunks, wqkv, bqkv)


def attn_bwd_kernel(
    s_ref, qkv_ref, ot_ref, lse_ref, d0, d1, d2, d3, gs_ref, w_ref,
    dqkv_ref, g0, g1, g2, g3, sums_ref, dot_, do_, kt, delta, dqt, dk, dv,
):
    me = s_ref[0]
    parts = (d0, d1, d2, d3)
    short = jnp.zeros((CH, 256), f32)
    for r in range(4):
        src = me ^ r
        dot_[:, pl.ds(pl.multiple_of(FR * src, 128), FR)] = parts[r][:, 0:FR]
        short += parts[r][:, FR : FR + 256].astype(f32)
    dot_[:, SLOTS:TROWS] = short.astype(bf16)
    whole = dot_[...].astype(f32)
    do_[...] = whole.T.astype(bf16)
    prod = whole * ot_ref[...]
    delta[...] = jnp.zeros_like(delta)
    for h in range(3):
        delta[h : h + 1, :] = jnp.sum(prod[64 * h : 64 * h + 64], axis=0, keepdims=True)
    kt[...] = qkv_ref[:, 256:448].astype(f32).T.astype(bf16)

    for h in range(3):
        cols = slice(64 * h, 64 * h + 64)
        dk[...] = jnp.zeros_like(dk)
        dv[...] = jnp.zeros_like(dv)

        def step(q0, key0, keys, masked):
            query = qkv_ref[pl.ds(q0, 256), 0:256][:, cols]
            scaled = (query.astype(f32) * 0.125).astype(bf16)
            grad = do_[pl.ds(q0, 256), :][:, cols]
            grad_t = dot_[cols, pl.ds(q0, 256)]
            lse = lse_ref[h : h + 1, pl.ds(q0, 256)]
            dl = delta[h : h + 1, pl.ds(q0, 256)]
            grad_q = jnp.zeros((64, 256), f32)
            piece = min(keys, 512)
            for at in range(key0, key0 + keys, piece):
                key = qkv_ref[at : at + piece, 256:512][:, cols]
                val = qkv_ref[at : at + piece, 512:768][:, cols]
                probs = jnp.exp(mm_nt(key, scaled) - lse)
                if masked:
                    slot = lax.broadcasted_iota(jnp.int32, probs.shape, 0)
                    probs = jnp.where(slot < SHORT, probs, 0.0)
                grad_p = mm(val, grad_t)
                grad_s = (probs * (grad_p - dl)).astype(bf16)
                dv[at : at + piece, :] += mm(probs.astype(bf16), grad)
                dk[at : at + piece, :] += mm(grad_s, query)
                grad_q += mm(kt[cols, at : at + piece], grad_s)
            dqt[cols, pl.ds(q0, 256)] = grad_q * 0.125

        def body(j, carry):
            step(pl.multiple_of(256 * j, 256), 0, SLOTS, False)
            return carry

        lax.fori_loop(0, 6, body, 0)
        step(SLOTS, SLOTS, 128, True)
        zeros = jnp.zeros((TROWS, 64), f32)
        if h == 0:
            keep_k, keep_v = [], []
        keep_k.append((dk[...] * 0.125).astype(bf16))
        keep_v.append(dv[...].astype(bf16))
    dqkv_ref[:, 0:192] = dqt[...].T.astype(bf16)
    dqkv_ref[:, 192:256] = jnp.zeros((TROWS, 64), bf16)
    dqkv_ref[:, 256:512] = jnp.concatenate(keep_k + [zeros.astype(bf16)], axis=1)
    dqkv_ref[:, 512:768] = jnp.concatenate(keep_v + [zeros.astype(bf16)], axis=1)
    sums_ref[...] = jnp.sum(dqkv_ref[...].astype(f32), axis=0, keepdims=True)
    outs = (g0, g1, g2, g3)
    lanes = pl.multiple_of(FR * me, 128)
    for r in range(4):
        rows = pl.ds(pl.multiple_of(192 * (me ^ r), 64), 192)
        part = mm_nt(w_ref[rows, :], dqkv_ref[...])
        outs[r][...] = part.astype(bf16)
        own = gs_ref[rows, 0:FR].astype(f32)
        outs[r][:, pl.ds(lanes, FR)] = (outs[r][:, pl.ds(lanes, FR)].astype(f32) + own).astype(bf16)
        outs[r][:, SLOTS:TROWS] = (part[:, SLOTS:TROWS] + gs_ref[rows, FR : FR + 256].astype(f32)).astype(bf16)


def attn_bwd(scal, qkv, ot, lse, dparts, gst, wqkv):
    return pl.pallas_call(
        attn_bwd_kernel,
        in_specs=[smem()] + [vmem()] * 9,
        out_specs=[vmem()] * 6,
        out_shape=[jax.ShapeDtypeStruct((TROWS, 768), bf16)]
        + [jax.ShapeDtypeStruct((CH, TROWS), bf16)] * 4
        + [jax.ShapeDtypeStruct((1, 768), f32)],
        scratch_shapes=[
            pltpu.VMEM((CH, TROWS), bf16),
            pltpu.VMEM((TROWS, CH), bf16),
            pltpu.VMEM((CH, TROWS), bf16),
            pltpu.VMEM((8, TROWS), f32),
            pltpu.VMEM((CH, TROWS), f32),
            pltpu.VMEM((TROWS, 64), f32),
            pltpu.VMEM((TROWS, 64), f32),
        ],
        compiler_params=params(),
        name="attn_bwd",
    )(scal, qkv, ot, lse, *dparts, gst, wqkv)


def qkv_wgrad_kernel(c0, c1, c2, c3, d_ref, o0, o1, o2, o3):
    for chunk, out in zip((c0, c1, c2, c3), (o0, o1, o2, o3)):
        turned = chunk[...].astype(f32).T.astype(bf16)
        out[...] = (
            mm(turned[0:192, 0:768], d_ref[0:768, :])
            + mm(turned[0:192, 768:864], d_ref[SLOTS : SLOTS + 96, :])
            + mm(turned[192:384, 0:768], d_ref[768:1536, :])
            + mm(turned[192:384, 768:864], d_ref[SLOTS + 96 : SLOTS + 192, :])
        ).astype(bf16)


def qkv_wgrad(chunks, dqkv):
    return pl.pallas_call(
        qkv_wgrad_kernel,
        in_specs=[vmem()] * 5,
        out_specs=[vmem()] * 4,
        out_shape=[jax.ShapeDtypeStruct((192, 768), bf16)] * 4,
        compiler_params=params(),
        name="qkv_wgrad",
    )(*chunks, dqkv)


def conv_bwd_kernel(
    s_ref, c0, c1, c2, c3, pre_ref, x_ref, wd_ref,
    gk_ref, gb_ref, f0, f1, f2, f3,
    gf, gp, g_ref, p0, p1, y_ref, t_ref, bb, g2, xt, fg,
):
    c = pl.program_id(0)
    me = s_ref[0]
    total = c0[...].astype(f32) + c1[...].astype(f32) + c2[...].astype(f32) + c3[...].astype(f32)
    pad = jnp.zeros((16, TROWS), f32)
    rows = jnp.concatenate([total[0:48], pad, total[48:96], pad], axis=0)
    gf[0:SLOTS, :] = rows[:, 0:SLOTS].T
    gf[SLOTS:SBASE, :] = jnp.zeros((SBASE - SLOTS, 128), f32)
    gf[SBASE:TROWS, :] = rows[:, SLOTS:TROWS].T[0 : TROWS - SBASE]
    g_ref[0:64, :] = jnp.zeros((64, 128), bf16)
    g_ref[1856:1936, :] = jnp.zeros((80, 128), bf16)
    gp[0:16, :] = jnp.zeros((16, 128), f32)
    gb_ref[...] = jnp.zeros_like(gb_ref)

    def front(j, carry):
        n0 = pl.multiple_of(256 * j, 256)
        pre = pre_ref[0, pl.ds(n0, 256), :]
        slope = gelu_parts(pre) + pre * density(pre)
        grad = (gf[pl.ds(n0, 256), :] * slope).astype(bf16)
        wide = grad.astype(f32)
        gb_ref[0] += jnp.sum(wide, axis=0, keepdims=True)
        row = n0 + lax.broadcasted_iota(jnp.int32, (256, 128), 0)
        wide = jnp.where(row < SBASE + UNIQUE, wide, 0.0)
        gp[pl.ds(pl.multiple_of(n0 + 16, 16), 256), :] = wide
        g_ref[pl.ds(pl.multiple_of(n0 + 64, 64), 256), :] = wide.astype(bf16)
        return carry

    lax.fori_loop(0, 7, front, 0)

    lane = lax.broadcasted_iota(jnp.int32, (TROWS, 128), 1)
    here, before = gp[16 : 16 + TROWS, :], gp[15 : 15 + TROWS, :]
    a, b = pair_slots(x_ref.at[0], 1920)
    p0[...] = a
    p1[...] = b
    pack0, pack1 = gather_slots((256, 384), 0), gather_slots((256, 384), 192)
    for j in range(2):
        bb[0:16, :] = jnp.zeros((16, 128), f32)
        if j == 0:
            bb[16 : 16 + TROWS, :] = jnp.where(lane < 64, here, pltpu.roll(before, 64, 1))
        else:
            bb[16 : 16 + TROWS, :] = jnp.where(lane < 64, pltpu.roll(here, 64, 1), before)
        for p in range(8):
            g2[:, 128 * p : 128 * p + 128] = bb[16 - 2 * p : 16 - 2 * p + TROWS, :].astype(bf16)
        slots = (p0, p1)[j]
        for q in range(4):
            xt[128 * q : 128 * q + 128, :] = slots[32 * q : 32 * q + TROWS, :].astype(f32).T.astype(bf16)

        def body(m, carry):
            lhs = xt[pl.ds(pl.multiple_of(128 * m, 128), 128), :]
            for half in range(2):
                base = 512 * half
                left = mm(lhs, g2[:, base : base + 256]).astype(bf16)
                right = mm(lhs, g2[:, base + 256 : base + 512]).astype(bf16)
                packed = (mm(left, pack0) + mm(right, pack1)).astype(bf16)
                for i in range(2):
                    at = pl.multiple_of(96 * m + 48 * i, 16)
                    gk_ref[j, pl.ds(at, 48), 384 * half : 384 * half + 384] = packed[64 * i : 64 * i + 48]
            return carry

        lax.fori_loop(0, 4, body, 0)

    a, b = pair_slots(g_ref, 1920)
    p0[...] = a
    p1[...] = b

    def back(j, carry):
        n0 = pl.multiple_of(256 * j, 256)
        value = conv_block((p0, p1), wd_ref, y_ref, t_ref, n0, 1) + gf[pl.ds(n0, 256), :]
        fg[c, pl.ds(n0, 256), :] = value.astype(bf16)
        return carry

    lax.fori_loop(0, 7, back, 0)

    @pl.when(c == 1)
    def _():
        def rows_of(lo, n):
            return jnp.concatenate([fg[0, lo : lo + n, :], fg[1, lo : lo + n, :]], axis=1)

        for d in range(4):
            low = jnp.concatenate([rows_of(FR * d + 256, 128), rows_of(SBASE, 128)], axis=0)
            chunk = (mm(rows_of(FR * d, 256), pack0) + mm(low, pack1)).astype(bf16)
            for r in range(4):

                @pl.when((me ^ d) == r)
                def _():
                    (f0, f1, f2, f3)[r][...] = chunk


def conv_bwd(scal, parts, pre, xp, wd):
    return pl.pallas_call(
        conv_bwd_kernel,
        grid=(2,),
        in_specs=[smem()]
        + [pl.BlockSpec((96, TROWS), lambda c: (c, 0))] * 4
        + [
            pl.BlockSpec((1, TROWS, 128), lambda c: (c, 0, 0)),
            pl.BlockSpec((1, 1936, 128), lambda c: (c, 0, 0)),
            pl.BlockSpec((2, 512, 1024), lambda c: (c, 0, 0)),
        ],
        out_specs=[
            pl.BlockSpec((2, 384, 768), lambda c: (c, 0, 0)),
            pl.BlockSpec((1, 1, 128), lambda c: (c, 0, 0)),
        ]
        + [full((256, 384))] * 4,
        out_shape=[jax.ShapeDtypeStruct((4, 384, 768), bf16), jax.ShapeDtypeStruct((2, 1, 128), f32)]
        + [jax.ShapeDtypeStruct((256, 384), bf16)] * 4,
        scratch_shapes=[
            pltpu.VMEM((TROWS, 128), f32),
            pltpu.VMEM((16 + TROWS, 128), f32),
            pltpu.VMEM((1936, 128), bf16),
            pltpu.VMEM((1920, 128), bf16),
            pltpu.VMEM((1920, 128), bf16),
            pltpu.VMEM((2, 272, 1024), f32),
            pltpu.VMEM((264, 128), f32),
            pltpu.VMEM((16 + TROWS, 128), f32),
            pltpu.VMEM((TROWS, 1024), bf16),
            pltpu.VMEM((512, TROWS), bf16),
            pltpu.VMEM((2, TROWS, 128), bf16),
        ],
        compiler_params=params(),
        name="conv_bwd",
    )(scal, *parts, pre, xp, wd)


def unpack_frames_kernel(s_ref, c0, c1, c2, c3, o_ref):
    me, li = s_ref[0], s_ref[1]
    r_i, c_i = iota2((256, 768))
    top = jnp.zeros((256, 768), f32)
    low = jnp.zeros((256, 768), f32)
    for r, chunk in enumerate((c0, c1, c2, c3)):
        base = 192 * (me ^ r)
        inside = (c_i >= base) & (c_i < base + 192)
        top += mm(chunk[:, 0:256], ((c_i - base == r_i) & inside).astype(f32).astype(bf16))
        low += mm(chunk[:, 128:384], ((c_i - base == r_i - 64) & inside).astype(f32).astype(bf16))
    o_ref[li, 0:256, :] = top.astype(bf16)
    o_ref[li, 256:384, :] = low[0:128].astype(bf16)
    slot = me * FR + lax.broadcasted_iota(jnp.int32, (128, 768), 0)
    o_ref[1 - li, 0:128, :] = jnp.where(slot < SHORT, low[128:], 0.0).astype(bf16)
    o_ref[1 - li, 128:384, :] = jnp.zeros((256, 768), bf16)


def unpack_frames(scal, chunks):
    return pl.pallas_call(
        unpack_frames_kernel,
        in_specs=[smem()] + [vmem()] * 4,
        out_specs=vmem(),
        out_shape=jax.ShapeDtypeStruct((2, FR, 768), bf16),
        compiler_params=params(),
        name="unpack_frames",
    )(scal, *chunks)


def kernel_out_kernel(x_ref, o_ref):
    for k2 in range(2):
        for b in range(16):
            lane0 = (48 * b) // 128 * 128
            skip = 48 * b - lane0
            wide = 256 if skip + 48 > 128 else 128
            move = place((wide, 48), skip, skip + 48, 0)
            o_ref[16 * k2 + b, 0] = mm(x_ref[0, k2, :, lane0 : lane0 + wide], move)


def kernel_out(x):
    return pl.pallas_call(
        kernel_out_kernel,
        grid=(16,),
        in_specs=[pl.BlockSpec((1, 2, 48, 768), lambda g: (g, 0, 0, 0))],
        out_specs=pl.BlockSpec((32, 1, 48, 48), lambda g: (0, g, 0, 0)),
        out_shape=jax.ShapeDtypeStruct((32, 16, 48, 48), f32),
        compiler_params=params(),
        name="kernel_grad_out",
    )(x)


def layer_norm(value, gain, shift):
    center = value - jnp.mean(value, axis=-1, keepdims=True)
    spread_ = jnp.mean(center * center, axis=-1, keepdims=True)
    return center * lax.rsqrt(spread_ + eps_norm) * gain + shift


def gelu_exact(value):
    return jax.nn.gelu(value, approximate=False)


def from_others(chunks):
    moved = [lax.ppermute(chunks[r], "wide", [(i, i ^ r) for i in range(4)]) for r in (3, 1, 2)]
    return [chunks[0], moved[1], moved[2], moved[0]]


def gathered(chunk):
    return from_others([chunk] * 4)


def on_device(
    frames_in, lengths, kernel, conv_bias, w_query, b_query, w_key, w_value, b_value, w_out, b_out,
    gain_one, shift_one, w_up, b_up, w_down, b_down, gain_two, shift_two, out_grad,
):
    me = lax.axis_index("wide")
    li = jnp.where(lengths[0] >= lengths[1], 0, 1).astype(jnp.int32)
    scal = jnp.stack([me.astype(jnp.int32), li])
    frames = from_others(pack_frames(scal, frames_in))

    wt, wd = prep_weights(scal, kernel)

    def own(v):
        return lax.dynamic_slice_in_dim(v, me * CH, CH, axis=v.ndim - 1)

    def three(a, b, c):
        gap = [(0, 0)] * (a.ndim - 1) + [(0, 64)]
        return jnp.concatenate([jnp.pad(a, gap), jnp.pad(b, gap), jnp.pad(c, gap)], axis=-1)

    wqkv = three(own(w_query), own(w_key), own(w_value))
    bqkv = three(own(b_query), jnp.zeros((CH,), bf16), own(b_value)).astype(f32)[None]
    bias = jnp.pad(own(conv_bias).astype(f32).reshape(2, 2, 48), ((0, 0), (0, 0), (0, 16))).reshape(2, 1, 128)

    pre, xp, packed = conv_fwd(scal, frames, wt, bias)
    first = gathered(packed)
    qkv, mixed_t, lse, rows = attn_fwd(scal, first, wqkv, bqkv)
    low_t = mixed_t.astype(bf16)

    def rel_rows(v):
        return jnp.concatenate([lax.dynamic_slice_in_dim(v, (me ^ r) * CH, CH, axis=0) for r in range(4)], axis=0)

    w_out_rel = rel_rows(w_out)

    def mixed_for(r):
        return jnp.concatenate(
            [lax.dynamic_slice_in_dim(low_t, (me ^ r) * FR, FR, axis=1), low_t[:, SLOTS:]], axis=1
        )

    mix = jnp.concatenate(from_others([mixed_for(r) for r in range(4)]), axis=0)

    slot = jnp.arange(FR)[:, None]
    unique = (slot < UNIQUE) & (me == 0)

    def expand(v):
        tail = v[FR : FR + SROWS]
        grown = jnp.concatenate([tail, jnp.zeros((FR - SROWS, tail.shape[1]), tail.dtype)], axis=0)
        return jnp.concatenate([v[:FR], jnp.where(unique, grown, tail[UNIQUE : UNIQUE + 1])], axis=0)

    def collapse(v):
        rest = jnp.sum(jnp.where(unique, 0.0, v[FR:]), axis=0, keepdims=True)
        tail = jnp.where(unique, v[FR:], 0.0)[:UNIQUE]
        return jnp.concatenate([v[:FR], tail, rest, jnp.zeros((640 - FR - UNIQUE - 1, v.shape[1]), v.dtype)], axis=0)

    wide32 = lambda v: v.astype(f32)
    attn_out = lax.dot_general(mix, w_out_rel, (((0,), (0,)), ((), ())), preferred_element_type=f32) + wide32(b_out)
    sum_one = expand(wide32(rows)) + expand(attn_out)
    norm_one, pull_one = jax.vjp(layer_norm, sum_one, wide32(gain_one), wide32(shift_one))
    norm_low = norm_one.astype(bf16)
    up_pre = mm(norm_low, w_up) + wide32(b_up)
    up_act, pull_up = jax.vjp(gelu_exact, up_pre)
    up_low = up_act.astype(bf16)
    down_out = mm(up_low, w_down) + wide32(b_down)
    layer_out, pull_two = jax.vjp(layer_norm, norm_one + down_out, wide32(gain_two), wide32(shift_two))
    cot = jnp.where(li == 0, out_grad.reshape(2 * FR, 768), jnp.concatenate([out_grad[1], out_grad[0]], axis=0))
    grad_sum_two, grad_gain_two, grad_shift_two = pull_two(wide32(cot))
    grad_down = grad_sum_two.astype(bf16)
    tn = lambda a, b: lax.dot_general(a, b, (((0,), (0,)), ((), ())), preferred_element_type=f32)
    grad_w_down = tn(up_low, grad_down)
    grad_b_down = jnp.sum(wide32(grad_down), axis=0)
    grad_up = pull_up(mm_nt(grad_down, w_down))[0].astype(bf16)
    grad_w_up = tn(norm_low, grad_up)
    grad_b_up = jnp.sum(wide32(grad_up), axis=0)
    grad_norm_one = grad_sum_two + mm_nt(grad_up, w_up)
    grad_sum_one, grad_gain_one, grad_shift_one = pull_one(grad_norm_one)
    grad_attn = grad_sum_one.astype(bf16)
    grad_b_out = jnp.sum(wide32(grad_attn), axis=0)
    grad_attn_c = collapse(wide32(grad_attn)).astype(bf16)
    grad_w_out_rel = mm(mix, grad_attn_c)
    grad_mix = mm_nt(w_out_rel, grad_attn_c).astype(bf16)
    dparts = from_others([grad_mix[CH * r : CH * r + CH] for r in range(4)])
    gst = collapse(grad_sum_one).astype(bf16).T
    dqkv, g0, g1, g2, g3, sums = attn_bwd(scal, qkv, mixed_t, lse, dparts, gst, wqkv)
    gparts = from_others([g0, g1, g2, g3])
    gk, gcb, f0, f1, f2, f3 = conv_bwd(scal, gparts, pre, xp, wd)
    frames_grad = unpack_frames(scal, from_others([f0, f1, f2, f3]))
    qkv_chunks = qkv_wgrad(first, dqkv)

    def over_narrow(v):
        return lax.psum(v.astype(bf16), "narrow").astype(f32)

    def scatter(v):
        return over_narrow(lax.psum_scatter(v.astype(bf16), "wide", scatter_dimension=0, tiled=True))

    gk4 = gk.reshape(4, 4, 96, 768)
    gk_rel = from_others([lax.dynamic_index_in_dim(gk4, me ^ r, 1, keepdims=False) for r in range(4)])
    order = jnp.stack([me ^ j for j in range(4)])

    def by_source(parts):
        return jnp.take(jnp.stack(parts), order, axis=0)

    gk_all = lax.psum(by_source(gk_rel), "narrow").reshape(16, 2, 48, 768)
    grad_kernel = kernel_out(gk_all)
    qkv_all = lax.psum(by_source(from_others(qkv_chunks)), "narrow").astype(f32)

    def columns(k):
        return jnp.transpose(qkv_all[:, :, 256 * k : 256 * k + 192], (1, 0, 2)).reshape(CH, 768)

    def own_vec(v):
        return over_narrow(v)

    grad_w_out = over_narrow(
        sum(wide32(p) for p in from_others([grad_w_out_rel[CH * r : CH * r + CH].astype(bf16) for r in range(4)]))
    )
    gcb_v = gcb.reshape(4, 64)[:, :48].reshape(CH)
    result = layer_out.astype(bf16)
    layer_rows = jnp.where(li == 0, result, jnp.concatenate([result[FR:], result[:FR]], axis=0)).reshape(2, FR, 768)
    return (
        layer_rows,
        frames_grad,
        grad_kernel,
        own_vec(gcb_v),
        columns(0),
        own_vec(sums[0, 0:192]),
        columns(1),
        columns(2),
        own_vec(sums[0, 512:704]),
        grad_w_out,
        scatter(grad_b_out),
        scatter(grad_gain_one),
        scatter(grad_shift_one),
        scatter(grad_w_up),
        scatter(grad_b_up),
        scatter(grad_w_down),
        scatter(grad_b_down),
        scatter(grad_gain_two),
        scatter(grad_shift_two),
    )


def with_halo(x, sides, width):
    for axis, dim in sides:
        count, length = (lax.axis_size(axis), x.shape[dim])
        up = [(i, (i + 1) % count) for i in range(count - 1)]
        down = [(j, i) for i, j in up]
        last = lax.slice_in_dim(x, length - width, length, axis=dim)
        initial = lax.slice_in_dim(x, 0, width, axis=dim)
        before = lax.ppermute(last, axis, up)
        after = lax.ppermute(initial, axis, down)
        x = jnp.concatenate([before, x, after], axis=dim)
    return x


def project(rows_in, weight):
    return jnp.einsum("cfd,de->cfe", rows_in, weight, preferred_element_type=jnp.float32)


def project_back(grad_in, weight):
    return jnp.einsum("cfe,de->cfd", grad_in, weight, preferred_element_type=jnp.float32)


def weight_grad(rows_in, grad_in):
    return jnp.einsum("cfd,cfe->de", rows_in, grad_in, preferred_element_type=jnp.float32)


def row_total(grad_in):
    return jnp.sum(grad_in.astype(jnp.float32), axis=(0, 1))


def head_view(rows_in):
    return rows_in.reshape(rows_in.shape[0], rows_in.shape[1], HEADS, rows_in.shape[2] // HEADS)


def conv_apply(padded, weight, frames):
    kernel_span, groups, inner_ch, outer_ch = weight.shape
    taps_weight = jnp.transpose(weight, (0, 2, 1, 3)).reshape(
        kernel_span, inner_ch, groups * outer_ch
    )
    result = lax.conv_general_dilated(
        padded,
        taps_weight,
        (1,),
        "VALID",
        dimension_numbers=("NWC", "WIO", "NWC"),
        feature_group_count=groups,
        preferred_element_type=jnp.float32,
    )
    return result[:, :frames, :]


def conv_weight_grad(padded, grad_in, kernel_shape):
    kernel_span, groups, inner_ch, outer_ch = kernel_shape
    result = lax.conv_general_dilated(
        padded,
        grad_in,
        (1,),
        "VALID",
        dimension_numbers=("CWN", "IWO", "NWC"),
        batch_group_count=groups,
        preferred_element_type=jnp.float32,
    )
    result = result[:, :kernel_span, :].reshape(inner_ch, kernel_span, groups, outer_ch)
    return jnp.transpose(result, (1, 2, 0, 3))


def key_valid_at(lengths, first_row, row_count):
    return (first_row + jnp.arange(row_count, dtype=jnp.int32))[None, :] < lengths[:, None]


def masked_scores(query_h, keys_h, valid_keys, score_scale):
    scores = (
        jnp.einsum("cqhd,ckhd->cqhk", query_h, keys_h, preferred_element_type=jnp.float32)
        * score_scale
    )
    return jnp.where(valid_keys[:, None, None, :], scores, neg_large)


def block_terms(query_h, grad_h, lse_rows, delta_rows, keys_h, values_h, valid_keys, score_scale):
    scores = masked_scores(query_h, keys_h, valid_keys, score_scale)
    probs = jnp.where(valid_keys[:, None, None, :], jnp.exp(scores - lse_rows[..., None]), 0.0)
    grad_probs = jnp.einsum("cqhd,ckhd->cqhk", grad_h, values_h, preferred_element_type=jnp.float32)
    grad_scores = (probs * (grad_probs - delta_rows[..., None])).astype(jnp.bfloat16)
    results = []
    results.append(
        jnp.einsum("cqhk,ckhd->cqhd", grad_scores, keys_h, preferred_element_type=jnp.float32)
        * score_scale
    )
    results.append(
        jnp.einsum("cqhk,cqhd->ckhd", grad_scores, query_h, preferred_element_type=jnp.float32)
        * score_scale
    )
    results.append(
        jnp.einsum(
            "cqhk,cqhd->ckhd",
            probs.astype(jnp.bfloat16),
            grad_h,
            preferred_element_type=jnp.float32,
        )
    )
    return tuple(results)


def on_device_any(
    frames_in,
    lengths,
    kernel,
    conv_bias,
    w_query,
    b_query,
    w_key,
    w_value,
    b_value,
    w_out,
    b_out,
    gain_one,
    shift_one,
    w_up,
    b_up,
    w_down,
    b_down,
    gain_two,
    shift_two,
    out_grad,
):
    clip_count, frames, width = frames_in.shape
    head_dim = width // HEADS
    score_scale = head_dim ** (-0.5)
    half_span = kernel.shape[0] // 2
    wide_size = lax.axis_size("wide")
    positions = lax.axis_index("wide") * frames + jnp.arange(frames, dtype=jnp.int32)
    frame_valid = positions[None, :] < lengths[:, None]
    masked = jnp.where(frame_valid[..., None], frames_in, jnp.zeros((), jnp.bfloat16))
    padded = with_halo(masked, (("wide", 1),), half_span)
    pre_act = conv_apply(padded, kernel, frames) + conv_bias.astype(jnp.float32)
    first_act, pull_first = jax.vjp(gelu_exact, pre_act)
    first_out = masked.astype(jnp.float32) + first_act
    first_low = first_out.astype(jnp.bfloat16)
    query_rows = (project(first_low, w_query) + b_query.astype(jnp.float32)).astype(jnp.bfloat16)
    key_rows = project(first_low, w_key).astype(jnp.bfloat16)
    value_rows = (project(first_low, w_value) + b_value.astype(jnp.float32)).astype(jnp.bfloat16)
    query_h = head_view(query_rows)
    per_step = max(1, min(wide_size, 512 // frames))
    while wide_size % per_step:
        per_step -= 1
    run_max = jnp.full((clip_count, frames, HEADS), neg_large, jnp.float32)
    run_acc = jnp.zeros((clip_count, frames, HEADS, head_dim), jnp.float32)
    keys_p = lax.all_gather(key_rows, "wide", axis=1, tiled=True)
    values_p = lax.all_gather(value_rows, "wide", axis=1, tiled=True)
    row_count = keys_p.shape[1]
    valid_keys = key_valid_at(lengths, jnp.int32(0), row_count)
    scores = masked_scores(query_h, head_view(keys_p), valid_keys, score_scale)
    new_max = jnp.maximum(run_max, jnp.max(scores, axis=-1))
    weights = jnp.where(valid_keys[:, None, None, :], jnp.exp(scores - new_max[..., None]), 0.0)
    factor = jnp.exp(run_max - new_max)
    run_sum = jnp.sum(weights, axis=-1)
    run_acc = run_acc * factor[..., None] + jnp.einsum(
        "cqhk,ckhd->cqhd",
        weights.astype(jnp.bfloat16),
        head_view(values_p),
        preferred_element_type=jnp.float32,
    )
    run_max, run_sum, run_acc = (new_max, run_sum, run_acc)
    lse_rows = run_max + jnp.log(run_sum)
    mixed_heads = run_acc / run_sum[..., None]
    mixed_low = mixed_heads.reshape(clip_count, frames, width).astype(jnp.bfloat16)
    attn_out = project(mixed_low, w_out) + b_out.astype(jnp.float32)
    sum_one = first_out + attn_out
    norm_one, pull_one = jax.vjp(
        layer_norm, sum_one, gain_one.astype(jnp.float32), shift_one.astype(jnp.float32)
    )
    norm_low = norm_one.astype(jnp.bfloat16)
    up_pre = project(norm_low, w_up) + b_up.astype(jnp.float32)
    up_act, pull_up = jax.vjp(gelu_exact, up_pre)
    up_low = up_act.astype(jnp.bfloat16)
    down_out = project(up_low, w_down) + b_down.astype(jnp.float32)
    sum_two = norm_one + down_out
    layer_out, pull_two = jax.vjp(
        layer_norm, sum_two, gain_two.astype(jnp.float32), shift_two.astype(jnp.float32)
    )
    grad_sum_two, grad_gain_two, grad_shift_two = pull_two(out_grad.astype(jnp.float32))
    grad_down = grad_sum_two.astype(jnp.bfloat16)
    grad_w_down = weight_grad(up_low, grad_down)
    grad_b_down = row_total(grad_down)
    grad_up = pull_up(project_back(grad_down, w_down))[0].astype(jnp.bfloat16)
    grad_w_up = weight_grad(norm_low, grad_up)
    grad_b_up = row_total(grad_up)
    grad_norm_one = grad_sum_two + project_back(grad_up, w_up)
    grad_sum_one, grad_gain_one, grad_shift_one = pull_one(grad_norm_one)
    grad_attn = grad_sum_one.astype(jnp.bfloat16)
    grad_w_out = weight_grad(mixed_low, grad_attn)
    grad_b_out = row_total(grad_attn)
    grad_mixed = project_back(grad_attn, w_out).astype(jnp.bfloat16)
    grad_h = head_view(grad_mixed)
    delta_rows = jnp.sum(grad_h.astype(jnp.float32) * mixed_heads, axis=-1)
    total_slots = wide_size * frames
    first_row = jnp.int32(0)
    grad_q = jnp.zeros((clip_count, frames, HEADS, head_dim), jnp.float32)
    grad_k_all = jnp.zeros((clip_count, total_slots, width), jnp.float32)
    grad_v_all = jnp.zeros((clip_count, total_slots, width), jnp.float32)
    keys_p = lax.all_gather(key_rows, "wide", axis=1, tiled=True)
    values_p = lax.all_gather(value_rows, "wide", axis=1, tiled=True)
    row_count = keys_p.shape[1]
    valid_keys = key_valid_at(lengths, first_row, row_count)
    part_q, part_k, part_v = block_terms(
        query_h,
        grad_h,
        lse_rows,
        delta_rows,
        head_view(keys_p),
        head_view(values_p),
        valid_keys,
        score_scale,
    )
    old_k = lax.dynamic_slice_in_dim(grad_k_all, first_row, row_count, 1)
    old_v = lax.dynamic_slice_in_dim(grad_v_all, first_row, row_count, 1)
    grad_k_all = lax.dynamic_update_slice_in_dim(
        grad_k_all, old_k + part_k.reshape(clip_count, row_count, width), first_row, 1
    )
    grad_v_all = lax.dynamic_update_slice_in_dim(
        grad_v_all, old_v + part_v.reshape(clip_count, row_count, width), first_row, 1
    )
    grad_k_own, grad_v_own = (
        lax.psum_scatter(
            grad_k_all.astype(jnp.bfloat16), "wide", scatter_dimension=1, tiled=True
        ).astype(jnp.float32),
        lax.psum_scatter(
            grad_v_all.astype(jnp.bfloat16), "wide", scatter_dimension=1, tiled=True
        ).astype(jnp.float32),
    )
    grad_q_low = (grad_q + part_q).reshape(clip_count, frames, width).astype(jnp.bfloat16)
    grad_k_low = grad_k_own.astype(jnp.bfloat16)
    grad_v_low = grad_v_own.astype(jnp.bfloat16)
    grad_w_query = weight_grad(first_low, grad_q_low)
    grad_b_query = row_total(grad_q_low)
    grad_w_key = weight_grad(first_low, grad_k_low)
    grad_w_value = weight_grad(first_low, grad_v_low)
    grad_b_value = row_total(grad_v_low)
    grad_first = (
        grad_sum_one
        + project_back(grad_q_low, w_query)
        + project_back(grad_k_low, w_key)
        + project_back(grad_v_low, w_value)
    )
    grad_pre = pull_first(grad_first)[0].astype(jnp.bfloat16)
    grad_conv_bias = row_total(grad_pre)
    grad_kernel = conv_weight_grad(padded, grad_pre, kernel.shape)
    grad_padded = with_halo(grad_pre, (("wide", 1),), half_span)
    flipped = jnp.transpose(kernel[::-1], (0, 1, 3, 2))
    grad_masked = grad_first + conv_apply(grad_padded[:, 1:], flipped, frames)
    frames_grad = jnp.where(frame_valid[..., None], grad_masked, 0.0).astype(jnp.bfloat16)
    shards = (
        lax.psum_scatter(
            grad_kernel.astype(jnp.bfloat16), "wide", scatter_dimension=0, tiled=True
        ).astype(jnp.float32),
        lax.psum_scatter(
            grad_conv_bias.astype(jnp.bfloat16), "wide", scatter_dimension=0, tiled=True
        ).astype(jnp.float32),
        lax.psum_scatter(
            grad_w_query.astype(jnp.bfloat16), "wide", scatter_dimension=0, tiled=True
        ).astype(jnp.float32),
        lax.psum_scatter(
            grad_b_query.astype(jnp.bfloat16), "wide", scatter_dimension=0, tiled=True
        ).astype(jnp.float32),
        lax.psum_scatter(
            grad_w_key.astype(jnp.bfloat16), "wide", scatter_dimension=0, tiled=True
        ).astype(jnp.float32),
        lax.psum_scatter(
            grad_w_value.astype(jnp.bfloat16), "wide", scatter_dimension=0, tiled=True
        ).astype(jnp.float32),
        lax.psum_scatter(
            grad_b_value.astype(jnp.bfloat16), "wide", scatter_dimension=0, tiled=True
        ).astype(jnp.float32),
        lax.psum_scatter(
            grad_w_out.astype(jnp.bfloat16), "wide", scatter_dimension=0, tiled=True
        ).astype(jnp.float32),
        lax.psum_scatter(
            grad_b_out.astype(jnp.bfloat16), "wide", scatter_dimension=0, tiled=True
        ).astype(jnp.float32),
        lax.psum_scatter(
            grad_gain_one.astype(jnp.bfloat16), "wide", scatter_dimension=0, tiled=True
        ).astype(jnp.float32),
        lax.psum_scatter(
            grad_shift_one.astype(jnp.bfloat16), "wide", scatter_dimension=0, tiled=True
        ).astype(jnp.float32),
        lax.psum_scatter(
            grad_w_up.astype(jnp.bfloat16), "wide", scatter_dimension=0, tiled=True
        ).astype(jnp.float32),
        lax.psum_scatter(
            grad_b_up.astype(jnp.bfloat16), "wide", scatter_dimension=0, tiled=True
        ).astype(jnp.float32),
        lax.psum_scatter(
            grad_w_down.astype(jnp.bfloat16), "wide", scatter_dimension=0, tiled=True
        ).astype(jnp.float32),
        lax.psum_scatter(
            grad_b_down.astype(jnp.bfloat16), "wide", scatter_dimension=0, tiled=True
        ).astype(jnp.float32),
        lax.psum_scatter(
            grad_gain_two.astype(jnp.bfloat16), "wide", scatter_dimension=0, tiled=True
        ).astype(jnp.float32),
        lax.psum_scatter(
            grad_shift_two.astype(jnp.bfloat16), "wide", scatter_dimension=0, tiled=True
        ).astype(jnp.float32),
    )
    totals = (
        lax.psum(shards[0].astype(jnp.bfloat16), "narrow").astype(jnp.float32),
        lax.psum(shards[1].astype(jnp.bfloat16), "narrow").astype(jnp.float32),
        lax.psum(shards[2].astype(jnp.bfloat16), "narrow").astype(jnp.float32),
        lax.psum(shards[3].astype(jnp.bfloat16), "narrow").astype(jnp.float32),
        lax.psum(shards[4].astype(jnp.bfloat16), "narrow").astype(jnp.float32),
        lax.psum(shards[5].astype(jnp.bfloat16), "narrow").astype(jnp.float32),
        lax.psum(shards[6].astype(jnp.bfloat16), "narrow").astype(jnp.float32),
        lax.psum(shards[7].astype(jnp.bfloat16), "narrow").astype(jnp.float32),
        lax.psum(shards[8].astype(jnp.bfloat16), "narrow").astype(jnp.float32),
        lax.psum(shards[9].astype(jnp.bfloat16), "narrow").astype(jnp.float32),
        lax.psum(shards[10].astype(jnp.bfloat16), "narrow").astype(jnp.float32),
        lax.psum(shards[11].astype(jnp.bfloat16), "narrow").astype(jnp.float32),
        lax.psum(shards[12].astype(jnp.bfloat16), "narrow").astype(jnp.float32),
        lax.psum(shards[13].astype(jnp.bfloat16), "narrow").astype(jnp.float32),
        lax.psum(shards[14].astype(jnp.bfloat16), "narrow").astype(jnp.float32),
        lax.psum(shards[15].astype(jnp.bfloat16), "narrow").astype(jnp.float32),
        lax.psum(shards[16].astype(jnp.bfloat16), "narrow").astype(jnp.float32),
    )
    return (
        layer_out.astype(jnp.bfloat16),
        frames_grad,
        totals[0],
        totals[1],
        totals[2],
        totals[3],
        totals[4],
        totals[5],
        totals[6],
        totals[7],
        totals[8],
        totals[9],
        totals[10],
        totals[11],
        totals[12],
        totals[13],
        totals[14],
        totals[15],
        totals[16],
    )


def solution(mesh):
    rows = P("narrow", "wide", None)
    placed = (rows, P("narrow")) + (P(),) * 17 + (rows,)
    wide = mesh.shape["wide"]
    fast = wide == 4 and HEADS % wide == 0
    return jax.shard_map(
        on_device if fast else on_device_any,
        mesh=mesh,
        in_specs=placed,
        out_specs=(rows, rows)
        + (P("wide", None, None, None), P("wide"), P("wide", None), P("wide"), P("wide", None), P("wide", None))
        + (P("wide"), P("wide", None), P("wide"), P("wide"), P("wide"), P("wide", None), P("wide"))
        + (P("wide", None), P("wide"), P("wide"), P("wide")),
        check_vma=False,
    )
```

```python
import functools

import jax
import jax.numpy as jnp
from jax import lax
from jax.experimental import pallas as pl
from jax.experimental.pallas import tpu as pltpu
from jax.sharding import PartitionSpec as P

HEADS = 12
GROUP_CH = 48
SHORT = 102
HALF = 64
UNIQUE = SHORT + HALF
FR = 384
SLOTS = 1536
SROWS = 192
TROWS = 1792
SBASE = 1600
CH = 192
eps_norm = 1e-05
neg_large = -1e30
bf16 = jnp.bfloat16
f32 = jnp.float32
VLIM = 60 * 1024 * 1024


def mm(a, b):
    return jnp.dot(a, b, preferred_element_type=f32)


def mm_nt(a, b):
    return lax.dot_general(a, b, (((1,), (1,)), ((), ())), preferred_element_type=f32)


def iota2(shape):
    return lax.broadcasted_iota(jnp.int32, shape, 0), lax.broadcasted_iota(jnp.int32, shape, 1)


def place(shape, rows_from, rows_to, cols_from):
    r, c = iota2(shape)
    hit = (c - cols_from == r - rows_from) & (r >= rows_from) & (r < rows_to)
    return hit.astype(f32).astype(bf16)


def spread(shape, lane0, start):
    r, c = iota2(shape)
    slot, inner = c >> 6, c & 63
    hit = (r == lane0 + start + slot * GROUP_CH + inner) & (inner < GROUP_CH)
    return hit.astype(f32).astype(bf16)


def gather_slots(shape, col0):
    r, c = iota2(shape)
    slot, inner = r >> 6, r & 63
    hit = (c == col0 + slot * GROUP_CH + inner) & (inner < GROUP_CH)
    return hit.astype(f32).astype(bf16)


def full(shape):
    return pl.BlockSpec(shape, lambda *_: (0,) * len(shape))


def smem():
    return pl.BlockSpec(memory_space=pltpu.SMEM)


def vmem():
    return pl.BlockSpec(memory_space=pltpu.VMEM)


def params(**kw):
    return pltpu.CompilerParams(vmem_limit_bytes=VLIM, **kw)


def cost(us):
    return pl.CostEstimate(flops=int(us * 1e9), bytes_accessed=int(us * 3.4e6), transcendentals=0)


def put(keeping, keep, send, rel, row0, data, lane0=0):
    rows, lanes = data.shape

    @pl.when(keeping)
    def _():
        keep[rel, row0 : row0 + rows, lane0 : lane0 + lanes] = data

    @pl.when(jnp.logical_not(keeping))
    def _():
        send[rel, row0 : row0 + rows, lane0 : lane0 + lanes] = data


def gelu_parts(v):
    cdf = 0.5 * (1.0 + lax.erf(v * (2.0 ** -0.5)))
    return cdf


def density(v):
    return jnp.exp(-0.5 * v * v) * 0.3989422804014327


def pack_frames_kernel(s_ref, x_ref, *outs):
    me, li = s_ref[0], s_ref[1]
    long, short = x_ref[li], x_ref[1 - li]
    slot = me * FR + lax.broadcasted_iota(jnp.int32, (128, 768), 0)
    short = jnp.where(slot < SHORT, short[:128].astype(f32), 0.0).astype(bf16)
    top = long[:256]
    low = jnp.concatenate([long[256:], short], axis=0)
    for d in range(4):
        first = 192 * d - (64 if d % 2 else 0)
        skip = 64 if d % 2 else 0
        chunk = mm(top[:, first : first + 256], place((256, 384), skip, skip + 192, 0)) + mm(
            low[:, first : first + 256], place((256, 384), skip, skip + 192, 192)
        )
        chunk = chunk.astype(bf16)
        for r in range(4):

            @pl.when((me ^ d) == r)
            def _():
                outs[r][...] = chunk


def pack_frames(scal, frames_in):
    return pl.pallas_call(
        pack_frames_kernel,
        out_shape=[jax.ShapeDtypeStruct((256, 384), bf16)] * 4,
        in_specs=[smem(), vmem()],
        out_specs=[vmem()] * 4,
        compiler_params=params(),
        cost_estimate=cost(3),
        name="pack_frames",
    )(scal, frames_in)


def prep_kernel(s_ref, w_ref, wt_ref, wd_ref, z_ref, taps):
    left, right = place((48, 128), 0, 48, 0), place((48, 128), 0, 48, 64)
    wt_ref[...] = jnp.zeros_like(wt_ref)
    z_ref[...] = jnp.zeros_like(z_ref)
    for i in range(48):
        taps[pl.ds(i, 128, stride=48), 0:48] = w_ref[0, i].astype(f32).T

    def rows(k, n):
        return taps[48 * k : 48 * (k + n), 0:48].astype(bf16)

    for k2 in range(8):
        pairs = rows(16 * k2, 16).reshape(8, 2, 48, 48)
        tile = mm(pairs[:, 0].reshape(384, 48), left) + mm(pairs[:, 1].reshape(384, 48), right)
        tile = tile.astype(bf16)
        for p in range(8):
            wt_ref[0, 64 * k2 : 64 * k2 + 48, 128 * p : 128 * p + 128] = tile[48 * p : 48 * p + 48]
    for q in range(4):
        tile = mm(rows(112 - 32 * q, 16), left) + mm(rows(96 - 32 * q, 16), right)
        for b in range(16):
            z_ref[64 * b : 64 * b + 48, :] = tile[48 * (15 - b) : 48 * (15 - b) + 48]
        wd_ref[0, 128 * q : 128 * q + 128, :] = z_ref[...].T.astype(bf16)


def prep_weights(scal, kernel):
    return pl.pallas_call(
        prep_kernel,
        grid_spec=pltpu.PrefetchScalarGridSpec(
            num_scalar_prefetch=1,
            grid=(4,),
            in_specs=[pl.BlockSpec((1, 48, 48, 128), lambda g, s: (4 * s[0] + g, 0, 0, 0))],
            out_specs=[pl.BlockSpec((1, 512, 1024), lambda g, s: (g, 0, 0))] * 2,
            scratch_shapes=[pltpu.VMEM((1024, 128), f32), pltpu.VMEM((48 * 128, 128), f32)],
        ),
        out_shape=[jax.ShapeDtypeStruct((4, 512, 1024), bf16)] * 2,
        compiler_params=params(),
        cost_estimate=cost(11),
        name="conv_weights",
    )(scal, jnp.transpose(kernel, (1, 2, 3, 0)))


def pair_slots(t_ref, rows):
    wide = jnp.concatenate([t_ref[0:rows, :], t_ref[16 : rows + 16, :]], axis=1)
    r, c = iota2((256, 128))
    out = []
    for j in range(2):
        hit = ((r < 128) & (c == r - 64 * j) & (c < 64)) | ((r >= 128) & (c - 64 == r - 128 - 64 * j) & (c >= 64))
        out.append(mm(wide, hit.astype(f32).astype(bf16)).astype(bf16))
    return out


def conv_block(p_refs, w_ref, y_ref, s_ref, n0, shift):
    lane = lax.broadcasted_iota(jnp.int32, (256, 128), 1)
    parts = []
    for j in range(2):
        lhs = jnp.concatenate(
            [p_refs[j][pl.ds(pl.multiple_of(n0 + 32 * q, 16), 272), :] for q in range(4)], axis=1
        )
        y_ref[j] = mm(lhs, w_ref[j])
        total = y_ref[j, shift : shift + 257, 0:128]
        for p in range(1, 8):
            total += y_ref[j, shift + 2 * p : shift + 2 * p + 257, 128 * p : 128 * p + 128]
        s_ref[0:257, :] = total
        here, after = s_ref[0:256, :], s_ref[1:257, :]
        if j == 0:
            parts.append(here + pltpu.roll(after, 64, 1))
        else:
            parts.append(pltpu.roll(here, 64, 1) + after)
    return jnp.where(lane < 64, parts[0], parts[1])


def conv_fwd_kernel(s_ref, c0, c1, c2, c3, w_ref, b_ref, pre_ref, x_ref, packed_ref, p0, p1, y_ref, t_ref, first):
    c = pl.program_id(0)
    me = s_ref[0]
    chunks = (c0, c1, c2, c3)
    x_ref[0, 0:64, :] = jnp.zeros((64, 128), bf16)
    x_ref[0, 1600:1664, :] = jnp.zeros((64, 128), bf16)
    x_ref[0, 1792:1936, :] = jnp.zeros((144, 128), bf16)
    top_map = spread((256, 128), 0, 96 * c)
    low_map = spread((256, 128), 64, 96 * c)
    for r in range(4):
        src = me ^ r
        top = mm(chunks[r][:, 0:256], top_map).astype(bf16)
        low = mm(chunks[r][:, 128:384], low_map).astype(bf16)
        base = pl.multiple_of(64 + FR * src, 64)
        x_ref[0, pl.ds(base, 256), :] = top
        x_ref[0, pl.ds(pl.multiple_of(base + 256, 64), 128), :] = low[:128]

        @pl.when(src == 0)
        def _():
            x_ref[0, 1664:1792, :] = low[128:]

    a, b = pair_slots(x_ref.at[0], 1920)
    p0[...] = a
    p1[...] = b
    bias = b_ref[0]

    def body(j, carry):
        n0 = pl.multiple_of(256 * j, 256)
        pre = conv_block((p0, p1), w_ref, y_ref, t_ref, n0, 0) + bias
        pre_ref[0, pl.ds(n0, 256), :] = pre
        center = x_ref[0, pl.ds(pl.multiple_of(n0 + 64, 64), 256), :].astype(f32)
        first[c, pl.ds(n0, 256), :] = (center + pre * gelu_parts(pre)).astype(bf16)
        return carry

    lax.fori_loop(0, 7, body, 0)

    @pl.when(c == 1)
    def _():
        h0, h1 = gather_slots((256, 384), 0), gather_slots((256, 384), 192)

        def rows(lo, n):
            return jnp.concatenate([first[0, lo : lo + n, :], first[1, lo : lo + n, :]], axis=1)

        packed_ref[0:768, :] = (mm(rows(0, 768), h0) + mm(rows(768, 768), h1)).astype(bf16)
        packed_ref[768:864, :] = (mm(rows(SBASE, 96), h0) + mm(rows(SBASE + 96, 96), h1)).astype(bf16)


def conv_fwd(scal, chunks, wt, bias):
    return pl.pallas_call(
        conv_fwd_kernel,
        grid=(2,),
        in_specs=[smem()]
        + [full((256, 384))] * 4
        + [pl.BlockSpec((2, 512, 1024), lambda c: (c, 0, 0)), pl.BlockSpec((1, 1, 128), lambda c: (c, 0, 0))],
        out_specs=[
            pl.BlockSpec((1, TROWS, 128), lambda c: (c, 0, 0)),
            pl.BlockSpec((1, 1936, 128), lambda c: (c, 0, 0)),
            full((864, 384)),
        ],
        out_shape=[
            jax.ShapeDtypeStruct((2, TROWS, 128), f32),
            jax.ShapeDtypeStruct((2, 1936, 128), bf16),
            jax.ShapeDtypeStruct((864, 384), bf16),
        ],
        scratch_shapes=[
            pltpu.VMEM((1920, 128), bf16),
            pltpu.VMEM((1920, 128), bf16),
            pltpu.VMEM((2, 272, 1024), f32),
            pltpu.VMEM((264, 128), f32),
            pltpu.VMEM((2, TROWS, 128), bf16),
        ],
        compiler_params=params(),
        cost_estimate=cost(19),
        name="conv_fwd",
    )(scal, *chunks, wt, bias)


def attn_fwd_kernel(
    s_ref, c0, c1, c2, c3, w_ref, b_ref, qkv_ref, ot_ref, lse_ref, rows_ref, x0, x1, x2, x3, wz, vt
):
    me = s_ref[0]
    chunks = (c0, c1, c2, c3)
    wz[:, 0:64, :] = jnp.zeros((4, 64, 768), bf16)
    wz[:, 256:320, :] = jnp.zeros((4, 64, 768), bf16)
    for r in range(4):
        wz[r, 64:256, :] = w_ref[pl.ds(pl.multiple_of(192 * (me ^ r), 64), 192), :]
    bias = b_ref[...]
    for half in range(2):
        row0 = 64 * (1 - half)

        def project(start, n):
            total = bias + jnp.zeros((n, 768), f32)
            for r in range(4):
                total += mm(
                    chunks[r][pl.ds(start, n), 128 * half : 128 * half + 256], wz[r, row0 : row0 + 256, :]
                )
            return total.astype(bf16)

        def body(j, carry):
            start = pl.multiple_of(256 * j, 256)
            qkv_ref[pl.ds(pl.multiple_of(768 * half + start, 256), 256), :] = project(start, 256)
            return carry

        lax.fori_loop(0, 3, body, 0)
        qkv_ref[SLOTS + 96 * half : SLOTS + 96 * half + 96, :] = project(768, 96)
    qkv_ref[SLOTS + SROWS : TROWS, :] = jnp.zeros((TROWS - SLOTS - SROWS, 768), bf16)

    half = me >> 1
    start = pl.multiple_of(FR * (me & 1), 128)
    lane0 = pl.multiple_of(128 * half, 128)
    r_i, c_i = iota2((256, 768))
    own = jnp.zeros((FR, 768), f32)
    extra0 = jnp.zeros((96, 768), f32)
    extra1 = jnp.zeros((96, 768), f32)
    for r in range(4):
        base = 192 * (me ^ r)
        inside = (c_i >= base) & (c_i < base + 192)
        sel0 = ((c_i - base == r_i) & inside).astype(f32).astype(bf16)
        sel1 = ((c_i - base == r_i - 64) & inside).astype(f32).astype(bf16)
        mid = ((c_i - base == r_i - 64 * half) & inside).astype(f32).astype(bf16)
        own += mm(chunks[r][pl.ds(start, FR), pl.ds(lane0, 256)], mid)
        extra0 += mm(chunks[r][768:864, 0:256], sel0)
        extra1 += mm(chunks[r][768:864, 128:384], sel1)
    rows_ref[0:FR, :] = own.astype(bf16)
    rows_ref[FR : FR + 96, :] = extra0.astype(bf16)
    rows_ref[FR + 96 : FR + 192, :] = extra1.astype(bf16)

    vt[...] = qkv_ref[:, 512:704].astype(f32).T.astype(bf16)
    lse_ref[...] = jnp.zeros_like(lse_ref)
    for h in range(3):
        cols = slice(64 * h, 64 * h + 64)

        def attend(q0, key0, keys, masked):
            query = (qkv_ref[pl.ds(q0, 256), 0:256][:, cols].astype(f32) * 0.125).astype(bf16)
            key = qkv_ref[key0 : key0 + keys, 256:512][:, cols]
            scores = mm_nt(key, query)
            if masked:
                slot = lax.broadcasted_iota(jnp.int32, scores.shape, 0)
                scores = jnp.where(slot < SHORT, scores, neg_large)
            top = jnp.max(scores, axis=0, keepdims=True)
            weights = jnp.exp(scores - top)
            total = jnp.sum(weights, axis=0, keepdims=True)
            out = mm(vt[cols, key0 : key0 + keys], weights.astype(bf16))
            ot_ref[cols, pl.ds(q0, 256)] = out / total
            lse_ref[h : h + 1, pl.ds(q0, 256)] = top + jnp.log(total)

        def body(j, carry):
            attend(pl.multiple_of(256 * j, 256), 0, SLOTS, False)
            return carry

        lax.fori_loop(0, 6, body, 0)
        attend(SLOTS, SLOTS, 128, True)
    for r, out in enumerate((x0, x1, x2, x3)):
        out[:, 0:FR] = ot_ref[:, pl.ds(pl.multiple_of(FR * (me ^ r), 128), FR)].astype(bf16)
        out[:, FR:640] = ot_ref[:, SLOTS:TROWS].astype(bf16)


def attn_fwd(scal, chunks, wqkv, bqkv):
    return pl.pallas_call(
        attn_fwd_kernel,
        in_specs=[smem()] + [vmem()] * 6,
        out_specs=[vmem()] * 8,
        out_shape=[
            jax.ShapeDtypeStruct((TROWS, 768), bf16),
            jax.ShapeDtypeStruct((CH, TROWS), f32),
            jax.ShapeDtypeStruct((8, TROWS), f32),
            jax.ShapeDtypeStruct((576, 768), bf16),
        ]
        + [jax.ShapeDtypeStruct((CH, 640), bf16)] * 4,
        scratch_shapes=[pltpu.VMEM((4, 320, 768), bf16), pltpu.VMEM((CH, TROWS), bf16)],
        compiler_params=params(),
        cost_estimate=cost(28),
        name="attn_fwd",
    )(scal, *chunks, wqkv, bqkv)


def attn_bwd_kernel(
    s_ref, qkv_ref, ot_ref, lse_ref, d0, d1, d2, d3, gs_ref, w_ref,
    dqkv_ref, g0, g1, g2, g3, sums_ref, dot_, do_, kt, delta, dqt, dk, dv,
):
    me = s_ref[0]
    parts = (d0, d1, d2, d3)
    short = jnp.zeros((CH, 256), f32)
    for r in range(4):
        src = me ^ r
        dot_[:, pl.ds(pl.multiple_of(FR * src, 128), FR)] = parts[r][:, 0:FR]
        short += parts[r][:, FR : FR + 256].astype(f32)
    dot_[:, SLOTS:TROWS] = short.astype(bf16)
    whole = dot_[...].astype(f32)
    do_[...] = whole.T.astype(bf16)
    prod = whole * ot_ref[...]
    delta[...] = jnp.zeros_like(delta)
    for h in range(3):
        delta[h : h + 1, :] = jnp.sum(prod[64 * h : 64 * h + 64], axis=0, keepdims=True)
    kt[...] = qkv_ref[:, 256:448].astype(f32).T.astype(bf16)

    for h in range(3):
        cols = slice(64 * h, 64 * h + 64)
        dk[...] = jnp.zeros_like(dk)
        dv[...] = jnp.zeros_like(dv)

        def step(q0, key0, keys, masked):
            query = qkv_ref[pl.ds(q0, 256), 0:256][:, cols]
            scaled = (query.astype(f32) * 0.125).astype(bf16)
            grad = do_[pl.ds(q0, 256), :][:, cols]
            grad_t = dot_[cols, pl.ds(q0, 256)]
            lse = lse_ref[h : h + 1, pl.ds(q0, 256)]
            dl = delta[h : h + 1, pl.ds(q0, 256)]
            grad_q = jnp.zeros((64, 256), f32)
            piece = min(keys, 512)
            for at in range(key0, key0 + keys, piece):
                key = qkv_ref[at : at + piece, 256:512][:, cols]
                val = qkv_ref[at : at + piece, 512:768][:, cols]
                probs = jnp.exp(mm_nt(key, scaled) - lse)
                if masked:
                    slot = lax.broadcasted_iota(jnp.int32, probs.shape, 0)
                    probs = jnp.where(slot < SHORT, probs, 0.0)
                grad_p = mm(val, grad_t)
                grad_s = (probs * (grad_p - dl)).astype(bf16)
                dv[at : at + piece, :] += mm(probs.astype(bf16), grad)
                dk[at : at + piece, :] += mm(grad_s, query)
                grad_q += mm(kt[cols, at : at + piece], grad_s)
            dqt[cols, pl.ds(q0, 256)] = grad_q * 0.125

        def body(j, carry):
            step(pl.multiple_of(256 * j, 256), 0, SLOTS, False)
            return carry

        lax.fori_loop(0, 6, body, 0)
        step(SLOTS, SLOTS, 128, True)
        zeros = jnp.zeros((TROWS, 64), f32)
        if h == 0:
            keep_k, keep_v = [], []
        keep_k.append((dk[...] * 0.125).astype(bf16))
        keep_v.append(dv[...].astype(bf16))
    dqkv_ref[:, 0:192] = dqt[...].T.astype(bf16)
    dqkv_ref[:, 192:256] = jnp.zeros((TROWS, 64), bf16)
    dqkv_ref[:, 256:512] = jnp.concatenate(keep_k + [zeros.astype(bf16)], axis=1)
    dqkv_ref[:, 512:768] = jnp.concatenate(keep_v + [zeros.astype(bf16)], axis=1)
    sums_ref[...] = jnp.sum(dqkv_ref[...].astype(f32), axis=0, keepdims=True)
    outs = (g0, g1, g2, g3)
    lanes = pl.multiple_of(FR * me, 128)
    for r in range(4):
        rows = pl.ds(pl.multiple_of(192 * (me ^ r), 64), 192)
        part = mm_nt(w_ref[rows, :], dqkv_ref[...])
        outs[r][...] = part.astype(bf16)
        own = gs_ref[rows, 0:FR].astype(f32)
        outs[r][:, pl.ds(lanes, FR)] = (outs[r][:, pl.ds(lanes, FR)].astype(f32) + own).astype(bf16)
        outs[r][:, SLOTS:TROWS] = (part[:, SLOTS:TROWS] + gs_ref[rows, FR : FR + 256].astype(f32)).astype(bf16)


def attn_bwd(scal, qkv, ot, lse, dparts, gst, wqkv):
    return pl.pallas_call(
        attn_bwd_kernel,
        in_specs=[smem()] + [vmem()] * 9,
        out_specs=[vmem()] * 6,
        out_shape=[jax.ShapeDtypeStruct((TROWS, 768), bf16)]
        + [jax.ShapeDtypeStruct((CH, TROWS), bf16)] * 4
        + [jax.ShapeDtypeStruct((1, 768), f32)],
        scratch_shapes=[
            pltpu.VMEM((CH, TROWS), bf16),
            pltpu.VMEM((TROWS, CH), bf16),
            pltpu.VMEM((CH, TROWS), bf16),
            pltpu.VMEM((8, TROWS), f32),
            pltpu.VMEM((CH, TROWS), f32),
            pltpu.VMEM((TROWS, 64), f32),
            pltpu.VMEM((TROWS, 64), f32),
        ],
        compiler_params=params(),
        cost_estimate=cost(33),
        name="attn_bwd",
    )(scal, qkv, ot, lse, *dparts, gst, wqkv)


def qkv_wgrad_kernel(s_ref, c0, c1, c2, c3, d_ref, keep, send):
    core = s_ref[2]
    for r, chunk in enumerate((c0, c1, c2, c3)):
        turned = chunk[...].astype(f32).T.astype(bf16)
        value = (
            mm(turned[0:192, 0:768], d_ref[0:768, :])
            + mm(turned[0:192, 768:864], d_ref[SLOTS : SLOTS + 96, :])
            + mm(turned[192:384, 0:768], d_ref[768:1536, :])
            + mm(turned[192:384, 768:864], d_ref[SLOTS + 96 : SLOTS + 192, :])
        ).astype(bf16)
        put(core == 0, keep, send, r, 0, value[0:96])
        put(core == 1, keep, send, r, 0, value[96:192])


def qkv_wgrad(scal, chunks, dqkv):
    return pl.pallas_call(
        qkv_wgrad_kernel,
        in_specs=[smem()] + [vmem()] * 5,
        out_specs=[vmem()] * 2,
        out_shape=[jax.ShapeDtypeStruct((4, 96, 768), bf16)] * 2,
        compiler_params=params(),
        cost_estimate=cost(8),
        name="qkv_wgrad",
    )(scal, *chunks, dqkv)


def conv_wgrad_kernel(
    s_ref, c0, c1, c2, c3, pre_ref, x_ref, sums_ref,
    keep, send, gf_ref, g_ref,
    gp, p0, p1, bb, g2, xt,
):
    c = pl.program_id(0)
    me, core = s_ref[0], s_ref[2]
    total = c0[...].astype(f32) + c1[...].astype(f32) + c2[...].astype(f32) + c3[...].astype(f32)
    pad = jnp.zeros((16, TROWS), f32)
    rows = jnp.concatenate([total[0:48], pad, total[48:96], pad], axis=0)
    gf = gf_ref.at[0]
    gf[0:SLOTS, :] = rows[:, 0:SLOTS].T
    gf[SLOTS:SBASE, :] = jnp.zeros((SBASE - SLOTS, 128), f32)
    gf[SBASE:TROWS, :] = rows[:, SLOTS:TROWS].T[0 : TROWS - SBASE]
    g_ref[0, 0:64, :] = jnp.zeros((64, 128), bf16)
    g_ref[0, 1856:1936, :] = jnp.zeros((80, 128), bf16)
    gp[0:16, :] = jnp.zeros((16, 128), f32)

    def front(j, carry):
        n0 = pl.multiple_of(256 * j, 256)
        pre = pre_ref[0, pl.ds(n0, 256), :]
        slope = gelu_parts(pre) + pre * density(pre)
        wide = (gf[pl.ds(n0, 256), :] * slope).astype(bf16).astype(f32)
        bias = carry + jnp.sum(wide, axis=0, keepdims=True)
        row = n0 + lax.broadcasted_iota(jnp.int32, (256, 128), 0)
        wide = jnp.where(row < SBASE + UNIQUE, wide, 0.0)
        gp[pl.ds(pl.multiple_of(n0 + 16, 16), 256), :] = wide
        g_ref[0, pl.ds(pl.multiple_of(n0 + 64, 64), 256), :] = wide.astype(bf16)
        return bias

    bias_sum = lax.fori_loop(0, 7, front, jnp.zeros((1, 128), f32))
    extra = jnp.concatenate(
        [sums_ref[...], jnp.concatenate([bias_sum, jnp.zeros((1, 640), f32)], axis=1), jnp.zeros((14, 768), f32)], axis=0
    )
    put(core == c, keep, send, 0, 192, extra.astype(bf16))

    lane = lax.broadcasted_iota(jnp.int32, (TROWS, 128), 1)
    here, before = gp[16 : 16 + TROWS, :], gp[15 : 15 + TROWS, :]
    a, b = pair_slots(x_ref.at[0], 1920)
    p0[...] = a
    p1[...] = b
    pack0, pack1 = gather_slots((256, 384), 0), gather_slots((256, 384), 192)
    for j in range(2):
        bb[0:16, :] = jnp.zeros((16, 128), f32)
        if j == 0:
            bb[16 : 16 + TROWS, :] = jnp.where(lane < 64, here, pltpu.roll(before, 64, 1))
        else:
            bb[16 : 16 + TROWS, :] = jnp.where(lane < 64, pltpu.roll(here, 64, 1), before)
        for p in range(8):
            g2[:, 128 * p : 128 * p + 128] = bb[16 - 2 * p : 16 - 2 * p + TROWS, :].astype(bf16)
        slots = (p0, p1)[j]
        for q in range(4):
            xt[128 * q : 128 * q + 128, :] = slots[32 * q : 32 * q + TROWS, :].astype(f32).T.astype(bf16)

        def body(m, carry):
            lhs = xt[pl.ds(pl.multiple_of(128 * m, 128), 128), :]
            for half in range(2):
                base = 512 * half
                left = mm(lhs, g2[:, base : base + 256]).astype(bf16)
                right = mm(lhs, g2[:, base + 256 : base + 512]).astype(bf16)
                packed = (mm(left, pack0) + mm(right, pack1)).astype(bf16)
                packed = jnp.concatenate([packed[0:48], packed[64:112]], axis=0)
                put(core == c, keep, send, me ^ m, 96 * j, packed, 384 * half)
            return carry

        lax.fori_loop(0, 4, body, 0)


def conv_wgrad(scal, parts, pre, xp, sums):
    pairs = lambda rows: pl.BlockSpec((1, rows, 128), lambda c: (c, 0, 0))
    return pl.pallas_call(
        conv_wgrad_kernel,
        grid=(2,),
        in_specs=[smem()]
        + [pl.BlockSpec((96, TROWS), lambda c: (c, 0))] * 4
        + [pairs(TROWS), pairs(1936), full((1, 768))],
        out_specs=[full((4, 208, 768))] * 2 + [pairs(TROWS), pairs(1936)],
        out_shape=[jax.ShapeDtypeStruct((4, 208, 768), bf16)] * 2
        + [jax.ShapeDtypeStruct((2, TROWS, 128), f32), jax.ShapeDtypeStruct((2, 1936, 128), bf16)],
        scratch_shapes=[
            pltpu.VMEM((16 + TROWS, 128), f32),
            pltpu.VMEM((1920, 128), bf16),
            pltpu.VMEM((1920, 128), bf16),
            pltpu.VMEM((16 + TROWS, 128), f32),
            pltpu.VMEM((TROWS, 1024), bf16),
            pltpu.VMEM((512, TROWS), bf16),
        ],
        compiler_params=params(),
        cost_estimate=cost(28),
        name="conv_wgrad",
    )(scal, *parts, pre, xp, sums)


def conv_dgrad_kernel(s_ref, gf, g_ref, wd_ref, f0, f1, f2, f3, p0, p1, y_ref, t_ref, fg):
    c = pl.program_id(0)
    me = s_ref[0]
    a, b = pair_slots(g_ref.at[0], 1920)
    p0[...] = a
    p1[...] = b

    def back(j, carry):
        n0 = pl.multiple_of(256 * j, 256)
        value = conv_block((p0, p1), wd_ref, y_ref, t_ref, n0, 1) + gf[0, pl.ds(n0, 256), :]
        fg[c, pl.ds(n0, 256), :] = value.astype(bf16)
        return carry

    lax.fori_loop(0, 7, back, 0)

    @pl.when(c == 1)
    def _():
        pack0, pack1 = gather_slots((256, 384), 0), gather_slots((256, 384), 192)

        def rows_of(lo, n):
            return jnp.concatenate([fg[0, lo : lo + n, :], fg[1, lo : lo + n, :]], axis=1)

        for d in range(4):
            low = jnp.concatenate([rows_of(FR * d + 256, 128), rows_of(SBASE, 128)], axis=0)
            chunk = (mm(rows_of(FR * d, 256), pack0) + mm(low, pack1)).astype(bf16)
            for r in range(4):

                @pl.when((me ^ d) == r)
                def _():
                    (f0, f1, f2, f3)[r][...] = chunk


def conv_dgrad(scal, gf, g, wd):
    pairs = lambda rows: pl.BlockSpec((1, rows, 128), lambda c: (c, 0, 0))
    return pl.pallas_call(
        conv_dgrad_kernel,
        grid=(2,),
        in_specs=[smem(), pairs(TROWS), pairs(1936), pl.BlockSpec((2, 512, 1024), lambda c: (c, 0, 0))],
        out_specs=[full((256, 384))] * 4,
        out_shape=[jax.ShapeDtypeStruct((256, 384), bf16)] * 4,
        scratch_shapes=[
            pltpu.VMEM((1920, 128), bf16),
            pltpu.VMEM((1920, 128), bf16),
            pltpu.VMEM((2, 272, 1024), f32),
            pltpu.VMEM((264, 128), f32),
            pltpu.VMEM((2, TROWS, 128), bf16),
        ],
        compiler_params=params(),
        cost_estimate=cost(17),
        name="conv_dgrad",
    )(scal, gf, g, wd)


def z_sum_kernel(b, c, fb, fc, ob, oc, eb, ec, yb, yc, se, re, sy, ry, st, sf, rt, sc, rc):
    n, w = lax.axis_index("narrow"), lax.axis_index("wide")
    z, core = n // 2, n % 2
    pieces = [(0, r, 0, 96) for r in range(4)]
    for r in range(4):
        pieces += [(1, r, 0, 112), (1, r, 112, 96)]
    count = len(pieces)

    def view(refs, k):
        which, r, row, rows = pieces[k]
        return refs[which].at[r, row : row + rows]

    x, e, y, f, o = ([view(refs, k) for k in range(count)] for refs in ((b, c), (eb, ec), (yb, yc), (fb, fc), (ob, oc)))

    def copy(src, dst, send, recv, zz, cc=core):
        return pltpu.make_async_remote_copy(
            src_ref=src, dst_ref=dst, send_sem=send, recv_sem=recv, device_id=(2 * zz + cc, w),
            device_id_type=pl.DeviceIdType.MESH,
        )

    barrier = pltpu.get_barrier_semaphore()

    def greet(zz, cc):
        pl.semaphore_signal(barrier, inc=1, device_id=(2 * zz + cc, w), device_id_type=pl.DeviceIdType.MESH)

    @pl.when(z > 0)
    def _():
        greet(z - 1, core)

    @pl.when(z < 3)
    def _():
        greet(z + 1, core)

    greet(z, 1 - core)
    pl.semaphore_wait(barrier, 1 + jnp.minimum(z, 1) + jnp.minimum(3 - z, 1))

    def swap(k):
        return copy(f[k], o[k], sc.at[k], rc.at[k], z, 1 - core)

    def outer(here, inward):
        sent = [copy(x[k], e[k], se.at[k], re.at[k], inward) for k in range(count)]
        for s in sent:
            s.start()
        swaps = [swap(k) for k in range(count)]
        for k in range(count):
            copy(f[k], f[k], sf.at[k], rt.at[k], inward).wait_recv()
            swaps[k].start()
        for k in range(count):
            sent[k].wait_send()
            swaps[k].wait()

    def inner(here):
        outward, across = (0, 2) if here == 1 else (3, 1)
        first = [k % 2 == (0 if here == 1 else 1) for k in range(count)]
        swaps = [swap(k) for k in range(count)]
        over = [copy(y[k], y[k], sy.at[k], ry.at[k], across) for k in range(count)]
        back = [copy(f[k], f[k], st.at[k], rt.at[k], across) for k in range(count)]
        out = [copy(f[k], f[k], sf.at[k], rt.at[k], outward) for k in range(count)]

        def forward(k):
            if first[k]:
                back[k].wait_recv()
                out[k].start()
                swaps[k].start()

        for k0 in range(0, count, 2):
            for k in (k0, k0 + 1):
                copy(x[k], e[k], se.at[k], re.at[k], outward).wait_recv()
                if first[k]:
                    y[k][...] = (x[k][...].astype(f32) + e[k][...].astype(f32)).astype(bf16)
                    over[k].start()
            for k in (k0, k0 + 1):
                if not first[k]:
                    over[k].wait_recv()
                    f[k][...] = (x[k][...].astype(f32) + e[k][...].astype(f32) + y[k][...].astype(f32)).astype(bf16)
                    back[k].start()
                    out[k].start()
                    swaps[k].start()
            if k0:
                forward(k0 - 2)
                forward(k0 - 1)
        forward(count - 2)
        forward(count - 1)
        for k in range(count):
            if first[k]:
                over[k].wait_send()
            else:
                back[k].wait_send()
            out[k].wait_send()
            swaps[k].wait()

    pl.when(z == 0)(lambda: outer(0, 1))
    pl.when(z == 3)(lambda: outer(3, 2))
    pl.when(z == 1)(lambda: inner(1))
    pl.when(z == 2)(lambda: inner(2))


def z_sum(b, c):
    shapes = [jax.ShapeDtypeStruct((4, 96, 768), bf16), jax.ShapeDtypeStruct((4, 208, 768), bf16)]
    room = [pltpu.VMEM((4, 96, 768), bf16), pltpu.VMEM((4, 208, 768), bf16)]
    return pl.pallas_call(
        z_sum_kernel,
        in_specs=[vmem()] * 2,
        out_specs=[vmem()] * 4,
        out_shape=shapes * 2,
        scratch_shapes=room * 2 + [pltpu.SemaphoreType.DMA((12,))] * 9,
        compiler_params=params(collective_id=1, has_side_effects=True),
        cost_estimate=cost(50),
        name="z_sum",
    )(b, c)


def unpack_frames_kernel(s_ref, c0, c1, c2, c3, o_ref):
    me, li = s_ref[0], s_ref[1]
    r_i, c_i = iota2((256, 768))
    top = jnp.zeros((256, 768), f32)
    low = jnp.zeros((256, 768), f32)
    for r, chunk in enumerate((c0, c1, c2, c3)):
        base = 192 * (me ^ r)
        inside = (c_i >= base) & (c_i < base + 192)
        top += mm(chunk[:, 0:256], ((c_i - base == r_i) & inside).astype(f32).astype(bf16))
        low += mm(chunk[:, 128:384], ((c_i - base == r_i - 64) & inside).astype(f32).astype(bf16))
    o_ref[li, 0:256, :] = top.astype(bf16)
    o_ref[li, 256:384, :] = low[0:128].astype(bf16)
    slot = me * FR + lax.broadcasted_iota(jnp.int32, (128, 768), 0)
    o_ref[1 - li, 0:128, :] = jnp.where(slot < SHORT, low[128:], 0.0).astype(bf16)
    o_ref[1 - li, 128:384, :] = jnp.zeros((256, 768), bf16)


def unpack_frames(scal, chunks):
    return pl.pallas_call(
        unpack_frames_kernel,
        in_specs=[smem()] + [vmem()] * 4,
        out_specs=vmem(),
        out_shape=jax.ShapeDtypeStruct((2, FR, 768), bf16),
        compiler_params=params(),
        cost_estimate=cost(3),
        name="unpack_frames",
    )(scal, *chunks)


def kernel_out_kernel(s_ref, own_ref, other_ref, o_ref, small_ref):
    g = pl.program_id(0)
    core = s_ref[2]
    half = (g >> 1) & 1
    row = pl.multiple_of(96 * (g & 1), 32)
    x = jnp.where(half == core, own_ref[0, 0, pl.ds(row, 96)], other_ref[0, 0, pl.ds(row, 96)]).astype(f32)
    for k2 in range(2):
        for b in range(16):
            o_ref[16 * k2 + b, 0] = x[48 * k2 : 48 * k2 + 48, 48 * b : 48 * b + 48]

    @pl.when(g == 0)
    def _():
        small_ref[...] = jnp.zeros_like(small_ref)

    @pl.when(((g >> 2) == s_ref[0]) & ((g & 1) == 0))
    def _():
        small_ref[half] = jnp.where(half == core, own_ref[0, 0, 192:208], other_ref[0, 0, 192:208])


def kernel_out(scal, own, other):
    def at(g, s):
        return ((g >> 2) ^ s[0], 0, 0, 0)

    return pl.pallas_call(
        kernel_out_kernel,
        grid_spec=pltpu.PrefetchScalarGridSpec(
            num_scalar_prefetch=1,
            grid=(16,),
            in_specs=[pl.BlockSpec((1, 1, 208, 768), at)] * 2,
            out_specs=[
                pl.BlockSpec((32, 1, 48, 48), lambda g, s: (0, g, 0, 0)),
                pl.BlockSpec((2, 16, 768), lambda g, s: (0, 0, 0)),
            ],
        ),
        out_shape=[jax.ShapeDtypeStruct((32, 16, 48, 48), f32), jax.ShapeDtypeStruct((2, 16, 768), bf16)],
        compiler_params=params(),
        cost_estimate=cost(12),
        name="kernel_grad_out",
    )(scal, own.reshape(4, 1, 208, 768), other.reshape(4, 1, 208, 768))


def norm(v):
    center = v - jnp.mean(v, axis=-1, keepdims=True)
    scale = lax.rsqrt(jnp.mean(center * center, axis=-1, keepdims=True) + eps_norm)
    return center * scale, scale


def norm_back(e, n, scale):
    return (e - jnp.mean(e, axis=-1, keepdims=True) - n * jnp.mean(e * n, axis=-1, keepdims=True)) * scale


def ffn_kernel(
    s_ref, rows_ref, m0, m1, m2, m3, wo, wu, bu, wd, vecs, og,
    lo, ul, gu, nl, gd, gac, x0, x1, x2, x3, gst, sums,
    sc, slope, v, cot, gsc, rest,
):
    t = pl.program_id(0)
    me, li = s_ref[0], s_ref[1]
    const = FR + UNIQUE
    bo, g1, s1, bd, g2, s2 = (vecs[k : k + 1, :] for k in range(6))

    def total(x):
        return jnp.sum(x, axis=0, keepdims=True)

    @pl.when(t == 0)
    def _():
        mix = jnp.concatenate([m0[...], m1[...], m2[...], m3[...]], axis=0)
        out = lax.dot_general(mix, wo[...], (((0,), (0,)), ((), ())), preferred_element_type=f32)
        sc[...] = rows_ref[...].astype(f32) + out[0:576] + bo[...]
        sums[...] = jnp.zeros_like(sums)
        rest[...] = jnp.zeros_like(rest)
        gsc[...] = jnp.zeros_like(gsc)
        gac[...] = jnp.zeros_like(gac)
        v[...] = sc[0:256, :]
        cot[...] = og[li, 0:256].astype(f32)

    mine = jnp.where(me == 0, 1.0, 0.0)
    keep_low = (lax.broadcasted_iota(jnp.int32, (64, 768), 0) < UNIQUE - 128).astype(f32) * mine

    @pl.when(t == 1)
    def _():
        v[0:128, :] = sc[256:384, :]
        v[128:256, :] = jnp.where(me == 0, sc[FR : FR + 128, :], sc[const : const + 1, :])
        cot[0:128, :] = og[li, 256:384].astype(f32)
        cot[128:256, :] = og[1 - li, 0:128].astype(f32)

    @pl.when(t == 2)
    def _():
        v[...] = jnp.broadcast_to(sc[const : const + 1, :], (256, 768))
        v[0:64, :] = jnp.where(keep_low > 0.5, sc[FR + 128 : FR + 192, :], sc[const : const + 1, :])
        cot[...] = og[1 - li, 128:384].astype(f32)

    n1, scale1 = norm(v[...])
    norm_one = n1 * g1[...] + s1[...]
    low = norm_one.astype(bf16)
    nl[...] = low
    down = norm_one + bd[...]
    for j in range(4):
        cols = slice(768 * j, 768 * j + 768)
        up = mm(low, wu[:, cols]) + bu[:, cols]
        cdf = gelu_parts(up)
        slope[:, cols] = cdf + up * density(up)
        act = (up * cdf).astype(bf16)
        ul[:, cols] = act
        down += mm(act, wd[cols, :])
    n2, scale2 = norm(down)
    result = (n2 * g2[...] + s2[...]).astype(bf16)

    @pl.when(t == 0)
    def _():
        lo[li, 0:256] = result

    @pl.when(t == 1)
    def _():
        lo[li, 256:384] = result[0:128]
        lo[1 - li, 0:128] = result[128:256]

    @pl.when(t == 2)
    def _():
        lo[1 - li, 128:384] = result

    given = cot[...]
    sums[8:9, :] += total(given * n2)
    sums[9:10, :] += total(given)
    grad_two = norm_back(given * g2[...], n2, scale2)
    grad_down = grad_two.astype(bf16)
    gd[...] = grad_down
    sums[7:8, :] += total(grad_down.astype(f32))
    grad_n = grad_two
    for j in range(4):
        cols = slice(768 * j, 768 * j + 768)
        grad_up = (mm_nt(grad_down, wd[cols, :]) * slope[:, cols]).astype(bf16)
        gu[:, cols] = grad_up
        sums[j : j + 1, :] += total(grad_up.astype(f32))
        grad_n += mm_nt(grad_up, wu[:, cols])
    sums[5:6, :] += total(grad_n * n1)
    sums[6:7, :] += total(grad_n)
    grad_one = norm_back(grad_n * g1[...], n1, scale1)
    grad_attn = grad_one.astype(bf16).astype(f32)
    sums[4:5, :] += total(grad_attn)

    @pl.when(t == 0)
    def _():
        gac[0:256, :] = grad_attn.astype(bf16)
        gsc[0:256, :] = grad_one

    @pl.when(t == 1)
    def _():
        gac[256:384, :] = grad_attn[0:128].astype(bf16)
        gsc[256:384, :] = grad_one[0:128]
        gac[FR : FR + 128, :] = (grad_attn[128:256] * mine).astype(bf16)
        gsc[FR : FR + 128, :] = grad_one[128:256] * mine
        rest[0:1, :] += total(grad_attn[128:256]) * (1.0 - mine)
        rest[1:2, :] += total(grad_one[128:256]) * (1.0 - mine)

    @pl.when(t == 2)
    def _():
        kept, kept_one = grad_attn[0:64] * keep_low, grad_one[0:64] * keep_low
        at = lax.broadcasted_iota(jnp.int32, (64, 768), 0) == UNIQUE - 128
        rest_attn = rest[0:1, :] + total(grad_attn) - total(kept)
        rest_one = rest[1:2, :] + total(grad_one) - total(kept_one)
        gac[FR + 128 : FR + 192, :] = jnp.where(at, rest_attn, kept).astype(bf16)
        gsc[FR + 128 : FR + 192, :] = jnp.where(at, rest_one, kept_one)
        for r, out in enumerate((x0, x1, x2, x3)):
            out[...] = mm_nt(wo[192 * r : 192 * r + 192, :], gac[...]).astype(bf16)
        gst[...] = gsc[...].T.astype(bf16)


def ffn(scal, rows, mix, wo, wu, bu, wd, vecs, og):
    sds = jax.ShapeDtypeStruct

    def step(width):
        return pl.BlockSpec((256, width), lambda t: (t, 0))

    def one(v):
        return full(v.shape)

    given = [rows, *mix, wo, wu, bu, wd, vecs, og]
    return pl.pallas_call(
        ffn_kernel,
        grid=(3,),
        in_specs=[smem()] + [one(v) for v in given],
        out_specs=[full((2, FR, 768)), step(3072), step(3072), step(768), step(768), full((640, 768))]
        + [full((CH, 640))] * 4
        + [full((768, 640)), full((16, 768))],
        out_shape=[
            sds((2, FR, 768), bf16), sds((768, 3072), bf16), sds((768, 3072), bf16), sds((768, 768), bf16),
            sds((768, 768), bf16), sds((640, 768), bf16),
        ]
        + [sds((CH, 640), bf16)] * 4
        + [sds((768, 640), bf16), sds((16, 768), f32)],
        scratch_shapes=[
            pltpu.VMEM((576, 768), f32),
            pltpu.VMEM((256, 3072), f32),
            pltpu.VMEM((256, 768), f32),
            pltpu.VMEM((256, 768), f32),
            pltpu.VMEM((640, 768), f32),
            pltpu.VMEM((8, 768), f32),
        ],
        compiler_params=params(),
        cost_estimate=cost(33),
        name="ffn",
    )(scal, *given)


def tn(a, b):
    return lax.dot_general(a, b, (((0,), (0,)), ((), ())), preferred_element_type=f32)


def up_wgrad_kernel(s_ref, nl, gu, keep, send):
    j = pl.program_id(0)
    me, core = s_ref[0], s_ref[2]
    up = tn(nl[...], gu[...]).astype(bf16)
    row0 = pl.multiple_of(192 * (j & 1), 64)
    stays = core == (j >> 1)

    @pl.when(stays)
    def _():
        for e in range(4):
            keep[me ^ e, pl.ds(row0, 192), :] = up[192 * e : 192 * e + 192]

    @pl.when(jnp.logical_not(stays))
    def _():
        for e in range(4):
            send[me ^ e, pl.ds(row0, 192), :] = up[192 * e : 192 * e + 192]


def up_wgrad(scal, nl, gu):
    return pl.pallas_call(
        up_wgrad_kernel,
        grid=(4,),
        in_specs=[smem(), full((768, 768)), pl.BlockSpec((768, 768), lambda j: (0, j))],
        out_specs=[full((4, 384, 768))] * 2,
        out_shape=[jax.ShapeDtypeStruct((4, 384, 768), bf16)] * 2,
        compiler_params=params(),
        cost_estimate=cost(9),
        name="up_wgrad",
    )(scal, nl, gu)


def down_wgrad_kernel(s_ref, ul, gd, m0, m1, m2, m3, gac, sums, keep, send):
    j = pl.program_id(0)
    core = s_ref[2]
    rel = j ^ s_ref[0]
    down = tn(ul[...], gd[...]).astype(bf16)
    put(core == 0, keep, send, 0, 0, down[0:512])
    put(core == 1, keep, send, 0, 0, down[512:768])
    extra = jnp.concatenate([sums[...], jnp.zeros((48, 768), f32)], axis=0).astype(bf16)
    put(core == 1, keep, send, 0, 448, extra)
    for r, m in enumerate((m0, m1, m2, m3)):

        @pl.when(rel == r)
        def _():
            put(core == 1, keep, send, 0, 256, mm(m[...], gac[...]).astype(bf16))


def down_wgrad(scal, ul, gd, mix, gac, sums):
    return pl.pallas_call(
        down_wgrad_kernel,
        grid_spec=pltpu.PrefetchScalarGridSpec(
            num_scalar_prefetch=1,
            grid=(4,),
            in_specs=[pl.BlockSpec((768, 768), lambda j, s: (0, j)), full((768, 768))]
            + [full((CH, 640))] * 4
            + [full((640, 768)), full((16, 768))],
            out_specs=[pl.BlockSpec((1, 512, 768), lambda j, s: (j ^ s[0], 0, 0))] * 2,
        ),
        out_shape=[jax.ShapeDtypeStruct((4, 512, 768), bf16)] * 2,
        compiler_params=params(),
        cost_estimate=cost(10),
        name="down_wgrad",
    )(scal, ul, gd, *mix, gac, sums)


def finish_kernel(s_ref, own1, other1, own2, other2, ownb, otherb, up, down, out, wq, wk, wv, small, a1, a2, b_ref):
    me, core = s_ref[0], s_ref[2]
    for buf, own, other in ((a1, own1, other1), (a2, own2, other2)):
        buf[core] = own[...]
        buf[1 - core] = other[...]
    b_ref[:, pl.ds(pl.multiple_of(96 * core, 32), 96), :] = ownb[...]
    b_ref[:, pl.ds(pl.multiple_of(96 - 96 * core, 32), 96), :] = otherb[...]
    for j in range(4):
        row = 192 * (j & 1)
        up[:, 768 * j : 768 * j + 768] = a1[j >> 1, row : row + 192, :].astype(f32)
    down[0:512, :] = a2[0].astype(f32)
    down[512:768, :] = a2[1, 0:256, :].astype(f32)
    out[...] = a2[1, 256:448, :].astype(f32)
    small[...] = a2[1, 448:464, :].astype(f32)
    r_i, c_i = iota2((256, 768))
    totals = [jnp.zeros((CH, 768), f32)] * 3
    for r in range(4):
        base = 192 * (me ^ r)
        hit = (c_i - base == r_i) & (r_i < 192)
        move = hit.astype(f32).astype(bf16)
        for k in range(3):
            totals[k] = totals[k] + mm(b_ref[r, :, 256 * k : 256 * k + 256], move)
    wq[...], wk[...], wv[...] = totals


def finish(scal, *parts):
    sds = jax.ShapeDtypeStruct
    return pl.pallas_call(
        finish_kernel,
        in_specs=[smem()] + [vmem()] * 6,
        out_specs=[vmem()] * 7,
        out_shape=[sds((CH, 3072), f32), sds((768, 768), f32)] + [sds((CH, 768), f32)] * 4 + [sds((16, 768), f32)],
        scratch_shapes=[
            pltpu.VMEM((2, 384, 768), bf16),
            pltpu.VMEM((2, 512, 768), bf16),
            pltpu.VMEM((4, CH, 768), bf16),
        ],
        compiler_params=params(),
        cost_estimate=cost(6),
        name="weight_grads_out",
    )(scal, *parts)


def from_others(chunks):
    moved = [lax.ppermute(chunks[r], "wide", [(i, i ^ r) for i in range(4)]) for r in (3, 1, 2)]
    return [chunks[0], moved[1], moved[2], moved[0]]


def gathered(chunk):
    return from_others([chunk] * 4)


def narrow_move(v, d):
    return lax.ppermute(v, "narrow", [(i, i ^ d) for i in range(8)])


def core_move(v):
    return narrow_move(v, 1)


def added(parts):
    total = parts[0].astype(f32)
    for part in parts[1:]:
        total = total + part.astype(f32)
    return total.astype(bf16)


def along_z(v):
    return lax.psum(v, "narrow", axis_index_groups=[[2 * k + c for k in range(4)] for c in range(2)])


def after(v, *others):
    return lax.optimization_barrier((v, *others))[0]


def on_device(
    frames_in, lengths, kernel, conv_bias, w_query, b_query, w_key, w_value, b_value, w_out, b_out,
    gain_one, shift_one, w_up, b_up, w_down, b_down, gain_two, shift_two, out_grad,
):
    me = lax.axis_index("wide").astype(jnp.int32)
    place_n = lax.axis_index("narrow").astype(jnp.int32)
    core, z = place_n & 1, place_n >> 1
    li = jnp.where(lengths[0] >= lengths[1], 0, 1).astype(jnp.int32)
    scal = jnp.stack([me, li, core, z])
    frames = from_others(pack_frames(scal, frames_in))
    wt, wd = prep_weights(scal, kernel)

    def own(v):
        return lax.dynamic_slice_in_dim(v, me * CH, CH, axis=v.ndim - 1)

    def three(a, b, c):
        gap = [(0, 0)] * (a.ndim - 1) + [(0, 64)]
        return jnp.concatenate([jnp.pad(a, gap), jnp.pad(b, gap), jnp.pad(c, gap)], axis=-1)

    wqkv = three(own(w_query), own(w_key), own(w_value))
    bqkv = three(own(b_query), jnp.zeros((CH,), bf16), own(b_value)).astype(f32)[None]
    bias = jnp.pad(own(conv_bias).astype(f32).reshape(2, 2, 48), ((0, 0), (0, 0), (0, 16))).reshape(2, 1, 128)
    w_out_rel = jnp.concatenate(
        [lax.dynamic_slice_in_dim(w_out, (me ^ r) * CH, CH, axis=0) for r in range(4)], axis=0
    )
    vecs = jnp.stack([b_out, gain_one, shift_one, b_down, gain_two, shift_two]).astype(f32)
    bu = b_up.astype(f32)[None]

    pre, xp, packed = conv_fwd(scal, frames, wt, bias)
    first = gathered(packed)
    qkv, mixed_t, lse, rows, *mixed = attn_fwd(scal, first, wqkv, bqkv)
    mix = from_others(mixed)
    layer_out, ul, gu, nl, gd, gac, x0, x1, x2, x3, gst, sums = ffn(
        scal, rows, mix, w_out_rel, w_up, bu, w_down, vecs, out_grad
    )
    dparts = from_others([x0, x1, x2, x3])
    keep1, send1 = up_wgrad(scal, nl, gu)
    got1 = core_move(send1)
    keep2, send2 = down_wgrad(scal, after(ul, send1), gd, mix, gac, sums)
    halves1 = [added([keep1[r], got1[r]]) for r in range(4)]
    got2 = core_move(send2)
    d0 = after(dparts[0], *halves1)

    dqkv, g0, g1, g2, g3, qkv_sums = attn_bwd(scal, qkv, mixed_t, lse, [d0] + dparts[1:], gst, wqkv)
    moved1 = from_others(halves1)
    gs = lax.optimization_barrier((g0, g1, g2, g3, got2, *moved1[1:]))
    got2, moved1 = gs[4], moved1[:1] + list(gs[5:])
    gparts = from_others(gs[:4])
    total1 = along_z(added(moved1))
    halves2 = [added([keep2[r], got2[r]]) for r in range(4)]
    qkeep, qsend = qkv_wgrad(scal, first, after(dqkv, gparts[3]))
    p0 = after(gparts[0], qsend)

    ckeep, csend, gf, g = conv_wgrad(scal, [p0] + gparts[1:], pre, xp, qkv_sums)
    moved2 = from_others([after(h, total1, p0) for h in halves2])
    qgot = core_move(qsend)
    g, qgot, *moved2 = lax.optimization_barrier((g, qgot, *moved2))
    cgot = core_move(csend)
    total2 = along_z(added(moved2))
    qhalves = [added([qkeep[r], qgot[r]]) for r in range(4)]
    qmoved = from_others(qhalves)
    f0, f1, f2, f3 = conv_dgrad(scal, gf, g, wd)
    chalves = [added([ckeep[r], cgot[r]]) for r in range(4)]
    cmoved = from_others(chalves)
    ownb, ownc, otherb, otherc = z_sum(jnp.stack(qmoved), jnp.stack(cmoved))
    frames_grad = unpack_frames(scal, from_others([f0, f1, f2, f3]))
    up, down, out, wq, wk, wv, small = finish(
        scal, total1, core_move(total1), total2, core_move(total2), ownb, otherb
    )
    grad_kernel, tiny = kernel_out(scal, ownc, otherc)
    tiny = tiny.astype(f32)

    def mine(row):
        return lax.dynamic_slice_in_dim(small[row], me * CH, CH, axis=0)

    bias_grad = jnp.concatenate([tiny[0, 1, :128], tiny[1, 1, :128]]).reshape(4, 64)[:, :48].reshape(CH)
    grad_b_up = lax.dynamic_index_in_dim(small[:4], me, 0, keepdims=False)
    return (
        layer_out,
        frames_grad,
        grad_kernel,
        bias_grad,
        wq,
        tiny[0, 0, 0:192],
        wk,
        wv,
        tiny[0, 0, 512:704],
        out,
        mine(4),
        mine(5),
        mine(6),
        up,
        grad_b_up,
        down,
        mine(7),
        mine(8),
        mine(9),
    )


def with_halo(x, sides, width):
    for axis, dim in sides:
        count, length = (lax.axis_size(axis), x.shape[dim])
        up = [(i, (i + 1) % count) for i in range(count - 1)]
        down = [(j, i) for i, j in up]
        last = lax.slice_in_dim(x, length - width, length, axis=dim)
        initial = lax.slice_in_dim(x, 0, width, axis=dim)
        before = lax.ppermute(last, axis, up)
        after = lax.ppermute(initial, axis, down)
        x = jnp.concatenate([before, x, after], axis=dim)
    return x


def layer_norm(value, gain, shift):
    center = value - jnp.mean(value, axis=-1, keepdims=True)
    spread = jnp.mean(center * center, axis=-1, keepdims=True)
    return center * lax.rsqrt(spread + eps_norm) * gain + shift


def gelu_exact(value):
    return jax.nn.gelu(value, approximate=False)


def project(rows_in, weight):
    return jnp.einsum("cfd,de->cfe", rows_in, weight, preferred_element_type=jnp.float32)


def project_back(grad_in, weight):
    return jnp.einsum("cfe,de->cfd", grad_in, weight, preferred_element_type=jnp.float32)


def weight_grad(rows_in, grad_in):
    return jnp.einsum("cfd,cfe->de", rows_in, grad_in, preferred_element_type=jnp.float32)


def row_total(grad_in):
    return jnp.sum(grad_in.astype(jnp.float32), axis=(0, 1))


def head_view(rows_in):
    return rows_in.reshape(rows_in.shape[0], rows_in.shape[1], HEADS, rows_in.shape[2] // HEADS)


def conv_apply(padded, weight, frames):
    kernel_span, groups, inner_ch, outer_ch = weight.shape
    taps_weight = jnp.transpose(weight, (0, 2, 1, 3)).reshape(
        kernel_span, inner_ch, groups * outer_ch
    )
    result = lax.conv_general_dilated(
        padded,
        taps_weight,
        (1,),
        "VALID",
        dimension_numbers=("NWC", "WIO", "NWC"),
        feature_group_count=groups,
        preferred_element_type=jnp.float32,
    )
    return result[:, :frames, :]


def conv_weight_grad(padded, grad_in, kernel_shape):
    kernel_span, groups, inner_ch, outer_ch = kernel_shape
    result = lax.conv_general_dilated(
        padded,
        grad_in,
        (1,),
        "VALID",
        dimension_numbers=("CWN", "IWO", "NWC"),
        batch_group_count=groups,
        preferred_element_type=jnp.float32,
    )
    result = result[:, :kernel_span, :].reshape(inner_ch, kernel_span, groups, outer_ch)
    return jnp.transpose(result, (1, 2, 0, 3))


def key_valid_at(lengths, first_row, row_count):
    return (first_row + jnp.arange(row_count, dtype=jnp.int32))[None, :] < lengths[:, None]


def masked_scores(query_h, keys_h, valid_keys, score_scale):
    scores = (
        jnp.einsum("cqhd,ckhd->cqhk", query_h, keys_h, preferred_element_type=jnp.float32)
        * score_scale
    )
    return jnp.where(valid_keys[:, None, None, :], scores, neg_large)


def block_terms(query_h, grad_h, lse_rows, delta_rows, keys_h, values_h, valid_keys, score_scale):
    scores = masked_scores(query_h, keys_h, valid_keys, score_scale)
    probs = jnp.where(valid_keys[:, None, None, :], jnp.exp(scores - lse_rows[..., None]), 0.0)
    grad_probs = jnp.einsum("cqhd,ckhd->cqhk", grad_h, values_h, preferred_element_type=jnp.float32)
    grad_scores = (probs * (grad_probs - delta_rows[..., None])).astype(jnp.bfloat16)
    results = []
    results.append(
        jnp.einsum("cqhk,ckhd->cqhd", grad_scores, keys_h, preferred_element_type=jnp.float32)
        * score_scale
    )
    results.append(
        jnp.einsum("cqhk,cqhd->ckhd", grad_scores, query_h, preferred_element_type=jnp.float32)
        * score_scale
    )
    results.append(
        jnp.einsum(
            "cqhk,cqhd->ckhd",
            probs.astype(jnp.bfloat16),
            grad_h,
            preferred_element_type=jnp.float32,
        )
    )
    return tuple(results)


def on_device_any(
    frames_in,
    lengths,
    kernel,
    conv_bias,
    w_query,
    b_query,
    w_key,
    w_value,
    b_value,
    w_out,
    b_out,
    gain_one,
    shift_one,
    w_up,
    b_up,
    w_down,
    b_down,
    gain_two,
    shift_two,
    out_grad,
):
    clip_count, frames, width = frames_in.shape
    head_dim = width // HEADS
    score_scale = head_dim ** (-0.5)
    half_span = kernel.shape[0] // 2
    wide_size = lax.axis_size("wide")
    positions = lax.axis_index("wide") * frames + jnp.arange(frames, dtype=jnp.int32)
    frame_valid = positions[None, :] < lengths[:, None]
    masked = jnp.where(frame_valid[..., None], frames_in, jnp.zeros((), jnp.bfloat16))
    padded = with_halo(masked, (("wide", 1),), half_span)
    pre_act = conv_apply(padded, kernel, frames) + conv_bias.astype(jnp.float32)
    first_act, pull_first = jax.vjp(gelu_exact, pre_act)
    first_out = masked.astype(jnp.float32) + first_act
    first_low = first_out.astype(jnp.bfloat16)
    query_rows = (project(first_low, w_query) + b_query.astype(jnp.float32)).astype(jnp.bfloat16)
    key_rows = project(first_low, w_key).astype(jnp.bfloat16)
    value_rows = (project(first_low, w_value) + b_value.astype(jnp.float32)).astype(jnp.bfloat16)
    query_h = head_view(query_rows)
    per_step = max(1, min(wide_size, 512 // frames))
    while wide_size % per_step:
        per_step -= 1
    run_max = jnp.full((clip_count, frames, HEADS), neg_large, jnp.float32)
    run_acc = jnp.zeros((clip_count, frames, HEADS, head_dim), jnp.float32)
    keys_p = lax.all_gather(key_rows, "wide", axis=1, tiled=True)
    values_p = lax.all_gather(value_rows, "wide", axis=1, tiled=True)
    row_count = keys_p.shape[1]
    valid_keys = key_valid_at(lengths, jnp.int32(0), row_count)
    scores = masked_scores(query_h, head_view(keys_p), valid_keys, score_scale)
    new_max = jnp.maximum(run_max, jnp.max(scores, axis=-1))
    weights = jnp.where(valid_keys[:, None, None, :], jnp.exp(scores - new_max[..., None]), 0.0)
    factor = jnp.exp(run_max - new_max)
    run_sum = jnp.sum(weights, axis=-1)
    run_acc = run_acc * factor[..., None] + jnp.einsum(
        "cqhk,ckhd->cqhd",
        weights.astype(jnp.bfloat16),
        head_view(values_p),
        preferred_element_type=jnp.float32,
    )
    run_max, run_sum, run_acc = (new_max, run_sum, run_acc)
    lse_rows = run_max + jnp.log(run_sum)
    mixed_heads = run_acc / run_sum[..., None]
    mixed_low = mixed_heads.reshape(clip_count, frames, width).astype(jnp.bfloat16)
    attn_out = project(mixed_low, w_out) + b_out.astype(jnp.float32)
    sum_one = first_out + attn_out
    norm_one, pull_one = jax.vjp(
        layer_norm, sum_one, gain_one.astype(jnp.float32), shift_one.astype(jnp.float32)
    )
    norm_low = norm_one.astype(jnp.bfloat16)
    up_pre = project(norm_low, w_up) + b_up.astype(jnp.float32)
    up_act, pull_up = jax.vjp(gelu_exact, up_pre)
    up_low = up_act.astype(jnp.bfloat16)
    down_out = project(up_low, w_down) + b_down.astype(jnp.float32)
    sum_two = norm_one + down_out
    layer_out, pull_two = jax.vjp(
        layer_norm, sum_two, gain_two.astype(jnp.float32), shift_two.astype(jnp.float32)
    )
    grad_sum_two, grad_gain_two, grad_shift_two = pull_two(out_grad.astype(jnp.float32))
    grad_down = grad_sum_two.astype(jnp.bfloat16)
    grad_w_down = weight_grad(up_low, grad_down)
    grad_b_down = row_total(grad_down)
    grad_up = pull_up(project_back(grad_down, w_down))[0].astype(jnp.bfloat16)
    grad_w_up = weight_grad(norm_low, grad_up)
    grad_b_up = row_total(grad_up)
    grad_norm_one = grad_sum_two + project_back(grad_up, w_up)
    grad_sum_one, grad_gain_one, grad_shift_one = pull_one(grad_norm_one)
    grad_attn = grad_sum_one.astype(jnp.bfloat16)
    grad_w_out = weight_grad(mixed_low, grad_attn)
    grad_b_out = row_total(grad_attn)
    grad_mixed = project_back(grad_attn, w_out).astype(jnp.bfloat16)
    grad_h = head_view(grad_mixed)
    delta_rows = jnp.sum(grad_h.astype(jnp.float32) * mixed_heads, axis=-1)
    total_slots = wide_size * frames
    first_row = jnp.int32(0)
    grad_q = jnp.zeros((clip_count, frames, HEADS, head_dim), jnp.float32)
    grad_k_all = jnp.zeros((clip_count, total_slots, width), jnp.float32)
    grad_v_all = jnp.zeros((clip_count, total_slots, width), jnp.float32)
    keys_p = lax.all_gather(key_rows, "wide", axis=1, tiled=True)
    values_p = lax.all_gather(value_rows, "wide", axis=1, tiled=True)
    row_count = keys_p.shape[1]
    valid_keys = key_valid_at(lengths, first_row, row_count)
    part_q, part_k, part_v = block_terms(
        query_h,
        grad_h,
        lse_rows,
        delta_rows,
        head_view(keys_p),
        head_view(values_p),
        valid_keys,
        score_scale,
    )
    old_k = lax.dynamic_slice_in_dim(grad_k_all, first_row, row_count, 1)
    old_v = lax.dynamic_slice_in_dim(grad_v_all, first_row, row_count, 1)
    grad_k_all = lax.dynamic_update_slice_in_dim(
        grad_k_all, old_k + part_k.reshape(clip_count, row_count, width), first_row, 1
    )
    grad_v_all = lax.dynamic_update_slice_in_dim(
        grad_v_all, old_v + part_v.reshape(clip_count, row_count, width), first_row, 1
    )
    grad_k_own, grad_v_own = (
        lax.psum_scatter(
            grad_k_all.astype(jnp.bfloat16), "wide", scatter_dimension=1, tiled=True
        ).astype(jnp.float32),
        lax.psum_scatter(
            grad_v_all.astype(jnp.bfloat16), "wide", scatter_dimension=1, tiled=True
        ).astype(jnp.float32),
    )
    grad_q_low = (grad_q + part_q).reshape(clip_count, frames, width).astype(jnp.bfloat16)
    grad_k_low = grad_k_own.astype(jnp.bfloat16)
    grad_v_low = grad_v_own.astype(jnp.bfloat16)
    grad_w_query = weight_grad(first_low, grad_q_low)
    grad_b_query = row_total(grad_q_low)
    grad_w_key = weight_grad(first_low, grad_k_low)
    grad_w_value = weight_grad(first_low, grad_v_low)
    grad_b_value = row_total(grad_v_low)
    grad_first = (
        grad_sum_one
        + project_back(grad_q_low, w_query)
        + project_back(grad_k_low, w_key)
        + project_back(grad_v_low, w_value)
    )
    grad_pre = pull_first(grad_first)[0].astype(jnp.bfloat16)
    grad_conv_bias = row_total(grad_pre)
    grad_kernel = conv_weight_grad(padded, grad_pre, kernel.shape)
    grad_padded = with_halo(grad_pre, (("wide", 1),), half_span)
    flipped = jnp.transpose(kernel[::-1], (0, 1, 3, 2))
    grad_masked = grad_first + conv_apply(grad_padded[:, 1:], flipped, frames)
    frames_grad = jnp.where(frame_valid[..., None], grad_masked, 0.0).astype(jnp.bfloat16)
    shards = (
        lax.psum_scatter(
            grad_kernel.astype(jnp.bfloat16), "wide", scatter_dimension=0, tiled=True
        ).astype(jnp.float32),
        lax.psum_scatter(
            grad_conv_bias.astype(jnp.bfloat16), "wide", scatter_dimension=0, tiled=True
        ).astype(jnp.float32),
        lax.psum_scatter(
            grad_w_query.astype(jnp.bfloat16), "wide", scatter_dimension=0, tiled=True
        ).astype(jnp.float32),
        lax.psum_scatter(
            grad_b_query.astype(jnp.bfloat16), "wide", scatter_dimension=0, tiled=True
        ).astype(jnp.float32),
        lax.psum_scatter(
            grad_w_key.astype(jnp.bfloat16), "wide", scatter_dimension=0, tiled=True
        ).astype(jnp.float32),
        lax.psum_scatter(
            grad_w_value.astype(jnp.bfloat16), "wide", scatter_dimension=0, tiled=True
        ).astype(jnp.float32),
        lax.psum_scatter(
            grad_b_value.astype(jnp.bfloat16), "wide", scatter_dimension=0, tiled=True
        ).astype(jnp.float32),
        lax.psum_scatter(
            grad_w_out.astype(jnp.bfloat16), "wide", scatter_dimension=0, tiled=True
        ).astype(jnp.float32),
        lax.psum_scatter(
            grad_b_out.astype(jnp.bfloat16), "wide", scatter_dimension=0, tiled=True
        ).astype(jnp.float32),
        lax.psum_scatter(
            grad_gain_one.astype(jnp.bfloat16), "wide", scatter_dimension=0, tiled=True
        ).astype(jnp.float32),
        lax.psum_scatter(
            grad_shift_one.astype(jnp.bfloat16), "wide", scatter_dimension=0, tiled=True
        ).astype(jnp.float32),
        lax.psum_scatter(
            grad_w_up.astype(jnp.bfloat16), "wide", scatter_dimension=0, tiled=True
        ).astype(jnp.float32),
        lax.psum_scatter(
            grad_b_up.astype(jnp.bfloat16), "wide", scatter_dimension=0, tiled=True
        ).astype(jnp.float32),
        lax.psum_scatter(
            grad_w_down.astype(jnp.bfloat16), "wide", scatter_dimension=0, tiled=True
        ).astype(jnp.float32),
        lax.psum_scatter(
            grad_b_down.astype(jnp.bfloat16), "wide", scatter_dimension=0, tiled=True
        ).astype(jnp.float32),
        lax.psum_scatter(
            grad_gain_two.astype(jnp.bfloat16), "wide", scatter_dimension=0, tiled=True
        ).astype(jnp.float32),
        lax.psum_scatter(
            grad_shift_two.astype(jnp.bfloat16), "wide", scatter_dimension=0, tiled=True
        ).astype(jnp.float32),
    )
    totals = (
        lax.psum(shards[0].astype(jnp.bfloat16), "narrow").astype(jnp.float32),
        lax.psum(shards[1].astype(jnp.bfloat16), "narrow").astype(jnp.float32),
        lax.psum(shards[2].astype(jnp.bfloat16), "narrow").astype(jnp.float32),
        lax.psum(shards[3].astype(jnp.bfloat16), "narrow").astype(jnp.float32),
        lax.psum(shards[4].astype(jnp.bfloat16), "narrow").astype(jnp.float32),
        lax.psum(shards[5].astype(jnp.bfloat16), "narrow").astype(jnp.float32),
        lax.psum(shards[6].astype(jnp.bfloat16), "narrow").astype(jnp.float32),
        lax.psum(shards[7].astype(jnp.bfloat16), "narrow").astype(jnp.float32),
        lax.psum(shards[8].astype(jnp.bfloat16), "narrow").astype(jnp.float32),
        lax.psum(shards[9].astype(jnp.bfloat16), "narrow").astype(jnp.float32),
        lax.psum(shards[10].astype(jnp.bfloat16), "narrow").astype(jnp.float32),
        lax.psum(shards[11].astype(jnp.bfloat16), "narrow").astype(jnp.float32),
        lax.psum(shards[12].astype(jnp.bfloat16), "narrow").astype(jnp.float32),
        lax.psum(shards[13].astype(jnp.bfloat16), "narrow").astype(jnp.float32),
        lax.psum(shards[14].astype(jnp.bfloat16), "narrow").astype(jnp.float32),
        lax.psum(shards[15].astype(jnp.bfloat16), "narrow").astype(jnp.float32),
        lax.psum(shards[16].astype(jnp.bfloat16), "narrow").astype(jnp.float32),
    )
    return (
        layer_out.astype(jnp.bfloat16),
        frames_grad,
        totals[0],
        totals[1],
        totals[2],
        totals[3],
        totals[4],
        totals[5],
        totals[6],
        totals[7],
        totals[8],
        totals[9],
        totals[10],
        totals[11],
        totals[12],
        totals[13],
        totals[14],
        totals[15],
        totals[16],
    )


def solution(mesh):
    rows = P("narrow", "wide", None)
    placed = (rows, P("narrow")) + (P(),) * 17 + (rows,)
    wide = mesh.shape["wide"]
    fast = wide == 4 and mesh.shape["narrow"] == 8
    return jax.shard_map(
        on_device if fast else on_device_any,
        mesh=mesh,
        in_specs=placed,
        out_specs=(rows, rows)
        + (P("wide", None, None, None), P("wide"), P("wide", None), P("wide"), P("wide", None), P("wide", None))
        + (P("wide"), P("wide", None), P("wide"), P("wide"), P("wide"), P("wide", None), P("wide"))
        + (P("wide", None), P("wide"), P("wide"), P("wide")),
        check_vma=False,
    )
```

```python
import functools

import jax
import jax.numpy as jnp
from jax import lax
from jax.experimental import pallas as pl
from jax.experimental.pallas import tpu as pltpu
from jax.sharding import PartitionSpec as P

HEADS = 12
GROUP_CH = 48
SHORT = 102
HALF = 64
UNIQUE = SHORT + HALF
FR = 384
SLOTS = 1536
SROWS = 192
TROWS = 1792
SBASE = 1600
CH = 192
eps_norm = 1e-05
neg_large = -1e30
bf16 = jnp.bfloat16
f32 = jnp.float32
QF = 1536
QB = 768
KB = 1536
CB = 1792
VLIM = 60 * 1024 * 1024


def mm(a, b):
    return jnp.dot(a, b, preferred_element_type=f32)


def mm_nt(a, b):
    return lax.dot_general(a, b, (((1,), (1,)), ((), ())), preferred_element_type=f32)


def iota2(shape):
    return lax.broadcasted_iota(jnp.int32, shape, 0), lax.broadcasted_iota(jnp.int32, shape, 1)


def place(shape, rows_from, rows_to, cols_from):
    r, c = iota2(shape)
    hit = (c - cols_from == r - rows_from) & (r >= rows_from) & (r < rows_to)
    return hit.astype(f32).astype(bf16)


def spread(shape, lane0, start):
    r, c = iota2(shape)
    slot, inner = c >> 6, c & 63
    hit = (r == lane0 + start + slot * GROUP_CH + inner) & (inner < GROUP_CH)
    return hit.astype(f32).astype(bf16)


def gather_slots(shape, col0):
    r, c = iota2(shape)
    slot, inner = r >> 6, r & 63
    hit = (c == col0 + slot * GROUP_CH + inner) & (inner < GROUP_CH)
    return hit.astype(f32).astype(bf16)


def full(shape):
    return pl.BlockSpec(shape, lambda *_: (0,) * len(shape))


def smem():
    return pl.BlockSpec(memory_space=pltpu.SMEM)


def vmem():
    return pl.BlockSpec(memory_space=pltpu.VMEM)


def params(**kw):
    return pltpu.CompilerParams(vmem_limit_bytes=VLIM, **kw)


def cost(us):
    return pl.CostEstimate(flops=int(us * 1e9), bytes_accessed=int(us * 3.4e6), transcendentals=0)


def put(keeping, keep, send, rel, row0, data, lane0=0):
    rows, lanes = data.shape

    @pl.when(keeping)
    def _():
        keep[rel, row0 : row0 + rows, lane0 : lane0 + lanes] = data

    @pl.when(jnp.logical_not(keeping))
    def _():
        send[rel, row0 : row0 + rows, lane0 : lane0 + lanes] = data


def xor2(a, b):
    return (a + b) % 2 + 2 * ((a // 2 + b // 2) % 2)


def gelu_parts(v):
    cdf = 0.5 * (1.0 + lax.erf(v * (2.0 ** -0.5)))
    return cdf


def density(v):
    return jnp.exp(-0.5 * v * v) * 0.3989422804014327


def pack_frames_kernel(s_ref, x_ref, *outs):
    me, li = s_ref[0], s_ref[1]
    long, short = x_ref[li], x_ref[1 - li]
    slot = me * FR + lax.broadcasted_iota(jnp.int32, (128, 768), 0)
    short = jnp.where(slot < SHORT, short[:128].astype(f32), 0.0).astype(bf16)
    top = long[:256]
    low = jnp.concatenate([long[256:], short], axis=0)
    for d in range(4):
        first = 192 * d - (64 if d % 2 else 0)
        skip = 64 if d % 2 else 0
        chunk = mm(top[:, first : first + 256], place((256, 384), skip, skip + 192, 0)) + mm(
            low[:, first : first + 256], place((256, 384), skip, skip + 192, 192)
        )
        chunk = chunk.astype(bf16)
        for r in range(4):

            @pl.when((me ^ d) == r)
            def _():
                outs[r][...] = chunk


def pack_frames(scal, frames_in):
    return pl.pallas_call(
        pack_frames_kernel,
        out_shape=[jax.ShapeDtypeStruct((256, 384), bf16)] * 4,
        in_specs=[smem(), vmem()],
        out_specs=[vmem()] * 4,
        compiler_params=params(),
        cost_estimate=cost(3),
        name="pack_frames",
    )(scal, frames_in)


def prep_kernel(s_ref, w_ref, wt_ref, wd_ref, z_ref, taps):
    left, right = place((48, 128), 0, 48, 0), place((48, 128), 0, 48, 64)
    wt_ref[...] = jnp.zeros_like(wt_ref)
    z_ref[...] = jnp.zeros_like(z_ref)
    for i in range(48):
        taps[pl.ds(i, 128, stride=48), 0:48] = w_ref[0, i].astype(f32).T

    def rows(k, n):
        return taps[48 * k : 48 * (k + n), 0:48].astype(bf16)

    for k2 in range(8):
        pairs = rows(16 * k2, 16).reshape(8, 2, 48, 48)
        tile = mm(pairs[:, 0].reshape(384, 48), left) + mm(pairs[:, 1].reshape(384, 48), right)
        tile = tile.astype(bf16)
        for p in range(8):
            wt_ref[0, 64 * k2 : 64 * k2 + 48, 128 * p : 128 * p + 128] = tile[48 * p : 48 * p + 48]
    for q in range(4):
        tile = mm(rows(112 - 32 * q, 16), left) + mm(rows(96 - 32 * q, 16), right)
        for b in range(16):
            z_ref[64 * b : 64 * b + 48, :] = tile[48 * (15 - b) : 48 * (15 - b) + 48]
        wd_ref[0, 128 * q : 128 * q + 128, :] = z_ref[...].T.astype(bf16)


def prep_weights(scal, kernel):
    return pl.pallas_call(
        prep_kernel,
        grid_spec=pltpu.PrefetchScalarGridSpec(
            num_scalar_prefetch=1,
            grid=(4,),
            in_specs=[pl.BlockSpec((1, 48, 48, 128), lambda g, s: (4 * s[0] + g, 0, 0, 0))],
            out_specs=[pl.BlockSpec((1, 512, 1024), lambda g, s: (g, 0, 0))] * 2,
            scratch_shapes=[pltpu.VMEM((1024, 128), f32), pltpu.VMEM((48 * 128, 128), f32)],
        ),
        out_shape=[jax.ShapeDtypeStruct((4, 512, 1024), bf16)] * 2,
        compiler_params=params(),
        cost_estimate=cost(11),
        name="conv_weights",
    )(scal, jnp.transpose(kernel, (1, 2, 3, 0)))


def pair_slots(t_ref, rows):
    wide = jnp.concatenate([t_ref[0:rows, :], t_ref[16 : rows + 16, :]], axis=1)
    r, c = iota2((256, 128))
    out = []
    for j in range(2):
        hit = ((r < 128) & (c == r - 64 * j) & (c < 64)) | ((r >= 128) & (c - 64 == r - 128 - 64 * j) & (c >= 64))
        out.append(mm(wide, hit.astype(f32).astype(bf16)).astype(bf16))
    return out


def conv_block(p_refs, w_ref, y_ref, s_ref, shift):
    lane = lax.broadcasted_iota(jnp.int32, (CB, 128), 1)
    parts = []
    for j in range(2):
        lhs = jnp.concatenate([p_refs[j][32 * q : 32 * q + CB + 16, :] for q in range(4)], axis=1)
        y_ref[...] = mm(lhs, w_ref[j])
        total = y_ref[shift : shift + CB + 1, 0:128]
        for p in range(1, 8):
            total += y_ref[shift + 2 * p : shift + 2 * p + CB + 1, 128 * p : 128 * p + 128]
        s_ref[0 : CB + 1, :] = total
        here, after = s_ref[0:CB, :], s_ref[1 : CB + 1, :]
        if j == 0:
            parts.append(here + pltpu.roll(after, 64, 1))
        else:
            parts.append(pltpu.roll(here, 64, 1) + after)
    return jnp.where(lane < 64, parts[0], parts[1])


def conv_fwd_kernel(s_ref, c0, c1, c2, c3, w_ref, b_ref, pre_ref, x_ref, packed_ref, p0, p1, y_ref, t_ref, first):
    c = pl.program_id(0)
    me = s_ref[0]
    chunks = (c0, c1, c2, c3)
    x_ref[0, 0:64, :] = jnp.zeros((64, 128), bf16)
    x_ref[0, 1600:1664, :] = jnp.zeros((64, 128), bf16)
    x_ref[0, 1792:1936, :] = jnp.zeros((144, 128), bf16)
    top_map = spread((256, 128), 0, 96 * c)
    low_map = spread((256, 128), 64, 96 * c)
    for r in range(4):
        src = me ^ r
        top = mm(chunks[r][:, 0:256], top_map).astype(bf16)
        low = mm(chunks[r][:, 128:384], low_map).astype(bf16)
        base = pl.multiple_of(64 + FR * src, 64)
        x_ref[0, pl.ds(base, 256), :] = top
        x_ref[0, pl.ds(pl.multiple_of(base + 256, 64), 128), :] = low[:128]

        @pl.when(src == 0)
        def _():
            x_ref[0, 1664:1792, :] = low[128:]

    a, b = pair_slots(x_ref.at[0], 1920)
    p0[...] = a
    p1[...] = b
    bias = b_ref[0]

    pre = conv_block((p0, p1), w_ref, y_ref, t_ref, 0) + bias
    pre_ref[0] = pre
    center = x_ref[0, 64 : 64 + CB, :].astype(f32)
    first[c] = (center + pre * gelu_parts(pre)).astype(bf16)

    @pl.when(c == 1)
    def _():
        h0, h1 = gather_slots((256, 384), 0), gather_slots((256, 384), 192)

        def rows(lo, n):
            return jnp.concatenate([first[0, lo : lo + n, :], first[1, lo : lo + n, :]], axis=1)

        packed_ref[0:768, :] = (mm(rows(0, 768), h0) + mm(rows(768, 768), h1)).astype(bf16)
        packed_ref[768:864, :] = (mm(rows(SBASE, 96), h0) + mm(rows(SBASE + 96, 96), h1)).astype(bf16)


def conv_fwd(scal, chunks, wt, bias):
    return pl.pallas_call(
        conv_fwd_kernel,
        grid=(2,),
        in_specs=[smem()]
        + [full((256, 384))] * 4
        + [pl.BlockSpec((2, 512, 1024), lambda c: (c, 0, 0)), pl.BlockSpec((1, 1, 128), lambda c: (c, 0, 0))],
        out_specs=[
            pl.BlockSpec((1, TROWS, 128), lambda c: (c, 0, 0)),
            pl.BlockSpec((1, 1936, 128), lambda c: (c, 0, 0)),
            full((864, 384)),
        ],
        out_shape=[
            jax.ShapeDtypeStruct((2, TROWS, 128), f32),
            jax.ShapeDtypeStruct((2, 1936, 128), bf16),
            jax.ShapeDtypeStruct((864, 384), bf16),
        ],
        scratch_shapes=[
            pltpu.VMEM((1920, 128), bf16),
            pltpu.VMEM((1920, 128), bf16),
            pltpu.VMEM((CB + 16, 1024), f32),
            pltpu.VMEM((CB + 8, 128), f32),
            pltpu.VMEM((2, TROWS, 128), bf16),
        ],
        compiler_params=params(),
        cost_estimate=cost(19),
        name="conv_fwd",
    )(scal, *chunks, wt, bias)


def attn_fwd_kernel(
    s_ref, c0, c1, c2, c3, w_ref, b_ref, qkv_ref, ot_ref, lse_ref, rows_ref, x0, x1, x2, x3, wz, vt
):
    me = s_ref[0]
    chunks = (c0, c1, c2, c3)
    wz[:, 0:64, :] = jnp.zeros((4, 64, 768), bf16)
    wz[:, 256:320, :] = jnp.zeros((4, 64, 768), bf16)
    for r in range(4):
        wz[r, 64:256, :] = w_ref[pl.ds(pl.multiple_of(192 * (me ^ r), 64), 192), :]
    bias = b_ref[...]
    for half in range(2):
        row0 = 64 * (1 - half)

        def project(start, n):
            total = bias + jnp.zeros((n, 768), f32)
            for r in range(4):
                total += mm(
                    chunks[r][pl.ds(start, n), 128 * half : 128 * half + 256], wz[r, row0 : row0 + 256, :]
                )
            return total.astype(bf16)

        def body(j, carry):
            start = pl.multiple_of(256 * j, 256)
            qkv_ref[pl.ds(pl.multiple_of(768 * half + start, 256), 256), :] = project(start, 256)
            return carry

        lax.fori_loop(0, 3, body, 0)
        qkv_ref[SLOTS + 96 * half : SLOTS + 96 * half + 96, :] = project(768, 96)
    qkv_ref[SLOTS + SROWS : TROWS, :] = jnp.zeros((TROWS - SLOTS - SROWS, 768), bf16)

    half = me >> 1
    start = pl.multiple_of(FR * (me & 1), 128)
    lane0 = pl.multiple_of(128 * half, 128)
    r_i, c_i = iota2((256, 768))
    own = jnp.zeros((FR, 768), f32)
    extra0 = jnp.zeros((96, 768), f32)
    extra1 = jnp.zeros((96, 768), f32)
    for r in range(4):
        base = 192 * (me ^ r)
        inside = (c_i >= base) & (c_i < base + 192)
        sel0 = ((c_i - base == r_i) & inside).astype(f32).astype(bf16)
        sel1 = ((c_i - base == r_i - 64) & inside).astype(f32).astype(bf16)
        mid = ((c_i - base == r_i - 64 * half) & inside).astype(f32).astype(bf16)
        own += mm(chunks[r][pl.ds(start, FR), pl.ds(lane0, 256)], mid)
        extra0 += mm(chunks[r][768:864, 0:256], sel0)
        extra1 += mm(chunks[r][768:864, 128:384], sel1)
    rows_ref[0:FR, :] = own.astype(bf16)
    rows_ref[FR : FR + 96, :] = extra0.astype(bf16)
    rows_ref[FR + 96 : FR + 192, :] = extra1.astype(bf16)

    vt[...] = qkv_ref[:, 512:704].astype(f32).T.astype(bf16)
    lse_ref[...] = jnp.zeros_like(lse_ref)
    for h in range(3):
        cols = slice(64 * h, 64 * h + 64)

        def attend(q0, queries, key0, keys, masked):
            query = (qkv_ref[q0 : q0 + queries, 0:256][:, cols].astype(f32) * 0.125).astype(bf16)
            key = qkv_ref[key0 : key0 + keys, 256:512][:, cols]
            scores = mm_nt(key, query)
            if masked:
                slot = lax.broadcasted_iota(jnp.int32, scores.shape, 0)
                scores = jnp.where(slot < SHORT, scores, neg_large)
            top = jnp.max(scores, axis=0, keepdims=True)
            weights = jnp.exp(scores - top)
            total = jnp.sum(weights, axis=0, keepdims=True)
            out = mm(vt[cols, key0 : key0 + keys], weights.astype(bf16))
            ot_ref[cols, q0 : q0 + queries] = out / total
            lse_ref[h : h + 1, q0 : q0 + queries] = top + jnp.log(total)

        for q0 in range(0, SLOTS, QF):
            attend(q0, QF, 0, SLOTS, False)
        attend(SLOTS, 256, SLOTS, 128, True)
    for r, out in enumerate((x0, x1, x2, x3)):
        out[:, 0:FR] = ot_ref[:, pl.ds(pl.multiple_of(FR * (me ^ r), 128), FR)].astype(bf16)
        out[:, FR:640] = ot_ref[:, SLOTS:TROWS].astype(bf16)


def attn_fwd(scal, chunks, wqkv, bqkv):
    return pl.pallas_call(
        attn_fwd_kernel,
        in_specs=[smem()] + [vmem()] * 6,
        out_specs=[vmem()] * 8,
        out_shape=[
            jax.ShapeDtypeStruct((TROWS, 768), bf16),
            jax.ShapeDtypeStruct((CH, TROWS), f32),
            jax.ShapeDtypeStruct((8, TROWS), f32),
            jax.ShapeDtypeStruct((576, 768), bf16),
        ]
        + [jax.ShapeDtypeStruct((CH, 640), bf16)] * 4,
        scratch_shapes=[pltpu.VMEM((4, 320, 768), bf16), pltpu.VMEM((CH, TROWS), bf16)],
        compiler_params=params(),
        cost_estimate=cost(28),
        name="attn_fwd",
    )(scal, *chunks, wqkv, bqkv)


def attn_bwd_kernel(
    s_ref, qkv_ref, ot_ref, lse_ref, d0, d1, d2, d3, gs_ref, w_ref,
    dqkv_ref, g0, g1, g2, g3, sums_ref, dot_, do_, kt, delta, dqt, dk, dv,
):
    me = s_ref[0]
    parts = (d0, d1, d2, d3)
    short = jnp.zeros((CH, 256), f32)
    for r in range(4):
        src = me ^ r
        dot_[:, pl.ds(pl.multiple_of(FR * src, 128), FR)] = parts[r][:, 0:FR]
        short += parts[r][:, FR : FR + 256].astype(f32)
    dot_[:, SLOTS:TROWS] = short.astype(bf16)
    whole = dot_[...].astype(f32)
    do_[...] = whole.T.astype(bf16)
    prod = whole * ot_ref[...]
    delta[...] = jnp.zeros_like(delta)
    for h in range(3):
        delta[h : h + 1, :] = jnp.sum(prod[64 * h : 64 * h + 64], axis=0, keepdims=True)
    kt[...] = qkv_ref[:, 256:448].astype(f32).T.astype(bf16)

    for h in range(3):
        cols = slice(64 * h, 64 * h + 64)
        dk[...] = jnp.zeros_like(dk)
        dv[...] = jnp.zeros_like(dv)

        def step(q0, queries, key0, keys, masked):
            at_q = pl.ds(q0, queries)
            query = qkv_ref[at_q, 0:256][:, cols]
            scaled = (query.astype(f32) * 0.125).astype(bf16)
            grad = do_[at_q, :][:, cols]
            grad_t = dot_[cols, at_q]
            lse = lse_ref[h : h + 1, at_q]
            dl = delta[h : h + 1, at_q]
            grad_q = jnp.zeros((64, queries), f32)
            piece = min(keys, KB)
            for at in range(key0, key0 + keys, piece):
                key = qkv_ref[at : at + piece, 256:512][:, cols]
                val = qkv_ref[at : at + piece, 512:768][:, cols]
                probs = jnp.exp(mm_nt(key, scaled) - lse)
                if masked:
                    slot = lax.broadcasted_iota(jnp.int32, probs.shape, 0)
                    probs = jnp.where(slot < SHORT, probs, 0.0)
                grad_p = mm(val, grad_t)
                grad_s = (probs * (grad_p - dl)).astype(bf16)
                dv[at : at + piece, :] += mm(probs.astype(bf16), grad)
                dk[at : at + piece, :] += mm(grad_s, query)
                grad_q += mm(kt[cols, at : at + piece], grad_s)
            dqt[cols, at_q] = grad_q * 0.125

        for q0 in range(0, SLOTS, QB):
            step(q0, QB, 0, SLOTS, False)
        step(SLOTS, 256, SLOTS, 128, True)
        zeros = jnp.zeros((TROWS, 64), f32)
        if h == 0:
            keep_k, keep_v = [], []
        keep_k.append((dk[...] * 0.125).astype(bf16))
        keep_v.append(dv[...].astype(bf16))
    dqkv_ref[:, 0:192] = dqt[...].T.astype(bf16)
    dqkv_ref[:, 192:256] = jnp.zeros((TROWS, 64), bf16)
    dqkv_ref[:, 256:512] = jnp.concatenate(keep_k + [zeros.astype(bf16)], axis=1)
    dqkv_ref[:, 512:768] = jnp.concatenate(keep_v + [zeros.astype(bf16)], axis=1)
    sums_ref[...] = jnp.sum(dqkv_ref[...].astype(f32), axis=0, keepdims=True)
    outs = (g0, g1, g2, g3)
    lanes = pl.multiple_of(FR * me, 128)
    for r in range(4):
        rows = pl.ds(pl.multiple_of(192 * (me ^ r), 64), 192)
        part = mm_nt(w_ref[rows, :], dqkv_ref[...])
        outs[r][...] = part.astype(bf16)
        own = gs_ref[rows, 0:FR].astype(f32)
        outs[r][:, pl.ds(lanes, FR)] = (outs[r][:, pl.ds(lanes, FR)].astype(f32) + own).astype(bf16)
        outs[r][:, SLOTS:TROWS] = (part[:, SLOTS:TROWS] + gs_ref[rows, FR : FR + 256].astype(f32)).astype(bf16)


def attn_bwd(scal, qkv, ot, lse, dparts, gst, wqkv):
    return pl.pallas_call(
        attn_bwd_kernel,
        in_specs=[smem()] + [vmem()] * 9,
        out_specs=[vmem()] * 6,
        out_shape=[jax.ShapeDtypeStruct((TROWS, 768), bf16)]
        + [jax.ShapeDtypeStruct((CH, TROWS), bf16)] * 4
        + [jax.ShapeDtypeStruct((1, 768), f32)],
        scratch_shapes=[
            pltpu.VMEM((CH, TROWS), bf16),
            pltpu.VMEM((TROWS, CH), bf16),
            pltpu.VMEM((CH, TROWS), bf16),
            pltpu.VMEM((8, TROWS), f32),
            pltpu.VMEM((CH, TROWS), f32),
            pltpu.VMEM((TROWS, 64), f32),
            pltpu.VMEM((TROWS, 64), f32),
        ],
        compiler_params=params(),
        cost_estimate=cost(33),
        name="attn_bwd",
    )(scal, qkv, ot, lse, *dparts, gst, wqkv)


def qkv_wgrad_kernel(s_ref, c0, c1, c2, c3, d_ref, keep, send):
    core = s_ref[2]
    for r, chunk in enumerate((c0, c1, c2, c3)):
        turned = chunk[...].astype(f32).T.astype(bf16)
        value = (
            mm(turned[0:192, 0:768], d_ref[0:768, :])
            + mm(turned[0:192, 768:864], d_ref[SLOTS : SLOTS + 96, :])
            + mm(turned[192:384, 0:768], d_ref[768:1536, :])
            + mm(turned[192:384, 768:864], d_ref[SLOTS + 96 : SLOTS + 192, :])
        ).astype(bf16)
        put(core == 0, keep, send, r, 0, value[0:96])
        put(core == 1, keep, send, r, 0, value[96:192])


def qkv_wgrad(scal, chunks, dqkv):
    return pl.pallas_call(
        qkv_wgrad_kernel,
        in_specs=[smem()] + [vmem()] * 5,
        out_specs=[vmem()] * 2,
        out_shape=[jax.ShapeDtypeStruct((4, 96, 768), bf16)] * 2,
        compiler_params=params(),
        cost_estimate=cost(8),
        name="qkv_wgrad",
    )(scal, *chunks, dqkv)


def wgrad_pair(pair, me, parts, pre_ref, x_ref, sums_ref, half, gf, g_ref, gp, p0, p1, bb, g2, xt):
    at = pl.ds(pl.multiple_of(96 * pair, 32), 96)
    total = parts[0][at, :].astype(f32)
    for part in parts[1:]:
        total += part[at, :].astype(f32)
    pad = jnp.zeros((16, TROWS), f32)
    rows = jnp.concatenate([total[0:48], pad, total[48:96], pad], axis=0)
    gf[0:SLOTS, :] = rows[:, 0:SLOTS].T
    gf[SLOTS:SBASE, :] = jnp.zeros((SBASE - SLOTS, 128), f32)
    gf[SBASE:TROWS, :] = rows[:, SLOTS:TROWS].T[0 : TROWS - SBASE]
    g_ref[0:64, :] = jnp.zeros((64, 128), bf16)
    g_ref[1856:1936, :] = jnp.zeros((80, 128), bf16)
    gp[0:16, :] = jnp.zeros((16, 128), f32)
    pre = pre_ref[pair]
    slope = gelu_parts(pre) + pre * density(pre)
    wide = (gf[...] * slope).astype(bf16).astype(f32)
    bias_sum = jnp.sum(wide, axis=0, keepdims=True)
    row = lax.broadcasted_iota(jnp.int32, (TROWS, 128), 0)
    wide = jnp.where(row < SBASE + UNIQUE, wide, 0.0)
    gp[16 : 16 + TROWS, :] = wide
    g_ref[64 : 64 + TROWS, :] = wide.astype(bf16)
    extra = jnp.concatenate(
        [sums_ref[...], jnp.concatenate([bias_sum, jnp.zeros((1, 640), f32)], axis=1), jnp.zeros((14, 768), f32)], axis=0
    )
    for r in range(4):
        half[r, 192:208, :] = extra.astype(bf16)

    lane = lax.broadcasted_iota(jnp.int32, (TROWS, 128), 1)
    here, before = gp[16 : 16 + TROWS, :], gp[15 : 15 + TROWS, :]
    a, b = pair_slots(x_ref.at[pair], 1920)
    p0[...] = a
    p1[...] = b
    pack0, pack1 = gather_slots((256, 384), 0), gather_slots((256, 384), 192)
    for j in range(2):
        bb[0:16, :] = jnp.zeros((16, 128), f32)
        if j == 0:
            bb[16 : 16 + TROWS, :] = jnp.where(lane < 64, here, pltpu.roll(before, 64, 1))
        else:
            bb[16 : 16 + TROWS, :] = jnp.where(lane < 64, pltpu.roll(here, 64, 1), before)
        for p in range(8):
            g2[:, 128 * p : 128 * p + 128] = bb[16 - 2 * p : 16 - 2 * p + TROWS, :].astype(bf16)
        slots = (p0, p1)[j]
        for q in range(4):
            xt[128 * q : 128 * q + 128, :] = slots[32 * q : 32 * q + TROWS, :].astype(f32).T.astype(bf16)
        for side in range(2):
            base = 512 * side
            left = mm(xt[...], g2[:, base : base + 256]).astype(bf16)
            right = mm(xt[...], g2[:, base + 256 : base + 512]).astype(bf16)
            packed = (mm(left, pack0) + mm(right, pack1)).astype(bf16)
            for m in range(4):
                tile = jnp.concatenate([packed[128 * m : 128 * m + 48], packed[128 * m + 64 : 128 * m + 112]], axis=0)
                half[xor2(me, m), 96 * j : 96 * j + 96, 384 * side : 384 * side + 384] = tile


def conv_sync_kernel(
    c0, c1, c2, c3, pre_ref, x_ref, sums_ref, wd_ref, a0, a1, a2, a3, b0, b1, b2, b3,
    fa, fb, fc, oa, ob, oc, f0, f1, f2, f3,
    gp, p0, p1, bb, g2, xt, y_ref, t_ref, gf, g, fg, s1, s2, s3,
    csend, ckeep, cgot, ra, rb, rc, xa, xb, ea, eb, ec, ya, yb, yc,
    ss, so, re, rr, sc, rcv, wide_s, wide_r, core_s, core_r,
):
    n, me = lax.axis_index("narrow"), lax.axis_index("wide")
    z, core = n // 2, n % 2
    MESH = pl.DeviceIdType.MESH

    def copy(src, dst, send, recv, device):
        return pltpu.make_async_remote_copy(
            src_ref=src, dst_ref=dst, send_sem=send, recv_sem=recv, device_id=device, device_id_type=MESH
        )

    def along(zz, cc=core):
        return (2 * zz + cc, me)

    barrier = pltpu.get_barrier_semaphore()

    def greet(device):
        pl.semaphore_signal(barrier, inc=1, device_id=device, device_id_type=MESH)

    for r in range(1, 4):
        greet((n, xor2(me, r)))
    greet(along(z, 1 - core))

    @pl.when(z > 0)
    def _():
        greet(along(z - 1))

    @pl.when(z < 3)
    def _():
        greet(along(z + 1))

    pl.semaphore_wait(barrier, 4 + jnp.minimum(z, 1) + jnp.minimum(3 - z, 1))

    def over_wide(which, r, src, dst):
        return copy(src, dst, wide_s.at[3 * which + r - 1], wide_r.at[3 * which + r - 1], (n, xor2(me, r)))

    send_b = [over_wide(0, r, (b1, b2, b3)[r - 1], rb.at[r - 1]) for r in (3, 1, 2)]
    send_a = [over_wide(1, r, (a1, a2, a3)[r - 1], ra.at[r - 1]) for r in (3, 1, 2)]
    for c in send_b + send_a:
        c.start()

    pieces = [(0, r, 0, 96) for r in range(4)] + [(1, None, 128 * r, 128) for r in range(4)]
    for r in range(4):
        pieces += [(2, r, 0, 112), (2, r, 112, 96)]
    count = len(pieces)
    set_b, set_a, set_c = range(0, 4), range(4, 8), range(8, count)

    def views(refs):
        out = []
        for which, r, row, rows in pieces:
            ref = refs[which]
            out.append(ref.at[row : row + rows] if r is None else ref.at[r, row : row + rows])
        return out

    x, e, y, f, o = (views(refs) for refs in ((xb, xa, csend), (eb, ea, ec), (yb, ya, yc), (fb, fa, fc), (ob, oa, oc)))

    def first(k, here):
        return k % 2 == (0 if here == 1 else 1)

    def swap(k):
        return copy(f[k], o[k], sc.at[k], rcv.at[k], along(z, 1 - core))

    def inward(k, here):
        return copy(x[k], e[k], ss.at[k], re.at[k], along(1 if here == 0 else 2))

    def across(k, here):
        src = y[k] if first(k, here) else f[k]
        return copy(src, src, ss.at[k], rr.at[k], along(3 - here))

    def outward(k, here):
        return copy(f[k], f[k], so.at[k], rr.at[k], along(0 if here == 1 else 3))

    def at_ends(do):
        pl.when(z == 0)(lambda: do(0))
        pl.when(z == 3)(lambda: do(3))

    def at_inner(do):
        pl.when(z == 1)(lambda: do(1))
        pl.when(z == 2)(lambda: do(2))

    def begin(ks):
        def do(here):
            for k in ks:
                inward(k, here).start()

        at_ends(do)

    def meet(ks, here):
        for k in ks:
            inward(k, here).wait_recv()
            if first(k, here):
                y[k][...] = (x[k][...].astype(f32) + e[k][...].astype(f32)).astype(bf16)
                across(k, here).start()

    def close(ks, here):
        for k in ks:
            if not first(k, here):
                across(k, here).wait_recv()
                f[k][...] = (x[k][...].astype(f32) + e[k][...].astype(f32) + y[k][...].astype(f32)).astype(bf16)
                across(k, here).start()
                outward(k, here).start()
                swap(k).start()

    def pass_on(ks, here):
        for k in ks:
            if first(k, here):
                across(k, here).wait_recv()
                outward(k, here).start()
                swap(k).start()

    def wgrad(pair, half, slot):
        wgrad_pair(
            pair, me, (c0, c1, c2, c3), pre_ref, x_ref, sums_ref, half, gf.at[slot], g.at[slot],
            gp, p0, p1, bb, g2, xt,
        )

    def dgrad(pair, slot):
        a, b = pair_slots(g.at[slot], 1920)
        p0[...] = a
        p1[...] = b
        value = conv_block((p0, p1), wd_ref.at[pl.ds(2 * pair, 2)], y_ref, t_ref, 1) + gf[slot]
        fg[pair] = value.astype(bf16)

    wgrad(1 - core, csend, 0)
    to_core = copy(csend, cgot, core_s, core_r, along(z, 1 - core))
    to_core.start()
    for c in send_b:
        c.wait()
    for r, own in enumerate((b0, b1, b2, b3)):
        xb[r] = b0[...] if r == 0 else rb[r - 1]
    begin(set_b)

    wgrad(core, ckeep, 1)
    to_core.wait()
    for r in range(4):
        ckeep[r] = (ckeep[r].astype(f32) + cgot[r].astype(f32)).astype(bf16)
    send_c = [over_wide(2, r, ckeep.at[r], rc.at[r - 1]) for r in (3, 1, 2)]
    for c in send_c:
        c.start()
    at_inner(lambda here: meet(set_b, here))
    dgrad(1 - core, 0)
    at_inner(lambda here: close(set_b, here))
    for c in send_a:
        c.wait()
    xa[...] = (a0[...].astype(f32) + ra[0].astype(f32) + ra[1].astype(f32) + ra[2].astype(f32)).astype(bf16)
    begin(set_a)
    dgrad(core, 1)
    pack0, pack1 = gather_slots((256, 384), 0), gather_slots((256, 384), 192)

    def rows_of(lo, rows):
        return jnp.concatenate([fg[0, lo : lo + rows, :], fg[1, lo : lo + rows, :]], axis=1)

    outs = (f0, s1, s2, s3)
    for d in range(4):
        low = jnp.concatenate([rows_of(FR * d + 256, 128), rows_of(SBASE, 128)], axis=0)
        chunk = (mm(rows_of(FR * d, 256), pack0) + mm(low, pack1)).astype(bf16)
        for r in range(4):

            @pl.when(xor2(me, d) == r)
            def _():
                outs[r][...] = chunk

    for c in send_c:
        c.wait()
    csend[0] = ckeep[0]
    for r in range(1, 4):
        csend[r] = rc[r - 1]
    begin(set_c)
    send_f = [over_wide(3, r, (s1, s2, s3)[r - 1], (f1, f2, f3)[r - 1]) for r in (3, 1, 2)]
    for c in send_f:
        c.start()

    def inner(here):
        pass_on(set_b, here)
        rest = list(set_a) + list(set_c)
        for i in range(0, len(rest), 2):
            pair = rest[i : i + 2]
            meet(pair, here)
            close(pair, here)
            if i:
                pass_on(rest[i - 2 : i], here)
        pass_on(rest[-2:], here)
        for k in range(count):
            across(k, here).wait_send()
            outward(k, here).wait_send()
            swap(k).wait()

    def outer(here):
        for k in range(count):
            copy(f[k], f[k], so.at[k], rr.at[k], along(z)).wait_recv()
            swap(k).start()
        for k in range(count):
            inward(k, here).wait_send()
            swap(k).wait()

    at_inner(inner)
    at_ends(outer)
    for c in send_f:
        c.wait()


def conv_sync(parts, pre, xp, sums, wd, ffn_halves, qkv_halves):
    sds = jax.ShapeDtypeStruct
    shapes = [(512, 768), (4, 96, 768), (4, 208, 768)]
    sem = pltpu.SemaphoreType.DMA
    return pl.pallas_call(
        conv_sync_kernel,
        in_specs=[vmem()] * 16,
        out_specs=[vmem()] * 10,
        out_shape=[sds(v, bf16) for v in shapes * 2] + [sds((256, 384), bf16)] * 4,
        scratch_shapes=[
            pltpu.VMEM((16 + TROWS, 128), f32),
            pltpu.VMEM((1920, 128), bf16),
            pltpu.VMEM((1920, 128), bf16),
            pltpu.VMEM((16 + TROWS, 128), f32),
            pltpu.VMEM((TROWS, 1024), bf16),
            pltpu.VMEM((512, TROWS), bf16),
            pltpu.VMEM((CB + 16, 1024), f32),
            pltpu.VMEM((CB + 8, 128), f32),
            pltpu.VMEM((2, TROWS, 128), f32),
            pltpu.VMEM((2, 1936, 128), bf16),
            pltpu.VMEM((2, TROWS, 128), bf16),
        ]
        + [pltpu.VMEM((256, 384), bf16)] * 3
        + [pltpu.VMEM((4, 208, 768), bf16)] * 3
        + [pltpu.VMEM((3, 512, 768), bf16), pltpu.VMEM((3, 96, 768), bf16), pltpu.VMEM((3, 208, 768), bf16)]
        + [pltpu.VMEM((512, 768), bf16), pltpu.VMEM((4, 96, 768), bf16)]
        + [pltpu.VMEM((512, 768), bf16), pltpu.VMEM((4, 96, 768), bf16), pltpu.VMEM((4, 208, 768), bf16)] * 2
        + [sem((16,))] * 6
        + [sem((12,)), sem((12,)), sem, sem],
        compiler_params=params(collective_id=1, has_side_effects=True),
        cost_estimate=cost(100),
        name="conv_sync",
    )(*parts, pre, xp, sums, wd, *ffn_halves, *qkv_halves)


def unpack_frames_kernel(s_ref, c0, c1, c2, c3, o_ref):
    me, li = s_ref[0], s_ref[1]
    r_i, c_i = iota2((256, 768))
    top = jnp.zeros((256, 768), f32)
    low = jnp.zeros((256, 768), f32)
    for r, chunk in enumerate((c0, c1, c2, c3)):
        base = 192 * (me ^ r)
        inside = (c_i >= base) & (c_i < base + 192)
        top += mm(chunk[:, 0:256], ((c_i - base == r_i) & inside).astype(f32).astype(bf16))
        low += mm(chunk[:, 128:384], ((c_i - base == r_i - 64) & inside).astype(f32).astype(bf16))
    o_ref[li, 0:256, :] = top.astype(bf16)
    o_ref[li, 256:384, :] = low[0:128].astype(bf16)
    slot = me * FR + lax.broadcasted_iota(jnp.int32, (128, 768), 0)
    o_ref[1 - li, 0:128, :] = jnp.where(slot < SHORT, low[128:], 0.0).astype(bf16)
    o_ref[1 - li, 128:384, :] = jnp.zeros((256, 768), bf16)


def unpack_frames(scal, chunks):
    return pl.pallas_call(
        unpack_frames_kernel,
        in_specs=[smem()] + [vmem()] * 4,
        out_specs=vmem(),
        out_shape=jax.ShapeDtypeStruct((2, FR, 768), bf16),
        compiler_params=params(),
        cost_estimate=cost(3),
        name="unpack_frames",
    )(scal, *chunks)


def kernel_out_kernel(s_ref, own_ref, other_ref, o_ref, small_ref):
    core = s_ref[2]
    for g in range(4):
        half, row = g >> 1, 96 * (g & 1)
        x = jnp.where(half == core, own_ref[0, row : row + 96], other_ref[0, row : row + 96]).astype(f32)
        for k2 in range(2):
            for b in range(16):
                o_ref[16 * k2 + b, g] = x[48 * k2 : 48 * k2 + 48, 48 * b : 48 * b + 48]

    @pl.when(pl.program_id(0) == s_ref[0])
    def _():
        for half in range(2):
            small_ref[half] = jnp.where(half == core, own_ref[0, 192:208], other_ref[0, 192:208])


def kernel_out(scal, own, other):
    return pl.pallas_call(
        kernel_out_kernel,
        grid_spec=pltpu.PrefetchScalarGridSpec(
            num_scalar_prefetch=1,
            grid=(4,),
            in_specs=[pl.BlockSpec((1, 208, 768), lambda i, s: (i ^ s[0], 0, 0))] * 2,
            out_specs=[
                pl.BlockSpec((32, 4, 48, 48), lambda i, s: (0, i, 0, 0)),
                pl.BlockSpec((2, 16, 768), lambda i, s: (0, 0, 0)),
            ],
        ),
        out_shape=[jax.ShapeDtypeStruct((32, 16, 48, 48), f32), jax.ShapeDtypeStruct((2, 16, 768), bf16)],
        compiler_params=params(),
        cost_estimate=cost(9),
        name="kernel_grad_out",
    )(scal, own, other)


def norm(v):
    center = v - jnp.mean(v, axis=-1, keepdims=True)
    scale = lax.rsqrt(jnp.mean(center * center, axis=-1, keepdims=True) + eps_norm)
    return center * scale, scale


def norm_back(e, n, scale):
    return (e - jnp.mean(e, axis=-1, keepdims=True) - n * jnp.mean(e * n, axis=-1, keepdims=True)) * scale


def ffn_kernel(
    s_ref, rows_ref, m0, m1, m2, m3, wo, wu_hbm, bu, wd_hbm, vecs, og,
    lo, ul_hbm, gu_hbm, nl, gd, gac, x0, x1, x2, x3, gst, sums,
    wu, wd, ul, gu, slope, v, gsc, sems,
):
    me, li = s_ref[0], s_ref[1]
    const = FR + UNIQUE
    bo, g1, s1, bd, g2, s2 = (vecs[k : k + 1, :] for k in range(6))
    loads = [
        pltpu.make_async_copy(wu_hbm, wu, sems.at[0]),
        pltpu.make_async_copy(wd_hbm, wd, sems.at[1]),
    ]
    for load in loads:
        load.start()

    def total(x):
        return jnp.sum(x, axis=0, keepdims=True)

    mix = jnp.concatenate([m0[...], m1[...], m2[...], m3[...]], axis=0)
    out = lax.dot_general(mix, wo[...], (((0,), (0,)), ((), ())), preferred_element_type=f32)
    gsc[0:576, :] = rows_ref[...].astype(f32) + out[0:576] + bo
    last = gsc[const : const + 1, :]
    v[0:FR, :] = gsc[0:FR, :]
    v[FR : FR + 128, :] = jnp.where(me == 0, gsc[FR : FR + 128, :], last)
    mine = jnp.where(me == 0, 1.0, 0.0)
    keep_low = (lax.broadcasted_iota(jnp.int32, (64, 768), 0) < UNIQUE - 128).astype(f32) * mine
    v[FR + 128 : FR + 192, :] = jnp.where(keep_low > 0.5, gsc[FR + 128 : FR + 192, :], last)
    v[FR + 192 :, :] = jnp.broadcast_to(last, (192, 768))

    n1, scale1 = norm(v[...])
    v[...] = n1
    norm_one = n1 * g1 + s1
    low = norm_one.astype(bf16)
    nl[...] = low
    down = norm_one + bd
    stores = []
    loads[0].wait()
    for j in range(4):
        cols = slice(768 * j, 768 * j + 768)
        up = mm(low, wu[:, cols]) + bu[:, cols]
        cdf = gelu_parts(up)
        slope[:, cols] = cdf + up * density(up)
        act = (up * cdf).astype(bf16)
        ul[:, cols] = act
        stores.append(pltpu.make_async_copy(ul.at[:, cols], ul_hbm.at[:, cols], sems.at[2 + j]))
        stores[-1].start()
        if j == 0:
            loads[1].wait()
        down += mm(act, wd[cols, :])
    n2, scale2 = norm(down)
    result = (n2 * g2 + s2).astype(bf16)
    lo[li] = result[0:FR]
    lo[1 - li] = result[FR:]
    given = jnp.concatenate([og[li], og[1 - li]], axis=0).astype(f32)
    sums[8:9, :] = total(given * n2)
    sums[9:10, :] = total(given)
    sums[10:16, :] = jnp.zeros((6, 768), f32)
    grad_two = norm_back(given * g2, n2, scale2)
    grad_down = grad_two.astype(bf16)
    gd[...] = grad_down
    sums[7:8, :] = total(grad_down.astype(f32))
    grad_n = grad_two
    for j in range(4):
        cols = slice(768 * j, 768 * j + 768)
        grad_up = (mm_nt(grad_down, wd[cols, :]) * slope[:, cols]).astype(bf16)
        gu[:, cols] = grad_up
        stores.append(pltpu.make_async_copy(gu.at[:, cols], gu_hbm.at[:, cols], sems.at[6 + j]))
        stores[-1].start()
        sums[j : j + 1, :] = total(grad_up.astype(f32))
        grad_n += mm_nt(grad_up, wu[:, cols])
    n1 = v[...]
    sums[5:6, :] = total(grad_n * n1)
    sums[6:7, :] = total(grad_n)
    grad_one = norm_back(grad_n * g1, n1, scale1)
    grad_attn = grad_one.astype(bf16).astype(f32)
    sums[4:5, :] = total(grad_attn)

    at = lax.broadcasted_iota(jnp.int32, (64, 768), 0) == UNIQUE - 128

    def collapsed(g):
        upper = g[FR : FR + 128] * mine
        lower = g[FR + 128 : FR + 192] * keep_low
        rest = total(g[FR:]) - total(upper) - total(lower)
        return jnp.concatenate(
            [g[0:FR], upper, jnp.where(at, rest, lower), jnp.zeros((64, 768), f32)], axis=0
        )

    gac[...] = collapsed(grad_attn).astype(bf16)
    for r, out in enumerate((x0, x1, x2, x3)):
        out[...] = mm_nt(wo[192 * r : 192 * r + 192, :], gac[...]).astype(bf16)
    gsc[...] = collapsed(grad_one)
    gst[...] = gsc[...].T.astype(bf16)
    for store in stores:
        store.wait()


def ffn(scal, rows, mix, wo, wu, bu, wd, vecs, og):
    sds = jax.ShapeDtypeStruct
    hbm = pl.BlockSpec(memory_space=pl.ANY)
    return pl.pallas_call(
        ffn_kernel,
        in_specs=[smem()] + [vmem()] * 6 + [hbm, vmem(), hbm, vmem(), vmem()],
        out_specs=[vmem(), hbm, hbm] + [vmem()] * 9,
        out_shape=[
            sds((2, FR, 768), bf16), sds((768, 3072), bf16), sds((768, 3072), bf16), sds((768, 768), bf16),
            sds((768, 768), bf16), sds((640, 768), bf16),
        ]
        + [sds((CH, 640), bf16)] * 4
        + [sds((768, 640), bf16), sds((16, 768), f32)],
        scratch_shapes=[
            pltpu.VMEM((768, 3072), bf16),
            pltpu.VMEM((3072, 768), bf16),
            pltpu.VMEM((768, 3072), bf16),
            pltpu.VMEM((768, 3072), bf16),
            pltpu.VMEM((768, 3072), f32),
            pltpu.VMEM((768, 768), f32),
            pltpu.VMEM((640, 768), f32),
            pltpu.SemaphoreType.DMA((10,)),
        ],
        compiler_params=params(),
        cost_estimate=cost(28),
        name="ffn",
    )(scal, rows, *mix, wo, wu, bu, wd, vecs, og)


def tn(a, b):
    return lax.dot_general(a, b, (((0,), (0,)), ((), ())), preferred_element_type=f32)


def up_wgrad_kernel(s_ref, nl, gu, keep, send):
    j = pl.program_id(0)
    me, core = s_ref[0], s_ref[2]
    up = tn(nl[...], gu[...]).astype(bf16)
    row0 = pl.multiple_of(192 * (j & 1), 64)
    stays = core == (j >> 1)

    @pl.when(stays)
    def _():
        for e in range(4):
            keep[me ^ e, pl.ds(row0, 192), :] = up[192 * e : 192 * e + 192]

    @pl.when(jnp.logical_not(stays))
    def _():
        for e in range(4):
            send[me ^ e, pl.ds(row0, 192), :] = up[192 * e : 192 * e + 192]


def up_wgrad(scal, nl, gu):
    return pl.pallas_call(
        up_wgrad_kernel,
        grid=(4,),
        in_specs=[smem(), full((768, 768)), pl.BlockSpec((768, 768), lambda j: (0, j))],
        out_specs=[full((4, 384, 768))] * 2,
        out_shape=[jax.ShapeDtypeStruct((4, 384, 768), bf16)] * 2,
        compiler_params=params(),
        cost_estimate=cost(9),
        name="up_wgrad",
    )(scal, nl, gu)


def down_wgrad_kernel(s_ref, ul, gd, m0, m1, m2, m3, gac, sums, keep, send):
    j = pl.program_id(0)
    core = s_ref[2]
    rel = j ^ s_ref[0]
    down = tn(ul[...], gd[...]).astype(bf16)
    put(core == 0, keep, send, 0, 0, down[0:512])
    put(core == 1, keep, send, 0, 0, down[512:768])
    extra = jnp.concatenate([sums[...], jnp.zeros((48, 768), f32)], axis=0).astype(bf16)
    put(core == 1, keep, send, 0, 448, extra)
    for r, m in enumerate((m0, m1, m2, m3)):

        @pl.when(rel == r)
        def _():
            put(core == 1, keep, send, 0, 256, mm(m[...], gac[...]).astype(bf16))


def down_wgrad(scal, ul, gd, mix, gac, sums):
    return pl.pallas_call(
        down_wgrad_kernel,
        grid_spec=pltpu.PrefetchScalarGridSpec(
            num_scalar_prefetch=1,
            grid=(4,),
            in_specs=[pl.BlockSpec((768, 768), lambda j, s: (0, j)), full((768, 768))]
            + [full((CH, 640))] * 4
            + [full((640, 768)), full((16, 768))],
            out_specs=[pl.BlockSpec((1, 512, 768), lambda j, s: (j ^ s[0], 0, 0))] * 2,
        ),
        out_shape=[jax.ShapeDtypeStruct((4, 512, 768), bf16)] * 2,
        compiler_params=params(),
        cost_estimate=cost(10),
        name="down_wgrad",
    )(scal, ul, gd, *mix, gac, sums)


def finish_kernel(s_ref, own1, other1, own2, other2, ownb, otherb, up, down, out, wq, wk, wv, small, a1, a2, b_ref):
    me, core = s_ref[0], s_ref[2]
    for buf, own, other in ((a1, own1, other1), (a2, own2, other2)):
        buf[core] = own[...]
        buf[1 - core] = other[...]
    b_ref[:, pl.ds(pl.multiple_of(96 * core, 32), 96), :] = ownb[...]
    b_ref[:, pl.ds(pl.multiple_of(96 - 96 * core, 32), 96), :] = otherb[...]
    for j in range(4):
        row = 192 * (j & 1)
        up[:, 768 * j : 768 * j + 768] = a1[j >> 1, row : row + 192, :].astype(f32)
    down[0:512, :] = a2[0].astype(f32)
    down[512:768, :] = a2[1, 0:256, :].astype(f32)
    out[...] = a2[1, 256:448, :].astype(f32)
    small[...] = a2[1, 448:464, :].astype(f32)
    r_i, c_i = iota2((256, 768))
    totals = [jnp.zeros((CH, 768), f32)] * 3
    for r in range(4):
        base = 192 * (me ^ r)
        hit = (c_i - base == r_i) & (r_i < 192)
        move = hit.astype(f32).astype(bf16)
        for k in range(3):
            totals[k] = totals[k] + mm(b_ref[r, :, 256 * k : 256 * k + 256], move)
    wq[...], wk[...], wv[...] = totals


def finish(scal, *parts):
    sds = jax.ShapeDtypeStruct
    return pl.pallas_call(
        finish_kernel,
        in_specs=[smem()] + [vmem()] * 6,
        out_specs=[vmem()] * 7,
        out_shape=[sds((CH, 3072), f32), sds((768, 768), f32)] + [sds((CH, 768), f32)] * 4 + [sds((16, 768), f32)],
        scratch_shapes=[
            pltpu.VMEM((2, 384, 768), bf16),
            pltpu.VMEM((2, 512, 768), bf16),
            pltpu.VMEM((4, CH, 768), bf16),
        ],
        compiler_params=params(),
        cost_estimate=cost(6),
        name="weight_grads_out",
    )(scal, *parts)


def from_others(chunks):
    moved = [lax.ppermute(chunks[r], "wide", [(i, i ^ r) for i in range(4)]) for r in (3, 1, 2)]
    return [chunks[0], moved[1], moved[2], moved[0]]


def gathered(chunk):
    return from_others([chunk] * 4)


def narrow_move(v, d):
    return lax.ppermute(v, "narrow", [(i, i ^ d) for i in range(8)])


def core_move(v):
    return narrow_move(v, 1)


def added(parts):
    total = parts[0].astype(f32)
    for part in parts[1:]:
        total = total + part.astype(f32)
    return total.astype(bf16)


def along_z(v):
    return lax.psum(v, "narrow", axis_index_groups=[[2 * k + c for k in range(4)] for c in range(2)])


def after(v, *others):
    return lax.optimization_barrier((v, *others))[0]


def on_device(
    frames_in, lengths, kernel, conv_bias, w_query, b_query, w_key, w_value, b_value, w_out, b_out,
    gain_one, shift_one, w_up, b_up, w_down, b_down, gain_two, shift_two, out_grad,
):
    me = lax.axis_index("wide").astype(jnp.int32)
    place_n = lax.axis_index("narrow").astype(jnp.int32)
    core, z = place_n & 1, place_n >> 1
    li = jnp.where(lengths[0] >= lengths[1], 0, 1).astype(jnp.int32)
    scal = jnp.stack([me, li, core, z])
    frames = from_others(pack_frames(scal, frames_in))
    wt, wd = prep_weights(scal, kernel)

    def own(v):
        return lax.dynamic_slice_in_dim(v, me * CH, CH, axis=v.ndim - 1)

    def three(a, b, c):
        gap = [(0, 0)] * (a.ndim - 1) + [(0, 64)]
        return jnp.concatenate([jnp.pad(a, gap), jnp.pad(b, gap), jnp.pad(c, gap)], axis=-1)

    wqkv = three(own(w_query), own(w_key), own(w_value))
    bqkv = three(own(b_query), jnp.zeros((CH,), bf16), own(b_value)).astype(f32)[None]
    bias = jnp.pad(own(conv_bias).astype(f32).reshape(2, 2, 48), ((0, 0), (0, 0), (0, 16))).reshape(2, 1, 128)
    w_out_rel = jnp.concatenate(
        [lax.dynamic_slice_in_dim(w_out, (me ^ r) * CH, CH, axis=0) for r in range(4)], axis=0
    )
    vecs = jnp.stack([b_out, gain_one, shift_one, b_down, gain_two, shift_two]).astype(f32)
    bu = b_up.astype(f32)[None]

    pre, xp, packed = conv_fwd(scal, frames, wt, bias)
    first = gathered(packed)
    qkv, mixed_t, lse, rows, *mixed = attn_fwd(scal, first, wqkv, bqkv)
    mix = from_others(mixed)
    layer_out, ul, gu, nl, gd, gac, x0, x1, x2, x3, gst, sums = ffn(
        scal, rows, mix, w_out_rel, w_up, bu, w_down, vecs, out_grad
    )
    dparts = from_others([x0, x1, x2, x3])
    keep1, send1 = up_wgrad(scal, nl, gu)
    got1 = core_move(send1)
    keep2, send2 = down_wgrad(scal, after(ul, send1), gd, mix, gac, sums)
    halves1 = [added([keep1[r], got1[r]]) for r in range(4)]
    got2 = core_move(send2)
    d0 = after(dparts[0], *halves1)

    dqkv, g0, g1, g2, g3, qkv_sums = attn_bwd(scal, qkv, mixed_t, lse, [d0] + dparts[1:], gst, wqkv)
    moved1 = from_others(halves1)
    gs = lax.optimization_barrier((g0, g1, g2, g3, got2, *moved1[1:]))
    got2, moved1 = gs[4], moved1[:1] + list(gs[5:])
    gparts = from_others(gs[:4])
    sum1 = added(moved1)
    total1 = along_z(sum1)
    halves2 = [added([keep2[r], got2[r]]) for r in range(4)]
    qkeep, qsend = qkv_wgrad(scal, first, after(dqkv, gparts[3], sum1, *halves2))
    p0 = after(gparts[0], qsend)

    qgot = core_move(qsend)
    qhalves = [added([qkeep[r], qgot[r]]) for r in range(4)]
    own2, ownb, ownc, other2, otherb, otherc, *fchunks = conv_sync(
        [p0] + gparts[1:], pre, xp, qkv_sums, wd, halves2, qhalves
    )
    frames_grad = unpack_frames(scal, fchunks)
    up, down, out, wq, wk, wv, small = finish(scal, total1, core_move(total1), own2, other2, ownb, otherb)
    grad_kernel, tiny = kernel_out(scal, ownc, otherc)
    tiny = tiny.astype(f32)

    def mine(row):
        return lax.dynamic_slice_in_dim(small[row], me * CH, CH, axis=0)

    bias_grad = jnp.concatenate([tiny[0, 1, :128], tiny[1, 1, :128]]).reshape(4, 64)[:, :48].reshape(CH)
    grad_b_up = lax.dynamic_index_in_dim(small[:4], me, 0, keepdims=False)
    return (
        layer_out,
        frames_grad,
        grad_kernel,
        bias_grad,
        wq,
        tiny[0, 0, 0:192],
        wk,
        wv,
        tiny[0, 0, 512:704],
        out,
        mine(4),
        mine(5),
        mine(6),
        up,
        grad_b_up,
        down,
        mine(7),
        mine(8),
        mine(9),
    )


def with_halo(x, sides, width):
    for axis, dim in sides:
        count, length = (lax.axis_size(axis), x.shape[dim])
        up = [(i, (i + 1) % count) for i in range(count - 1)]
        down = [(j, i) for i, j in up]
        last = lax.slice_in_dim(x, length - width, length, axis=dim)
        initial = lax.slice_in_dim(x, 0, width, axis=dim)
        before = lax.ppermute(last, axis, up)
        after = lax.ppermute(initial, axis, down)
        x = jnp.concatenate([before, x, after], axis=dim)
    return x


def layer_norm(value, gain, shift):
    center = value - jnp.mean(value, axis=-1, keepdims=True)
    spread = jnp.mean(center * center, axis=-1, keepdims=True)
    return center * lax.rsqrt(spread + eps_norm) * gain + shift


def gelu_exact(value):
    return jax.nn.gelu(value, approximate=False)


def project(rows_in, weight):
    return jnp.einsum("cfd,de->cfe", rows_in, weight, preferred_element_type=jnp.float32)


def project_back(grad_in, weight):
    return jnp.einsum("cfe,de->cfd", grad_in, weight, preferred_element_type=jnp.float32)


def weight_grad(rows_in, grad_in):
    return jnp.einsum("cfd,cfe->de", rows_in, grad_in, preferred_element_type=jnp.float32)


def row_total(grad_in):
    return jnp.sum(grad_in.astype(jnp.float32), axis=(0, 1))


def head_view(rows_in):
    return rows_in.reshape(rows_in.shape[0], rows_in.shape[1], HEADS, rows_in.shape[2] // HEADS)


def conv_apply(padded, weight, frames):
    kernel_span, groups, inner_ch, outer_ch = weight.shape
    taps_weight = jnp.transpose(weight, (0, 2, 1, 3)).reshape(
        kernel_span, inner_ch, groups * outer_ch
    )
    result = lax.conv_general_dilated(
        padded,
        taps_weight,
        (1,),
        "VALID",
        dimension_numbers=("NWC", "WIO", "NWC"),
        feature_group_count=groups,
        preferred_element_type=jnp.float32,
    )
    return result[:, :frames, :]


def conv_weight_grad(padded, grad_in, kernel_shape):
    kernel_span, groups, inner_ch, outer_ch = kernel_shape
    result = lax.conv_general_dilated(
        padded,
        grad_in,
        (1,),
        "VALID",
        dimension_numbers=("CWN", "IWO", "NWC"),
        batch_group_count=groups,
        preferred_element_type=jnp.float32,
    )
    result = result[:, :kernel_span, :].reshape(inner_ch, kernel_span, groups, outer_ch)
    return jnp.transpose(result, (1, 2, 0, 3))


def key_valid_at(lengths, first_row, row_count):
    return (first_row + jnp.arange(row_count, dtype=jnp.int32))[None, :] < lengths[:, None]


def masked_scores(query_h, keys_h, valid_keys, score_scale):
    scores = (
        jnp.einsum("cqhd,ckhd->cqhk", query_h, keys_h, preferred_element_type=jnp.float32)
        * score_scale
    )
    return jnp.where(valid_keys[:, None, None, :], scores, neg_large)


def block_terms(query_h, grad_h, lse_rows, delta_rows, keys_h, values_h, valid_keys, score_scale):
    scores = masked_scores(query_h, keys_h, valid_keys, score_scale)
    probs = jnp.where(valid_keys[:, None, None, :], jnp.exp(scores - lse_rows[..., None]), 0.0)
    grad_probs = jnp.einsum("cqhd,ckhd->cqhk", grad_h, values_h, preferred_element_type=jnp.float32)
    grad_scores = (probs * (grad_probs - delta_rows[..., None])).astype(jnp.bfloat16)
    results = []
    results.append(
        jnp.einsum("cqhk,ckhd->cqhd", grad_scores, keys_h, preferred_element_type=jnp.float32)
        * score_scale
    )
    results.append(
        jnp.einsum("cqhk,cqhd->ckhd", grad_scores, query_h, preferred_element_type=jnp.float32)
        * score_scale
    )
    results.append(
        jnp.einsum(
            "cqhk,cqhd->ckhd",
            probs.astype(jnp.bfloat16),
            grad_h,
            preferred_element_type=jnp.float32,
        )
    )
    return tuple(results)


def on_device_any(
    frames_in,
    lengths,
    kernel,
    conv_bias,
    w_query,
    b_query,
    w_key,
    w_value,
    b_value,
    w_out,
    b_out,
    gain_one,
    shift_one,
    w_up,
    b_up,
    w_down,
    b_down,
    gain_two,
    shift_two,
    out_grad,
):
    clip_count, frames, width = frames_in.shape
    head_dim = width // HEADS
    score_scale = head_dim ** (-0.5)
    half_span = kernel.shape[0] // 2
    wide_size = lax.axis_size("wide")
    positions = lax.axis_index("wide") * frames + jnp.arange(frames, dtype=jnp.int32)
    frame_valid = positions[None, :] < lengths[:, None]
    masked = jnp.where(frame_valid[..., None], frames_in, jnp.zeros((), jnp.bfloat16))
    padded = with_halo(masked, (("wide", 1),), half_span)
    pre_act = conv_apply(padded, kernel, frames) + conv_bias.astype(jnp.float32)
    first_act, pull_first = jax.vjp(gelu_exact, pre_act)
    first_out = masked.astype(jnp.float32) + first_act
    first_low = first_out.astype(jnp.bfloat16)
    query_rows = (project(first_low, w_query) + b_query.astype(jnp.float32)).astype(jnp.bfloat16)
    key_rows = project(first_low, w_key).astype(jnp.bfloat16)
    value_rows = (project(first_low, w_value) + b_value.astype(jnp.float32)).astype(jnp.bfloat16)
    query_h = head_view(query_rows)
    per_step = max(1, min(wide_size, 512 // frames))
    while wide_size % per_step:
        per_step -= 1
    run_max = jnp.full((clip_count, frames, HEADS), neg_large, jnp.float32)
    run_acc = jnp.zeros((clip_count, frames, HEADS, head_dim), jnp.float32)
    keys_p = lax.all_gather(key_rows, "wide", axis=1, tiled=True)
    values_p = lax.all_gather(value_rows, "wide", axis=1, tiled=True)
    row_count = keys_p.shape[1]
    valid_keys = key_valid_at(lengths, jnp.int32(0), row_count)
    scores = masked_scores(query_h, head_view(keys_p), valid_keys, score_scale)
    new_max = jnp.maximum(run_max, jnp.max(scores, axis=-1))
    weights = jnp.where(valid_keys[:, None, None, :], jnp.exp(scores - new_max[..., None]), 0.0)
    factor = jnp.exp(run_max - new_max)
    run_sum = jnp.sum(weights, axis=-1)
    run_acc = run_acc * factor[..., None] + jnp.einsum(
        "cqhk,ckhd->cqhd",
        weights.astype(jnp.bfloat16),
        head_view(values_p),
        preferred_element_type=jnp.float32,
    )
    run_max, run_sum, run_acc = (new_max, run_sum, run_acc)
    lse_rows = run_max + jnp.log(run_sum)
    mixed_heads = run_acc / run_sum[..., None]
    mixed_low = mixed_heads.reshape(clip_count, frames, width).astype(jnp.bfloat16)
    attn_out = project(mixed_low, w_out) + b_out.astype(jnp.float32)
    sum_one = first_out + attn_out
    norm_one, pull_one = jax.vjp(
        layer_norm, sum_one, gain_one.astype(jnp.float32), shift_one.astype(jnp.float32)
    )
    norm_low = norm_one.astype(jnp.bfloat16)
    up_pre = project(norm_low, w_up) + b_up.astype(jnp.float32)
    up_act, pull_up = jax.vjp(gelu_exact, up_pre)
    up_low = up_act.astype(jnp.bfloat16)
    down_out = project(up_low, w_down) + b_down.astype(jnp.float32)
    sum_two = norm_one + down_out
    layer_out, pull_two = jax.vjp(
        layer_norm, sum_two, gain_two.astype(jnp.float32), shift_two.astype(jnp.float32)
    )
    grad_sum_two, grad_gain_two, grad_shift_two = pull_two(out_grad.astype(jnp.float32))
    grad_down = grad_sum_two.astype(jnp.bfloat16)
    grad_w_down = weight_grad(up_low, grad_down)
    grad_b_down = row_total(grad_down)
    grad_up = pull_up(project_back(grad_down, w_down))[0].astype(jnp.bfloat16)
    grad_w_up = weight_grad(norm_low, grad_up)
    grad_b_up = row_total(grad_up)
    grad_norm_one = grad_sum_two + project_back(grad_up, w_up)
    grad_sum_one, grad_gain_one, grad_shift_one = pull_one(grad_norm_one)
    grad_attn = grad_sum_one.astype(jnp.bfloat16)
    grad_w_out = weight_grad(mixed_low, grad_attn)
    grad_b_out = row_total(grad_attn)
    grad_mixed = project_back(grad_attn, w_out).astype(jnp.bfloat16)
    grad_h = head_view(grad_mixed)
    delta_rows = jnp.sum(grad_h.astype(jnp.float32) * mixed_heads, axis=-1)
    total_slots = wide_size * frames
    first_row = jnp.int32(0)
    grad_q = jnp.zeros((clip_count, frames, HEADS, head_dim), jnp.float32)
    grad_k_all = jnp.zeros((clip_count, total_slots, width), jnp.float32)
    grad_v_all = jnp.zeros((clip_count, total_slots, width), jnp.float32)
    keys_p = lax.all_gather(key_rows, "wide", axis=1, tiled=True)
    values_p = lax.all_gather(value_rows, "wide", axis=1, tiled=True)
    row_count = keys_p.shape[1]
    valid_keys = key_valid_at(lengths, first_row, row_count)
    part_q, part_k, part_v = block_terms(
        query_h,
        grad_h,
        lse_rows,
        delta_rows,
        head_view(keys_p),
        head_view(values_p),
        valid_keys,
        score_scale,
    )
    old_k = lax.dynamic_slice_in_dim(grad_k_all, first_row, row_count, 1)
    old_v = lax.dynamic_slice_in_dim(grad_v_all, first_row, row_count, 1)
    grad_k_all = lax.dynamic_update_slice_in_dim(
        grad_k_all, old_k + part_k.reshape(clip_count, row_count, width), first_row, 1
    )
    grad_v_all = lax.dynamic_update_slice_in_dim(
        grad_v_all, old_v + part_v.reshape(clip_count, row_count, width), first_row, 1
    )
    grad_k_own, grad_v_own = (
        lax.psum_scatter(
            grad_k_all.astype(jnp.bfloat16), "wide", scatter_dimension=1, tiled=True
        ).astype(jnp.float32),
        lax.psum_scatter(
            grad_v_all.astype(jnp.bfloat16), "wide", scatter_dimension=1, tiled=True
        ).astype(jnp.float32),
    )
    grad_q_low = (grad_q + part_q).reshape(clip_count, frames, width).astype(jnp.bfloat16)
    grad_k_low = grad_k_own.astype(jnp.bfloat16)
    grad_v_low = grad_v_own.astype(jnp.bfloat16)
    grad_w_query = weight_grad(first_low, grad_q_low)
    grad_b_query = row_total(grad_q_low)
    grad_w_key = weight_grad(first_low, grad_k_low)
    grad_w_value = weight_grad(first_low, grad_v_low)
    grad_b_value = row_total(grad_v_low)
    grad_first = (
        grad_sum_one
        + project_back(grad_q_low, w_query)
        + project_back(grad_k_low, w_key)
        + project_back(grad_v_low, w_value)
    )
    grad_pre = pull_first(grad_first)[0].astype(jnp.bfloat16)
    grad_conv_bias = row_total(grad_pre)
    grad_kernel = conv_weight_grad(padded, grad_pre, kernel.shape)
    grad_padded = with_halo(grad_pre, (("wide", 1),), half_span)
    flipped = jnp.transpose(kernel[::-1], (0, 1, 3, 2))
    grad_masked = grad_first + conv_apply(grad_padded[:, 1:], flipped, frames)
    frames_grad = jnp.where(frame_valid[..., None], grad_masked, 0.0).astype(jnp.bfloat16)
    shards = (
        lax.psum_scatter(
            grad_kernel.astype(jnp.bfloat16), "wide", scatter_dimension=0, tiled=True
        ).astype(jnp.float32),
        lax.psum_scatter(
            grad_conv_bias.astype(jnp.bfloat16), "wide", scatter_dimension=0, tiled=True
        ).astype(jnp.float32),
        lax.psum_scatter(
            grad_w_query.astype(jnp.bfloat16), "wide", scatter_dimension=0, tiled=True
        ).astype(jnp.float32),
        lax.psum_scatter(
            grad_b_query.astype(jnp.bfloat16), "wide", scatter_dimension=0, tiled=True
        ).astype(jnp.float32),
        lax.psum_scatter(
            grad_w_key.astype(jnp.bfloat16), "wide", scatter_dimension=0, tiled=True
        ).astype(jnp.float32),
        lax.psum_scatter(
            grad_w_value.astype(jnp.bfloat16), "wide", scatter_dimension=0, tiled=True
        ).astype(jnp.float32),
        lax.psum_scatter(
            grad_b_value.astype(jnp.bfloat16), "wide", scatter_dimension=0, tiled=True
        ).astype(jnp.float32),
        lax.psum_scatter(
            grad_w_out.astype(jnp.bfloat16), "wide", scatter_dimension=0, tiled=True
        ).astype(jnp.float32),
        lax.psum_scatter(
            grad_b_out.astype(jnp.bfloat16), "wide", scatter_dimension=0, tiled=True
        ).astype(jnp.float32),
        lax.psum_scatter(
            grad_gain_one.astype(jnp.bfloat16), "wide", scatter_dimension=0, tiled=True
        ).astype(jnp.float32),
        lax.psum_scatter(
            grad_shift_one.astype(jnp.bfloat16), "wide", scatter_dimension=0, tiled=True
        ).astype(jnp.float32),
        lax.psum_scatter(
            grad_w_up.astype(jnp.bfloat16), "wide", scatter_dimension=0, tiled=True
        ).astype(jnp.float32),
        lax.psum_scatter(
            grad_b_up.astype(jnp.bfloat16), "wide", scatter_dimension=0, tiled=True
        ).astype(jnp.float32),
        lax.psum_scatter(
            grad_w_down.astype(jnp.bfloat16), "wide", scatter_dimension=0, tiled=True
        ).astype(jnp.float32),
        lax.psum_scatter(
            grad_b_down.astype(jnp.bfloat16), "wide", scatter_dimension=0, tiled=True
        ).astype(jnp.float32),
        lax.psum_scatter(
            grad_gain_two.astype(jnp.bfloat16), "wide", scatter_dimension=0, tiled=True
        ).astype(jnp.float32),
        lax.psum_scatter(
            grad_shift_two.astype(jnp.bfloat16), "wide", scatter_dimension=0, tiled=True
        ).astype(jnp.float32),
    )
    totals = (
        lax.psum(shards[0].astype(jnp.bfloat16), "narrow").astype(jnp.float32),
        lax.psum(shards[1].astype(jnp.bfloat16), "narrow").astype(jnp.float32),
        lax.psum(shards[2].astype(jnp.bfloat16), "narrow").astype(jnp.float32),
        lax.psum(shards[3].astype(jnp.bfloat16), "narrow").astype(jnp.float32),
        lax.psum(shards[4].astype(jnp.bfloat16), "narrow").astype(jnp.float32),
        lax.psum(shards[5].astype(jnp.bfloat16), "narrow").astype(jnp.float32),
        lax.psum(shards[6].astype(jnp.bfloat16), "narrow").astype(jnp.float32),
        lax.psum(shards[7].astype(jnp.bfloat16), "narrow").astype(jnp.float32),
        lax.psum(shards[8].astype(jnp.bfloat16), "narrow").astype(jnp.float32),
        lax.psum(shards[9].astype(jnp.bfloat16), "narrow").astype(jnp.float32),
        lax.psum(shards[10].astype(jnp.bfloat16), "narrow").astype(jnp.float32),
        lax.psum(shards[11].astype(jnp.bfloat16), "narrow").astype(jnp.float32),
        lax.psum(shards[12].astype(jnp.bfloat16), "narrow").astype(jnp.float32),
        lax.psum(shards[13].astype(jnp.bfloat16), "narrow").astype(jnp.float32),
        lax.psum(shards[14].astype(jnp.bfloat16), "narrow").astype(jnp.float32),
        lax.psum(shards[15].astype(jnp.bfloat16), "narrow").astype(jnp.float32),
        lax.psum(shards[16].astype(jnp.bfloat16), "narrow").astype(jnp.float32),
    )
    return (
        layer_out.astype(jnp.bfloat16),
        frames_grad,
        totals[0],
        totals[1],
        totals[2],
        totals[3],
        totals[4],
        totals[5],
        totals[6],
        totals[7],
        totals[8],
        totals[9],
        totals[10],
        totals[11],
        totals[12],
        totals[13],
        totals[14],
        totals[15],
        totals[16],
    )


def solution(mesh):
    rows = P("narrow", "wide", None)
    placed = (rows, P("narrow")) + (P(),) * 17 + (rows,)
    wide = mesh.shape["wide"]
    fast = wide == 4 and mesh.shape["narrow"] == 8
    return jax.shard_map(
        on_device if fast else on_device_any,
        mesh=mesh,
        in_specs=placed,
        out_specs=(rows, rows)
        + (P("wide", None, None, None), P("wide"), P("wide", None), P("wide"), P("wide", None), P("wide", None))
        + (P("wide"), P("wide", None), P("wide"), P("wide"), P("wide"), P("wide", None), P("wide"))
        + (P("wide", None), P("wide"), P("wide"), P("wide")),
        check_vma=False,
    )
```

```python
import functools

import jax
import jax.numpy as jnp
from jax import lax
from jax.experimental import pallas as pl
from jax.experimental.pallas import tpu as pltpu
from jax.sharding import PartitionSpec as P

HEADS = 12
GROUP_CH = 48
SHORT = 102
HALF = 64
UNIQUE = SHORT + HALF
FR = 384
SLOTS = 1536
SROWS = 192
TROWS = 1792
SBASE = 1600
CH = 192
eps_norm = 1e-05
neg_large = -1e30
bf16 = jnp.bfloat16
f32 = jnp.float32
QF = 1536
QB = 768
KB = 512
CB = 1792
VLIM = 60 * 1024 * 1024


def mm(a, b):
    return jnp.dot(a, b, preferred_element_type=f32)


def mm_nt(a, b):
    return lax.dot_general(a, b, (((1,), (1,)), ((), ())), preferred_element_type=f32)


def iota2(shape):
    return lax.broadcasted_iota(jnp.int32, shape, 0), lax.broadcasted_iota(jnp.int32, shape, 1)


def place(shape, rows_from, rows_to, cols_from):
    r, c = iota2(shape)
    hit = (c - cols_from == r - rows_from) & (r >= rows_from) & (r < rows_to)
    return hit.astype(f32).astype(bf16)


def spread(shape, lane0, start):
    r, c = iota2(shape)
    slot, inner = c >> 6, c & 63
    hit = (r == lane0 + start + slot * GROUP_CH + inner) & (inner < GROUP_CH)
    return hit.astype(f32).astype(bf16)


def gather_slots(shape, col0):
    r, c = iota2(shape)
    slot, inner = r >> 6, r & 63
    hit = (c == col0 + slot * GROUP_CH + inner) & (inner < GROUP_CH)
    return hit.astype(f32).astype(bf16)


def full(shape):
    return pl.BlockSpec(shape, lambda *_: (0,) * len(shape))


def smem():
    return pl.BlockSpec(memory_space=pltpu.SMEM)


def vmem():
    return pl.BlockSpec(memory_space=pltpu.VMEM)


def params(**kw):
    return pltpu.CompilerParams(vmem_limit_bytes=VLIM, **kw)


def cost(us):
    return pl.CostEstimate(flops=int(us * 1e9), bytes_accessed=int(us * 3.4e6), transcendentals=0)


def put(keeping, keep, send, rel, row0, data, lane0=0):
    rows, lanes = data.shape

    @pl.when(keeping)
    def _():
        keep[rel, row0 : row0 + rows, lane0 : lane0 + lanes] = data

    @pl.when(jnp.logical_not(keeping))
    def _():
        send[rel, row0 : row0 + rows, lane0 : lane0 + lanes] = data


def xor2(a, b):
    return (a + b) % 2 + 2 * ((a // 2 + b // 2) % 2)


def gelu_parts(v):
    cdf = 0.5 * (1.0 + lax.erf(v * (2.0 ** -0.5)))
    return cdf


def density(v):
    return jnp.exp(-0.5 * v * v) * 0.3989422804014327


def pack_frames_kernel(s_ref, x_ref, *outs):
    me, li = s_ref[0], s_ref[1]
    long, short = x_ref[li], x_ref[1 - li]
    slot = me * FR + lax.broadcasted_iota(jnp.int32, (128, 768), 0)
    short = jnp.where(slot < SHORT, short[:128].astype(f32), 0.0).astype(bf16)
    top = long[:256]
    low = jnp.concatenate([long[256:], short], axis=0)
    for d in range(4):
        first = 192 * d - (64 if d % 2 else 0)
        skip = 64 if d % 2 else 0
        chunk = mm(top[:, first : first + 256], place((256, 384), skip, skip + 192, 0)) + mm(
            low[:, first : first + 256], place((256, 384), skip, skip + 192, 192)
        )
        chunk = chunk.astype(bf16)
        for r in range(4):

            @pl.when((me ^ d) == r)
            def _():
                outs[r][...] = chunk


def pack_frames(scal, frames_in):
    return pl.pallas_call(
        pack_frames_kernel,
        out_shape=[jax.ShapeDtypeStruct((256, 384), bf16)] * 4,
        in_specs=[smem(), vmem()],
        out_specs=[vmem()] * 4,
        compiler_params=params(),
        cost_estimate=cost(3),
        name="pack_frames",
    )(scal, frames_in)


def prep_kernel(s_ref, w_ref, wt_ref, wd_ref, z_ref, taps):
    left, right = place((48, 128), 0, 48, 0), place((48, 128), 0, 48, 64)
    wt_ref[...] = jnp.zeros_like(wt_ref)
    z_ref[...] = jnp.zeros_like(z_ref)
    for i in range(48):
        taps[pl.ds(i, 128, stride=48), 0:48] = w_ref[0, i].astype(f32).T

    def rows(k, n):
        return taps[48 * k : 48 * (k + n), 0:48].astype(bf16)

    for k2 in range(8):
        pairs = rows(16 * k2, 16).reshape(8, 2, 48, 48)
        tile = mm(pairs[:, 0].reshape(384, 48), left) + mm(pairs[:, 1].reshape(384, 48), right)
        tile = tile.astype(bf16)
        for p in range(8):
            wt_ref[0, 64 * k2 : 64 * k2 + 48, 128 * p : 128 * p + 128] = tile[48 * p : 48 * p + 48]
    for q in range(4):
        tile = mm(rows(112 - 32 * q, 16), left) + mm(rows(96 - 32 * q, 16), right)
        for b in range(16):
            z_ref[64 * b : 64 * b + 48, :] = tile[48 * (15 - b) : 48 * (15 - b) + 48]
        wd_ref[0, 128 * q : 128 * q + 128, :] = z_ref[...].T.astype(bf16)


def prep_weights(scal, kernel):
    return pl.pallas_call(
        prep_kernel,
        grid_spec=pltpu.PrefetchScalarGridSpec(
            num_scalar_prefetch=1,
            grid=(4,),
            in_specs=[pl.BlockSpec((1, 48, 48, 128), lambda g, s: (4 * s[0] + g, 0, 0, 0))],
            out_specs=[pl.BlockSpec((1, 512, 1024), lambda g, s: (g, 0, 0))] * 2,
            scratch_shapes=[pltpu.VMEM((1024, 128), f32), pltpu.VMEM((48 * 128, 128), f32)],
        ),
        out_shape=[jax.ShapeDtypeStruct((4, 512, 1024), bf16)] * 2,
        compiler_params=params(),
        cost_estimate=cost(11),
        name="conv_weights",
    )(scal, jnp.transpose(kernel, (1, 2, 3, 0)))


def pair_slots(t_ref, rows):
    wide = jnp.concatenate([t_ref[0:rows, :], t_ref[16 : rows + 16, :]], axis=1)
    r, c = iota2((256, 128))
    out = []
    for j in range(2):
        hit = ((r < 128) & (c == r - 64 * j) & (c < 64)) | ((r >= 128) & (c - 64 == r - 128 - 64 * j) & (c >= 64))
        out.append(mm(wide, hit.astype(f32).astype(bf16)).astype(bf16))
    return out


def conv_block(p_refs, w_ref, y_ref, s_ref, shift):
    lane = lax.broadcasted_iota(jnp.int32, (CB, 128), 1)
    parts = []
    for j in range(2):
        lhs = jnp.concatenate([p_refs[j][32 * q : 32 * q + CB + 16, :] for q in range(4)], axis=1)
        y_ref[...] = mm(lhs, w_ref[j])
        total = y_ref[shift : shift + CB + 1, 0:128]
        for p in range(1, 8):
            total += y_ref[shift + 2 * p : shift + 2 * p + CB + 1, 128 * p : 128 * p + 128]
        s_ref[0 : CB + 1, :] = total
        here, after = s_ref[0:CB, :], s_ref[1 : CB + 1, :]
        if j == 0:
            parts.append(here + pltpu.roll(after, 64, 1))
        else:
            parts.append(pltpu.roll(here, 64, 1) + after)
    return jnp.where(lane < 64, parts[0], parts[1])


def conv_fwd_kernel(s_ref, c0, c1, c2, c3, w_ref, b_ref, pre_ref, x_ref, packed_ref, p0, p1, y_ref, t_ref, first):
    c = pl.program_id(0)
    me = s_ref[0]
    chunks = (c0, c1, c2, c3)
    x_ref[0, 0:64, :] = jnp.zeros((64, 128), bf16)
    x_ref[0, 1600:1664, :] = jnp.zeros((64, 128), bf16)
    x_ref[0, 1792:1936, :] = jnp.zeros((144, 128), bf16)
    top_map = spread((256, 128), 0, 96 * c)
    low_map = spread((256, 128), 64, 96 * c)
    for r in range(4):
        src = me ^ r
        top = mm(chunks[r][:, 0:256], top_map).astype(bf16)
        low = mm(chunks[r][:, 128:384], low_map).astype(bf16)
        base = pl.multiple_of(64 + FR * src, 64)
        x_ref[0, pl.ds(base, 256), :] = top
        x_ref[0, pl.ds(pl.multiple_of(base + 256, 64), 128), :] = low[:128]

        @pl.when(src == 0)
        def _():
            x_ref[0, 1664:1792, :] = low[128:]

    a, b = pair_slots(x_ref.at[0], 1920)
    p0[...] = a
    p1[...] = b
    bias = b_ref[0]

    pre = conv_block((p0, p1), w_ref, y_ref, t_ref, 0) + bias
    pre_ref[0] = pre
    center = x_ref[0, 64 : 64 + CB, :].astype(f32)
    first[c] = (center + pre * gelu_parts(pre)).astype(bf16)

    @pl.when(c == 1)
    def _():
        h0, h1 = gather_slots((256, 384), 0), gather_slots((256, 384), 192)

        def rows(lo, n):
            return jnp.concatenate([first[0, lo : lo + n, :], first[1, lo : lo + n, :]], axis=1)

        packed_ref[0:768, :] = (mm(rows(0, 768), h0) + mm(rows(768, 768), h1)).astype(bf16)
        packed_ref[768:864, :] = (mm(rows(SBASE, 96), h0) + mm(rows(SBASE + 96, 96), h1)).astype(bf16)


def conv_fwd(scal, chunks, wt, bias):
    return pl.pallas_call(
        conv_fwd_kernel,
        grid=(2,),
        in_specs=[smem()]
        + [full((256, 384))] * 4
        + [pl.BlockSpec((2, 512, 1024), lambda c: (c, 0, 0)), pl.BlockSpec((1, 1, 128), lambda c: (c, 0, 0))],
        out_specs=[
            pl.BlockSpec((1, TROWS, 128), lambda c: (c, 0, 0)),
            pl.BlockSpec((1, 1936, 128), lambda c: (c, 0, 0)),
            full((864, 384)),
        ],
        out_shape=[
            jax.ShapeDtypeStruct((2, TROWS, 128), f32),
            jax.ShapeDtypeStruct((2, 1936, 128), bf16),
            jax.ShapeDtypeStruct((864, 384), bf16),
        ],
        scratch_shapes=[
            pltpu.VMEM((1920, 128), bf16),
            pltpu.VMEM((1920, 128), bf16),
            pltpu.VMEM((CB + 16, 1024), f32),
            pltpu.VMEM((CB + 8, 128), f32),
            pltpu.VMEM((2, TROWS, 128), bf16),
        ],
        compiler_params=params(),
        cost_estimate=cost(19),
        name="conv_fwd",
    )(scal, *chunks, wt, bias)


def attn_fwd_kernel(
    s_ref, c0, c1, c2, c3, w_ref, b_ref, qkv_ref, ot_ref, lse_ref, rows_ref, x0, x1, x2, x3, wz, vt
):
    me = s_ref[0]
    chunks = (c0, c1, c2, c3)
    wz[:, 0:64, :] = jnp.zeros((4, 64, 768), bf16)
    wz[:, 256:320, :] = jnp.zeros((4, 64, 768), bf16)
    for r in range(4):
        wz[r, 64:256, :] = w_ref[pl.ds(pl.multiple_of(192 * (me ^ r), 64), 192), :]
    bias = b_ref[...]
    for half in range(2):
        row0 = 64 * (1 - half)

        def project(start, n):
            total = bias + jnp.zeros((n, 768), f32)
            for r in range(4):
                total += mm(
                    chunks[r][pl.ds(start, n), 128 * half : 128 * half + 256], wz[r, row0 : row0 + 256, :]
                )
            return total.astype(bf16)

        def body(j, carry):
            start = pl.multiple_of(256 * j, 256)
            qkv_ref[pl.ds(pl.multiple_of(768 * half + start, 256), 256), :] = project(start, 256)
            return carry

        lax.fori_loop(0, 3, body, 0)
        qkv_ref[SLOTS + 96 * half : SLOTS + 96 * half + 96, :] = project(768, 96)
    qkv_ref[SLOTS + SROWS : TROWS, :] = jnp.zeros((TROWS - SLOTS - SROWS, 768), bf16)

    half = me >> 1
    start = pl.multiple_of(FR * (me & 1), 128)
    lane0 = pl.multiple_of(128 * half, 128)
    r_i, c_i = iota2((256, 768))
    own = jnp.zeros((FR, 768), f32)
    extra0 = jnp.zeros((96, 768), f32)
    extra1 = jnp.zeros((96, 768), f32)
    for r in range(4):
        base = 192 * (me ^ r)
        inside = (c_i >= base) & (c_i < base + 192)
        sel0 = ((c_i - base == r_i) & inside).astype(f32).astype(bf16)
        sel1 = ((c_i - base == r_i - 64) & inside).astype(f32).astype(bf16)
        mid = ((c_i - base == r_i - 64 * half) & inside).astype(f32).astype(bf16)
        own += mm(chunks[r][pl.ds(start, FR), pl.ds(lane0, 256)], mid)
        extra0 += mm(chunks[r][768:864, 0:256], sel0)
        extra1 += mm(chunks[r][768:864, 128:384], sel1)
    rows_ref[0:FR, :] = own.astype(bf16)
    rows_ref[FR : FR + 96, :] = extra0.astype(bf16)
    rows_ref[FR + 96 : FR + 192, :] = extra1.astype(bf16)

    vt[...] = qkv_ref[:, 512:704].astype(f32).T.astype(bf16)
    lse_ref[...] = jnp.zeros_like(lse_ref)
    for h in range(3):
        cols = slice(64 * h, 64 * h + 64)

        def attend(q0, queries, key0, keys, masked):
            query = (qkv_ref[q0 : q0 + queries, 0:256][:, cols].astype(f32) * 0.125).astype(bf16)
            key = qkv_ref[key0 : key0 + keys, 256:512][:, cols]
            scores = mm_nt(key, query)
            if masked:
                slot = lax.broadcasted_iota(jnp.int32, scores.shape, 0)
                scores = jnp.where(slot < SHORT, scores, neg_large)
            top = jnp.max(scores, axis=0, keepdims=True)
            weights = jnp.exp(scores - top)
            total = jnp.sum(weights, axis=0, keepdims=True)
            out = mm(vt[cols, key0 : key0 + keys], weights.astype(bf16))
            ot_ref[cols, q0 : q0 + queries] = out / total
            lse_ref[h : h + 1, q0 : q0 + queries] = top + jnp.log(total)

        for q0 in range(0, SLOTS, QF):
            attend(q0, QF, 0, SLOTS, False)
        attend(SLOTS, 256, SLOTS, 128, True)
    for r, out in enumerate((x0, x1, x2, x3)):
        out[:, 0:FR] = ot_ref[:, pl.ds(pl.multiple_of(FR * (me ^ r), 128), FR)].astype(bf16)
        out[:, FR:640] = ot_ref[:, SLOTS:TROWS].astype(bf16)


def attn_fwd(scal, chunks, wqkv, bqkv):
    return pl.pallas_call(
        attn_fwd_kernel,
        in_specs=[smem()] + [vmem()] * 6,
        out_specs=[vmem()] * 8,
        out_shape=[
            jax.ShapeDtypeStruct((TROWS, 768), bf16),
            jax.ShapeDtypeStruct((CH, TROWS), f32),
            jax.ShapeDtypeStruct((8, TROWS), f32),
            jax.ShapeDtypeStruct((576, 768), bf16),
        ]
        + [jax.ShapeDtypeStruct((CH, 640), bf16)] * 4,
        scratch_shapes=[pltpu.VMEM((4, 320, 768), bf16), pltpu.VMEM((CH, TROWS), bf16)],
        compiler_params=params(),
        cost_estimate=cost(28),
        name="attn_fwd",
    )(scal, *chunks, wqkv, bqkv)


def attn_sync_kernel(
    qkv_ref, ot_ref, lse_ref, d0, d1, d2, d3, gst, w_ref, h0, h1, h2, h3,
    nl, gd, ul_hbm, gu_hbm, m0, m1, m2, m3, gac, sums,
    a1_out, a2_out, b_out, g_out, qsums,
    ring, load_s, dot_, do_, kt, delta, dqt, dk, dv, dqkv, keep1, send1, got1, keep2, send2, got2,
    bkeep, bsend, bgot, ra, rd, g0, g1, g2, g3, rg, core_s, core_r, wide_s, wide_r,
):
    n, me = lax.axis_index("narrow"), lax.axis_index("wide")
    core = n % 2
    other = n + 1 - 2 * core
    MESH = pl.DeviceIdType.MESH

    barrier = pltpu.get_barrier_semaphore()
    peers = [(n, xor2(me, r)) for r in range(1, 4)] + [(other, me)]
    for peer in peers:
        pl.semaphore_signal(barrier, inc=1, device_id=peer, device_id_type=MESH)

    def load(i):
        if i < 4:
            j = 2 * (1 - core) + i if i < 2 else 2 * core + i - 2
            src = gu_hbm.at[:, pl.ds(pl.multiple_of(768 * j, 128), 768)]
        else:
            src = ul_hbm.at[:, 768 * (i - 4) : 768 * (i - 3)]
        return pltpu.make_async_copy(src, ring.at[i % 2], load_s.at[i])

    load(0).start()
    load(1).start()
    pl.semaphore_wait(barrier, 4)

    def to_wide(i, r, src, dst):
        return pltpu.make_async_remote_copy(
            src_ref=src, dst_ref=dst, send_sem=wide_s.at[i], recv_sem=wide_r.at[i],
            device_id=(n, xor2(me, r)), device_id_type=MESH,
        )

    def to_core(i, src, dst):
        return pltpu.make_async_remote_copy(
            src_ref=src, dst_ref=dst, send_sem=core_s.at[i], recv_sem=core_r.at[i],
            device_id=(other, me), device_id_type=MESH,
        )

    send_d = [to_wide(r - 1, r, (d1, d2, d3)[r - 1], rd.at[r - 1]) for r in (3, 1, 2)]
    for c in send_d:
        c.start()

    core1, core2, coreb = to_core(0, send1, got1), to_core(1, send2, got2), to_core(2, bsend, bgot)
    for i in range(4):
        load(i).wait()
        up = tn(nl[...], ring[i % 2]).astype(bf16)
        to = send1 if i < 2 else keep1
        row = 192 * (i % 2)
        for e in range(4):
            to[xor2(me, e), row : row + 192, :] = up[192 * e : 192 * e + 192]
        load(i + 2).start()
        if i == 1:
            core1.start()
    extra = jnp.concatenate([sums[...], jnp.zeros((48, 768), f32)], axis=0).astype(bf16)
    for j in range(4):
        load(4 + j).wait()
        down = tn(ring[j % 2], gd[...]).astype(bf16)
        rel = xor2(me, j)
        put(core == 0, keep2, send2, rel, 0, down[0:512])
        put(core == 1, keep2, send2, rel, 0, down[512:768])
        if j < 2:
            load(6 + j).start()
    for r, m in enumerate((m0, m1, m2, m3)):
        put(core == 1, keep2, send2, r, 256, mm(m[...], gac[...]).astype(bf16))
        put(core == 1, keep2, send2, r, 448, extra)
    core2.start()
    core1.wait()
    for r in range(4):
        keep1[r] = (keep1[r].astype(f32) + got1[r].astype(f32)).astype(bf16)
    send_a = [to_wide(2 + r, r, keep1.at[r], ra.at[r - 1]) for r in (3, 1, 2)]
    for c in send_d:
        c.wait()
    for c in send_a:
        c.start()

    short = d0[:, FR : FR + 256].astype(f32)
    dot_[:, pl.ds(pl.multiple_of(FR * me, 128), FR)] = d0[:, 0:FR]
    for r in range(1, 4):
        dot_[:, pl.ds(pl.multiple_of(FR * xor2(me, r), 128), FR)] = rd[r - 1, :, 0:FR]
        short += rd[r - 1, :, FR : FR + 256].astype(f32)
    dot_[:, SLOTS:TROWS] = short.astype(bf16)
    whole = dot_[...].astype(f32)
    do_[...] = whole.T.astype(bf16)
    prod = whole * ot_ref[...]
    for h in range(3):
        delta[h : h + 1, :] = jnp.sum(prod[64 * h : 64 * h + 64], axis=0, keepdims=True)
    kt[...] = qkv_ref[:, 256:448].astype(f32).T.astype(bf16)
    keep_k, keep_v = [], []
    for h in range(3):
        cols = slice(64 * h, 64 * h + 64)
        dk[...] = jnp.zeros_like(dk)
        dv[...] = jnp.zeros_like(dv)

        def step(q0, queries, key0, keys, masked):
            at_q = pl.ds(q0, queries)
            query = qkv_ref[at_q, 0:256][:, cols]
            scaled = (query.astype(f32) * 0.125).astype(bf16)
            grad = do_[at_q, :][:, cols]
            grad_t = dot_[cols, at_q]
            lse = lse_ref[h : h + 1, at_q]
            dl = delta[h : h + 1, at_q]
            grad_q = jnp.zeros((64, queries), f32)
            piece = min(keys, KB)
            for at in range(key0, key0 + keys, piece):
                key = qkv_ref[at : at + piece, 256:512][:, cols]
                val = qkv_ref[at : at + piece, 512:768][:, cols]
                probs = jnp.exp(mm_nt(key, scaled) - lse)
                if masked:
                    slot = lax.broadcasted_iota(jnp.int32, probs.shape, 0)
                    probs = jnp.where(slot < SHORT, probs, 0.0)
                grad_p = mm(val, grad_t)
                grad_s = (probs * (grad_p - dl)).astype(bf16)
                dv[at : at + piece, :] += mm(probs.astype(bf16), grad)
                dk[at : at + piece, :] += mm(grad_s, query)
                grad_q += mm(kt[cols, at : at + piece], grad_s)
            dqt[cols, at_q] = grad_q * 0.125

        for q0 in range(0, SLOTS, QB):
            step(q0, QB, 0, SLOTS, False)
        step(SLOTS, 256, SLOTS, 128, True)
        keep_k.append((dk[...] * 0.125).astype(bf16))
        keep_v.append(dv[...].astype(bf16))
    zeros = jnp.zeros((TROWS, 64), bf16)
    dqkv[:, 0:192] = dqt[...].T.astype(bf16)
    dqkv[:, 192:256] = zeros
    dqkv[:, 256:512] = jnp.concatenate(keep_k + [zeros], axis=1)
    dqkv[:, 512:768] = jnp.concatenate(keep_v + [zeros], axis=1)

    parts = (g0, g1, g2, g3)
    lanes = pl.multiple_of(FR * me, 128)
    near, far = slice(0, 896), slice(896, TROWS)

    def project(r):
        rows = pl.ds(pl.multiple_of(192 * xor2(me, r), 64), 192)
        part = mm_nt(w_ref[rows, :], dqkv[...])
        parts[r][...] = part.astype(bf16)
        own = gst[rows, 0:FR].astype(f32)
        parts[r][:, pl.ds(lanes, FR)] = (parts[r][:, pl.ds(lanes, FR)].astype(f32) + own).astype(bf16)
        parts[r][:, SLOTS:TROWS] = (part[:, SLOTS:TROWS] + gst[rows, FR : FR + 256].astype(f32)).astype(bf16)

    def hop(i, r, src, half):
        return to_wide(6 + i, r, src.at[:, half], rg.at[i])

    first = [hop(0, 1, g3, near), hop(1, 2, g3, far), hop(2, 1, g1, near), hop(3, 2, g2, far)]
    second = [hop(4, 2, g2, near), hop(5, 1, g1, far)]
    project(3)
    first[0].start()
    first[1].start()
    project(1)
    first[2].start()
    project(2)
    first[3].start()
    project(0)
    qsums[...] = jnp.sum(dqkv[...].astype(f32), axis=0, keepdims=True)

    def join(part, half, i):
        part[:, half] = (part[:, half].astype(f32) + rg[i].astype(f32)).astype(bf16)

    def chunk_grad(chunk, r):
        turned = chunk[...].astype(f32).T.astype(bf16)
        value = (
            mm(turned[0:192, 0:768], dqkv[0:768, :])
            + mm(turned[0:192, 768:864], dqkv[SLOTS : SLOTS + 96, :])
            + mm(turned[192:384, 0:768], dqkv[768:1536, :])
            + mm(turned[192:384, 768:864], dqkv[SLOTS + 96 : SLOTS + 192, :])
        ).astype(bf16)
        put(core == 0, bkeep, bsend, r, 0, value[0:96])
        put(core == 1, bkeep, bsend, r, 0, value[96:192])

    chunk_grad(h0, 0)
    chunk_grad(h1, 1)
    for c in send_a:
        c.wait()
    a1_out[...] = (keep1[0].astype(f32) + ra[0].astype(f32) + ra[1].astype(f32) + ra[2].astype(f32)).astype(bf16)
    first[0].wait()
    join(g2, near, 0)
    second[0].start()
    first[1].wait()
    join(g1, far, 1)
    second[1].start()
    chunk_grad(h2, 2)
    chunk_grad(h3, 3)
    coreb.start()
    core2.wait()
    for r in range(4):
        a2_out[r] = (keep2[r].astype(f32) + got2[r].astype(f32)).astype(bf16)
    first[2].wait()
    first[3].wait()
    coreb.wait()
    for r in range(4):
        b_out[r] = (bkeep[r].astype(f32) + bgot[r].astype(f32)).astype(bf16)
    second[0].wait()
    g_out[:, near] = g0[:, near].astype(f32) + rg[2].astype(f32) + rg[4].astype(f32)
    second[1].wait()
    g_out[:, far] = g0[:, far].astype(f32) + rg[3].astype(f32) + rg[5].astype(f32)


def attn_sync(qkv, ot, lse, dparts, gst, wqkv, first, nl, gd, ul, gu, mix, gac, sums):
    sds = jax.ShapeDtypeStruct
    hbm = pl.BlockSpec(memory_space=pl.ANY)
    sem = pltpu.SemaphoreType.DMA
    room = lambda *shape: pltpu.VMEM(shape, bf16)
    return pl.pallas_call(
        attn_sync_kernel,
        in_specs=[vmem()] * 15 + [hbm] * 2 + [vmem()] * 6,
        out_specs=[vmem()] * 5,
        out_shape=[
            sds((384, 768), bf16), sds((4, 512, 768), bf16), sds((4, 96, 768), bf16), sds((CH, TROWS), f32),
            sds((1, 768), f32),
        ],
        scratch_shapes=[
            room(2, 768, 768),
            sem((8,)),
            room(CH, TROWS),
            room(TROWS, CH),
            room(CH, TROWS),
            pltpu.VMEM((8, TROWS), f32),
            pltpu.VMEM((CH, TROWS), f32),
            pltpu.VMEM((TROWS, 64), f32),
            pltpu.VMEM((TROWS, 64), f32),
            room(TROWS, 768),
        ]
        + [room(4, 384, 768)] * 3
        + [room(4, 512, 768)] * 3
        + [room(4, 96, 768)] * 3
        + [room(3, 384, 768), room(3, CH, 640)]
        + [room(CH, TROWS)] * 4
        + [room(6, CH, 896), sem((3,)), sem((3,)), sem((12,)), sem((12,))],
        compiler_params=params(collective_id=2, has_side_effects=True),
        cost_estimate=cost(90),
        name="attn_sync",
    )(qkv, ot, lse, *dparts, gst, wqkv, *first, nl, gd, ul, gu, *mix, gac, sums)


def wgrad_pair(pair, me, gsum, pre_ref, x_ref, sums_ref, half, gf, g_ref, gp, p0, p1, bb, g2, xt):
    at = pl.ds(pl.multiple_of(96 * pair, 32), 96)
    total = gsum[at, :]
    pad = jnp.zeros((16, TROWS), f32)
    rows = jnp.concatenate([total[0:48], pad, total[48:96], pad], axis=0)
    gf[0:SLOTS, :] = rows[:, 0:SLOTS].T
    gf[SLOTS:SBASE, :] = jnp.zeros((SBASE - SLOTS, 128), f32)
    gf[SBASE:TROWS, :] = rows[:, SLOTS:TROWS].T[0 : TROWS - SBASE]
    g_ref[0:64, :] = jnp.zeros((64, 128), bf16)
    g_ref[1856:1936, :] = jnp.zeros((80, 128), bf16)
    gp[0:16, :] = jnp.zeros((16, 128), f32)
    pre = pre_ref[pair]
    slope = gelu_parts(pre) + pre * density(pre)
    wide = (gf[...] * slope).astype(bf16).astype(f32)
    bias_sum = jnp.sum(wide, axis=0, keepdims=True)
    row = lax.broadcasted_iota(jnp.int32, (TROWS, 128), 0)
    wide = jnp.where(row < SBASE + UNIQUE, wide, 0.0)
    gp[16 : 16 + TROWS, :] = wide
    g_ref[64 : 64 + TROWS, :] = wide.astype(bf16)
    extra = jnp.concatenate(
        [sums_ref[...], jnp.concatenate([bias_sum, jnp.zeros((1, 640), f32)], axis=1), jnp.zeros((14, 768), f32)], axis=0
    )
    for r in range(4):
        half[r, 192:208, :] = extra.astype(bf16)

    lane = lax.broadcasted_iota(jnp.int32, (TROWS, 128), 1)
    here, before = gp[16 : 16 + TROWS, :], gp[15 : 15 + TROWS, :]
    a, b = pair_slots(x_ref.at[pair], 1920)
    p0[...] = a
    p1[...] = b
    pack0, pack1 = gather_slots((256, 384), 0), gather_slots((256, 384), 192)
    for j in range(2):
        bb[0:16, :] = jnp.zeros((16, 128), f32)
        if j == 0:
            bb[16 : 16 + TROWS, :] = jnp.where(lane < 64, here, pltpu.roll(before, 64, 1))
        else:
            bb[16 : 16 + TROWS, :] = jnp.where(lane < 64, pltpu.roll(here, 64, 1), before)
        for p in range(8):
            g2[:, 128 * p : 128 * p + 128] = bb[16 - 2 * p : 16 - 2 * p + TROWS, :].astype(bf16)
        slots = (p0, p1)[j]
        for q in range(4):
            xt[128 * q : 128 * q + 128, :] = slots[32 * q : 32 * q + TROWS, :].astype(f32).T.astype(bf16)
        for side in range(2):
            base = 512 * side
            left = mm(xt[...], g2[:, base : base + 256]).astype(bf16)
            right = mm(xt[...], g2[:, base + 256 : base + 512]).astype(bf16)
            packed = (mm(left, pack0) + mm(right, pack1)).astype(bf16)
            for m in range(4):
                tile = jnp.concatenate([packed[128 * m : 128 * m + 48], packed[128 * m + 64 : 128 * m + 112]], axis=0)
                half[xor2(me, m), 96 * j : 96 * j + 96, 384 * side : 384 * side + 384] = tile


def conv_sync_kernel(
    gsum, pre_ref, x_ref, sums_ref, wd_ref, xu, a_ref, b_ref,
    fu, fa, fb, fc, ou, oa, ob, oc, f0, f1, f2, f3,
    gp, p0, p1, bb, g2, xt, y_ref, t_ref, gf, g, fg, s1, s2, s3,
    csend, ckeep, cgot, ra, rb, rc, xa, xb, eu, ea, eb, ec, yu, ya, yb, yc,
    ss, so, re, rr, sc, rcv, wide_s, wide_r, core_s, core_r,
):
    n, me = lax.axis_index("narrow"), lax.axis_index("wide")
    z, core = n // 2, n % 2
    MESH = pl.DeviceIdType.MESH

    def copy(src, dst, send, recv, device):
        return pltpu.make_async_remote_copy(
            src_ref=src, dst_ref=dst, send_sem=send, recv_sem=recv, device_id=device, device_id_type=MESH
        )

    def along(zz, cc=core):
        return (2 * zz + cc, me)

    barrier = pltpu.get_barrier_semaphore()

    def greet(device):
        pl.semaphore_signal(barrier, inc=1, device_id=device, device_id_type=MESH)

    for r in range(1, 4):
        greet((n, xor2(me, r)))
    greet(along(z, 1 - core))

    @pl.when(z > 0)
    def _():
        greet(along(z - 1))

    @pl.when(z < 3)
    def _():
        greet(along(z + 1))

    pl.semaphore_wait(barrier, 4 + jnp.minimum(z, 1) + jnp.minimum(3 - z, 1))

    def over_wide(which, r, src, dst):
        return copy(src, dst, wide_s.at[3 * which + r - 1], wide_r.at[3 * which + r - 1], (n, xor2(me, r)))

    send_b = [over_wide(0, r, b_ref.at[r], rb.at[r - 1]) for r in (3, 1, 2)]
    send_a = [over_wide(1, r, a_ref.at[r], ra.at[r - 1]) for r in (3, 1, 2)]
    for c in send_b + send_a:
        c.start()

    pieces = [(3, None, 96 * r, 96) for r in range(4)]
    pieces += [(0, r, 0, 96) for r in range(4)] + [(1, None, 128 * r, 128) for r in range(4)]
    for r in range(4):
        pieces += [(2, r, 0, 112), (2, r, 112, 96)]
    count = len(pieces)
    set_u, set_b, set_a, set_c = range(0, 4), range(4, 8), range(8, 12), range(12, count)

    def views(refs):
        out = []
        for which, r, row, rows in pieces:
            ref = refs[which]
            out.append(ref.at[row : row + rows] if r is None else ref.at[r, row : row + rows])
        return out

    x, e, y, f, o = (views(refs) for refs in ((xb, xa, csend, xu), (eb, ea, ec, eu), (yb, ya, yc, yu), (fb, fa, fc, fu), (ob, oa, oc, ou)))

    def first(k, here):
        return k % 2 == (0 if here == 1 else 1)

    def swap(k):
        return copy(f[k], o[k], sc.at[k], rcv.at[k], along(z, 1 - core))

    def inward(k, here):
        return copy(x[k], e[k], ss.at[k], re.at[k], along(1 if here == 0 else 2))

    def across(k, here):
        src = y[k] if first(k, here) else f[k]
        return copy(src, src, ss.at[k], rr.at[k], along(3 - here))

    def outward(k, here):
        return copy(f[k], f[k], so.at[k], rr.at[k], along(0 if here == 1 else 3))

    def at_ends(do):
        pl.when(z == 0)(lambda: do(0))
        pl.when(z == 3)(lambda: do(3))

    def at_inner(do):
        pl.when(z == 1)(lambda: do(1))
        pl.when(z == 2)(lambda: do(2))

    def begin(ks):
        def do(here):
            for k in ks:
                inward(k, here).start()

        at_ends(do)

    def meet(ks, here):
        for k in ks:
            inward(k, here).wait_recv()
            if first(k, here):
                y[k][...] = (x[k][...].astype(f32) + e[k][...].astype(f32)).astype(bf16)
                across(k, here).start()

    def close(ks, here):
        for k in ks:
            if not first(k, here):
                across(k, here).wait_recv()
                f[k][...] = (x[k][...].astype(f32) + e[k][...].astype(f32) + y[k][...].astype(f32)).astype(bf16)
                across(k, here).start()
                outward(k, here).start()
                swap(k).start()

    def pass_on(ks, here):
        for k in ks:
            if first(k, here):
                across(k, here).wait_recv()
                outward(k, here).start()
                swap(k).start()

    def wgrad(pair, half, slot):
        wgrad_pair(
            pair, me, gsum, pre_ref, x_ref, sums_ref, half, gf.at[slot], g.at[slot],
            gp, p0, p1, bb, g2, xt,
        )

    def dgrad(pair, slot):
        a, b = pair_slots(g.at[slot], 1920)
        p0[...] = a
        p1[...] = b
        value = conv_block((p0, p1), wd_ref.at[pl.ds(2 * pair, 2)], y_ref, t_ref, 1) + gf[slot]
        fg[pair] = value.astype(bf16)

    begin(set_u)
    wgrad(1 - core, csend, 0)
    to_core = copy(csend, cgot, core_s, core_r, along(z, 1 - core))
    to_core.start()
    for c in send_b:
        c.wait()
    xb[0] = b_ref[0]
    for r in range(1, 4):
        xb[r] = rb[r - 1]
    begin(set_b)
    at_inner(lambda here: meet(set_u, here))

    wgrad(core, ckeep, 1)
    to_core.wait()
    for r in range(4):
        ckeep[r] = (ckeep[r].astype(f32) + cgot[r].astype(f32)).astype(bf16)
    send_c = [over_wide(2, r, ckeep.at[r], rc.at[r - 1]) for r in (3, 1, 2)]
    for c in send_c:
        c.start()

    def inner_b(here):
        close(set_u, here)
        meet(set_b, here)

    at_inner(inner_b)
    dgrad(1 - core, 0)

    def inner_c(here):
        pass_on(set_u, here)
        close(set_b, here)

    at_inner(inner_c)
    for c in send_a:
        c.wait()
    xa[...] = (a_ref[0].astype(f32) + ra[0].astype(f32) + ra[1].astype(f32) + ra[2].astype(f32)).astype(bf16)
    begin(set_a)
    dgrad(core, 1)
    pack0, pack1 = gather_slots((256, 384), 0), gather_slots((256, 384), 192)

    def rows_of(lo, rows):
        return jnp.concatenate([fg[0, lo : lo + rows, :], fg[1, lo : lo + rows, :]], axis=1)

    outs = (f0, s1, s2, s3)
    for d in range(4):
        low = jnp.concatenate([rows_of(FR * d + 256, 128), rows_of(SBASE, 128)], axis=0)
        chunk = (mm(rows_of(FR * d, 256), pack0) + mm(low, pack1)).astype(bf16)
        for r in range(4):

            @pl.when(xor2(me, d) == r)
            def _():
                outs[r][...] = chunk

    for c in send_c:
        c.wait()
    csend[0] = ckeep[0]
    for r in range(1, 4):
        csend[r] = rc[r - 1]
    begin(set_c)
    send_f = [over_wide(3, r, (s1, s2, s3)[r - 1], (f1, f2, f3)[r - 1]) for r in (3, 1, 2)]
    for c in send_f:
        c.start()

    def inner(here):
        pass_on(set_b, here)
        rest = list(set_a) + list(set_c)
        for i in range(0, len(rest), 2):
            pair = rest[i : i + 2]
            meet(pair, here)
            close(pair, here)
            if i:
                pass_on(rest[i - 2 : i], here)
        pass_on(rest[-2:], here)
        for k in range(count):
            across(k, here).wait_send()
            outward(k, here).wait_send()
            swap(k).wait()

    def outer(here):
        for k in range(count):
            copy(f[k], f[k], so.at[k], rr.at[k], along(z)).wait_recv()
            swap(k).start()
        for k in range(count):
            inward(k, here).wait_send()
            swap(k).wait()

    at_inner(inner)
    at_ends(outer)
    for c in send_f:
        c.wait()


def conv_sync(gsum, pre, xp, sums, wd, up_sum, ffn_halves, qkv_halves):
    sds = jax.ShapeDtypeStruct
    shapes = [(384, 768), (512, 768), (4, 96, 768), (4, 208, 768)]
    sem = pltpu.SemaphoreType.DMA
    return pl.pallas_call(
        conv_sync_kernel,
        in_specs=[vmem()] * 8,
        out_specs=[vmem()] * 12,
        out_shape=[sds(v, bf16) for v in shapes * 2] + [sds((256, 384), bf16)] * 4,
        scratch_shapes=[
            pltpu.VMEM((16 + TROWS, 128), f32),
            pltpu.VMEM((1920, 128), bf16),
            pltpu.VMEM((1920, 128), bf16),
            pltpu.VMEM((16 + TROWS, 128), f32),
            pltpu.VMEM((TROWS, 1024), bf16),
            pltpu.VMEM((512, TROWS), bf16),
            pltpu.VMEM((CB + 16, 1024), f32),
            pltpu.VMEM((CB + 8, 128), f32),
            pltpu.VMEM((2, TROWS, 128), f32),
            pltpu.VMEM((2, 1936, 128), bf16),
            pltpu.VMEM((2, TROWS, 128), bf16),
        ]
        + [pltpu.VMEM((256, 384), bf16)] * 3
        + [pltpu.VMEM((4, 208, 768), bf16)] * 3
        + [pltpu.VMEM((3, 512, 768), bf16), pltpu.VMEM((3, 96, 768), bf16), pltpu.VMEM((3, 208, 768), bf16)]
        + [pltpu.VMEM((512, 768), bf16), pltpu.VMEM((4, 96, 768), bf16)]
        + [pltpu.VMEM(v, bf16) for v in shapes * 2]
        + [sem((20,))] * 6
        + [sem((12,)), sem((12,)), sem, sem],
        compiler_params=params(collective_id=1, has_side_effects=True),
        cost_estimate=cost(100),
        name="conv_sync",
    )(gsum, pre, xp, sums, wd, up_sum, ffn_halves, qkv_halves)


def unpack_frames_kernel(s_ref, c0, c1, c2, c3, o_ref):
    me, li = s_ref[0], s_ref[1]
    r_i, c_i = iota2((256, 768))
    top = jnp.zeros((256, 768), f32)
    low = jnp.zeros((256, 768), f32)
    for r, chunk in enumerate((c0, c1, c2, c3)):
        base = 192 * (me ^ r)
        inside = (c_i >= base) & (c_i < base + 192)
        top += mm(chunk[:, 0:256], ((c_i - base == r_i) & inside).astype(f32).astype(bf16))
        low += mm(chunk[:, 128:384], ((c_i - base == r_i - 64) & inside).astype(f32).astype(bf16))
    o_ref[li, 0:256, :] = top.astype(bf16)
    o_ref[li, 256:384, :] = low[0:128].astype(bf16)
    slot = me * FR + lax.broadcasted_iota(jnp.int32, (128, 768), 0)
    o_ref[1 - li, 0:128, :] = jnp.where(slot < SHORT, low[128:], 0.0).astype(bf16)
    o_ref[1 - li, 128:384, :] = jnp.zeros((256, 768), bf16)


def unpack_frames(scal, chunks):
    return pl.pallas_call(
        unpack_frames_kernel,
        in_specs=[smem()] + [vmem()] * 4,
        out_specs=vmem(),
        out_shape=jax.ShapeDtypeStruct((2, FR, 768), bf16),
        compiler_params=params(),
        cost_estimate=cost(3),
        name="unpack_frames",
    )(scal, *chunks)


def kernel_out_kernel(s_ref, own_ref, other_ref, o_ref, small_ref):
    core = s_ref[2]
    for g in range(4):
        half, row = g >> 1, 96 * (g & 1)
        x = jnp.where(half == core, own_ref[0, row : row + 96], other_ref[0, row : row + 96]).astype(f32)
        for k2 in range(2):
            for b in range(16):
                o_ref[16 * k2 + b, g] = x[48 * k2 : 48 * k2 + 48, 48 * b : 48 * b + 48]

    @pl.when(pl.program_id(0) == s_ref[0])
    def _():
        for half in range(2):
            small_ref[half] = jnp.where(half == core, own_ref[0, 192:208], other_ref[0, 192:208])


def kernel_out(scal, own, other):
    return pl.pallas_call(
        kernel_out_kernel,
        grid_spec=pltpu.PrefetchScalarGridSpec(
            num_scalar_prefetch=1,
            grid=(4,),
            in_specs=[pl.BlockSpec((1, 208, 768), lambda i, s: (i ^ s[0], 0, 0))] * 2,
            out_specs=[
                pl.BlockSpec((32, 4, 48, 48), lambda i, s: (0, i, 0, 0)),
                pl.BlockSpec((2, 16, 768), lambda i, s: (0, 0, 0)),
            ],
        ),
        out_shape=[jax.ShapeDtypeStruct((32, 16, 48, 48), f32), jax.ShapeDtypeStruct((2, 16, 768), bf16)],
        compiler_params=params(),
        cost_estimate=cost(9),
        name="kernel_grad_out",
    )(scal, own, other)


def norm(v):
    center = v - jnp.mean(v, axis=-1, keepdims=True)
    scale = lax.rsqrt(jnp.mean(center * center, axis=-1, keepdims=True) + eps_norm)
    return center * scale, scale


def norm_back(e, n, scale):
    return (e - jnp.mean(e, axis=-1, keepdims=True) - n * jnp.mean(e * n, axis=-1, keepdims=True)) * scale


def ffn_kernel(
    s_ref, rows_ref, m0, m1, m2, m3, wo, wu_hbm, bu, wd_hbm, vecs, og,
    lo, ul_hbm, gu_hbm, nl, gd, gac, x0, x1, x2, x3, gst, sums,
    wu, wd, ul, gu, slope, v, gsc, sems,
):
    me, li = s_ref[0], s_ref[1]
    const = FR + UNIQUE
    bo, g1, s1, bd, g2, s2 = (vecs[k : k + 1, :] for k in range(6))
    loads = [
        pltpu.make_async_copy(wu_hbm, wu, sems.at[0]),
        pltpu.make_async_copy(wd_hbm, wd, sems.at[1]),
    ]
    for load in loads:
        load.start()

    def total(x):
        return jnp.sum(x, axis=0, keepdims=True)

    mix = jnp.concatenate([m0[...], m1[...], m2[...], m3[...]], axis=0)
    out = lax.dot_general(mix, wo[...], (((0,), (0,)), ((), ())), preferred_element_type=f32)
    gsc[0:576, :] = rows_ref[...].astype(f32) + out[0:576] + bo
    last = gsc[const : const + 1, :]
    v[0:FR, :] = gsc[0:FR, :]
    v[FR : FR + 128, :] = jnp.where(me == 0, gsc[FR : FR + 128, :], last)
    mine = jnp.where(me == 0, 1.0, 0.0)
    keep_low = (lax.broadcasted_iota(jnp.int32, (64, 768), 0) < UNIQUE - 128).astype(f32) * mine
    v[FR + 128 : FR + 192, :] = jnp.where(keep_low > 0.5, gsc[FR + 128 : FR + 192, :], last)
    v[FR + 192 :, :] = jnp.broadcast_to(last, (192, 768))

    n1, scale1 = norm(v[...])
    v[...] = n1
    norm_one = n1 * g1 + s1
    low = norm_one.astype(bf16)
    nl[...] = low
    down = norm_one + bd
    stores = []
    loads[0].wait()
    for j in range(4):
        cols = slice(768 * j, 768 * j + 768)
        up = mm(low, wu[:, cols]) + bu[:, cols]
        cdf = gelu_parts(up)
        slope[:, cols] = cdf + up * density(up)
        act = (up * cdf).astype(bf16)
        ul[:, cols] = act
        stores.append(pltpu.make_async_copy(ul.at[:, cols], ul_hbm.at[:, cols], sems.at[2 + j]))
        stores[-1].start()
        if j == 0:
            loads[1].wait()
        down += mm(act, wd[cols, :])
    n2, scale2 = norm(down)
    result = (n2 * g2 + s2).astype(bf16)
    lo[li] = result[0:FR]
    lo[1 - li] = result[FR:]
    given = jnp.concatenate([og[li], og[1 - li]], axis=0).astype(f32)
    sums[8:9, :] = total(given * n2)
    sums[9:10, :] = total(given)
    sums[10:16, :] = jnp.zeros((6, 768), f32)
    grad_two = norm_back(given * g2, n2, scale2)
    grad_down = grad_two.astype(bf16)
    gd[...] = grad_down
    sums[7:8, :] = total(grad_down.astype(f32))
    grad_n = grad_two
    for j in range(4):
        cols = slice(768 * j, 768 * j + 768)
        grad_up = (mm_nt(grad_down, wd[cols, :]) * slope[:, cols]).astype(bf16)
        gu[:, cols] = grad_up
        stores.append(pltpu.make_async_copy(gu.at[:, cols], gu_hbm.at[:, cols], sems.at[6 + j]))
        stores[-1].start()
        sums[j : j + 1, :] = total(grad_up.astype(f32))
        grad_n += mm_nt(grad_up, wu[:, cols])
    n1 = v[...]
    sums[5:6, :] = total(grad_n * n1)
    sums[6:7, :] = total(grad_n)
    grad_one = norm_back(grad_n * g1, n1, scale1)
    grad_attn = grad_one.astype(bf16).astype(f32)
    sums[4:5, :] = total(grad_attn)

    at = lax.broadcasted_iota(jnp.int32, (64, 768), 0) == UNIQUE - 128

    def collapsed(g):
        upper = g[FR : FR + 128] * mine
        lower = g[FR + 128 : FR + 192] * keep_low
        rest = total(g[FR:]) - total(upper) - total(lower)
        return jnp.concatenate(
            [g[0:FR], upper, jnp.where(at, rest, lower), jnp.zeros((64, 768), f32)], axis=0
        )

    gac[...] = collapsed(grad_attn).astype(bf16)
    for r, out in enumerate((x0, x1, x2, x3)):
        out[...] = mm_nt(wo[192 * r : 192 * r + 192, :], gac[...]).astype(bf16)
    gsc[...] = collapsed(grad_one)
    gst[...] = gsc[...].T.astype(bf16)
    for store in stores:
        store.wait()


def ffn(scal, rows, mix, wo, wu, bu, wd, vecs, og):
    sds = jax.ShapeDtypeStruct
    hbm = pl.BlockSpec(memory_space=pl.ANY)
    return pl.pallas_call(
        ffn_kernel,
        in_specs=[smem()] + [vmem()] * 6 + [hbm, vmem(), hbm, vmem(), vmem()],
        out_specs=[vmem(), hbm, hbm] + [vmem()] * 9,
        out_shape=[
            sds((2, FR, 768), bf16), sds((768, 3072), bf16), sds((768, 3072), bf16), sds((768, 768), bf16),
            sds((768, 768), bf16), sds((640, 768), bf16),
        ]
        + [sds((CH, 640), bf16)] * 4
        + [sds((768, 640), bf16), sds((16, 768), f32)],
        scratch_shapes=[
            pltpu.VMEM((768, 3072), bf16),
            pltpu.VMEM((3072, 768), bf16),
            pltpu.VMEM((768, 3072), bf16),
            pltpu.VMEM((768, 3072), bf16),
            pltpu.VMEM((768, 3072), f32),
            pltpu.VMEM((768, 768), f32),
            pltpu.VMEM((640, 768), f32),
            pltpu.SemaphoreType.DMA((10,)),
        ],
        compiler_params=params(),
        cost_estimate=cost(28),
        name="ffn",
    )(scal, rows, *mix, wo, wu, bu, wd, vecs, og)


def tn(a, b):
    return lax.dot_general(a, b, (((0,), (0,)), ((), ())), preferred_element_type=f32)


def finish_kernel(s_ref, own1, other1, own2, other2, ownb, otherb, up, down, out, wq, wk, wv, small, a1, a2, b_ref):
    me, core = s_ref[0], s_ref[2]
    for buf, own, other in ((a1, own1, other1), (a2, own2, other2)):
        buf[core] = own[...]
        buf[1 - core] = other[...]
    b_ref[:, pl.ds(pl.multiple_of(96 * core, 32), 96), :] = ownb[...]
    b_ref[:, pl.ds(pl.multiple_of(96 - 96 * core, 32), 96), :] = otherb[...]
    for j in range(4):
        row = 192 * (j & 1)
        up[:, 768 * j : 768 * j + 768] = a1[j >> 1, row : row + 192, :].astype(f32)
    down[0:512, :] = a2[0].astype(f32)
    down[512:768, :] = a2[1, 0:256, :].astype(f32)
    out[...] = a2[1, 256:448, :].astype(f32)
    small[...] = a2[1, 448:464, :].astype(f32)
    r_i, c_i = iota2((256, 768))
    totals = [jnp.zeros((CH, 768), f32)] * 3
    for r in range(4):
        base = 192 * (me ^ r)
        hit = (c_i - base == r_i) & (r_i < 192)
        move = hit.astype(f32).astype(bf16)
        for k in range(3):
            totals[k] = totals[k] + mm(b_ref[r, :, 256 * k : 256 * k + 256], move)
    wq[...], wk[...], wv[...] = totals


def finish(scal, *parts):
    sds = jax.ShapeDtypeStruct
    return pl.pallas_call(
        finish_kernel,
        in_specs=[smem()] + [vmem()] * 6,
        out_specs=[vmem()] * 7,
        out_shape=[sds((CH, 3072), f32), sds((768, 768), f32)] + [sds((CH, 768), f32)] * 4 + [sds((16, 768), f32)],
        scratch_shapes=[
            pltpu.VMEM((2, 384, 768), bf16),
            pltpu.VMEM((2, 512, 768), bf16),
            pltpu.VMEM((4, CH, 768), bf16),
        ],
        compiler_params=params(),
        cost_estimate=cost(6),
        name="weight_grads_out",
    )(scal, *parts)


def from_others(chunks):
    moved = [lax.ppermute(chunks[r], "wide", [(i, i ^ r) for i in range(4)]) for r in (3, 1, 2)]
    return [chunks[0], moved[1], moved[2], moved[0]]


def gathered(chunk):
    return from_others([chunk] * 4)


def on_device(
    frames_in, lengths, kernel, conv_bias, w_query, b_query, w_key, w_value, b_value, w_out, b_out,
    gain_one, shift_one, w_up, b_up, w_down, b_down, gain_two, shift_two, out_grad,
):
    me = lax.axis_index("wide").astype(jnp.int32)
    place_n = lax.axis_index("narrow").astype(jnp.int32)
    core, z = place_n & 1, place_n >> 1
    li = jnp.where(lengths[0] >= lengths[1], 0, 1).astype(jnp.int32)
    scal = jnp.stack([me, li, core, z])
    frames = from_others(pack_frames(scal, frames_in))
    wt, wd = prep_weights(scal, kernel)

    def own(v):
        return lax.dynamic_slice_in_dim(v, me * CH, CH, axis=v.ndim - 1)

    def three(a, b, c):
        gap = [(0, 0)] * (a.ndim - 1) + [(0, 64)]
        return jnp.concatenate([jnp.pad(a, gap), jnp.pad(b, gap), jnp.pad(c, gap)], axis=-1)

    wqkv = three(own(w_query), own(w_key), own(w_value))
    bqkv = three(own(b_query), jnp.zeros((CH,), bf16), own(b_value)).astype(f32)[None]
    bias = jnp.pad(own(conv_bias).astype(f32).reshape(2, 2, 48), ((0, 0), (0, 0), (0, 16))).reshape(2, 1, 128)
    w_out_rel = jnp.concatenate(
        [lax.dynamic_slice_in_dim(w_out, (me ^ r) * CH, CH, axis=0) for r in range(4)], axis=0
    )
    vecs = jnp.stack([b_out, gain_one, shift_one, b_down, gain_two, shift_two]).astype(f32)
    bu = b_up.astype(f32)[None]

    pre, xp, packed = conv_fwd(scal, frames, wt, bias)
    first = gathered(packed)
    qkv, mixed_t, lse, rows, *mixed = attn_fwd(scal, first, wqkv, bqkv)
    mix = from_others(mixed)
    layer_out, ul, gu, nl, gd, gac, x0, x1, x2, x3, gst, sums = ffn(
        scal, rows, mix, w_out_rel, w_up, bu, w_down, vecs, out_grad
    )
    up_sum, ffn_halves, qkv_halves, gsum, qkv_sums = attn_sync(
        qkv, mixed_t, lse, [x0, x1, x2, x3], gst, wqkv, first, nl, gd, ul, gu, mix, gac, sums
    )
    own1, own2, ownb, ownc, other1, other2, otherb, otherc, *fchunks = conv_sync(
        gsum, pre, xp, qkv_sums, wd, up_sum, ffn_halves, qkv_halves
    )
    frames_grad = unpack_frames(scal, fchunks)
    up, down, out, wq, wk, wv, small = finish(scal, own1, other1, own2, other2, ownb, otherb)
    grad_kernel, tiny = kernel_out(scal, ownc, otherc)
    tiny = tiny.astype(f32)

    def mine(row):
        return lax.dynamic_slice_in_dim(small[row], me * CH, CH, axis=0)

    bias_grad = jnp.concatenate([tiny[0, 1, :128], tiny[1, 1, :128]]).reshape(4, 64)[:, :48].reshape(CH)
    grad_b_up = lax.dynamic_index_in_dim(small[:4], me, 0, keepdims=False)
    return (
        layer_out,
        frames_grad,
        grad_kernel,
        bias_grad,
        wq,
        tiny[0, 0, 0:192],
        wk,
        wv,
        tiny[0, 0, 512:704],
        out,
        mine(4),
        mine(5),
        mine(6),
        up,
        grad_b_up,
        down,
        mine(7),
        mine(8),
        mine(9),
    )


def with_halo(x, sides, width):
    for axis, dim in sides:
        count, length = (lax.axis_size(axis), x.shape[dim])
        up = [(i, (i + 1) % count) for i in range(count - 1)]
        down = [(j, i) for i, j in up]
        last = lax.slice_in_dim(x, length - width, length, axis=dim)
        initial = lax.slice_in_dim(x, 0, width, axis=dim)
        before = lax.ppermute(last, axis, up)
        after = lax.ppermute(initial, axis, down)
        x = jnp.concatenate([before, x, after], axis=dim)
    return x


def layer_norm(value, gain, shift):
    center = value - jnp.mean(value, axis=-1, keepdims=True)
    spread = jnp.mean(center * center, axis=-1, keepdims=True)
    return center * lax.rsqrt(spread + eps_norm) * gain + shift


def gelu_exact(value):
    return jax.nn.gelu(value, approximate=False)


def project(rows_in, weight):
    return jnp.einsum("cfd,de->cfe", rows_in, weight, preferred_element_type=jnp.float32)


def project_back(grad_in, weight):
    return jnp.einsum("cfe,de->cfd", grad_in, weight, preferred_element_type=jnp.float32)


def weight_grad(rows_in, grad_in):
    return jnp.einsum("cfd,cfe->de", rows_in, grad_in, preferred_element_type=jnp.float32)


def row_total(grad_in):
    return jnp.sum(grad_in.astype(jnp.float32), axis=(0, 1))


def head_view(rows_in):
    return rows_in.reshape(rows_in.shape[0], rows_in.shape[1], HEADS, rows_in.shape[2] // HEADS)


def conv_apply(padded, weight, frames):
    kernel_span, groups, inner_ch, outer_ch = weight.shape
    taps_weight = jnp.transpose(weight, (0, 2, 1, 3)).reshape(
        kernel_span, inner_ch, groups * outer_ch
    )
    result = lax.conv_general_dilated(
        padded,
        taps_weight,
        (1,),
        "VALID",
        dimension_numbers=("NWC", "WIO", "NWC"),
        feature_group_count=groups,
        preferred_element_type=jnp.float32,
    )
    return result[:, :frames, :]


def conv_weight_grad(padded, grad_in, kernel_shape):
    kernel_span, groups, inner_ch, outer_ch = kernel_shape
    result = lax.conv_general_dilated(
        padded,
        grad_in,
        (1,),
        "VALID",
        dimension_numbers=("CWN", "IWO", "NWC"),
        batch_group_count=groups,
        preferred_element_type=jnp.float32,
    )
    result = result[:, :kernel_span, :].reshape(inner_ch, kernel_span, groups, outer_ch)
    return jnp.transpose(result, (1, 2, 0, 3))


def key_valid_at(lengths, first_row, row_count):
    return (first_row + jnp.arange(row_count, dtype=jnp.int32))[None, :] < lengths[:, None]


def masked_scores(query_h, keys_h, valid_keys, score_scale):
    scores = (
        jnp.einsum("cqhd,ckhd->cqhk", query_h, keys_h, preferred_element_type=jnp.float32)
        * score_scale
    )
    return jnp.where(valid_keys[:, None, None, :], scores, neg_large)


def block_terms(query_h, grad_h, lse_rows, delta_rows, keys_h, values_h, valid_keys, score_scale):
    scores = masked_scores(query_h, keys_h, valid_keys, score_scale)
    probs = jnp.where(valid_keys[:, None, None, :], jnp.exp(scores - lse_rows[..., None]), 0.0)
    grad_probs = jnp.einsum("cqhd,ckhd->cqhk", grad_h, values_h, preferred_element_type=jnp.float32)
    grad_scores = (probs * (grad_probs - delta_rows[..., None])).astype(jnp.bfloat16)
    results = []
    results.append(
        jnp.einsum("cqhk,ckhd->cqhd", grad_scores, keys_h, preferred_element_type=jnp.float32)
        * score_scale
    )
    results.append(
        jnp.einsum("cqhk,cqhd->ckhd", grad_scores, query_h, preferred_element_type=jnp.float32)
        * score_scale
    )
    results.append(
        jnp.einsum(
            "cqhk,cqhd->ckhd",
            probs.astype(jnp.bfloat16),
            grad_h,
            preferred_element_type=jnp.float32,
        )
    )
    return tuple(results)


def on_device_any(
    frames_in,
    lengths,
    kernel,
    conv_bias,
    w_query,
    b_query,
    w_key,
    w_value,
    b_value,
    w_out,
    b_out,
    gain_one,
    shift_one,
    w_up,
    b_up,
    w_down,
    b_down,
    gain_two,
    shift_two,
    out_grad,
):
    clip_count, frames, width = frames_in.shape
    head_dim = width // HEADS
    score_scale = head_dim ** (-0.5)
    half_span = kernel.shape[0] // 2
    wide_size = lax.axis_size("wide")
    positions = lax.axis_index("wide") * frames + jnp.arange(frames, dtype=jnp.int32)
    frame_valid = positions[None, :] < lengths[:, None]
    masked = jnp.where(frame_valid[..., None], frames_in, jnp.zeros((), jnp.bfloat16))
    padded = with_halo(masked, (("wide", 1),), half_span)
    pre_act = conv_apply(padded, kernel, frames) + conv_bias.astype(jnp.float32)
    first_act, pull_first = jax.vjp(gelu_exact, pre_act)
    first_out = masked.astype(jnp.float32) + first_act
    first_low = first_out.astype(jnp.bfloat16)
    query_rows = (project(first_low, w_query) + b_query.astype(jnp.float32)).astype(jnp.bfloat16)
    key_rows = project(first_low, w_key).astype(jnp.bfloat16)
    value_rows = (project(first_low, w_value) + b_value.astype(jnp.float32)).astype(jnp.bfloat16)
    query_h = head_view(query_rows)
    per_step = max(1, min(wide_size, 512 // frames))
    while wide_size % per_step:
        per_step -= 1
    run_max = jnp.full((clip_count, frames, HEADS), neg_large, jnp.float32)
    run_acc = jnp.zeros((clip_count, frames, HEADS, head_dim), jnp.float32)
    keys_p = lax.all_gather(key_rows, "wide", axis=1, tiled=True)
    values_p = lax.all_gather(value_rows, "wide", axis=1, tiled=True)
    row_count = keys_p.shape[1]
    valid_keys = key_valid_at(lengths, jnp.int32(0), row_count)
    scores = masked_scores(query_h, head_view(keys_p), valid_keys, score_scale)
    new_max = jnp.maximum(run_max, jnp.max(scores, axis=-1))
    weights = jnp.where(valid_keys[:, None, None, :], jnp.exp(scores - new_max[..., None]), 0.0)
    factor = jnp.exp(run_max - new_max)
    run_sum = jnp.sum(weights, axis=-1)
    run_acc = run_acc * factor[..., None] + jnp.einsum(
        "cqhk,ckhd->cqhd",
        weights.astype(jnp.bfloat16),
        head_view(values_p),
        preferred_element_type=jnp.float32,
    )
    run_max, run_sum, run_acc = (new_max, run_sum, run_acc)
    lse_rows = run_max + jnp.log(run_sum)
    mixed_heads = run_acc / run_sum[..., None]
    mixed_low = mixed_heads.reshape(clip_count, frames, width).astype(jnp.bfloat16)
    attn_out = project(mixed_low, w_out) + b_out.astype(jnp.float32)
    sum_one = first_out + attn_out
    norm_one, pull_one = jax.vjp(
        layer_norm, sum_one, gain_one.astype(jnp.float32), shift_one.astype(jnp.float32)
    )
    norm_low = norm_one.astype(jnp.bfloat16)
    up_pre = project(norm_low, w_up) + b_up.astype(jnp.float32)
    up_act, pull_up = jax.vjp(gelu_exact, up_pre)
    up_low = up_act.astype(jnp.bfloat16)
    down_out = project(up_low, w_down) + b_down.astype(jnp.float32)
    sum_two = norm_one + down_out
    layer_out, pull_two = jax.vjp(
        layer_norm, sum_two, gain_two.astype(jnp.float32), shift_two.astype(jnp.float32)
    )
    grad_sum_two, grad_gain_two, grad_shift_two = pull_two(out_grad.astype(jnp.float32))
    grad_down = grad_sum_two.astype(jnp.bfloat16)
    grad_w_down = weight_grad(up_low, grad_down)
    grad_b_down = row_total(grad_down)
    grad_up = pull_up(project_back(grad_down, w_down))[0].astype(jnp.bfloat16)
    grad_w_up = weight_grad(norm_low, grad_up)
    grad_b_up = row_total(grad_up)
    grad_norm_one = grad_sum_two + project_back(grad_up, w_up)
    grad_sum_one, grad_gain_one, grad_shift_one = pull_one(grad_norm_one)
    grad_attn = grad_sum_one.astype(jnp.bfloat16)
    grad_w_out = weight_grad(mixed_low, grad_attn)
    grad_b_out = row_total(grad_attn)
    grad_mixed = project_back(grad_attn, w_out).astype(jnp.bfloat16)
    grad_h = head_view(grad_mixed)
    delta_rows = jnp.sum(grad_h.astype(jnp.float32) * mixed_heads, axis=-1)
    total_slots = wide_size * frames
    first_row = jnp.int32(0)
    grad_q = jnp.zeros((clip_count, frames, HEADS, head_dim), jnp.float32)
    grad_k_all = jnp.zeros((clip_count, total_slots, width), jnp.float32)
    grad_v_all = jnp.zeros((clip_count, total_slots, width), jnp.float32)
    keys_p = lax.all_gather(key_rows, "wide", axis=1, tiled=True)
    values_p = lax.all_gather(value_rows, "wide", axis=1, tiled=True)
    row_count = keys_p.shape[1]
    valid_keys = key_valid_at(lengths, first_row, row_count)
    part_q, part_k, part_v = block_terms(
        query_h,
        grad_h,
        lse_rows,
        delta_rows,
        head_view(keys_p),
        head_view(values_p),
        valid_keys,
        score_scale,
    )
    old_k = lax.dynamic_slice_in_dim(grad_k_all, first_row, row_count, 1)
    old_v = lax.dynamic_slice_in_dim(grad_v_all, first_row, row_count, 1)
    grad_k_all = lax.dynamic_update_slice_in_dim(
        grad_k_all, old_k + part_k.reshape(clip_count, row_count, width), first_row, 1
    )
    grad_v_all = lax.dynamic_update_slice_in_dim(
        grad_v_all, old_v + part_v.reshape(clip_count, row_count, width), first_row, 1
    )
    grad_k_own, grad_v_own = (
        lax.psum_scatter(
            grad_k_all.astype(jnp.bfloat16), "wide", scatter_dimension=1, tiled=True
        ).astype(jnp.float32),
        lax.psum_scatter(
            grad_v_all.astype(jnp.bfloat16), "wide", scatter_dimension=1, tiled=True
        ).astype(jnp.float32),
    )
    grad_q_low = (grad_q + part_q).reshape(clip_count, frames, width).astype(jnp.bfloat16)
    grad_k_low = grad_k_own.astype(jnp.bfloat16)
    grad_v_low = grad_v_own.astype(jnp.bfloat16)
    grad_w_query = weight_grad(first_low, grad_q_low)
    grad_b_query = row_total(grad_q_low)
    grad_w_key = weight_grad(first_low, grad_k_low)
    grad_w_value = weight_grad(first_low, grad_v_low)
    grad_b_value = row_total(grad_v_low)
    grad_first = (
        grad_sum_one
        + project_back(grad_q_low, w_query)
        + project_back(grad_k_low, w_key)
        + project_back(grad_v_low, w_value)
    )
    grad_pre = pull_first(grad_first)[0].astype(jnp.bfloat16)
    grad_conv_bias = row_total(grad_pre)
    grad_kernel = conv_weight_grad(padded, grad_pre, kernel.shape)
    grad_padded = with_halo(grad_pre, (("wide", 1),), half_span)
    flipped = jnp.transpose(kernel[::-1], (0, 1, 3, 2))
    grad_masked = grad_first + conv_apply(grad_padded[:, 1:], flipped, frames)
    frames_grad = jnp.where(frame_valid[..., None], grad_masked, 0.0).astype(jnp.bfloat16)
    shards = (
        lax.psum_scatter(
            grad_kernel.astype(jnp.bfloat16), "wide", scatter_dimension=0, tiled=True
        ).astype(jnp.float32),
        lax.psum_scatter(
            grad_conv_bias.astype(jnp.bfloat16), "wide", scatter_dimension=0, tiled=True
        ).astype(jnp.float32),
        lax.psum_scatter(
            grad_w_query.astype(jnp.bfloat16), "wide", scatter_dimension=0, tiled=True
        ).astype(jnp.float32),
        lax.psum_scatter(
            grad_b_query.astype(jnp.bfloat16), "wide", scatter_dimension=0, tiled=True
        ).astype(jnp.float32),
        lax.psum_scatter(
            grad_w_key.astype(jnp.bfloat16), "wide", scatter_dimension=0, tiled=True
        ).astype(jnp.float32),
        lax.psum_scatter(
            grad_w_value.astype(jnp.bfloat16), "wide", scatter_dimension=0, tiled=True
        ).astype(jnp.float32),
        lax.psum_scatter(
            grad_b_value.astype(jnp.bfloat16), "wide", scatter_dimension=0, tiled=True
        ).astype(jnp.float32),
        lax.psum_scatter(
            grad_w_out.astype(jnp.bfloat16), "wide", scatter_dimension=0, tiled=True
        ).astype(jnp.float32),
        lax.psum_scatter(
            grad_b_out.astype(jnp.bfloat16), "wide", scatter_dimension=0, tiled=True
        ).astype(jnp.float32),
        lax.psum_scatter(
            grad_gain_one.astype(jnp.bfloat16), "wide", scatter_dimension=0, tiled=True
        ).astype(jnp.float32),
        lax.psum_scatter(
            grad_shift_one.astype(jnp.bfloat16), "wide", scatter_dimension=0, tiled=True
        ).astype(jnp.float32),
        lax.psum_scatter(
            grad_w_up.astype(jnp.bfloat16), "wide", scatter_dimension=0, tiled=True
        ).astype(jnp.float32),
        lax.psum_scatter(
            grad_b_up.astype(jnp.bfloat16), "wide", scatter_dimension=0, tiled=True
        ).astype(jnp.float32),
        lax.psum_scatter(
            grad_w_down.astype(jnp.bfloat16), "wide", scatter_dimension=0, tiled=True
        ).astype(jnp.float32),
        lax.psum_scatter(
            grad_b_down.astype(jnp.bfloat16), "wide", scatter_dimension=0, tiled=True
        ).astype(jnp.float32),
        lax.psum_scatter(
            grad_gain_two.astype(jnp.bfloat16), "wide", scatter_dimension=0, tiled=True
        ).astype(jnp.float32),
        lax.psum_scatter(
            grad_shift_two.astype(jnp.bfloat16), "wide", scatter_dimension=0, tiled=True
        ).astype(jnp.float32),
    )
    totals = (
        lax.psum(shards[0].astype(jnp.bfloat16), "narrow").astype(jnp.float32),
        lax.psum(shards[1].astype(jnp.bfloat16), "narrow").astype(jnp.float32),
        lax.psum(shards[2].astype(jnp.bfloat16), "narrow").astype(jnp.float32),
        lax.psum(shards[3].astype(jnp.bfloat16), "narrow").astype(jnp.float32),
        lax.psum(shards[4].astype(jnp.bfloat16), "narrow").astype(jnp.float32),
        lax.psum(shards[5].astype(jnp.bfloat16), "narrow").astype(jnp.float32),
        lax.psum(shards[6].astype(jnp.bfloat16), "narrow").astype(jnp.float32),
        lax.psum(shards[7].astype(jnp.bfloat16), "narrow").astype(jnp.float32),
        lax.psum(shards[8].astype(jnp.bfloat16), "narrow").astype(jnp.float32),
        lax.psum(shards[9].astype(jnp.bfloat16), "narrow").astype(jnp.float32),
        lax.psum(shards[10].astype(jnp.bfloat16), "narrow").astype(jnp.float32),
        lax.psum(shards[11].astype(jnp.bfloat16), "narrow").astype(jnp.float32),
        lax.psum(shards[12].astype(jnp.bfloat16), "narrow").astype(jnp.float32),
        lax.psum(shards[13].astype(jnp.bfloat16), "narrow").astype(jnp.float32),
        lax.psum(shards[14].astype(jnp.bfloat16), "narrow").astype(jnp.float32),
        lax.psum(shards[15].astype(jnp.bfloat16), "narrow").astype(jnp.float32),
        lax.psum(shards[16].astype(jnp.bfloat16), "narrow").astype(jnp.float32),
    )
    return (
        layer_out.astype(jnp.bfloat16),
        frames_grad,
        totals[0],
        totals[1],
        totals[2],
        totals[3],
        totals[4],
        totals[5],
        totals[6],
        totals[7],
        totals[8],
        totals[9],
        totals[10],
        totals[11],
        totals[12],
        totals[13],
        totals[14],
        totals[15],
        totals[16],
    )


def solution(mesh):
    rows = P("narrow", "wide", None)
    placed = (rows, P("narrow")) + (P(),) * 17 + (rows,)
    wide = mesh.shape["wide"]
    fast = wide == 4 and mesh.shape["narrow"] == 8
    return jax.shard_map(
        on_device if fast else on_device_any,
        mesh=mesh,
        in_specs=placed,
        out_specs=(rows, rows)
        + (P("wide", None, None, None), P("wide"), P("wide", None), P("wide"), P("wide", None), P("wide", None))
        + (P("wide"), P("wide", None), P("wide"), P("wide"), P("wide"), P("wide", None), P("wide"))
        + (P("wide", None), P("wide"), P("wide"), P("wide")),
        check_vma=False,
    )
```

```python
import functools

import jax
import jax.numpy as jnp
from jax import lax
from jax.experimental import pallas as pl
from jax.experimental.pallas import tpu as pltpu
from jax.sharding import PartitionSpec as P

HEADS = 12
GROUP_CH = 48
SHORT = 102
HALF = 64
UNIQUE = SHORT + HALF
FR = 384
SLOTS = 1536
SROWS = 192
TROWS = 1792
SBASE = 1600
CH = 192
eps_norm = 1e-05
neg_large = -1e30
bf16 = jnp.bfloat16
f32 = jnp.float32
QF = 1536
QB = 768
KB = 512
CB = 1792
VLIM = 60 * 1024 * 1024


def mm(a, b):
    return jnp.dot(a, b, preferred_element_type=f32)


def mm_nt(a, b):
    return lax.dot_general(a, b, (((1,), (1,)), ((), ())), preferred_element_type=f32)


def iota2(shape):
    return lax.broadcasted_iota(jnp.int32, shape, 0), lax.broadcasted_iota(jnp.int32, shape, 1)


def place(shape, rows_from, rows_to, cols_from):
    r, c = iota2(shape)
    hit = (c - cols_from == r - rows_from) & (r >= rows_from) & (r < rows_to)
    return hit.astype(f32).astype(bf16)


def spread(shape, lane0, start):
    r, c = iota2(shape)
    slot, inner = c >> 6, c & 63
    hit = (r == lane0 + start + slot * GROUP_CH + inner) & (inner < GROUP_CH)
    return hit.astype(f32).astype(bf16)


def gather_slots(shape, col0):
    r, c = iota2(shape)
    slot, inner = r >> 6, r & 63
    hit = (c == col0 + slot * GROUP_CH + inner) & (inner < GROUP_CH)
    return hit.astype(f32).astype(bf16)


def full(shape):
    return pl.BlockSpec(shape, lambda *_: (0,) * len(shape))


def smem():
    return pl.BlockSpec(memory_space=pltpu.SMEM)


def vmem():
    return pl.BlockSpec(memory_space=pltpu.VMEM)


def params(**kw):
    return pltpu.CompilerParams(vmem_limit_bytes=VLIM, **kw)


def cost(us):
    return pl.CostEstimate(flops=int(us * 1e9), bytes_accessed=int(us * 3.4e6), transcendentals=0)


def put(keeping, keep, send, rel, row0, data, lane0=0):
    rows, lanes = data.shape

    @pl.when(keeping)
    def _():
        keep[rel, row0 : row0 + rows, lane0 : lane0 + lanes] = data

    @pl.when(jnp.logical_not(keeping))
    def _():
        send[rel, row0 : row0 + rows, lane0 : lane0 + lanes] = data


def xor2(a, b):
    return (a + b) % 2 + 2 * ((a // 2 + b // 2) % 2)


def gelu_parts(v):
    cdf = 0.5 * (1.0 + lax.erf(v * (2.0 ** -0.5)))
    return cdf


def density(v):
    return jnp.exp(-0.5 * v * v) * 0.3989422804014327


def pack_frames_kernel(s_ref, x_ref, *outs):
    me, li = s_ref[0], s_ref[1]
    long, short = x_ref[li], x_ref[1 - li]
    slot = me * FR + lax.broadcasted_iota(jnp.int32, (128, 768), 0)
    short = jnp.where(slot < SHORT, short[:128].astype(f32), 0.0).astype(bf16)
    top = long[:256]
    low = jnp.concatenate([long[256:], short], axis=0)
    for d in range(4):
        first = 192 * d - (64 if d % 2 else 0)
        skip = 64 if d % 2 else 0
        chunk = mm(top[:, first : first + 256], place((256, 384), skip, skip + 192, 0)) + mm(
            low[:, first : first + 256], place((256, 384), skip, skip + 192, 192)
        )
        chunk = chunk.astype(bf16)
        for r in range(4):

            @pl.when((me ^ d) == r)
            def _():
                outs[r][...] = chunk


def pack_frames(scal, frames_in):
    return pl.pallas_call(
        pack_frames_kernel,
        out_shape=[jax.ShapeDtypeStruct((256, 384), bf16)] * 4,
        in_specs=[smem(), vmem()],
        out_specs=[vmem()] * 4,
        compiler_params=params(),
        cost_estimate=cost(3),
        name="pack_frames",
    )(scal, frames_in)


def prep_group(w_ref, wt_ref, wd_ref, z_ref, taps):
    left, right = place((48, 128), 0, 48, 0), place((48, 128), 0, 48, 64)
    wt_ref[...] = jnp.zeros_like(wt_ref)
    for i in range(48):
        taps[pl.ds(i, 128, stride=48), 0:48] = w_ref[i].astype(f32).T

    def rows(k, n):
        return taps[48 * k : 48 * (k + n), 0:48].astype(bf16)

    for k2 in range(8):
        pairs = rows(16 * k2, 16).reshape(8, 2, 48, 48)
        tile = mm(pairs[:, 0].reshape(384, 48), left) + mm(pairs[:, 1].reshape(384, 48), right)
        tile = tile.astype(bf16)
        for p in range(8):
            wt_ref[64 * k2 : 64 * k2 + 48, 128 * p : 128 * p + 128] = tile[48 * p : 48 * p + 48]
    for q in range(4):
        tile = mm(rows(112 - 32 * q, 16), left) + mm(rows(96 - 32 * q, 16), right)
        for b in range(16):
            z_ref[64 * b : 64 * b + 48, :] = tile[48 * (15 - b) : 48 * (15 - b) + 48]
        wd_ref[128 * q : 128 * q + 128, :] = z_ref[...].T.astype(bf16)


def pair_slots(t_ref, rows):
    wide = jnp.concatenate([t_ref[0:rows, :], t_ref[16 : rows + 16, :]], axis=1)
    r, c = iota2((256, 128))
    out = []
    for j in range(2):
        hit = ((r < 128) & (c == r - 64 * j) & (c < 64)) | ((r >= 128) & (c - 64 == r - 128 - 64 * j) & (c >= 64))
        out.append(mm(wide, hit.astype(f32).astype(bf16)).astype(bf16))
    return out


def conv_block(p_refs, w_ref, y_ref, s_ref, shift, n0=0, rows=CB):
    lane = lax.broadcasted_iota(jnp.int32, (rows, 128), 1)
    parts = []
    for j in range(2):
        lhs = jnp.concatenate([p_refs[j][n0 + 32 * q : n0 + 32 * q + rows + 16, :] for q in range(4)], axis=1)
        y_ref[0 : rows + 16] = mm(lhs, w_ref[j])
        total = y_ref[shift : shift + rows + 1, 0:128]
        for p in range(1, 8):
            total += y_ref[shift + 2 * p : shift + 2 * p + rows + 1, 128 * p : 128 * p + 128]
        s_ref[0 : rows + 1, :] = total
        here, after = s_ref[0:rows, :], s_ref[1 : rows + 1, :]
        if j == 0:
            parts.append(here + pltpu.roll(after, 64, 1))
        else:
            parts.append(pltpu.roll(here, 64, 1) + after)
    return jnp.where(lane < 64, parts[0], parts[1])


def front_sync_kernel(
    p0, p1, p2, p3, k_hbm, vec, wq, wk, wv,
    wd, pre_ref, xp, h0, h1, h2, h3, qkv, ot, lse_ref, rows_ref, w_own, m0, m1, m2, m3,
    kg, load_s, wt, taps, zt, rf, slots, y_ref, t_ref, first, wz, vt, o1, o2, o3, frame_s, frame_r, gat_s, gat_r, mix_s, mix_r,
):
    n, me = lax.axis_index("narrow"), lax.axis_index("wide")
    barrier = pltpu.get_barrier_semaphore()

    def device(r):
        return (n, xor2(me, r))

    for r in range(1, 4):
        pl.semaphore_signal(barrier, inc=1, device_id=device(r), device_id_type=pl.DeviceIdType.MESH)
    load = pltpu.make_async_copy(k_hbm.at[pl.ds(4 * me, 4)], kg, load_s)
    load.start()
    pl.semaphore_wait(barrier, 3)

    def copy(r, src, dst, send, recv):
        return pltpu.make_async_remote_copy(
            src_ref=src, dst_ref=dst, send_sem=send, recv_sem=recv, device_id=device(r),
            device_id_type=pl.DeviceIdType.MESH,
        )

    frames = [copy(r, (p1, p2, p3)[r - 1], rf.at[r - 1], frame_s.at[r - 1], frame_r.at[r - 1]) for r in (3, 1, 2)]
    for c in frames:
        c.start()

    zt[...] = jnp.zeros_like(zt)
    load.wait()

    def prep(g, carry):
        prep_group(kg.at[g], wt.at[g], wd.at[g], zt, taps)
        return carry

    lax.fori_loop(0, 4, prep, 0)
    r_i, c_i = iota2((768, 256))
    pick = ((r_i == 192 * me + c_i) & (c_i < 192)).astype(f32).astype(bf16)
    for k, w in enumerate((wq, wk, wv)):
        w_own[:, 256 * k : 256 * k + 256] = mm(w[...], pick).astype(bf16)
    own_vec = mm(vec[...], pick)
    bias_qkv = jnp.concatenate([own_vec[1:2], jnp.zeros((1, 256), f32), own_vec[2:3]], axis=1)
    bias = [mm(vec[...], spread((768, 128), 0, 192 * me + 96 * c))[0:1] for c in range(2)]
    wz[:, 0:64, :] = jnp.zeros((4, 64, 768), bf16)
    wz[:, 256:320, :] = jnp.zeros((4, 64, 768), bf16)
    for r in range(4):
        wz[r, 64:256, :] = w_own[pl.ds(pl.multiple_of(192 * xor2(me, r), 64), 192), :]

    for c in frames:
        c.wait()
    for c in range(2):
        xp[c, 0:64, :] = jnp.zeros((64, 128), bf16)
        xp[c, 1600:1664, :] = jnp.zeros((64, 128), bf16)
        xp[c, 1792:1936, :] = jnp.zeros((144, 128), bf16)
        top_map, low_map = spread((256, 128), 0, 96 * c), spread((256, 128), 64, 96 * c)
        short = jnp.zeros((128, 128), f32)
        for r in range(4):
            src = xor2(me, r)
            chunk = p0 if r == 0 else rf.at[r - 1]
            low = mm(chunk[:, 128:384], low_map)
            base = pl.multiple_of(64 + FR * src, 64)
            xp[c, pl.ds(base, 256), :] = mm(chunk[:, 0:256], top_map).astype(bf16)
            xp[c, pl.ds(pl.multiple_of(base + 256, 64), 128), :] = low[:128].astype(bf16)
            short += jnp.where(src == 0, low[128:], 0.0)
        xp[c, 1664:1792, :] = short.astype(bf16)
        a, b = pair_slots(xp.at[c], 1920)
        slots[2 * c] = a
        slots[2 * c + 1] = b

    left, right = gather_slots((256, 384), 0), gather_slots((256, 384), 192)

    def rows_of(lo, rows):
        return jnp.concatenate([first[0, lo : lo + rows, :], first[1, lo : lo + rows, :]], axis=1)

    held = (h0, h1, h2, h3)
    spans = [(0, 384), (384, 384), (768, 96)]

    def direct(i, r):
        at = pl.ds(*spans[i])
        return copy(r, h0.at[at], held[r].at[at], gat_s.at[4 * i + r - 1], gat_r.at[4 * i + r - 1])

    def relay(i, r):
        row, rows = spans[i]
        at = pl.ds(row, rows // 2) if r == 1 else pl.ds(row + rows // 2, rows // 2)
        sem = 4 * i + 1 + r
        return copy(3 - r, held[r].at[at], h3.at[at], gat_s.at[sem], gat_r.at[sem])

    def conv(block):
        n0 = 896 * block
        for c in range(2):
            pre = conv_block((slots.at[2 * c], slots.at[2 * c + 1]), wt.at[2 * c : 2 * c + 2], y_ref, t_ref, 0, n0, 896)
            pre = pre + bias[c]
            pre_ref[c, n0 : n0 + 896, :] = pre
            center = xp[c, 64 + n0 : 64 + n0 + 896, :].astype(f32)
            first[c, n0 : n0 + 896, :] = (center + pre * gelu_parts(pre)).astype(bf16)

    def pack(row, lo, rows):
        h0[row : row + rows, :] = (mm(rows_of(lo, rows), left) + mm(rows_of(lo + rows, rows), right)).astype(bf16)

    conv(0)
    pack(0, 0, 384)
    for r in (1, 2):
        direct(0, r).start()
    conv(1)
    pack(384, 768, 384)
    pack(768, SBASE, 96)
    for i in (1, 2):
        for r in (1, 2):
            direct(i, r).start()
    for i in range(3):
        for r in (1, 2):
            direct(i, r).wait()
            relay(i, r).start()
    for i in range(3):
        for r in (1, 2):
            relay(i, r).wait()

    def project(row, rows, half):
        row0 = 64 * (1 - half)
        total = bias_qkv + jnp.zeros((rows, 768), f32)
        for r in range(4):
            total += mm(held[r][row : row + rows, 128 * half : 128 * half + 256], wz[r, row0 : row0 + 256, :])
        return total.astype(bf16)

    for half in range(2):
        qkv[384 * half : 384 * half + 384, :] = project(0, 384, half)
        qkv[768 + 384 * half : 1152 + 384 * half, :] = project(384, 384, half)
        qkv[SLOTS + 96 * half : SLOTS + 96 * half + 96, :] = project(768, 96, half)
    qkv[SLOTS + SROWS : TROWS, :] = jnp.zeros((TROWS - SLOTS - SROWS, 768), bf16)
    vt[...] = qkv[:, 512:704].astype(f32).T.astype(bf16)

    outs = (m0, o1, o2, o3)
    lse_ref[...] = jnp.zeros_like(lse_ref)
    sent = []
    for h in range(3):
        cols = slice(64 * h, 64 * h + 64)

        def attend(q0, queries, key0, keys, masked):
            query = (qkv[q0 : q0 + queries, 0:256][:, cols].astype(f32) * 0.125).astype(bf16)
            key = qkv[key0 : key0 + keys, 256:512][:, cols]
            scores = mm_nt(key, query)
            if masked:
                slot = lax.broadcasted_iota(jnp.int32, scores.shape, 0)
                scores = jnp.where(slot < SHORT, scores, neg_large)
            top = jnp.max(scores, axis=0, keepdims=True)
            weights = jnp.exp(scores - top)
            total = jnp.sum(weights, axis=0, keepdims=True)
            out = mm(vt[cols, key0 : key0 + keys], weights.astype(bf16))
            ot[cols, q0 : q0 + queries] = out / total
            lse_ref[h : h + 1, q0 : q0 + queries] = top + jnp.log(total)

        for q0 in range(0, SLOTS, QF):
            attend(q0, QF, 0, SLOTS, False)
        attend(SLOTS, 256, SLOTS, 128, True)
        for r in (3, 1, 2, 0):
            src = pl.multiple_of(FR * xor2(me, r), 128)
            outs[r][cols, 0:FR] = ot[cols, pl.ds(src, FR)].astype(bf16)
            outs[r][cols, FR:640] = ot[cols, SLOTS:TROWS].astype(bf16)
            if r:
                at = pl.ds(64 * h, 64)
                sem = 3 * h + r - 1
                c = copy(r, outs[r].at[at], (m1, m2, m3)[r - 1].at[at], mix_s.at[sem], mix_r.at[sem])
                c.start()
                sent.append(c)

    start = pl.multiple_of(FR * (me // 2), 128)
    lane0 = pl.multiple_of(128 * (me % 2), 128)
    r_i, c_i = iota2((256, 768))
    own = jnp.zeros((FR, 768), f32)
    extra0 = jnp.zeros((96, 768), f32)
    extra1 = jnp.zeros((96, 768), f32)
    for r in range(4):
        base = 192 * xor2(me, r)
        inside = (c_i >= base) & (c_i < base + 192)
        sel0 = ((c_i - base == r_i) & inside).astype(f32).astype(bf16)
        sel1 = ((c_i - base == r_i - 64) & inside).astype(f32).astype(bf16)
        own += mm(held[r][pl.ds(start, FR), pl.ds(lane0, 256)], jnp.where(me % 2 == 0, sel0, sel1))
        extra0 += mm(held[r][768:864, 0:256], sel0)
        extra1 += mm(held[r][768:864, 128:384], sel1)
    rows_ref[0:FR, :] = own.astype(bf16)
    rows_ref[FR : FR + 96, :] = extra0.astype(bf16)
    rows_ref[FR + 96 : FR + 192, :] = extra1.astype(bf16)
    for c in sent:
        c.wait()


def front_sync(chunks, kernel, vec, wq, wk, wv):
    sds = jax.ShapeDtypeStruct
    sem = pltpu.SemaphoreType.DMA
    room = lambda *shape: pltpu.VMEM(shape, bf16)
    return pl.pallas_call(
        front_sync_kernel,
        in_specs=[vmem()] * 4 + [pl.BlockSpec(memory_space=pl.ANY)] + [vmem()] * 4,
        out_specs=[vmem()] * 16,
        out_shape=[sds((4, 512, 1024), bf16), sds((2, TROWS, 128), f32), sds((2, 1936, 128), bf16)]
        + [sds((864, 384), bf16)] * 4
        + [sds((TROWS, 768), bf16), sds((CH, TROWS), f32), sds((8, TROWS), f32), sds((576, 768), bf16)]
        + [sds((768, 768), bf16)]
        + [sds((CH, 640), bf16)] * 4,
        scratch_shapes=[
            room(4, 48, 48, 128),
            sem,
            room(4, 512, 1024),
            pltpu.VMEM((48 * 128, 128), f32),
            pltpu.VMEM((1024, 128), f32),
            room(3, 256, 384),
            room(4, 1920, 128),
            pltpu.VMEM((912, 1024), f32),
            pltpu.VMEM((904, 128), f32),
            room(2, TROWS, 128),
            room(4, 320, 768),
            room(CH, TROWS),
        ]
        + [room(CH, 640)] * 3
        + [sem((3,)), sem((3,)), sem((12,)), sem((12,)), sem((9,)), sem((9,))],
        compiler_params=params(collective_id=3, has_side_effects=True),
        cost_estimate=cost(65),
        name="front_sync",
    )(*chunks, jnp.transpose(kernel, (1, 2, 3, 0)), vec, wq, wk, wv)


def attn_sync_kernel(
    qkv_ref, ot_ref, lse_ref, d0, d1, d2, d3, gst, w_ref, h0, h1, h2, h3,
    nl, gd, ul_hbm, gu_hbm, m0, m1, m2, m3, gac, sums,
    a1_out, a2_out, b_out, g_out, qsums,
    ring, load_s, dot_, do_, kt, delta, dqt, dk, dv, dqkv, keep1, send1, got1, keep2, send2, got2,
    bkeep, bsend, bgot, ra, rd, g0, g1, g2, g3, rg, core_s, core_r, wide_s, wide_r,
):
    n, me = lax.axis_index("narrow"), lax.axis_index("wide")
    core = n % 2
    other = n + 1 - 2 * core
    MESH = pl.DeviceIdType.MESH

    barrier = pltpu.get_barrier_semaphore()
    peers = [(n, xor2(me, r)) for r in range(1, 4)] + [(other, me)]
    for peer in peers:
        pl.semaphore_signal(barrier, inc=1, device_id=peer, device_id_type=MESH)

    def load(i):
        if i < 4:
            j = 2 * (1 - core) + i if i < 2 else 2 * core + i - 2
            src = gu_hbm.at[:, pl.ds(pl.multiple_of(768 * j, 128), 768)]
        else:
            src = ul_hbm.at[:, 768 * (i - 4) : 768 * (i - 3)]
        return pltpu.make_async_copy(src, ring.at[i % 2], load_s.at[i])

    load(0).start()
    load(1).start()
    pl.semaphore_wait(barrier, 4)

    def to_wide(i, r, src, dst):
        return pltpu.make_async_remote_copy(
            src_ref=src, dst_ref=dst, send_sem=wide_s.at[i], recv_sem=wide_r.at[i],
            device_id=(n, xor2(me, r)), device_id_type=MESH,
        )

    def to_core(i, src, dst):
        return pltpu.make_async_remote_copy(
            src_ref=src, dst_ref=dst, send_sem=core_s.at[i], recv_sem=core_r.at[i],
            device_id=(other, me), device_id_type=MESH,
        )

    send_d = [to_wide(r - 1, r, (d1, d2, d3)[r - 1], rd.at[r - 1]) for r in (3, 1, 2)]
    for c in send_d:
        c.start()

    core1, core2, coreb = to_core(0, send1, got1), to_core(1, send2, got2), to_core(2, bsend, bgot)
    for i in range(4):
        load(i).wait()
        up = tn(nl[...], ring[i % 2]).astype(bf16)
        to = send1 if i < 2 else keep1
        row = 192 * (i % 2)
        for e in range(4):
            to[xor2(me, e), row : row + 192, :] = up[192 * e : 192 * e + 192]
        load(i + 2).start()
        if i == 1:
            core1.start()
    extra = jnp.concatenate([sums[...], jnp.zeros((48, 768), f32)], axis=0).astype(bf16)
    for j in range(4):
        load(4 + j).wait()
        down = tn(ring[j % 2], gd[...]).astype(bf16)
        rel = xor2(me, j)
        put(core == 0, keep2, send2, rel, 0, down[0:512])
        put(core == 1, keep2, send2, rel, 0, down[512:768])
        if j < 2:
            load(6 + j).start()
    for r, m in enumerate((m0, m1, m2, m3)):
        put(core == 1, keep2, send2, r, 256, mm(m[...], gac[...]).astype(bf16))
        put(core == 1, keep2, send2, r, 448, extra)
    core2.start()
    core1.wait()
    for r in range(4):
        keep1[r] = (keep1[r].astype(f32) + got1[r].astype(f32)).astype(bf16)
    send_a = [to_wide(2 + r, r, keep1.at[r], ra.at[r - 1]) for r in (3, 1, 2)]
    for c in send_d:
        c.wait()
    for c in send_a:
        c.start()

    short = d0[:, FR : FR + 256].astype(f32)
    dot_[:, pl.ds(pl.multiple_of(FR * me, 128), FR)] = d0[:, 0:FR]
    for r in range(1, 4):
        dot_[:, pl.ds(pl.multiple_of(FR * xor2(me, r), 128), FR)] = rd[r - 1, :, 0:FR]
        short += rd[r - 1, :, FR : FR + 256].astype(f32)
    dot_[:, SLOTS:TROWS] = short.astype(bf16)
    whole = dot_[...].astype(f32)
    do_[...] = whole.T.astype(bf16)
    prod = whole * ot_ref[...]
    for h in range(3):
        delta[h : h + 1, :] = jnp.sum(prod[64 * h : 64 * h + 64], axis=0, keepdims=True)
    kt[...] = qkv_ref[:, 256:448].astype(f32).T.astype(bf16)
    keep_k, keep_v = [], []
    for h in range(3):
        cols = slice(64 * h, 64 * h + 64)
        dk[...] = jnp.zeros_like(dk)
        dv[...] = jnp.zeros_like(dv)

        def step(q0, queries, key0, keys, masked):
            at_q = pl.ds(q0, queries)
            query = qkv_ref[at_q, 0:256][:, cols]
            scaled = (query.astype(f32) * 0.125).astype(bf16)
            grad = do_[at_q, :][:, cols]
            grad_t = dot_[cols, at_q]
            lse = lse_ref[h : h + 1, at_q]
            dl = delta[h : h + 1, at_q]
            grad_q = jnp.zeros((64, queries), f32)
            piece = min(keys, KB)
            for at in range(key0, key0 + keys, piece):
                key = qkv_ref[at : at + piece, 256:512][:, cols]
                val = qkv_ref[at : at + piece, 512:768][:, cols]
                probs = jnp.exp(mm_nt(key, scaled) - lse)
                if masked:
                    slot = lax.broadcasted_iota(jnp.int32, probs.shape, 0)
                    probs = jnp.where(slot < SHORT, probs, 0.0)
                grad_p = mm(val, grad_t)
                grad_s = (probs * (grad_p - dl)).astype(bf16)
                dv[at : at + piece, :] += mm(probs.astype(bf16), grad)
                dk[at : at + piece, :] += mm(grad_s, query)
                grad_q += mm(kt[cols, at : at + piece], grad_s)
            dqt[cols, at_q] = grad_q * 0.125

        for q0 in range(0, SLOTS, QB):
            step(q0, QB, 0, SLOTS, False)
        step(SLOTS, 256, SLOTS, 128, True)
        keep_k.append((dk[...] * 0.125).astype(bf16))
        keep_v.append(dv[...].astype(bf16))
    zeros = jnp.zeros((TROWS, 64), bf16)
    dqkv[:, 0:192] = dqt[...].T.astype(bf16)
    dqkv[:, 192:256] = zeros
    dqkv[:, 256:512] = jnp.concatenate(keep_k + [zeros], axis=1)
    dqkv[:, 512:768] = jnp.concatenate(keep_v + [zeros], axis=1)

    parts = (g0, g1, g2, g3)
    lanes = pl.multiple_of(FR * me, 128)
    near, far = slice(0, 896), slice(896, TROWS)

    def project(r):
        rows = pl.ds(pl.multiple_of(192 * xor2(me, r), 64), 192)
        part = mm_nt(w_ref[rows, :], dqkv[...])
        parts[r][...] = part.astype(bf16)
        own = gst[rows, 0:FR].astype(f32)
        parts[r][:, pl.ds(lanes, FR)] = (parts[r][:, pl.ds(lanes, FR)].astype(f32) + own).astype(bf16)
        parts[r][:, SLOTS:TROWS] = (part[:, SLOTS:TROWS] + gst[rows, FR : FR + 256].astype(f32)).astype(bf16)

    def hop(i, r, src, half):
        return to_wide(6 + i, r, src.at[:, half], rg.at[i])

    first = [hop(0, 1, g3, near), hop(1, 2, g3, far), hop(2, 1, g1, near), hop(3, 2, g2, far)]
    second = [hop(4, 2, g2, near), hop(5, 1, g1, far)]
    project(3)
    first[0].start()
    first[1].start()
    project(1)
    first[2].start()
    project(2)
    first[3].start()
    project(0)
    qsums[...] = jnp.sum(dqkv[...].astype(f32), axis=0, keepdims=True)

    def join(part, half, i):
        part[:, half] = (part[:, half].astype(f32) + rg[i].astype(f32)).astype(bf16)

    def chunk_grad(chunk, r):
        turned = chunk[...].astype(f32).T.astype(bf16)
        value = (
            mm(turned[0:192, 0:384], dqkv[0:384, :])
            + mm(turned[192:384, 0:384], dqkv[384:768, :])
            + mm(turned[0:192, 384:768], dqkv[768:1152, :])
            + mm(turned[192:384, 384:768], dqkv[1152:1536, :])
            + mm(turned[0:192, 768:864], dqkv[SLOTS : SLOTS + 96, :])
            + mm(turned[192:384, 768:864], dqkv[SLOTS + 96 : SLOTS + 192, :])
        ).astype(bf16)
        put(core == 0, bkeep, bsend, r, 0, value[0:96])
        put(core == 1, bkeep, bsend, r, 0, value[96:192])

    chunk_grad(h0, 0)
    chunk_grad(h1, 1)
    for c in send_a:
        c.wait()
    a1_out[...] = (keep1[0].astype(f32) + ra[0].astype(f32) + ra[1].astype(f32) + ra[2].astype(f32)).astype(bf16)
    first[0].wait()
    join(g2, near, 0)
    second[0].start()
    first[1].wait()
    join(g1, far, 1)
    second[1].start()
    chunk_grad(h2, 2)
    chunk_grad(h3, 3)
    coreb.start()
    core2.wait()
    for r in range(4):
        a2_out[r] = (keep2[r].astype(f32) + got2[r].astype(f32)).astype(bf16)
    first[2].wait()
    first[3].wait()
    coreb.wait()
    for r in range(4):
        b_out[r] = (bkeep[r].astype(f32) + bgot[r].astype(f32)).astype(bf16)
    second[0].wait()
    g_out[:, near] = g0[:, near].astype(f32) + rg[2].astype(f32) + rg[4].astype(f32)
    second[1].wait()
    g_out[:, far] = g0[:, far].astype(f32) + rg[3].astype(f32) + rg[5].astype(f32)


def attn_sync(qkv, ot, lse, dparts, gst, wqkv, first, nl, gd, ul, gu, mix, gac, sums):
    sds = jax.ShapeDtypeStruct
    hbm = pl.BlockSpec(memory_space=pl.ANY)
    sem = pltpu.SemaphoreType.DMA
    room = lambda *shape: pltpu.VMEM(shape, bf16)
    return pl.pallas_call(
        attn_sync_kernel,
        in_specs=[vmem()] * 15 + [hbm] * 2 + [vmem()] * 6,
        out_specs=[vmem()] * 5,
        out_shape=[
            sds((384, 768), bf16), sds((4, 512, 768), bf16), sds((4, 96, 768), bf16), sds((CH, TROWS), f32),
            sds((1, 768), f32),
        ],
        scratch_shapes=[
            room(2, 768, 768),
            sem((8,)),
            room(CH, TROWS),
            room(TROWS, CH),
            room(CH, TROWS),
            pltpu.VMEM((8, TROWS), f32),
            pltpu.VMEM((CH, TROWS), f32),
            pltpu.VMEM((TROWS, 64), f32),
            pltpu.VMEM((TROWS, 64), f32),
            room(TROWS, 768),
        ]
        + [room(4, 384, 768)] * 3
        + [room(4, 512, 768)] * 3
        + [room(4, 96, 768)] * 3
        + [room(3, 384, 768), room(3, CH, 640)]
        + [room(CH, TROWS)] * 4
        + [room(6, CH, 896), sem((3,)), sem((3,)), sem((12,)), sem((12,))],
        compiler_params=params(collective_id=2, has_side_effects=True),
        cost_estimate=cost(90),
        name="attn_sync",
    )(qkv, ot, lse, *dparts, gst, wqkv, *first, nl, gd, ul, gu, *mix, gac, sums)


def wgrad_pair(pair, me, gsum, pre_ref, x_ref, sums_ref, half, gf, g_ref, gp, p0, p1, bb, g2, xt):
    at = pl.ds(pl.multiple_of(96 * pair, 32), 96)
    total = gsum[at, :]
    pad = jnp.zeros((16, TROWS), f32)
    rows = jnp.concatenate([total[0:48], pad, total[48:96], pad], axis=0)
    gf[0:SLOTS, :] = rows[:, 0:SLOTS].T
    gf[SLOTS:SBASE, :] = jnp.zeros((SBASE - SLOTS, 128), f32)
    gf[SBASE:TROWS, :] = rows[:, SLOTS:TROWS].T[0 : TROWS - SBASE]
    g_ref[0:64, :] = jnp.zeros((64, 128), bf16)
    g_ref[1856:1936, :] = jnp.zeros((80, 128), bf16)
    gp[0:16, :] = jnp.zeros((16, 128), f32)
    pre = pre_ref[pair]
    slope = gelu_parts(pre) + pre * density(pre)
    wide = (gf[...] * slope).astype(bf16).astype(f32)
    bias_sum = jnp.sum(wide, axis=0, keepdims=True)
    row = lax.broadcasted_iota(jnp.int32, (TROWS, 128), 0)
    wide = jnp.where(row < SBASE + UNIQUE, wide, 0.0)
    gp[16 : 16 + TROWS, :] = wide
    g_ref[64 : 64 + TROWS, :] = wide.astype(bf16)
    extra = jnp.concatenate(
        [sums_ref[...], jnp.concatenate([bias_sum, jnp.zeros((1, 640), f32)], axis=1), jnp.zeros((14, 768), f32)], axis=0
    )
    for r in range(4):
        half[r, 192:208, :] = extra.astype(bf16)

    lane = lax.broadcasted_iota(jnp.int32, (TROWS, 128), 1)
    here, before = gp[16 : 16 + TROWS, :], gp[15 : 15 + TROWS, :]
    a, b = pair_slots(x_ref.at[pair], 1920)
    p0[...] = a
    p1[...] = b
    pack0, pack1 = gather_slots((256, 384), 0), gather_slots((256, 384), 192)
    for j in range(2):
        bb[0:16, :] = jnp.zeros((16, 128), f32)
        if j == 0:
            bb[16 : 16 + TROWS, :] = jnp.where(lane < 64, here, pltpu.roll(before, 64, 1))
        else:
            bb[16 : 16 + TROWS, :] = jnp.where(lane < 64, pltpu.roll(here, 64, 1), before)
        for p in range(8):
            g2[:, 128 * p : 128 * p + 128] = bb[16 - 2 * p : 16 - 2 * p + TROWS, :].astype(bf16)
        slots = (p0, p1)[j]
        for q in range(4):
            xt[128 * q : 128 * q + 128, :] = slots[32 * q : 32 * q + TROWS, :].astype(f32).T.astype(bf16)
        for side in range(2):
            base = 512 * side
            left = mm(xt[...], g2[:, base : base + 256]).astype(bf16)
            right = mm(xt[...], g2[:, base + 256 : base + 512]).astype(bf16)
            packed = (mm(left, pack0) + mm(right, pack1)).astype(bf16)
            for m in range(4):
                tile = jnp.concatenate([packed[128 * m : 128 * m + 48], packed[128 * m + 64 : 128 * m + 112]], axis=0)
                half[xor2(me, m), 96 * j : 96 * j + 96, 384 * side : 384 * side + 384] = tile


def conv_sync_kernel(
    gsum, pre_ref, x_ref, sums_ref, wd_ref, xu, a_ref, b_ref,
    fu, fa, fb, fc, ou, oa, ob, oc, f0, f1, f2, f3,
    gp, p0, p1, bb, g2, xt, y_ref, t_ref, gf, g, fg, s1, s2, s3,
    csend, ckeep, cgot, ra, rb, rc, xa, xb, eu, ea, eb, ec, yu, ya, yb, yc,
    ss, so, re, rr, sc, rcv, wide_s, wide_r, core_s, core_r,
):
    n, me = lax.axis_index("narrow"), lax.axis_index("wide")
    z, core = n // 2, n % 2
    MESH = pl.DeviceIdType.MESH

    def copy(src, dst, send, recv, device):
        return pltpu.make_async_remote_copy(
            src_ref=src, dst_ref=dst, send_sem=send, recv_sem=recv, device_id=device, device_id_type=MESH
        )

    def along(zz, cc=core):
        return (2 * zz + cc, me)

    barrier = pltpu.get_barrier_semaphore()

    def greet(device):
        pl.semaphore_signal(barrier, inc=1, device_id=device, device_id_type=MESH)

    for r in range(1, 4):
        greet((n, xor2(me, r)))
    greet(along(z, 1 - core))

    @pl.when(z > 0)
    def _():
        greet(along(z - 1))

    @pl.when(z < 3)
    def _():
        greet(along(z + 1))

    pl.semaphore_wait(barrier, 4 + jnp.minimum(z, 1) + jnp.minimum(3 - z, 1))

    def over_wide(which, r, src, dst):
        return copy(src, dst, wide_s.at[3 * which + r - 1], wide_r.at[3 * which + r - 1], (n, xor2(me, r)))

    send_b = [over_wide(0, r, b_ref.at[r], rb.at[r - 1]) for r in (3, 1, 2)]
    send_a = [over_wide(1, r, a_ref.at[r], ra.at[r - 1]) for r in (3, 1, 2)]
    for c in send_b + send_a:
        c.start()

    pieces = [(3, None, 96 * r, 96) for r in range(4)]
    pieces += [(0, r, 0, 96) for r in range(4)] + [(1, None, 128 * r, 128) for r in range(4)]
    for r in range(4):
        pieces += [(2, r, 0, 112), (2, r, 112, 96)]
    count = len(pieces)
    set_u, set_b, set_a, set_c = range(0, 4), range(4, 8), range(8, 12), range(12, count)

    def views(refs):
        out = []
        for which, r, row, rows in pieces:
            ref = refs[which]
            out.append(ref.at[row : row + rows] if r is None else ref.at[r, row : row + rows])
        return out

    x, e, y, f, o = (views(refs) for refs in ((xb, xa, csend, xu), (eb, ea, ec, eu), (yb, ya, yc, yu), (fb, fa, fc, fu), (ob, oa, oc, ou)))

    def first(k, here):
        return k % 2 == (0 if here == 1 else 1)

    def swap(k):
        return copy(f[k], o[k], sc.at[k], rcv.at[k], along(z, 1 - core))

    def inward(k, here):
        return copy(x[k], e[k], ss.at[k], re.at[k], along(1 if here == 0 else 2))

    def across(k, here):
        src = y[k] if first(k, here) else f[k]
        return copy(src, src, ss.at[k], rr.at[k], along(3 - here))

    def outward(k, here):
        return copy(f[k], f[k], so.at[k], rr.at[k], along(0 if here == 1 else 3))

    def at_ends(do):
        pl.when(z == 0)(lambda: do(0))
        pl.when(z == 3)(lambda: do(3))

    def at_inner(do):
        pl.when(z == 1)(lambda: do(1))
        pl.when(z == 2)(lambda: do(2))

    def begin(ks):
        def do(here):
            for k in ks:
                inward(k, here).start()

        at_ends(do)

    def meet(ks, here):
        for k in ks:
            inward(k, here).wait_recv()
            if first(k, here):
                y[k][...] = (x[k][...].astype(f32) + e[k][...].astype(f32)).astype(bf16)
                across(k, here).start()

    def close(ks, here):
        for k in ks:
            if not first(k, here):
                across(k, here).wait_recv()
                f[k][...] = (x[k][...].astype(f32) + e[k][...].astype(f32) + y[k][...].astype(f32)).astype(bf16)
                across(k, here).start()
                outward(k, here).start()
                swap(k).start()

    def pass_on(ks, here):
        for k in ks:
            if first(k, here):
                across(k, here).wait_recv()
                outward(k, here).start()
                swap(k).start()

    def wgrad(pair, half, slot):
        wgrad_pair(
            pair, me, gsum, pre_ref, x_ref, sums_ref, half, gf.at[slot], g.at[slot],
            gp, p0, p1, bb, g2, xt,
        )

    def dgrad(pair, slot):
        a, b = pair_slots(g.at[slot], 1920)
        p0[...] = a
        p1[...] = b
        value = conv_block((p0, p1), wd_ref.at[pl.ds(2 * pair, 2)], y_ref, t_ref, 1) + gf[slot]
        fg[pair] = value.astype(bf16)

    begin(set_u)
    wgrad(1 - core, csend, 0)
    to_core = copy(csend, cgot, core_s, core_r, along(z, 1 - core))
    to_core.start()
    for c in send_b:
        c.wait()
    xb[0] = b_ref[0]
    for r in range(1, 4):
        xb[r] = rb[r - 1]
    begin(set_b)
    at_inner(lambda here: meet(set_u, here))

    wgrad(core, ckeep, 1)
    to_core.wait()
    for r in range(4):
        ckeep[r] = (ckeep[r].astype(f32) + cgot[r].astype(f32)).astype(bf16)
    send_c = [over_wide(2, r, ckeep.at[r], rc.at[r - 1]) for r in (3, 1, 2)]
    for c in send_c:
        c.start()

    def inner_b(here):
        close(set_u, here)
        meet(set_b, here)

    at_inner(inner_b)
    dgrad(1 - core, 0)

    def inner_c(here):
        pass_on(set_u, here)
        close(set_b, here)

    at_inner(inner_c)
    for c in send_a:
        c.wait()
    xa[...] = (a_ref[0].astype(f32) + ra[0].astype(f32) + ra[1].astype(f32) + ra[2].astype(f32)).astype(bf16)
    begin(set_a)
    dgrad(core, 1)
    pack0, pack1 = gather_slots((256, 384), 0), gather_slots((256, 384), 192)

    def rows_of(lo, rows):
        return jnp.concatenate([fg[0, lo : lo + rows, :], fg[1, lo : lo + rows, :]], axis=1)

    outs = (f0, s1, s2, s3)
    for d in range(4):
        low = jnp.concatenate([rows_of(FR * d + 256, 128), rows_of(SBASE, 128)], axis=0)
        chunk = (mm(rows_of(FR * d, 256), pack0) + mm(low, pack1)).astype(bf16)
        for r in range(4):

            @pl.when(xor2(me, d) == r)
            def _():
                outs[r][...] = chunk

    for c in send_c:
        c.wait()
    csend[0] = ckeep[0]
    for r in range(1, 4):
        csend[r] = rc[r - 1]
    begin(set_c)
    send_f = [over_wide(3, r, (s1, s2, s3)[r - 1], (f1, f2, f3)[r - 1]) for r in (3, 1, 2)]
    for c in send_f:
        c.start()

    def inner(here):
        pass_on(set_b, here)
        rest = list(set_a) + list(set_c)
        for i in range(0, len(rest), 2):
            pair = rest[i : i + 2]
            meet(pair, here)
            close(pair, here)
            if i:
                pass_on(rest[i - 2 : i], here)
        pass_on(rest[-2:], here)
        for k in range(count):
            across(k, here).wait_send()
            outward(k, here).wait_send()
            swap(k).wait()

    def outer(here):
        for k in range(count):
            copy(f[k], f[k], so.at[k], rr.at[k], along(z)).wait_recv()
            swap(k).start()
        for k in range(count):
            inward(k, here).wait_send()
            swap(k).wait()

    at_inner(inner)
    at_ends(outer)
    for c in send_f:
        c.wait()


def conv_sync(gsum, pre, xp, sums, wd, up_sum, ffn_halves, qkv_halves):
    sds = jax.ShapeDtypeStruct
    shapes = [(384, 768), (512, 768), (4, 96, 768), (4, 208, 768)]
    sem = pltpu.SemaphoreType.DMA
    return pl.pallas_call(
        conv_sync_kernel,
        in_specs=[vmem()] * 8,
        out_specs=[vmem()] * 12,
        out_shape=[sds(v, bf16) for v in shapes * 2] + [sds((256, 384), bf16)] * 4,
        scratch_shapes=[
            pltpu.VMEM((16 + TROWS, 128), f32),
            pltpu.VMEM((1920, 128), bf16),
            pltpu.VMEM((1920, 128), bf16),
            pltpu.VMEM((16 + TROWS, 128), f32),
            pltpu.VMEM((TROWS, 1024), bf16),
            pltpu.VMEM((512, TROWS), bf16),
            pltpu.VMEM((CB + 16, 1024), f32),
            pltpu.VMEM((CB + 8, 128), f32),
            pltpu.VMEM((2, TROWS, 128), f32),
            pltpu.VMEM((2, 1936, 128), bf16),
            pltpu.VMEM((2, TROWS, 128), bf16),
        ]
        + [pltpu.VMEM((256, 384), bf16)] * 3
        + [pltpu.VMEM((4, 208, 768), bf16)] * 3
        + [pltpu.VMEM((3, 512, 768), bf16), pltpu.VMEM((3, 96, 768), bf16), pltpu.VMEM((3, 208, 768), bf16)]
        + [pltpu.VMEM((512, 768), bf16), pltpu.VMEM((4, 96, 768), bf16)]
        + [pltpu.VMEM(v, bf16) for v in shapes * 2]
        + [sem((20,))] * 6
        + [sem((12,)), sem((12,)), sem, sem],
        compiler_params=params(collective_id=1, has_side_effects=True),
        cost_estimate=cost(100),
        name="conv_sync",
    )(gsum, pre, xp, sums, wd, up_sum, ffn_halves, qkv_halves)


def unpack_frames_kernel(s_ref, c0, c1, c2, c3, o_ref):
    me, li = s_ref[0], s_ref[1]
    r_i, c_i = iota2((256, 768))
    top = jnp.zeros((256, 768), f32)
    low = jnp.zeros((256, 768), f32)
    for r, chunk in enumerate((c0, c1, c2, c3)):
        base = 192 * (me ^ r)
        inside = (c_i >= base) & (c_i < base + 192)
        top += mm(chunk[:, 0:256], ((c_i - base == r_i) & inside).astype(f32).astype(bf16))
        low += mm(chunk[:, 128:384], ((c_i - base == r_i - 64) & inside).astype(f32).astype(bf16))
    o_ref[li, 0:256, :] = top.astype(bf16)
    o_ref[li, 256:384, :] = low[0:128].astype(bf16)
    slot = me * FR + lax.broadcasted_iota(jnp.int32, (128, 768), 0)
    o_ref[1 - li, 0:128, :] = jnp.where(slot < SHORT, low[128:], 0.0).astype(bf16)
    o_ref[1 - li, 128:384, :] = jnp.zeros((256, 768), bf16)


def unpack_frames(scal, chunks):
    return pl.pallas_call(
        unpack_frames_kernel,
        in_specs=[smem()] + [vmem()] * 4,
        out_specs=vmem(),
        out_shape=jax.ShapeDtypeStruct((2, FR, 768), bf16),
        compiler_params=params(),
        cost_estimate=cost(3),
        name="unpack_frames",
    )(scal, *chunks)


def kernel_out_kernel(s_ref, own_ref, other_ref, o_ref, small_ref):
    core = s_ref[2]
    for g in range(4):
        half, row = g >> 1, 96 * (g & 1)
        x = jnp.where(half == core, own_ref[0, row : row + 96], other_ref[0, row : row + 96]).astype(f32)
        for k2 in range(2):
            for b in range(16):
                o_ref[16 * k2 + b, g] = x[48 * k2 : 48 * k2 + 48, 48 * b : 48 * b + 48]

    @pl.when(pl.program_id(0) == s_ref[0])
    def _():
        for half in range(2):
            small_ref[half] = jnp.where(half == core, own_ref[0, 192:208], other_ref[0, 192:208])


def kernel_out(scal, own, other):
    return pl.pallas_call(
        kernel_out_kernel,
        grid_spec=pltpu.PrefetchScalarGridSpec(
            num_scalar_prefetch=1,
            grid=(4,),
            in_specs=[pl.BlockSpec((1, 208, 768), lambda i, s: (i ^ s[0], 0, 0))] * 2,
            out_specs=[
                pl.BlockSpec((32, 4, 48, 48), lambda i, s: (0, i, 0, 0)),
                pl.BlockSpec((2, 16, 768), lambda i, s: (0, 0, 0)),
            ],
        ),
        out_shape=[jax.ShapeDtypeStruct((32, 16, 48, 48), f32), jax.ShapeDtypeStruct((2, 16, 768), bf16)],
        compiler_params=params(),
        cost_estimate=cost(9),
        name="kernel_grad_out",
    )(scal, own, other)


def norm(v):
    center = v - jnp.mean(v, axis=-1, keepdims=True)
    scale = lax.rsqrt(jnp.mean(center * center, axis=-1, keepdims=True) + eps_norm)
    return center * scale, scale


def norm_back(e, n, scale):
    return (e - jnp.mean(e, axis=-1, keepdims=True) - n * jnp.mean(e * n, axis=-1, keepdims=True)) * scale


def ffn_kernel(
    s_ref, rows_ref, m0, m1, m2, m3, wo, wu_hbm, bu, wd_hbm, vecs, og,
    lo, ul_hbm, gu_hbm, nl, gd, gac, x0, x1, x2, x3, gst, sums,
    wu, wd, ul, gu, slope, v, gsc, mix, sems,
):
    me, li = s_ref[0], s_ref[1]
    const = FR + UNIQUE
    bo, g1, s1, bd, g2, s2 = (vecs[k : k + 1, :] for k in range(6))
    loads = [
        pltpu.make_async_copy(wu_hbm, wu, sems.at[0]),
        pltpu.make_async_copy(wd_hbm, wd, sems.at[1]),
    ]
    for load in loads:
        load.start()

    def total(x):
        return jnp.sum(x, axis=0, keepdims=True)

    for r, m in enumerate((m0, m1, m2, m3)):
        mix[pl.ds(pl.multiple_of(192 * (me ^ r), 64), 192), :] = m[...]
    out = tn(mix[...], wo[...])
    gsc[0:576, :] = rows_ref[...].astype(f32) + out[0:576] + bo
    last = gsc[const : const + 1, :]
    v[0:FR, :] = gsc[0:FR, :]
    v[FR : FR + 128, :] = jnp.where(me == 0, gsc[FR : FR + 128, :], last)
    mine = jnp.where(me == 0, 1.0, 0.0)
    keep_low = (lax.broadcasted_iota(jnp.int32, (64, 768), 0) < UNIQUE - 128).astype(f32) * mine
    v[FR + 128 : FR + 192, :] = jnp.where(keep_low > 0.5, gsc[FR + 128 : FR + 192, :], last)
    v[FR + 192 :, :] = jnp.broadcast_to(last, (192, 768))

    n1, scale1 = norm(v[...])
    v[...] = n1
    norm_one = n1 * g1 + s1
    low = norm_one.astype(bf16)
    nl[...] = low
    down = norm_one + bd
    stores = []
    loads[0].wait()
    for j in range(4):
        cols = slice(768 * j, 768 * j + 768)
        up = mm(low, wu[:, cols]) + bu[:, cols]
        cdf = gelu_parts(up)
        slope[:, cols] = cdf + up * density(up)
        act = (up * cdf).astype(bf16)
        ul[:, cols] = act
        stores.append(pltpu.make_async_copy(ul.at[:, cols], ul_hbm.at[:, cols], sems.at[2 + j]))
        stores[-1].start()
        if j == 0:
            loads[1].wait()
        down += mm(act, wd[cols, :])
    n2, scale2 = norm(down)
    result = (n2 * g2 + s2).astype(bf16)
    lo[li] = result[0:FR]
    lo[1 - li] = result[FR:]
    given = jnp.concatenate([og[li], og[1 - li]], axis=0).astype(f32)
    sums[8:9, :] = total(given * n2)
    sums[9:10, :] = total(given)
    sums[10:16, :] = jnp.zeros((6, 768), f32)
    grad_two = norm_back(given * g2, n2, scale2)
    grad_down = grad_two.astype(bf16)
    gd[...] = grad_down
    sums[7:8, :] = total(grad_down.astype(f32))
    grad_n = grad_two
    for j in range(4):
        cols = slice(768 * j, 768 * j + 768)
        grad_up = (mm_nt(grad_down, wd[cols, :]) * slope[:, cols]).astype(bf16)
        gu[:, cols] = grad_up
        stores.append(pltpu.make_async_copy(gu.at[:, cols], gu_hbm.at[:, cols], sems.at[6 + j]))
        stores[-1].start()
        sums[j : j + 1, :] = total(grad_up.astype(f32))
        grad_n += mm_nt(grad_up, wu[:, cols])
    n1 = v[...]
    sums[5:6, :] = total(grad_n * n1)
    sums[6:7, :] = total(grad_n)
    grad_one = norm_back(grad_n * g1, n1, scale1)
    grad_attn = grad_one.astype(bf16).astype(f32)
    sums[4:5, :] = total(grad_attn)

    at = lax.broadcasted_iota(jnp.int32, (64, 768), 0) == UNIQUE - 128

    def collapsed(g):
        upper = g[FR : FR + 128] * mine
        lower = g[FR + 128 : FR + 192] * keep_low
        rest = total(g[FR:]) - total(upper) - total(lower)
        return jnp.concatenate(
            [g[0:FR], upper, jnp.where(at, rest, lower), jnp.zeros((64, 768), f32)], axis=0
        )

    gac[...] = collapsed(grad_attn).astype(bf16)
    for r, out in enumerate((x0, x1, x2, x3)):
        at_r = pl.ds(pl.multiple_of(192 * (me ^ r), 64), 192)
        out[...] = mm_nt(wo[at_r, :], gac[...]).astype(bf16)
    gsc[...] = collapsed(grad_one)
    gst[...] = gsc[...].T.astype(bf16)
    for store in stores:
        store.wait()


def ffn(scal, rows, mix, wo, wu, bu, wd, vecs, og):
    sds = jax.ShapeDtypeStruct
    hbm = pl.BlockSpec(memory_space=pl.ANY)
    return pl.pallas_call(
        ffn_kernel,
        in_specs=[smem()] + [vmem()] * 6 + [hbm, vmem(), hbm, vmem(), vmem()],
        out_specs=[vmem(), hbm, hbm] + [vmem()] * 9,
        out_shape=[
            sds((2, FR, 768), bf16), sds((768, 3072), bf16), sds((768, 3072), bf16), sds((768, 768), bf16),
            sds((768, 768), bf16), sds((640, 768), bf16),
        ]
        + [sds((CH, 640), bf16)] * 4
        + [sds((768, 640), bf16), sds((16, 768), f32)],
        scratch_shapes=[
            pltpu.VMEM((768, 3072), bf16),
            pltpu.VMEM((3072, 768), bf16),
            pltpu.VMEM((768, 3072), bf16),
            pltpu.VMEM((768, 3072), bf16),
            pltpu.VMEM((768, 3072), f32),
            pltpu.VMEM((768, 768), f32),
            pltpu.VMEM((640, 768), f32),
            pltpu.VMEM((768, 640), bf16),
            pltpu.SemaphoreType.DMA((10,)),
        ],
        compiler_params=params(),
        cost_estimate=cost(28),
        name="ffn",
    )(scal, rows, *mix, wo, wu, bu, wd, vecs, og)


def tn(a, b):
    return lax.dot_general(a, b, (((0,), (0,)), ((), ())), preferred_element_type=f32)


def finish_kernel(s_ref, own1, other1, own2, other2, ownb, otherb, up, down, out, wq, wk, wv, small, a1, a2, b_ref):
    me, core = s_ref[0], s_ref[2]
    for buf, own, other in ((a1, own1, other1), (a2, own2, other2)):
        buf[core] = own[...]
        buf[1 - core] = other[...]
    b_ref[:, pl.ds(pl.multiple_of(96 * core, 32), 96), :] = ownb[...]
    b_ref[:, pl.ds(pl.multiple_of(96 - 96 * core, 32), 96), :] = otherb[...]
    for j in range(4):
        row = 192 * (j & 1)
        up[:, 768 * j : 768 * j + 768] = a1[j >> 1, row : row + 192, :].astype(f32)
    down[0:512, :] = a2[0].astype(f32)
    down[512:768, :] = a2[1, 0:256, :].astype(f32)
    out[...] = a2[1, 256:448, :].astype(f32)
    small[...] = a2[1, 448:464, :].astype(f32)
    r_i, c_i = iota2((256, 768))
    totals = [jnp.zeros((CH, 768), f32)] * 3
    for r in range(4):
        base = 192 * (me ^ r)
        hit = (c_i - base == r_i) & (r_i < 192)
        move = hit.astype(f32).astype(bf16)
        for k in range(3):
            totals[k] = totals[k] + mm(b_ref[r, :, 256 * k : 256 * k + 256], move)
    wq[...], wk[...], wv[...] = totals


def finish(scal, *parts):
    sds = jax.ShapeDtypeStruct
    return pl.pallas_call(
        finish_kernel,
        in_specs=[smem()] + [vmem()] * 6,
        out_specs=[vmem()] * 7,
        out_shape=[sds((CH, 3072), f32), sds((768, 768), f32)] + [sds((CH, 768), f32)] * 4 + [sds((16, 768), f32)],
        scratch_shapes=[
            pltpu.VMEM((2, 384, 768), bf16),
            pltpu.VMEM((2, 512, 768), bf16),
            pltpu.VMEM((4, CH, 768), bf16),
        ],
        compiler_params=params(),
        cost_estimate=cost(6),
        name="weight_grads_out",
    )(scal, *parts)


def on_device(
    frames_in, lengths, kernel, conv_bias, w_query, b_query, w_key, w_value, b_value, w_out, b_out,
    gain_one, shift_one, w_up, b_up, w_down, b_down, gain_two, shift_two, out_grad,
):
    me = lax.axis_index("wide").astype(jnp.int32)
    place_n = lax.axis_index("narrow").astype(jnp.int32)
    core, z = place_n & 1, place_n >> 1
    li = jnp.where(lengths[0] >= lengths[1], 0, 1).astype(jnp.int32)
    scal = jnp.stack([me, li, core, z])
    chunks = pack_frames(scal, frames_in)
    vec = jnp.concatenate([jnp.stack([conv_bias, b_query, b_value]), jnp.zeros((13, conv_bias.shape[0]), bf16)], axis=0)
    vecs = jnp.stack([b_out, gain_one, shift_one, b_down, gain_two, shift_two]).astype(f32)
    bu = b_up.astype(f32)[None]

    wd, pre, xp, h0, h1, h2, h3, qkv, mixed_t, lse, rows, wqkv, *mix = front_sync(
        chunks, kernel, vec, w_query, w_key, w_value
    )
    first = [h0, h1, h2, h3]
    layer_out, ul, gu, nl, gd, gac, x0, x1, x2, x3, gst, sums = ffn(
        scal, rows, mix, w_out, w_up, bu, w_down, vecs, out_grad
    )
    up_sum, ffn_halves, qkv_halves, gsum, qkv_sums = attn_sync(
        qkv, mixed_t, lse, [x0, x1, x2, x3], gst, wqkv, first, nl, gd, ul, gu, mix, gac, sums
    )
    own1, own2, ownb, ownc, other1, other2, otherb, otherc, *fchunks = conv_sync(
        gsum, pre, xp, qkv_sums, wd, up_sum, ffn_halves, qkv_halves
    )
    frames_grad = unpack_frames(scal, fchunks)
    up, down, out, wq, wk, wv, small = finish(scal, own1, other1, own2, other2, ownb, otherb)
    grad_kernel, tiny = kernel_out(scal, ownc, otherc)
    tiny = tiny.astype(f32)

    def mine(row):
        return lax.dynamic_slice_in_dim(small[row], me * CH, CH, axis=0)

    bias_grad = jnp.concatenate([tiny[0, 1, :128], tiny[1, 1, :128]]).reshape(4, 64)[:, :48].reshape(CH)
    grad_b_up = lax.dynamic_index_in_dim(small[:4], me, 0, keepdims=False)
    return (
        layer_out,
        frames_grad,
        grad_kernel,
        bias_grad,
        wq,
        tiny[0, 0, 0:192],
        wk,
        wv,
        tiny[0, 0, 512:704],
        out,
        mine(4),
        mine(5),
        mine(6),
        up,
        grad_b_up,
        down,
        mine(7),
        mine(8),
        mine(9),
    )


def with_halo(x, sides, width):
    for axis, dim in sides:
        count, length = (lax.axis_size(axis), x.shape[dim])
        up = [(i, (i + 1) % count) for i in range(count - 1)]
        down = [(j, i) for i, j in up]
        last = lax.slice_in_dim(x, length - width, length, axis=dim)
        initial = lax.slice_in_dim(x, 0, width, axis=dim)
        before = lax.ppermute(last, axis, up)
        after = lax.ppermute(initial, axis, down)
        x = jnp.concatenate([before, x, after], axis=dim)
    return x


def layer_norm(value, gain, shift):
    center = value - jnp.mean(value, axis=-1, keepdims=True)
    spread = jnp.mean(center * center, axis=-1, keepdims=True)
    return center * lax.rsqrt(spread + eps_norm) * gain + shift


def gelu_exact(value):
    return jax.nn.gelu(value, approximate=False)


def project(rows_in, weight):
    return jnp.einsum("cfd,de->cfe", rows_in, weight, preferred_element_type=jnp.float32)


def project_back(grad_in, weight):
    return jnp.einsum("cfe,de->cfd", grad_in, weight, preferred_element_type=jnp.float32)


def weight_grad(rows_in, grad_in):
    return jnp.einsum("cfd,cfe->de", rows_in, grad_in, preferred_element_type=jnp.float32)


def row_total(grad_in):
    return jnp.sum(grad_in.astype(jnp.float32), axis=(0, 1))


def head_view(rows_in):
    return rows_in.reshape(rows_in.shape[0], rows_in.shape[1], HEADS, rows_in.shape[2] // HEADS)


def conv_apply(padded, weight, frames):
    kernel_span, groups, inner_ch, outer_ch = weight.shape
    taps_weight = jnp.transpose(weight, (0, 2, 1, 3)).reshape(
        kernel_span, inner_ch, groups * outer_ch
    )
    result = lax.conv_general_dilated(
        padded,
        taps_weight,
        (1,),
        "VALID",
        dimension_numbers=("NWC", "WIO", "NWC"),
        feature_group_count=groups,
        preferred_element_type=jnp.float32,
    )
    return result[:, :frames, :]


def conv_weight_grad(padded, grad_in, kernel_shape):
    kernel_span, groups, inner_ch, outer_ch = kernel_shape
    result = lax.conv_general_dilated(
        padded,
        grad_in,
        (1,),
        "VALID",
        dimension_numbers=("CWN", "IWO", "NWC"),
        batch_group_count=groups,
        preferred_element_type=jnp.float32,
    )
    result = result[:, :kernel_span, :].reshape(inner_ch, kernel_span, groups, outer_ch)
    return jnp.transpose(result, (1, 2, 0, 3))


def key_valid_at(lengths, first_row, row_count):
    return (first_row + jnp.arange(row_count, dtype=jnp.int32))[None, :] < lengths[:, None]


def masked_scores(query_h, keys_h, valid_keys, score_scale):
    scores = (
        jnp.einsum("cqhd,ckhd->cqhk", query_h, keys_h, preferred_element_type=jnp.float32)
        * score_scale
    )
    return jnp.where(valid_keys[:, None, None, :], scores, neg_large)


def block_terms(query_h, grad_h, lse_rows, delta_rows, keys_h, values_h, valid_keys, score_scale):
    scores = masked_scores(query_h, keys_h, valid_keys, score_scale)
    probs = jnp.where(valid_keys[:, None, None, :], jnp.exp(scores - lse_rows[..., None]), 0.0)
    grad_probs = jnp.einsum("cqhd,ckhd->cqhk", grad_h, values_h, preferred_element_type=jnp.float32)
    grad_scores = (probs * (grad_probs - delta_rows[..., None])).astype(jnp.bfloat16)
    results = []
    results.append(
        jnp.einsum("cqhk,ckhd->cqhd", grad_scores, keys_h, preferred_element_type=jnp.float32)
        * score_scale
    )
    results.append(
        jnp.einsum("cqhk,cqhd->ckhd", grad_scores, query_h, preferred_element_type=jnp.float32)
        * score_scale
    )
    results.append(
        jnp.einsum(
            "cqhk,cqhd->ckhd",
            probs.astype(jnp.bfloat16),
            grad_h,
            preferred_element_type=jnp.float32,
        )
    )
    return tuple(results)


def on_device_any(
    frames_in,
    lengths,
    kernel,
    conv_bias,
    w_query,
    b_query,
    w_key,
    w_value,
    b_value,
    w_out,
    b_out,
    gain_one,
    shift_one,
    w_up,
    b_up,
    w_down,
    b_down,
    gain_two,
    shift_two,
    out_grad,
):
    clip_count, frames, width = frames_in.shape
    head_dim = width // HEADS
    score_scale = head_dim ** (-0.5)
    half_span = kernel.shape[0] // 2
    wide_size = lax.axis_size("wide")
    positions = lax.axis_index("wide") * frames + jnp.arange(frames, dtype=jnp.int32)
    frame_valid = positions[None, :] < lengths[:, None]
    masked = jnp.where(frame_valid[..., None], frames_in, jnp.zeros((), jnp.bfloat16))
    padded = with_halo(masked, (("wide", 1),), half_span)
    pre_act = conv_apply(padded, kernel, frames) + conv_bias.astype(jnp.float32)
    first_act, pull_first = jax.vjp(gelu_exact, pre_act)
    first_out = masked.astype(jnp.float32) + first_act
    first_low = first_out.astype(jnp.bfloat16)
    query_rows = (project(first_low, w_query) + b_query.astype(jnp.float32)).astype(jnp.bfloat16)
    key_rows = project(first_low, w_key).astype(jnp.bfloat16)
    value_rows = (project(first_low, w_value) + b_value.astype(jnp.float32)).astype(jnp.bfloat16)
    query_h = head_view(query_rows)
    per_step = max(1, min(wide_size, 512 // frames))
    while wide_size % per_step:
        per_step -= 1
    run_max = jnp.full((clip_count, frames, HEADS), neg_large, jnp.float32)
    run_acc = jnp.zeros((clip_count, frames, HEADS, head_dim), jnp.float32)
    keys_p = lax.all_gather(key_rows, "wide", axis=1, tiled=True)
    values_p = lax.all_gather(value_rows, "wide", axis=1, tiled=True)
    row_count = keys_p.shape[1]
    valid_keys = key_valid_at(lengths, jnp.int32(0), row_count)
    scores = masked_scores(query_h, head_view(keys_p), valid_keys, score_scale)
    new_max = jnp.maximum(run_max, jnp.max(scores, axis=-1))
    weights = jnp.where(valid_keys[:, None, None, :], jnp.exp(scores - new_max[..., None]), 0.0)
    factor = jnp.exp(run_max - new_max)
    run_sum = jnp.sum(weights, axis=-1)
    run_acc = run_acc * factor[..., None] + jnp.einsum(
        "cqhk,ckhd->cqhd",
        weights.astype(jnp.bfloat16),
        head_view(values_p),
        preferred_element_type=jnp.float32,
    )
    run_max, run_sum, run_acc = (new_max, run_sum, run_acc)
    lse_rows = run_max + jnp.log(run_sum)
    mixed_heads = run_acc / run_sum[..., None]
    mixed_low = mixed_heads.reshape(clip_count, frames, width).astype(jnp.bfloat16)
    attn_out = project(mixed_low, w_out) + b_out.astype(jnp.float32)
    sum_one = first_out + attn_out
    norm_one, pull_one = jax.vjp(
        layer_norm, sum_one, gain_one.astype(jnp.float32), shift_one.astype(jnp.float32)
    )
    norm_low = norm_one.astype(jnp.bfloat16)
    up_pre = project(norm_low, w_up) + b_up.astype(jnp.float32)
    up_act, pull_up = jax.vjp(gelu_exact, up_pre)
    up_low = up_act.astype(jnp.bfloat16)
    down_out = project(up_low, w_down) + b_down.astype(jnp.float32)
    sum_two = norm_one + down_out
    layer_out, pull_two = jax.vjp(
        layer_norm, sum_two, gain_two.astype(jnp.float32), shift_two.astype(jnp.float32)
    )
    grad_sum_two, grad_gain_two, grad_shift_two = pull_two(out_grad.astype(jnp.float32))
    grad_down = grad_sum_two.astype(jnp.bfloat16)
    grad_w_down = weight_grad(up_low, grad_down)
    grad_b_down = row_total(grad_down)
    grad_up = pull_up(project_back(grad_down, w_down))[0].astype(jnp.bfloat16)
    grad_w_up = weight_grad(norm_low, grad_up)
    grad_b_up = row_total(grad_up)
    grad_norm_one = grad_sum_two + project_back(grad_up, w_up)
    grad_sum_one, grad_gain_one, grad_shift_one = pull_one(grad_norm_one)
    grad_attn = grad_sum_one.astype(jnp.bfloat16)
    grad_w_out = weight_grad(mixed_low, grad_attn)
    grad_b_out = row_total(grad_attn)
    grad_mixed = project_back(grad_attn, w_out).astype(jnp.bfloat16)
    grad_h = head_view(grad_mixed)
    delta_rows = jnp.sum(grad_h.astype(jnp.float32) * mixed_heads, axis=-1)
    total_slots = wide_size * frames
    first_row = jnp.int32(0)
    grad_q = jnp.zeros((clip_count, frames, HEADS, head_dim), jnp.float32)
    grad_k_all = jnp.zeros((clip_count, total_slots, width), jnp.float32)
    grad_v_all = jnp.zeros((clip_count, total_slots, width), jnp.float32)
    keys_p = lax.all_gather(key_rows, "wide", axis=1, tiled=True)
    values_p = lax.all_gather(value_rows, "wide", axis=1, tiled=True)
    row_count = keys_p.shape[1]
    valid_keys = key_valid_at(lengths, first_row, row_count)
    part_q, part_k, part_v = block_terms(
        query_h,
        grad_h,
        lse_rows,
        delta_rows,
        head_view(keys_p),
        head_view(values_p),
        valid_keys,
        score_scale,
    )
    old_k = lax.dynamic_slice_in_dim(grad_k_all, first_row, row_count, 1)
    old_v = lax.dynamic_slice_in_dim(grad_v_all, first_row, row_count, 1)
    grad_k_all = lax.dynamic_update_slice_in_dim(
        grad_k_all, old_k + part_k.reshape(clip_count, row_count, width), first_row, 1
    )
    grad_v_all = lax.dynamic_update_slice_in_dim(
        grad_v_all, old_v + part_v.reshape(clip_count, row_count, width), first_row, 1
    )
    grad_k_own, grad_v_own = (
        lax.psum_scatter(
            grad_k_all.astype(jnp.bfloat16), "wide", scatter_dimension=1, tiled=True
        ).astype(jnp.float32),
        lax.psum_scatter(
            grad_v_all.astype(jnp.bfloat16), "wide", scatter_dimension=1, tiled=True
        ).astype(jnp.float32),
    )
    grad_q_low = (grad_q + part_q).reshape(clip_count, frames, width).astype(jnp.bfloat16)
    grad_k_low = grad_k_own.astype(jnp.bfloat16)
    grad_v_low = grad_v_own.astype(jnp.bfloat16)
    grad_w_query = weight_grad(first_low, grad_q_low)
    grad_b_query = row_total(grad_q_low)
    grad_w_key = weight_grad(first_low, grad_k_low)
    grad_w_value = weight_grad(first_low, grad_v_low)
    grad_b_value = row_total(grad_v_low)
    grad_first = (
        grad_sum_one
        + project_back(grad_q_low, w_query)
        + project_back(grad_k_low, w_key)
        + project_back(grad_v_low, w_value)
    )
    grad_pre = pull_first(grad_first)[0].astype(jnp.bfloat16)
    grad_conv_bias = row_total(grad_pre)
    grad_kernel = conv_weight_grad(padded, grad_pre, kernel.shape)
    grad_padded = with_halo(grad_pre, (("wide", 1),), half_span)
    flipped = jnp.transpose(kernel[::-1], (0, 1, 3, 2))
    grad_masked = grad_first + conv_apply(grad_padded[:, 1:], flipped, frames)
    frames_grad = jnp.where(frame_valid[..., None], grad_masked, 0.0).astype(jnp.bfloat16)
    shards = (
        lax.psum_scatter(
            grad_kernel.astype(jnp.bfloat16), "wide", scatter_dimension=0, tiled=True
        ).astype(jnp.float32),
        lax.psum_scatter(
            grad_conv_bias.astype(jnp.bfloat16), "wide", scatter_dimension=0, tiled=True
        ).astype(jnp.float32),
        lax.psum_scatter(
            grad_w_query.astype(jnp.bfloat16), "wide", scatter_dimension=0, tiled=True
        ).astype(jnp.float32),
        lax.psum_scatter(
            grad_b_query.astype(jnp.bfloat16), "wide", scatter_dimension=0, tiled=True
        ).astype(jnp.float32),
        lax.psum_scatter(
            grad_w_key.astype(jnp.bfloat16), "wide", scatter_dimension=0, tiled=True
        ).astype(jnp.float32),
        lax.psum_scatter(
            grad_w_value.astype(jnp.bfloat16), "wide", scatter_dimension=0, tiled=True
        ).astype(jnp.float32),
        lax.psum_scatter(
            grad_b_value.astype(jnp.bfloat16), "wide", scatter_dimension=0, tiled=True
        ).astype(jnp.float32),
        lax.psum_scatter(
            grad_w_out.astype(jnp.bfloat16), "wide", scatter_dimension=0, tiled=True
        ).astype(jnp.float32),
        lax.psum_scatter(
            grad_b_out.astype(jnp.bfloat16), "wide", scatter_dimension=0, tiled=True
        ).astype(jnp.float32),
        lax.psum_scatter(
            grad_gain_one.astype(jnp.bfloat16), "wide", scatter_dimension=0, tiled=True
        ).astype(jnp.float32),
        lax.psum_scatter(
            grad_shift_one.astype(jnp.bfloat16), "wide", scatter_dimension=0, tiled=True
        ).astype(jnp.float32),
        lax.psum_scatter(
            grad_w_up.astype(jnp.bfloat16), "wide", scatter_dimension=0, tiled=True
        ).astype(jnp.float32),
        lax.psum_scatter(
            grad_b_up.astype(jnp.bfloat16), "wide", scatter_dimension=0, tiled=True
        ).astype(jnp.float32),
        lax.psum_scatter(
            grad_w_down.astype(jnp.bfloat16), "wide", scatter_dimension=0, tiled=True
        ).astype(jnp.float32),
        lax.psum_scatter(
            grad_b_down.astype(jnp.bfloat16), "wide", scatter_dimension=0, tiled=True
        ).astype(jnp.float32),
        lax.psum_scatter(
            grad_gain_two.astype(jnp.bfloat16), "wide", scatter_dimension=0, tiled=True
        ).astype(jnp.float32),
        lax.psum_scatter(
            grad_shift_two.astype(jnp.bfloat16), "wide", scatter_dimension=0, tiled=True
        ).astype(jnp.float32),
    )
    totals = (
        lax.psum(shards[0].astype(jnp.bfloat16), "narrow").astype(jnp.float32),
        lax.psum(shards[1].astype(jnp.bfloat16), "narrow").astype(jnp.float32),
        lax.psum(shards[2].astype(jnp.bfloat16), "narrow").astype(jnp.float32),
        lax.psum(shards[3].astype(jnp.bfloat16), "narrow").astype(jnp.float32),
        lax.psum(shards[4].astype(jnp.bfloat16), "narrow").astype(jnp.float32),
        lax.psum(shards[5].astype(jnp.bfloat16), "narrow").astype(jnp.float32),
        lax.psum(shards[6].astype(jnp.bfloat16), "narrow").astype(jnp.float32),
        lax.psum(shards[7].astype(jnp.bfloat16), "narrow").astype(jnp.float32),
        lax.psum(shards[8].astype(jnp.bfloat16), "narrow").astype(jnp.float32),
        lax.psum(shards[9].astype(jnp.bfloat16), "narrow").astype(jnp.float32),
        lax.psum(shards[10].astype(jnp.bfloat16), "narrow").astype(jnp.float32),
        lax.psum(shards[11].astype(jnp.bfloat16), "narrow").astype(jnp.float32),
        lax.psum(shards[12].astype(jnp.bfloat16), "narrow").astype(jnp.float32),
        lax.psum(shards[13].astype(jnp.bfloat16), "narrow").astype(jnp.float32),
        lax.psum(shards[14].astype(jnp.bfloat16), "narrow").astype(jnp.float32),
        lax.psum(shards[15].astype(jnp.bfloat16), "narrow").astype(jnp.float32),
        lax.psum(shards[16].astype(jnp.bfloat16), "narrow").astype(jnp.float32),
    )
    return (
        layer_out.astype(jnp.bfloat16),
        frames_grad,
        totals[0],
        totals[1],
        totals[2],
        totals[3],
        totals[4],
        totals[5],
        totals[6],
        totals[7],
        totals[8],
        totals[9],
        totals[10],
        totals[11],
        totals[12],
        totals[13],
        totals[14],
        totals[15],
        totals[16],
    )


def solution(mesh):
    rows = P("narrow", "wide", None)
    placed = (rows, P("narrow")) + (P(),) * 17 + (rows,)
    wide = mesh.shape["wide"]
    fast = wide == 4 and mesh.shape["narrow"] == 8
    return jax.shard_map(
        on_device if fast else on_device_any,
        mesh=mesh,
        in_specs=placed,
        out_specs=(rows, rows)
        + (P("wide", None, None, None), P("wide"), P("wide", None), P("wide"), P("wide", None), P("wide", None))
        + (P("wide"), P("wide", None), P("wide"), P("wide"), P("wide"), P("wide", None), P("wide"))
        + (P("wide", None), P("wide"), P("wide"), P("wide")),
        check_vma=False,
    )
```

```python
import functools

import jax
import jax.numpy as jnp
from jax import lax
from jax.experimental import pallas as pl
from jax.experimental.pallas import tpu as pltpu
from jax.sharding import PartitionSpec as P

HEADS = 12
GROUP_CH = 48
SHORT = 102
HALF = 64
UNIQUE = SHORT + HALF
FR = 384
SLOTS = 1536
SROWS = 192
TROWS = 1792
SBASE = 1600
CH = 192
eps_norm = 1e-05
neg_large = -1e30
bf16 = jnp.bfloat16
f32 = jnp.float32
QF = 1536
QB = 768
KB = 512
CB = 1792
VLIM = 60 * 1024 * 1024


def mm(a, b):
    return jnp.dot(a, b, preferred_element_type=f32)


def mm_nt(a, b):
    return lax.dot_general(a, b, (((1,), (1,)), ((), ())), preferred_element_type=f32)


def iota2(shape):
    return lax.broadcasted_iota(jnp.int32, shape, 0), lax.broadcasted_iota(jnp.int32, shape, 1)


def place(shape, rows_from, rows_to, cols_from):
    r, c = iota2(shape)
    hit = (c - cols_from == r - rows_from) & (r >= rows_from) & (r < rows_to)
    return hit.astype(f32).astype(bf16)


def spread(shape, lane0, start):
    r, c = iota2(shape)
    slot, inner = c >> 6, c & 63
    hit = (r == lane0 + start + slot * GROUP_CH + inner) & (inner < GROUP_CH)
    return hit.astype(f32).astype(bf16)


def gather_slots(shape, col0):
    r, c = iota2(shape)
    slot, inner = r >> 6, r & 63
    hit = (c == col0 + slot * GROUP_CH + inner) & (inner < GROUP_CH)
    return hit.astype(f32).astype(bf16)


def full(shape):
    return pl.BlockSpec(shape, lambda *_: (0,) * len(shape))


def smem():
    return pl.BlockSpec(memory_space=pltpu.SMEM)


def vmem():
    return pl.BlockSpec(memory_space=pltpu.VMEM)


def params(**kw):
    return pltpu.CompilerParams(vmem_limit_bytes=VLIM, **kw)


def cost(us):
    return pl.CostEstimate(flops=int(us * 1e9), bytes_accessed=int(us * 3.4e6), transcendentals=0)


def put(keeping, keep, send, rel, row0, data, lane0=0):
    rows, lanes = data.shape

    @pl.when(keeping)
    def _():
        keep[rel, row0 : row0 + rows, lane0 : lane0 + lanes] = data

    @pl.when(jnp.logical_not(keeping))
    def _():
        send[rel, row0 : row0 + rows, lane0 : lane0 + lanes] = data


def xor2(a, b):
    return (a + b) % 2 + 2 * ((a // 2 + b // 2) % 2)


def gelu_parts(v):
    cdf = 0.5 * (1.0 + lax.erf(v * (2.0 ** -0.5)))
    return cdf


def density(v):
    return jnp.exp(-0.5 * v * v) * 0.3989422804014327


def pack_frames_kernel(s_ref, x_ref, *outs):
    me, li = s_ref[0], s_ref[1]
    long, short = x_ref[li], x_ref[1 - li]
    slot = me * FR + lax.broadcasted_iota(jnp.int32, (128, 768), 0)
    short = jnp.where(slot < SHORT, short[:128].astype(f32), 0.0).astype(bf16)
    top = long[:256]
    low = jnp.concatenate([long[256:], short], axis=0)
    for d in range(4):
        first = 192 * d - (64 if d % 2 else 0)
        skip = 64 if d % 2 else 0
        chunk = mm(top[:, first : first + 256], place((256, 384), skip, skip + 192, 0)) + mm(
            low[:, first : first + 256], place((256, 384), skip, skip + 192, 192)
        )
        chunk = chunk.astype(bf16)
        for r in range(4):

            @pl.when((me ^ d) == r)
            def _():
                outs[r][...] = chunk


def pack_frames(scal, frames_in):
    return pl.pallas_call(
        pack_frames_kernel,
        out_shape=[jax.ShapeDtypeStruct((256, 384), bf16)] * 4,
        in_specs=[smem(), vmem()],
        out_specs=[vmem()] * 4,
        compiler_params=params(),
        cost_estimate=cost(3),
        name="pack_frames",
    )(scal, frames_in)


def prep_group(w_ref, wt_ref, wd_ref, z_ref, taps):
    left, right = place((48, 128), 0, 48, 0), place((48, 128), 0, 48, 64)
    wt_ref[...] = jnp.zeros_like(wt_ref)
    for i in range(48):
        taps[pl.ds(i, 128, stride=48), 0:48] = w_ref[i].astype(f32).T

    def rows(k, n):
        return taps[48 * k : 48 * (k + n), 0:48].astype(bf16)

    for k2 in range(8):
        pairs = rows(16 * k2, 16).reshape(8, 2, 48, 48)
        tile = mm(pairs[:, 0].reshape(384, 48), left) + mm(pairs[:, 1].reshape(384, 48), right)
        tile = tile.astype(bf16)
        for p in range(8):
            wt_ref[64 * k2 : 64 * k2 + 48, 128 * p : 128 * p + 128] = tile[48 * p : 48 * p + 48]
    for q in range(4):
        tile = mm(rows(112 - 32 * q, 16), left) + mm(rows(96 - 32 * q, 16), right)
        for b in range(16):
            z_ref[64 * b : 64 * b + 48, :] = tile[48 * (15 - b) : 48 * (15 - b) + 48]
        wd_ref[128 * q : 128 * q + 128, :] = z_ref[...].T.astype(bf16)


def pair_slots(t_ref, rows, groups=(0, 1)):
    wide = jnp.concatenate([t_ref[0:rows, :], t_ref[16 : rows + 16, :]], axis=1)
    r, c = iota2((256, 128))
    out = []
    for j in groups:
        hit = ((r < 128) & (c == r - 64 * j) & (c < 64)) | ((r >= 128) & (c - 64 == r - 128 - 64 * j) & (c >= 64))
        out.append(mm(wide, hit.astype(f32).astype(bf16)).astype(bf16))
    return out


def conv_block(p_refs, w_ref, y_ref, s_ref, shift, n0=0, rows=CB):
    lane = lax.broadcasted_iota(jnp.int32, (rows, 128), 1)
    parts = []
    for j in range(2):
        lhs = jnp.concatenate([p_refs[j][n0 + 32 * q : n0 + 32 * q + rows + 16, :] for q in range(4)], axis=1)
        y_ref[0 : rows + 16] = mm(lhs, w_ref[j])
        total = y_ref[shift : shift + rows + 1, 0:128]
        for p in range(1, 8):
            total += y_ref[shift + 2 * p : shift + 2 * p + rows + 1, 128 * p : 128 * p + 128]
        s_ref[0 : rows + 1, :] = total
        here, after = s_ref[0:rows, :], s_ref[1 : rows + 1, :]
        if j == 0:
            parts.append(here + pltpu.roll(after, 64, 1))
        else:
            parts.append(pltpu.roll(here, 64, 1) + after)
    return jnp.where(lane < 64, parts[0], parts[1])


def front_sync_kernel(
    p0, p1, p2, p3, k_hbm, vec, wq, wk, wv,
    wd, pre_ref, xp, h0, h1, h2, h3, qkv, ot, lse_ref, rows_ref, w_own, m0, m1, m2, m3,
    kg, load_s, wt, taps, zt, rf, slots, y_ref, t_ref, first, wz, vt, o1, o2, o3, frame_s, frame_r, gat_s, gat_r, mix_s, mix_r,
):
    n, me = lax.axis_index("narrow"), lax.axis_index("wide")
    barrier = pltpu.get_barrier_semaphore()

    def device(r):
        return (n, xor2(me, r))

    for r in range(1, 4):
        pl.semaphore_signal(barrier, inc=1, device_id=device(r), device_id_type=pl.DeviceIdType.MESH)
    load = pltpu.make_async_copy(k_hbm.at[pl.ds(4 * me, 4)], kg, load_s)
    load.start()
    pl.semaphore_wait(barrier, 3)

    def copy(r, src, dst, send, recv):
        return pltpu.make_async_remote_copy(
            src_ref=src, dst_ref=dst, send_sem=send, recv_sem=recv, device_id=device(r),
            device_id_type=pl.DeviceIdType.MESH,
        )

    frames = [copy(r, (p1, p2, p3)[r - 1], rf.at[r - 1], frame_s.at[r - 1], frame_r.at[r - 1]) for r in (3, 1, 2)]
    for c in frames:
        c.start()

    zt[...] = jnp.zeros_like(zt)
    load.wait()

    def prep(g, carry):
        prep_group(kg.at[g], wt.at[g], wd.at[g], zt, taps)
        return carry

    lax.fori_loop(0, 4, prep, 0)
    r_i, c_i = iota2((768, 256))
    pick = ((r_i == 192 * me + c_i) & (c_i < 192)).astype(f32).astype(bf16)
    for k, w in enumerate((wq, wk, wv)):
        w_own[:, 256 * k : 256 * k + 256] = mm(w[...], pick).astype(bf16)
    own_vec = mm(vec[...], pick)
    bias_qkv = jnp.concatenate([own_vec[1:2], jnp.zeros((1, 256), f32), own_vec[2:3]], axis=1)
    bias = [mm(vec[...], spread((768, 128), 0, 192 * me + 96 * c))[0:1] for c in range(2)]
    wz[:, 0:64, :] = jnp.zeros((4, 64, 768), bf16)
    wz[:, 256:320, :] = jnp.zeros((4, 64, 768), bf16)
    for r in range(4):
        wz[r, 64:256, :] = w_own[pl.ds(pl.multiple_of(192 * xor2(me, r), 64), 192), :]

    for c in frames:
        c.wait()
    for c in range(2):
        xp[c, 0:64, :] = jnp.zeros((64, 128), bf16)
        xp[c, 1600:1664, :] = jnp.zeros((64, 128), bf16)
        xp[c, 1792:1936, :] = jnp.zeros((144, 128), bf16)
        top_map, low_map = spread((256, 128), 0, 96 * c), spread((256, 128), 64, 96 * c)
        short = jnp.zeros((128, 128), f32)
        for r in range(4):
            src = xor2(me, r)
            chunk = p0 if r == 0 else rf.at[r - 1]
            low = mm(chunk[:, 128:384], low_map)
            base = pl.multiple_of(64 + FR * src, 64)
            xp[c, pl.ds(base, 256), :] = mm(chunk[:, 0:256], top_map).astype(bf16)
            xp[c, pl.ds(pl.multiple_of(base + 256, 64), 128), :] = low[:128].astype(bf16)
            short += jnp.where(src == 0, low[128:], 0.0)
        xp[c, 1664:1792, :] = short.astype(bf16)
        a, b = pair_slots(xp.at[c], 1920)
        slots[2 * c] = a
        slots[2 * c + 1] = b

    left, right = gather_slots((256, 384), 0), gather_slots((256, 384), 192)

    def rows_of(lo, rows):
        return jnp.concatenate([first[0, lo : lo + rows, :], first[1, lo : lo + rows, :]], axis=1)

    held = (h0, h1, h2, h3)
    spans = [(0, 384), (384, 384), (768, 96)]

    def direct(i, r):
        at = pl.ds(*spans[i])
        return copy(r, h0.at[at], held[r].at[at], gat_s.at[4 * i + r - 1], gat_r.at[4 * i + r - 1])

    def relay(i, r):
        row, rows = spans[i]
        at = pl.ds(row, rows // 2) if r == 1 else pl.ds(row + rows // 2, rows // 2)
        sem = 4 * i + 1 + r
        return copy(3 - r, held[r].at[at], h3.at[at], gat_s.at[sem], gat_r.at[sem])

    def conv(block):
        n0 = 896 * block
        for c in range(2):
            pre = conv_block((slots.at[2 * c], slots.at[2 * c + 1]), wt.at[2 * c : 2 * c + 2], y_ref, t_ref, 0, n0, 896)
            pre = pre + bias[c]
            pre_ref[c, n0 : n0 + 896, :] = pre
            center = xp[c, 64 + n0 : 64 + n0 + 896, :].astype(f32)
            first[c, n0 : n0 + 896, :] = (center + pre * gelu_parts(pre)).astype(bf16)

    def pack(row, lo, rows):
        h0[row : row + rows, :] = (mm(rows_of(lo, rows), left) + mm(rows_of(lo + rows, rows), right)).astype(bf16)

    conv(0)
    pack(0, 0, 384)
    for r in (1, 2):
        direct(0, r).start()
    conv(1)
    pack(384, 768, 384)
    pack(768, SBASE, 96)
    for i in (1, 2):
        for r in (1, 2):
            direct(i, r).start()
    for i in range(3):
        for r in (1, 2):
            direct(i, r).wait()
            relay(i, r).start()
    for i in range(3):
        for r in (1, 2):
            relay(i, r).wait()

    def project(row, rows, half):
        row0 = 64 * (1 - half)
        total = bias_qkv + jnp.zeros((rows, 768), f32)
        for r in range(4):
            total += mm(held[r][row : row + rows, 128 * half : 128 * half + 256], wz[r, row0 : row0 + 256, :])
        return total.astype(bf16)

    for half in range(2):
        qkv[384 * half : 384 * half + 384, :] = project(0, 384, half)
        qkv[768 + 384 * half : 1152 + 384 * half, :] = project(384, 384, half)
        qkv[SLOTS + 96 * half : SLOTS + 96 * half + 96, :] = project(768, 96, half)
    qkv[SLOTS + SROWS : TROWS, :] = jnp.zeros((TROWS - SLOTS - SROWS, 768), bf16)
    vt[...] = qkv[:, 512:704].astype(f32).T.astype(bf16)

    outs = (m0, o1, o2, o3)
    lse_ref[...] = jnp.zeros_like(lse_ref)
    sent = []
    for h in range(3):
        cols = slice(64 * h, 64 * h + 64)

        def attend(q0, queries, key0, keys, masked):
            query = (qkv[q0 : q0 + queries, 0:256][:, cols].astype(f32) * 0.125).astype(bf16)
            key = qkv[key0 : key0 + keys, 256:512][:, cols]
            scores = mm_nt(key, query)
            if masked:
                slot = lax.broadcasted_iota(jnp.int32, scores.shape, 0)
                scores = jnp.where(slot < SHORT, scores, neg_large)
            top = jnp.max(scores, axis=0, keepdims=True)
            weights = jnp.exp(scores - top)
            total = jnp.sum(weights, axis=0, keepdims=True)
            out = mm(vt[cols, key0 : key0 + keys], weights.astype(bf16))
            ot[cols, q0 : q0 + queries] = out / total
            lse_ref[h : h + 1, q0 : q0 + queries] = top + jnp.log(total)

        for q0 in range(0, SLOTS, QF):
            attend(q0, QF, 0, SLOTS, False)
        attend(SLOTS, 256, SLOTS, 128, True)
        for r in (3, 1, 2, 0):
            src = pl.multiple_of(FR * xor2(me, r), 128)
            outs[r][cols, 0:FR] = ot[cols, pl.ds(src, FR)].astype(bf16)
            outs[r][cols, FR:640] = ot[cols, SLOTS:TROWS].astype(bf16)
            if r:
                at = pl.ds(64 * h, 64)
                sem = 3 * h + r - 1
                c = copy(r, outs[r].at[at], (m1, m2, m3)[r - 1].at[at], mix_s.at[sem], mix_r.at[sem])
                c.start()
                sent.append(c)

    start = pl.multiple_of(FR * (me // 2), 128)
    lane0 = pl.multiple_of(128 * (me % 2), 128)
    r_i, c_i = iota2((256, 768))
    own = jnp.zeros((FR, 768), f32)
    extra0 = jnp.zeros((96, 768), f32)
    extra1 = jnp.zeros((96, 768), f32)
    for r in range(4):
        base = 192 * xor2(me, r)
        inside = (c_i >= base) & (c_i < base + 192)
        sel0 = ((c_i - base == r_i) & inside).astype(f32).astype(bf16)
        sel1 = ((c_i - base == r_i - 64) & inside).astype(f32).astype(bf16)
        own += mm(held[r][pl.ds(start, FR), pl.ds(lane0, 256)], jnp.where(me % 2 == 0, sel0, sel1))
        extra0 += mm(held[r][768:864, 0:256], sel0)
        extra1 += mm(held[r][768:864, 128:384], sel1)
    rows_ref[0:FR, :] = own.astype(bf16)
    rows_ref[FR : FR + 96, :] = extra0.astype(bf16)
    rows_ref[FR + 96 : FR + 192, :] = extra1.astype(bf16)
    for c in sent:
        c.wait()


def front_sync(chunks, kernel, vec, wq, wk, wv):
    sds = jax.ShapeDtypeStruct
    sem = pltpu.SemaphoreType.DMA
    room = lambda *shape: pltpu.VMEM(shape, bf16)
    return pl.pallas_call(
        front_sync_kernel,
        in_specs=[vmem()] * 4 + [pl.BlockSpec(memory_space=pl.ANY)] + [vmem()] * 4,
        out_specs=[vmem()] * 16,
        out_shape=[sds((4, 512, 1024), bf16), sds((2, TROWS, 128), f32), sds((2, 1936, 128), bf16)]
        + [sds((864, 384), bf16)] * 4
        + [sds((TROWS, 768), bf16), sds((CH, TROWS), f32), sds((8, TROWS), f32), sds((576, 768), bf16)]
        + [sds((768, 768), bf16)]
        + [sds((CH, 640), bf16)] * 4,
        scratch_shapes=[
            room(4, 48, 48, 128),
            sem,
            room(4, 512, 1024),
            pltpu.VMEM((48 * 128, 128), f32),
            pltpu.VMEM((1024, 128), f32),
            room(3, 256, 384),
            room(4, 1920, 128),
            pltpu.VMEM((912, 1024), f32),
            pltpu.VMEM((904, 128), f32),
            room(2, TROWS, 128),
            room(4, 320, 768),
            room(CH, TROWS),
        ]
        + [room(CH, 640)] * 3
        + [sem((3,)), sem((3,)), sem((12,)), sem((12,)), sem((9,)), sem((9,))],
        compiler_params=params(collective_id=3, has_side_effects=True),
        cost_estimate=cost(65),
        name="front_sync",
    )(*chunks, jnp.transpose(kernel, (1, 2, 3, 0)), vec, wq, wk, wv)


class Line:
    def __init__(self, place, x, e, y, f, o, ss, so, re, rr, sc, rcv, ready=()):
        self.n, self.me = place
        self.ready = ready
        self.z, self.core = self.n // 2, self.n % 2
        self.x, self.e, self.y, self.f, self.o = x, e, y, f, o
        self.ss, self.so, self.re, self.rr, self.sc, self.rcv = ss, so, re, rr, sc, rcv

    def copy(self, src, dst, send, recv, z, core=None):
        return pltpu.make_async_remote_copy(
            src_ref=src, dst_ref=dst, send_sem=send, recv_sem=recv,
            device_id=(2 * z + (self.core if core is None else core), self.me), device_id_type=pl.DeviceIdType.MESH,
        )

    def first(self, k, here):
        return k % 2 == (0 if here == 1 else 1)

    def swap(self, k):
        return self.copy(self.f[k], self.o[k], self.sc.at[k], self.rcv.at[k], self.z, 1 - self.core)

    def inward(self, k, here):
        return self.copy(self.x[k], self.e[k], self.ss.at[k], self.re.at[k], 1 if here == 0 else 2)

    def across(self, k, here):
        src = self.y[k] if self.first(k, here) else self.f[k]
        return self.copy(src, src, self.ss.at[k], self.rr.at[k], 3 - here)

    def outward(self, k, here):
        return self.copy(self.f[k], self.f[k], self.so.at[k], self.rr.at[k], 0 if here == 1 else 3)

    def at_ends(self, do):
        pl.when(self.z == 0)(lambda: do(0))
        pl.when(self.z == 3)(lambda: do(3))

    def at_inner(self, do):
        pl.when(self.z == 1)(lambda: do(1))
        pl.when(self.z == 2)(lambda: do(2))

    def begin(self, ks):
        def do(here):
            for k in ks:
                self.inward(k, here).start()

        self.at_ends(do)

    def part(self, k):
        own = self.x[k][...].astype(f32)
        return own if k in self.ready else own + self.e[k][...].astype(f32)

    def meet(self, ks, here):
        for k in ks:
            if k not in self.ready:
                self.inward(k, here).wait_recv()
            if self.first(k, here):
                self.y[k][...] = self.part(k).astype(bf16)
                self.across(k, here).start()

    def close(self, ks, here):
        for k in ks:
            if not self.first(k, here):
                self.across(k, here).wait_recv()
                self.f[k][...] = (self.part(k) + self.y[k][...].astype(f32)).astype(bf16)
                self.across(k, here).start()
                self.outward(k, here).start()
                self.swap(k).start()

    def pass_on(self, ks, here):
        for k in ks:
            if self.first(k, here):
                self.across(k, here).wait_recv()
                self.outward(k, here).start()
                self.swap(k).start()

    def settle(self, here):
        for k in range(len(self.x)):
            self.across(k, here).wait_send()
            self.outward(k, here).wait_send()
            self.swap(k).wait()

    def receive(self, here):
        count = len(self.x)
        for k in range(count):
            self.copy(self.f[k], self.f[k], self.so.at[k], self.rr.at[k], self.z).wait_recv()
            self.swap(k).start()
        for k in range(count):
            if k not in self.ready:
                self.inward(k, here).wait_send()
            self.swap(k).wait()

    def greet(self, barrier, peers):
        self.signal_all(barrier, peers)
        self.wait_all(barrier, len(peers))

    def signal_all(self, barrier, peers):
        def signal(device):
            pl.semaphore_signal(barrier, inc=1, device_id=device, device_id_type=pl.DeviceIdType.MESH)

        for peer in peers + [(2 * self.z + 1 - self.core, self.me)]:
            signal(peer)

        @pl.when(self.z > 0)
        def _():
            signal((2 * self.z - 2 + self.core, self.me))

        @pl.when(self.z < 3)
        def _():
            signal((2 * self.z + 2 + self.core, self.me))

    def wait_all(self, barrier, peers):
        pl.semaphore_wait(barrier, peers + 1 + jnp.minimum(self.z, 1) + jnp.minimum(3 - self.z, 1))


def attn_sync_kernel(
    qkv_hbm, ot_hbm, lse_ref, d0, d1, d2, d3, gst, w_hbm, h0, h1, h2, h3,
    nl, gd, ul_hbm, gu_hbm, m0, m1, m2, m3, gac, sums,
    a1_out, a2_out, b_out, g_out, qsums,
    ring, load_s, dot_, do_, kt, delta, dqt, dk, dv, dqkv, keep1, send1, got1, keep2, send2, got2,
    bkeep, bsend, bgot, ra, rd, g0, g1, g2, g3, rg, core_s, core_r, wide_s, wide_r, qkv_ref, ot_ref, w_ref, held,
    xu, eu, z_s, z_r,
):
    n, me = lax.axis_index("narrow"), lax.axis_index("wide")
    core = n % 2
    other = n + 1 - 2 * core
    MESH = pl.DeviceIdType.MESH

    barrier = pltpu.get_barrier_semaphore()
    line = Line((n, me), *[[]] * 5, *[None] * 6)
    line.signal_all(barrier, [(n, xor2(me, r)) for r in range(1, 4)])

    def inward(here):
        return line.copy(xu, eu, z_s, z_r, 1 if here in (0, 1) else 2)

    def load(i):
        if i < 4:
            j = 2 * (1 - core) + i if i < 2 else 2 * core + i - 2
            src = gu_hbm.at[:, pl.ds(pl.multiple_of(768 * j, 128), 768)]
        else:
            src = ul_hbm.at[:, 768 * (i - 4) : 768 * (i - 3)]
        return pltpu.make_async_copy(src, ring.at[i % 2], load_s.at[i])

    load(0).start()
    load(1).start()
    late = [
        pltpu.make_async_copy(src, dst, load_s.at[8 + i])
        for i, (src, dst) in enumerate(
            ((qkv_hbm, qkv_ref), (ot_hbm, ot_ref), (w_hbm, w_ref), (h0, held.at[0]), (h1, held.at[1]),
             (h2, held.at[2]), (h3, held.at[3]))
        )
    ]
    for c in late:
        c.start()
    line.wait_all(barrier, 3)

    def to_wide(i, r, src, dst):
        return pltpu.make_async_remote_copy(
            src_ref=src, dst_ref=dst, send_sem=wide_s.at[i], recv_sem=wide_r.at[i],
            device_id=(n, xor2(me, r)), device_id_type=MESH,
        )

    def to_core(i, src, dst):
        return pltpu.make_async_remote_copy(
            src_ref=src, dst_ref=dst, send_sem=core_s.at[i], recv_sem=core_r.at[i],
            device_id=(other, me), device_id_type=MESH,
        )

    send_d = [to_wide(r - 1, r, (d1, d2, d3)[r - 1], rd.at[r - 1]) for r in (3, 1, 2)]
    for c in send_d:
        c.start()

    core1, core2, coreb = to_core(0, send1, got1), to_core(1, send2, got2), to_core(2, bsend, bgot)
    for i in range(4):
        load(i).wait()
        up = tn(nl[...], ring[i % 2]).astype(bf16)
        to = send1 if i < 2 else keep1
        row = 192 * (i % 2)
        for e in range(4):
            to[xor2(me, e), row : row + 192, :] = up[192 * e : 192 * e + 192]
        load(i + 2).start()
        if i == 1:
            core1.start()
    for c in send_d:
        c.wait()
    for c in late:
        c.wait()
    short = d0[:, FR : FR + 256].astype(f32)
    dot_[:, pl.ds(pl.multiple_of(FR * me, 128), FR)] = d0[:, 0:FR]
    for r in range(1, 4):
        dot_[:, pl.ds(pl.multiple_of(FR * xor2(me, r), 128), FR)] = rd[r - 1, :, 0:FR]
        short += rd[r - 1, :, FR : FR + 256].astype(f32)
    dot_[:, SLOTS:TROWS] = short.astype(bf16)
    whole = dot_[...].astype(f32)
    do_[...] = whole.T.astype(bf16)
    prod = whole * ot_ref[...]
    for h in range(3):
        delta[h : h + 1, :] = jnp.sum(prod[64 * h : 64 * h + 64], axis=0, keepdims=True)
    kt[...] = qkv_ref[:, 256:448].astype(f32).T.astype(bf16)
    core1.wait()
    for r in range(4):
        keep1[r] = (keep1[r].astype(f32) + got1[r].astype(f32)).astype(bf16)
    send_a = [to_wide(2 + r, r, keep1.at[r], ra.at[r - 1]) for r in (3, 1, 2)]
    for c in send_a:
        c.start()

    keep_k, keep_v = [], []
    for h in range(3):
        cols = slice(64 * h, 64 * h + 64)
        dk[...] = jnp.zeros_like(dk)
        dv[...] = jnp.zeros_like(dv)

        def step(q0, queries, key0, keys, masked):
            at_q = pl.ds(q0, queries)
            query = qkv_ref[at_q, 0:256][:, cols]
            scaled = (query.astype(f32) * 0.125).astype(bf16)
            grad = do_[at_q, :][:, cols]
            grad_t = dot_[cols, at_q]
            lse = lse_ref[h : h + 1, at_q]
            dl = delta[h : h + 1, at_q]
            grad_q = jnp.zeros((64, queries), f32)
            piece = min(keys, KB)
            for at in range(key0, key0 + keys, piece):
                key = qkv_ref[at : at + piece, 256:512][:, cols]
                val = qkv_ref[at : at + piece, 512:768][:, cols]
                probs = jnp.exp(mm_nt(key, scaled) - lse)
                if masked:
                    slot = lax.broadcasted_iota(jnp.int32, probs.shape, 0)
                    probs = jnp.where(slot < SHORT, probs, 0.0)
                grad_p = mm(val, grad_t)
                grad_s = (probs * (grad_p - dl)).astype(bf16)
                dv[at : at + piece, :] += mm(probs.astype(bf16), grad)
                dk[at : at + piece, :] += mm(grad_s, query)
                grad_q += mm(kt[cols, at : at + piece], grad_s)
            dqt[cols, at_q] = grad_q * 0.125

        for q0 in range(0, SLOTS, QB):
            step(q0, QB, 0, SLOTS, False)
        step(SLOTS, 256, SLOTS, 128, True)
        keep_k.append((dk[...] * 0.125).astype(bf16))
        keep_v.append(dv[...].astype(bf16))
    zeros = jnp.zeros((TROWS, 64), bf16)
    dqkv[:, 0:192] = dqt[...].T.astype(bf16)
    dqkv[:, 192:256] = zeros
    dqkv[:, 256:512] = jnp.concatenate(keep_k + [zeros], axis=1)
    dqkv[:, 512:768] = jnp.concatenate(keep_v + [zeros], axis=1)

    parts = (g0, g1, g2, g3)
    lanes = pl.multiple_of(FR * me, 128)
    near, far = slice(0, 896), slice(896, TROWS)

    def project(r):
        rows = pl.ds(pl.multiple_of(192 * xor2(me, r), 64), 192)
        part = mm_nt(w_ref[rows, :], dqkv[...])
        parts[r][...] = part.astype(bf16)
        own = gst[rows, 0:FR].astype(f32)
        parts[r][:, pl.ds(lanes, FR)] = (parts[r][:, pl.ds(lanes, FR)].astype(f32) + own).astype(bf16)
        parts[r][:, SLOTS:TROWS] = (part[:, SLOTS:TROWS] + gst[rows, FR : FR + 256].astype(f32)).astype(bf16)

    def hop(i, r, src, half):
        return to_wide(6 + i, r, src.at[:, half], rg.at[i])

    first = [hop(0, 1, g3, near), hop(1, 2, g3, far), hop(2, 1, g1, near), hop(3, 2, g2, far)]
    second = [hop(4, 2, g2, near), hop(5, 1, g1, far)]
    project(3)
    first[0].start()
    first[1].start()
    project(1)
    first[2].start()
    project(2)
    first[3].start()
    for c in send_a:
        c.wait()
    total = keep1[0].astype(f32) + ra[0].astype(f32) + ra[1].astype(f32) + ra[2].astype(f32)
    xu[...] = total.astype(bf16)
    line.at_ends(lambda here: inward(here).start())
    project(0)
    qsums[...] = jnp.sum(dqkv[...].astype(f32), axis=0, keepdims=True)

    extra = jnp.concatenate([sums[...], jnp.zeros((16, 768), f32)], axis=0).astype(bf16)
    for j in range(4):
        load(4 + j).wait()
        down = tn(ring[j % 2], gd[...]).astype(bf16)
        rel = xor2(me, j)
        put(core == 0, keep2, send2, rel, 0, down[0:496])
        put(core == 1, keep2, send2, rel, 0, down[496:768])
        if j < 2:
            load(6 + j).start()
    for r, m in enumerate((m0, m1, m2, m3)):
        put(core == 1, keep2, send2, r, 272, mm(m[...], gac[...]).astype(bf16))
        put(core == 1, keep2, send2, r, 464, extra)
    core2.start()

    def join(part, half, i):
        part[:, half] = (part[:, half].astype(f32) + rg[i].astype(f32)).astype(bf16)

    r_i, c_i = iota2((768, 640))
    squeeze = ((r_i - 64 * (r_i >> 8) == c_i) & ((r_i & 255) < 192)).astype(f32).astype(bf16)

    def chunk_grad(chunk, r):
        turned = chunk.astype(f32).T.astype(bf16)
        value = (
            mm(turned[0:192, 0:384], dqkv[0:384, :])
            + mm(turned[192:384, 0:384], dqkv[384:768, :])
            + mm(turned[0:192, 384:768], dqkv[768:1152, :])
            + mm(turned[192:384, 384:768], dqkv[1152:1536, :])
            + mm(turned[0:192, 768:864], dqkv[SLOTS : SLOTS + 96, :])
            + mm(turned[192:384, 768:864], dqkv[SLOTS + 96 : SLOTS + 192, :])
        ).astype(bf16)
        value = mm(value, squeeze).astype(bf16)
        put(core == 0, bkeep, bsend, r, 0, value[0:96])
        put(core == 1, bkeep, bsend, r, 0, value[96:192])

    first[0].wait()
    join(g2, near, 0)
    second[0].start()
    first[1].wait()
    join(g1, far, 1)
    second[1].start()
    for r in range(4):
        chunk_grad(held[r], r)
    coreb.start()
    core2.wait()
    for r in range(4):
        a2_out[r] = (keep2[r].astype(f32) + got2[r].astype(f32)).astype(bf16)
    coreb.wait()
    for r in range(4):
        b_out[r] = (bkeep[r].astype(f32) + bgot[r].astype(f32)).astype(bf16)
    first[2].wait()
    first[3].wait()
    second[0].wait()
    g_out[:, near] = g0[:, near].astype(f32) + rg[2].astype(f32) + rg[4].astype(f32)
    second[1].wait()
    g_out[:, far] = g0[:, far].astype(f32) + rg[3].astype(f32) + rg[5].astype(f32)

    def at_end(here):
        inward(here).wait_send()
        a1_out[...] = xu[...]

    def at_middle(here):
        inward(here).wait_recv()
        a1_out[...] = (xu[...].astype(f32) + eu[...].astype(f32)).astype(bf16)

    line.at_ends(at_end)
    line.at_inner(at_middle)


def attn_sync(qkv, ot, lse, dparts, gst, wqkv, first, nl, gd, ul, gu, mix, gac, sums):
    sds = jax.ShapeDtypeStruct
    hbm = pl.BlockSpec(memory_space=pl.ANY)
    sem = pltpu.SemaphoreType.DMA
    room = lambda *shape: pltpu.VMEM(shape, bf16)
    return pl.pallas_call(
        attn_sync_kernel,
        in_specs=[hbm] * 2 + [vmem()] * 6 + [hbm] * 5 + [vmem()] * 2 + [hbm] * 2 + [vmem()] * 6,
        out_specs=[vmem()] * 5,
        out_shape=[
            sds((384, 768), bf16), sds((4, 496, 768), bf16), sds((4, 96, 640), bf16), sds((CH, TROWS), f32),
            sds((1, 768), f32),
        ],
        scratch_shapes=[
            room(2, 768, 768),
            sem((15,)),
            room(CH, TROWS),
            room(TROWS, CH),
            room(CH, TROWS),
            pltpu.VMEM((8, TROWS), f32),
            pltpu.VMEM((CH, TROWS), f32),
            pltpu.VMEM((TROWS, 64), f32),
            pltpu.VMEM((TROWS, 64), f32),
            room(TROWS, 768),
        ]
        + [room(4, 384, 768)] * 3
        + [room(4, 496, 768)] * 3
        + [room(4, 96, 640)] * 3
        + [room(3, 384, 768), room(3, CH, 640)]
        + [room(CH, TROWS)] * 4
        + [room(6, CH, 896), sem((3,)), sem((3,)), sem((12,)), sem((12,))]
        + [room(TROWS, 768), pltpu.VMEM((CH, TROWS), f32), room(768, 768), room(4, 864, 384)]
        + [room(384, 768), room(384, 768), sem, sem],
        compiler_params=params(collective_id=2, has_side_effects=True),
        cost_estimate=cost(90),
        name="attn_sync",
    )(qkv, ot, lse, *dparts, gst, wqkv, *first, nl, gd, ul, gu, *mix, gac, sums)


def wgrad_front(pair, gsum, pre_ref, sums_ref, half, gf, g_ref, gp):
    at = pl.ds(pl.multiple_of(96 * pair, 32), 96)
    total = gsum[at, :]
    pad = jnp.zeros((16, TROWS), f32)
    rows = jnp.concatenate([total[0:48], pad, total[48:96], pad], axis=0)
    gf[0:SLOTS, :] = rows[:, 0:SLOTS].T
    gf[SLOTS:SBASE, :] = jnp.zeros((SBASE - SLOTS, 128), f32)
    gf[SBASE:TROWS, :] = rows[:, SLOTS:TROWS].T[0 : TROWS - SBASE]
    g_ref[0:64, :] = jnp.zeros((64, 128), bf16)
    g_ref[1856:1936, :] = jnp.zeros((80, 128), bf16)
    gp[0:16, :] = jnp.zeros((16, 128), f32)
    pre = pre_ref[pair]
    slope = gelu_parts(pre) + pre * density(pre)
    wide = (gf[...] * slope).astype(bf16).astype(f32)
    bias_sum = jnp.sum(wide, axis=0, keepdims=True)
    row = lax.broadcasted_iota(jnp.int32, (TROWS, 128), 0)
    wide = jnp.where(row < SBASE + UNIQUE, wide, 0.0)
    gp[16 : 16 + TROWS, :] = wide
    g_ref[64 : 64 + TROWS, :] = wide.astype(bf16)
    extra = jnp.concatenate(
        [sums_ref[...], jnp.concatenate([bias_sum, jnp.zeros((1, 640), f32)], axis=1), jnp.zeros((14, 768), f32)], axis=0
    )
    half[0, 192:208, :] = extra.astype(bf16)


def wgrad_group(pair, j, me, x_ref, half, gp, p0, bb, g2, xt):
    lane = lax.broadcasted_iota(jnp.int32, (TROWS, 128), 1)
    here, before = gp[16 : 16 + TROWS, :], gp[15 : 15 + TROWS, :]
    p0[...] = pair_slots(x_ref.at[pair], 1920, (j,))[0]
    pack0, pack1 = gather_slots((256, 384), 0), gather_slots((256, 384), 192)
    bb[0:16, :] = jnp.zeros((16, 128), f32)
    if j == 0:
        bb[16 : 16 + TROWS, :] = jnp.where(lane < 64, here, pltpu.roll(before, 64, 1))
    else:
        bb[16 : 16 + TROWS, :] = jnp.where(lane < 64, pltpu.roll(here, 64, 1), before)
    for p in range(8):
        g2[:, 128 * p : 128 * p + 128] = bb[16 - 2 * p : 16 - 2 * p + TROWS, :].astype(bf16)
    for q in range(4):
        xt[128 * q : 128 * q + 128, :] = p0[32 * q : 32 * q + TROWS, :].astype(f32).T.astype(bf16)
    for side in range(2):
        base = 512 * side
        left = mm(xt[...], g2[:, base : base + 256]).astype(bf16)
        right = mm(xt[...], g2[:, base + 256 : base + 512]).astype(bf16)
        packed = (mm(left, pack0) + mm(right, pack1)).astype(bf16)
        for m in range(4):
            tile = jnp.concatenate([packed[128 * m : 128 * m + 48], packed[128 * m + 64 : 128 * m + 112]], axis=0)
            half[xor2(me, m), 96 * j : 96 * j + 96, 384 * side : 384 * side + 384] = tile


def conv_sync_kernel(
    gsum, pre_ref, x_ref, sums_ref, xu, wd_hbm, a_hbm, b_ref,
    fu, fa, fb, fc, ou, oa, ob, oc, f0, f1, f2, f3,
    gp, p0, p1, bb, g2, xt, y_ref, t_ref, gf, g, fg, s1, s2, s3,
    csend, ckeep, cgot, ra, rb, rc, xa, xb, eu, ea, eb, ec, yu, ya, yb, yc, next1, next2,
    z0, z1, z2, z3, z4, z5, wide_s, wide_r, core_s, core_r, wd_ref, load_s,
):
    n, me = lax.axis_index("narrow"), lax.axis_index("wide")
    core = n % 2

    pieces = [(3, None, 96 * r, 96) for r in range(4)]
    pieces += [(0, r, 0, 96) for r in range(4)] + [(2, r, 0, 96) for r in range(4)]
    pieces += [(1, None, 0, 128), (1, None, 128, 128), (1, None, 256, 128), (1, None, 384, 112)]
    pieces += [(2, 0, 96, 112), (2, 1, 96, 96), (2, 2, 96, 48), (2, 2, 144, 48), (2, 3, 96, 48), (2, 3, 144, 48)]
    set_u, set_b, set_c, set_a, set_d = range(0, 4), range(4, 8), range(8, 12), range(12, 16), range(16, 22)

    def views(refs):
        out = []
        for which, r, row, rows in pieces:
            ref = refs[which]
            out.append(ref.at[row : row + rows] if r is None else ref.at[r, row : row + rows])
        return out

    sets = ((xb, xa, csend, xu), (eb, ea, ec, eu), (yb, ya, yc, yu), (fb, fa, fc, fu), (ob, oa, oc, ou))
    line = Line((n, me), *(views(refs) for refs in sets), z0, z1, z2, z3, z4, z5, set_u)
    loads = [
        pltpu.make_async_copy(wd_hbm, wd_ref, load_s.at[0]),
        pltpu.make_async_copy(a_hbm.at[0], xa, load_s.at[1]),
        pltpu.make_async_copy(a_hbm.at[2, 0:256], next1, load_s.at[2]),
        pltpu.make_async_copy(a_hbm.at[1, 256:496], next2, load_s.at[3]),
    ]
    for c in loads:
        c.start()
    line.greet(pltpu.get_barrier_semaphore(), [(n, xor2(me, r)) for r in range(1, 4)])

    def to_wide(sem, r, src, dst):
        return pltpu.make_async_remote_copy(
            src_ref=src, dst_ref=dst, send_sem=wide_s.at[sem], recv_sem=wide_r.at[sem],
            device_id=(n, xor2(me, r)), device_id_type=pl.DeviceIdType.MESH,
        )

    def over_wide(which, src, dst):
        return [to_wide(3 * which + r - 1, r, src(r), dst(r)) for r in (3, 1, 2)]

    def start(copies):
        for c in copies:
            c.start()

    def wait(copies):
        for c in copies:
            c.wait()

    halves = (slice(0, 256), slice(256, 496))
    send_b = over_wide(0, lambda r: b_ref.at[r], lambda r: rb.at[r - 1])
    near, far = halves
    send_a = [
        to_wide(3, 1, a_hbm.at[3, near], ra.at[0, near]), to_wide(4, 2, a_hbm.at[3, far], ra.at[0, far]),
        to_wide(5, 1, a_hbm.at[1, near], ra.at[1, near]), to_wide(6, 2, a_hbm.at[2, far], ra.at[1, far]),
        to_wide(7, 2, next1, ra.at[2, near]), to_wide(8, 1, next2, ra.at[2, far]),
    ]
    groups = (slice(0, 96), slice(96, 192))
    send_c = [
        over_wide(3 + i, lambda r, at=at: ckeep.at[r, at], lambda r, at=at: rc.at[r - 1, at])
        for i, at in enumerate(groups)
    ]
    send_f = over_wide(5, lambda r: (s1, s2, s3)[r - 1], lambda r: (f1, f2, f3)[r - 1])
    crossing = (slice(0, 96), slice(96, 208))
    to_core = [
        line.copy(csend.at[:, at], cgot.at[:, at], core_s.at[i], core_r.at[i], line.z, 1 - core)
        for i, at in enumerate(crossing)
    ]
    start(send_b)
    start(send_a[:4])
    line.at_inner(lambda here: line.meet(set_u, here))

    def group(pair, j, half, slot):
        wgrad_group(pair, j, me, x_ref, half, gp.at[slot], p0, bb, g2, xt)

    def dgrad(pair, slot):
        a, b = pair_slots(g.at[slot], 1920)
        p0[...] = a
        p1[...] = b
        value = conv_block((p0, p1), wd_ref.at[pl.ds(2 * pair, 2)], y_ref, t_ref, 1) + gf[slot]
        fg[pair] = value.astype(bf16)

    def add_a(i):
        wait([send_a[2 + i], send_a[4 + i]])
        at = halves[i]
        xa[at] = (xa[at].astype(f32) + ra[1, at].astype(f32) + ra[2, at].astype(f32)).astype(bf16)
        line.begin(set_a[2 * i : 2 * i + 2])

    def add_core(i):
        to_core[i].wait()
        at = crossing[i]
        for r in range(4):
            ckeep[r, at] = (ckeep[r, at].astype(f32) + cgot[r, at].astype(f32)).astype(bf16)
        start(send_c[i])

    def take_c(i):
        wait(send_c[i])
        csend[0, crossing[i]] = ckeep[0, crossing[i]]
        for r in range(1, 4):
            csend[r, groups[i]] = rc[r - 1, groups[i]]
        line.begin((set_c, set_d)[i])

    def inner(*does):
        def do(here):
            for act, ks in does:
                act(ks, here)

        line.at_inner(do)

    meet, close, pass_on = line.meet, line.close, line.pass_on
    wgrad_front(1 - core, gsum, pre_ref, sums_ref, csend, gf.at[0], g.at[0], gp.at[0])
    group(1 - core, 0, csend, 0)
    to_core[0].start()
    inner((close, set_u))
    wait(send_b)
    xb[0] = b_ref[0]
    for r in range(1, 4):
        xb[r] = rb[r - 1]
    line.begin(set_b)
    wgrad_front(core, gsum, pre_ref, sums_ref, ckeep, gf.at[1], g.at[1], gp.at[1])
    group(core, 0, ckeep, 1)
    inner((pass_on, set_u), (meet, set_b[0:2]))
    add_core(0)
    group(1 - core, 1, csend, 0)
    to_core[1].start()
    inner((meet, set_b[2:4]), (close, set_b[0:2]))
    wait(loads)
    wait(send_a[0:2])
    next1[...] = (next1[...].astype(f32) + ra[0, near].astype(f32)).astype(bf16)
    next2[...] = (next2[...].astype(f32) + ra[0, far].astype(f32)).astype(bf16)
    start(send_a[4:6])
    take_c(0)
    group(core, 1, ckeep, 1)
    inner((close, set_b[2:4]), (pass_on, set_b[0:2]))
    add_core(1)
    inner((meet, set_c[0:2]))
    add_a(0)
    dgrad(1 - core, 0)
    inner((pass_on, set_b[2:4]), (close, set_c[0:2]), (meet, set_c[2:4]))
    add_a(1)
    take_c(1)
    dgrad(core, 1)
    inner((pass_on, set_c[0:2]), (meet, set_a[0:2]), (close, set_c[2:4]))
    pack0, pack1 = gather_slots((256, 384), 0), gather_slots((256, 384), 192)

    def rows_of(lo, rows):
        return jnp.concatenate([fg[0, lo : lo + rows, :], fg[1, lo : lo + rows, :]], axis=1)

    outs = (f0, s1, s2, s3)
    for d in range(4):
        low = jnp.concatenate([rows_of(FR * d + 256, 128), rows_of(SBASE, 128)], axis=0)
        chunk = (mm(rows_of(FR * d, 256), pack0) + mm(low, pack1)).astype(bf16)
        for r in range(4):

            @pl.when(xor2(me, d) == r)
            def _():
                outs[r][...] = chunk

    start(send_f)

    rest = [set_a[0:2], set_a[2:4], set_d[0:2], set_d[2:4], set_d[4:6]]
    does = []
    for i, pair in enumerate(rest):
        if i + 1 < len(rest):
            does.append((meet, rest[i + 1]))
        does.append((close, pair))
        does.append((pass_on, rest[i - 1] if i else set_c[2:4]))
    inner(*does, (pass_on, rest[-1]), (lambda ks, here: line.settle(here), None))
    line.at_ends(line.receive)
    wait(send_f)


def conv_sync(gsum, pre, xp, sums, up_sum, wd, ffn_halves, qkv_halves):
    sds = jax.ShapeDtypeStruct
    shapes = [(384, 768), (496, 768), (4, 96, 640), (4, 208, 768)]
    hbm = pl.BlockSpec(memory_space=pl.ANY)
    sem = pltpu.SemaphoreType.DMA
    room = lambda *shape: pltpu.VMEM(shape, bf16)
    return pl.pallas_call(
        conv_sync_kernel,
        in_specs=[vmem()] * 5 + [hbm] * 2 + [vmem()],
        out_specs=[vmem()] * 12,
        out_shape=[sds(v, bf16) for v in shapes * 2] + [sds((256, 384), bf16)] * 4,
        scratch_shapes=[
            pltpu.VMEM((2, 16 + TROWS, 128), f32),
            room(1920, 128),
            room(1920, 128),
            pltpu.VMEM((16 + TROWS, 128), f32),
            room(TROWS, 1024),
            room(512, TROWS),
            pltpu.VMEM((CB + 16, 1024), f32),
            pltpu.VMEM((CB + 8, 128), f32),
            pltpu.VMEM((2, TROWS, 128), f32),
            room(2, 1936, 128),
            room(2, TROWS, 128),
        ]
        + [room(256, 384)] * 3
        + [room(4, 208, 768)] * 3
        + [room(3, 496, 768), room(3, 96, 640), room(3, 192, 768), room(496, 768), room(4, 96, 640)]
        + [room(*v) for v in shapes * 2]
        + [room(256, 768), room(240, 768)]
        + [sem((22,))] * 6
        + [sem((18,)), sem((18,)), sem((2,)), sem((2,)), room(4, 512, 1024), sem((4,))],
        compiler_params=params(collective_id=1, has_side_effects=True),
        cost_estimate=cost(100),
        name="conv_sync",
    )(gsum, pre, xp, sums, up_sum, wd, ffn_halves, qkv_halves)


def unpack_frames_kernel(s_ref, c0, c1, c2, c3, o_ref):
    me, li = s_ref[0], s_ref[1]
    r_i, c_i = iota2((256, 768))
    top = jnp.zeros((256, 768), f32)
    low = jnp.zeros((256, 768), f32)
    for r, chunk in enumerate((c0, c1, c2, c3)):
        base = 192 * (me ^ r)
        inside = (c_i >= base) & (c_i < base + 192)
        top += mm(chunk[:, 0:256], ((c_i - base == r_i) & inside).astype(f32).astype(bf16))
        low += mm(chunk[:, 128:384], ((c_i - base == r_i - 64) & inside).astype(f32).astype(bf16))
    o_ref[li, 0:256, :] = top.astype(bf16)
    o_ref[li, 256:384, :] = low[0:128].astype(bf16)
    slot = me * FR + lax.broadcasted_iota(jnp.int32, (128, 768), 0)
    o_ref[1 - li, 0:128, :] = jnp.where(slot < SHORT, low[128:], 0.0).astype(bf16)
    o_ref[1 - li, 128:384, :] = jnp.zeros((256, 768), bf16)


def unpack_frames(scal, chunks):
    return pl.pallas_call(
        unpack_frames_kernel,
        in_specs=[smem()] + [vmem()] * 4,
        out_specs=vmem(),
        out_shape=jax.ShapeDtypeStruct((2, FR, 768), bf16),
        compiler_params=params(),
        cost_estimate=cost(3),
        name="unpack_frames",
    )(scal, *chunks)


def kernel_out_kernel(s_ref, own_ref, other_ref, o_ref, small_ref):
    core = s_ref[2]
    for g in range(4):
        half, row = g >> 1, 96 * (g & 1)
        x = jnp.where(half == core, own_ref[0, row : row + 96], other_ref[0, row : row + 96]).astype(f32)
        for k2 in range(2):
            for b in range(16):
                o_ref[16 * k2 + b, g] = x[48 * k2 : 48 * k2 + 48, 48 * b : 48 * b + 48]

    @pl.when(pl.program_id(0) == s_ref[0])
    def _():
        for half in range(2):
            small_ref[half] = jnp.where(half == core, own_ref[0, 192:208], other_ref[0, 192:208])


def kernel_out(scal, own, other):
    return pl.pallas_call(
        kernel_out_kernel,
        grid_spec=pltpu.PrefetchScalarGridSpec(
            num_scalar_prefetch=1,
            grid=(4,),
            in_specs=[pl.BlockSpec((1, 208, 768), lambda i, s: (i ^ s[0], 0, 0))] * 2,
            out_specs=[
                pl.BlockSpec((32, 4, 48, 48), lambda i, s: (0, i, 0, 0)),
                pl.BlockSpec((2, 16, 768), lambda i, s: (0, 0, 0)),
            ],
        ),
        out_shape=[jax.ShapeDtypeStruct((32, 16, 48, 48), f32), jax.ShapeDtypeStruct((2, 16, 768), bf16)],
        compiler_params=params(),
        cost_estimate=cost(9),
        name="kernel_grad_out",
    )(scal, own, other)


def norm(v):
    center = v - jnp.mean(v, axis=-1, keepdims=True)
    scale = lax.rsqrt(jnp.mean(center * center, axis=-1, keepdims=True) + eps_norm)
    return center * scale, scale


def norm_back(e, n, scale):
    return (e - jnp.mean(e, axis=-1, keepdims=True) - n * jnp.mean(e * n, axis=-1, keepdims=True)) * scale


def ffn_kernel(
    s_ref, rows_ref, m0, m1, m2, m3, wo, wu_hbm, bu, wd_hbm, vecs, og,
    lo, ul_hbm, gu_hbm, nl, gd, gac, x0, x1, x2, x3, gst, sums,
    wu, wd, ul, gu, slope, v, gsc, mix, sems,
):
    me, li = s_ref[0], s_ref[1]
    const = FR + UNIQUE
    bo, g1, s1, bd, g2, s2 = (vecs[k : k + 1, :] for k in range(6))
    loads = [
        pltpu.make_async_copy(wu_hbm, wu, sems.at[0]),
        pltpu.make_async_copy(wd_hbm, wd, sems.at[1]),
    ]
    for load in loads:
        load.start()

    def total(x):
        return jnp.sum(x, axis=0, keepdims=True)

    for r, m in enumerate((m0, m1, m2, m3)):
        mix[pl.ds(pl.multiple_of(192 * (me ^ r), 64), 192), :] = m[...]
    out = tn(mix[...], wo[...])
    gsc[0:576, :] = rows_ref[...].astype(f32) + out[0:576] + bo
    last = gsc[const : const + 1, :]
    v[0:FR, :] = gsc[0:FR, :]
    v[FR : FR + 128, :] = jnp.where(me == 0, gsc[FR : FR + 128, :], last)
    mine = jnp.where(me == 0, 1.0, 0.0)
    keep_low = (lax.broadcasted_iota(jnp.int32, (64, 768), 0) < UNIQUE - 128).astype(f32) * mine
    v[FR + 128 : FR + 192, :] = jnp.where(keep_low > 0.5, gsc[FR + 128 : FR + 192, :], last)
    v[FR + 192 :, :] = jnp.broadcast_to(last, (192, 768))

    n1, scale1 = norm(v[...])
    v[...] = n1
    norm_one = n1 * g1 + s1
    low = norm_one.astype(bf16)
    nl[...] = low
    down = norm_one + bd
    stores = []
    loads[0].wait()
    for j in range(4):
        cols = slice(768 * j, 768 * j + 768)
        up = mm(low, wu[:, cols]) + bu[:, cols]
        cdf = gelu_parts(up)
        slope[:, cols] = cdf + up * density(up)
        act = (up * cdf).astype(bf16)
        ul[:, cols] = act
        stores.append(pltpu.make_async_copy(ul.at[:, cols], ul_hbm.at[:, cols], sems.at[2 + j]))
        stores[-1].start()
        if j == 0:
            loads[1].wait()
        down += mm(act, wd[cols, :])
    n2, scale2 = norm(down)
    result = (n2 * g2 + s2).astype(bf16)
    lo[li] = result[0:FR]
    lo[1 - li] = result[FR:]
    given = jnp.concatenate([og[li], og[1 - li]], axis=0).astype(f32)
    sums[8:9, :] = total(given * n2)
    sums[9:10, :] = total(given)
    sums[10:16, :] = jnp.zeros((6, 768), f32)
    grad_two = norm_back(given * g2, n2, scale2)
    grad_down = grad_two.astype(bf16)
    gd[...] = grad_down
    sums[7:8, :] = total(grad_down.astype(f32))
    grad_n = grad_two
    for j in range(4):
        cols = slice(768 * j, 768 * j + 768)
        grad_up = (mm_nt(grad_down, wd[cols, :]) * slope[:, cols]).astype(bf16)
        gu[:, cols] = grad_up
        stores.append(pltpu.make_async_copy(gu.at[:, cols], gu_hbm.at[:, cols], sems.at[6 + j]))
        stores[-1].start()
        sums[j : j + 1, :] = total(grad_up.astype(f32))
        grad_n += mm_nt(grad_up, wu[:, cols])
    n1 = v[...]
    sums[5:6, :] = total(grad_n * n1)
    sums[6:7, :] = total(grad_n)
    grad_one = norm_back(grad_n * g1, n1, scale1)
    grad_attn = grad_one.astype(bf16).astype(f32)
    sums[4:5, :] = total(grad_attn)

    at = lax.broadcasted_iota(jnp.int32, (64, 768), 0) == UNIQUE - 128

    def collapsed(g):
        upper = g[FR : FR + 128] * mine
        lower = g[FR + 128 : FR + 192] * keep_low
        rest = total(g[FR:]) - total(upper) - total(lower)
        return jnp.concatenate(
            [g[0:FR], upper, jnp.where(at, rest, lower), jnp.zeros((64, 768), f32)], axis=0
        )

    gac[...] = collapsed(grad_attn).astype(bf16)
    for r, out in enumerate((x0, x1, x2, x3)):
        at_r = pl.ds(pl.multiple_of(192 * (me ^ r), 64), 192)
        out[...] = mm_nt(wo[at_r, :], gac[...]).astype(bf16)
    gsc[...] = collapsed(grad_one)
    gst[...] = gsc[...].T.astype(bf16)
    for store in stores:
        store.wait()


def ffn(scal, rows, mix, wo, wu, bu, wd, vecs, og):
    sds = jax.ShapeDtypeStruct
    hbm = pl.BlockSpec(memory_space=pl.ANY)
    return pl.pallas_call(
        ffn_kernel,
        in_specs=[smem()] + [vmem()] * 6 + [hbm, vmem(), hbm, vmem(), vmem()],
        out_specs=[vmem(), hbm, hbm] + [vmem()] * 9,
        out_shape=[
            sds((2, FR, 768), bf16), sds((768, 3072), bf16), sds((768, 3072), bf16), sds((768, 768), bf16),
            sds((768, 768), bf16), sds((640, 768), bf16),
        ]
        + [sds((CH, 640), bf16)] * 4
        + [sds((768, 640), bf16), sds((16, 768), f32)],
        scratch_shapes=[
            pltpu.VMEM((768, 3072), bf16),
            pltpu.VMEM((3072, 768), bf16),
            pltpu.VMEM((768, 3072), bf16),
            pltpu.VMEM((768, 3072), bf16),
            pltpu.VMEM((768, 3072), f32),
            pltpu.VMEM((768, 768), f32),
            pltpu.VMEM((640, 768), f32),
            pltpu.VMEM((768, 640), bf16),
            pltpu.SemaphoreType.DMA((10,)),
        ],
        compiler_params=params(),
        cost_estimate=cost(28),
        name="ffn",
    )(scal, rows, *mix, wo, wu, bu, wd, vecs, og)


def tn(a, b):
    return lax.dot_general(a, b, (((0,), (0,)), ((), ())), preferred_element_type=f32)


def finish_kernel(s_ref, own1, other1, own2, other2, ownb, otherb, up, down, out, wq, wk, wv, small, a1, a2, b_ref):
    me, core = s_ref[0], s_ref[2]
    for buf, own, other in ((a1, own1, other1), (a2, own2, other2)):
        buf[core] = own[...]
        buf[1 - core] = other[...]
    b_ref[:, pl.ds(pl.multiple_of(96 * core, 32), 96), :] = ownb[...]
    b_ref[:, pl.ds(pl.multiple_of(96 - 96 * core, 32), 96), :] = otherb[...]
    for j in range(4):
        row = 192 * (j & 1)
        up[:, 768 * j : 768 * j + 768] = a1[j >> 1, row : row + 192, :].astype(f32)
    down[0:496, :] = a2[0].astype(f32)
    down[496:768, :] = a2[1, 0:272, :].astype(f32)
    out[...] = a2[1, 272:464, :].astype(f32)
    small[...] = a2[1, 464:480, :].astype(f32)
    r_i, c_i = iota2((256, 768))
    totals = [jnp.zeros((CH, 768), f32)] * 3
    for r in range(4):
        base = 192 * (me ^ r)
        inside = (c_i >= base) & (c_i < base + 192)
        at0, at64 = (((c_i - base == r_i - skip) & inside).astype(f32).astype(bf16) for skip in (0, 64))
        for k, (lane0, move) in enumerate(((0, at0), (128, at64), (384, at0))):
            totals[k] = totals[k] + mm(b_ref[r, :, lane0 : lane0 + 256], move)
    wq[...], wk[...], wv[...] = totals


def finish(scal, *parts):
    sds = jax.ShapeDtypeStruct
    return pl.pallas_call(
        finish_kernel,
        in_specs=[smem()] + [vmem()] * 6,
        out_specs=[vmem()] * 7,
        out_shape=[sds((CH, 3072), f32), sds((768, 768), f32)] + [sds((CH, 768), f32)] * 4 + [sds((16, 768), f32)],
        scratch_shapes=[
            pltpu.VMEM((2, 384, 768), bf16),
            pltpu.VMEM((2, 496, 768), bf16),
            pltpu.VMEM((4, CH, 640), bf16),
        ],
        compiler_params=params(),
        cost_estimate=cost(6),
        name="weight_grads_out",
    )(scal, *parts)


def on_device(
    frames_in, lengths, kernel, conv_bias, w_query, b_query, w_key, w_value, b_value, w_out, b_out,
    gain_one, shift_one, w_up, b_up, w_down, b_down, gain_two, shift_two, out_grad,
):
    me = lax.axis_index("wide").astype(jnp.int32)
    place_n = lax.axis_index("narrow").astype(jnp.int32)
    core, z = place_n & 1, place_n >> 1
    li = jnp.where(lengths[0] >= lengths[1], 0, 1).astype(jnp.int32)
    scal = jnp.stack([me, li, core, z])
    chunks = pack_frames(scal, frames_in)
    vec = jnp.concatenate([jnp.stack([conv_bias, b_query, b_value]), jnp.zeros((13, conv_bias.shape[0]), bf16)], axis=0)
    vecs = jnp.stack([b_out, gain_one, shift_one, b_down, gain_two, shift_two]).astype(f32)
    bu = b_up.astype(f32)[None]

    wd, pre, xp, h0, h1, h2, h3, qkv, mixed_t, lse, rows, wqkv, *mix = front_sync(
        chunks, kernel, vec, w_query, w_key, w_value
    )
    first = [h0, h1, h2, h3]
    layer_out, ul, gu, nl, gd, gac, x0, x1, x2, x3, gst, sums = ffn(
        scal, rows, mix, w_out, w_up, bu, w_down, vecs, out_grad
    )
    up_sum, ffn_halves, qkv_halves, gsum, qkv_sums = attn_sync(
        qkv, mixed_t, lse, [x0, x1, x2, x3], gst, wqkv, first, nl, gd, ul, gu, mix, gac, sums
    )
    own1, own2, ownb, ownc, other1, other2, otherb, otherc, *fchunks = conv_sync(
        gsum, pre, xp, qkv_sums, up_sum, wd, ffn_halves, qkv_halves
    )
    frames_grad = unpack_frames(scal, fchunks)
    up, down, out, wq, wk, wv, small = finish(scal, own1, other1, own2, other2, ownb, otherb)
    grad_kernel, tiny = kernel_out(scal, ownc, otherc)
    tiny = tiny.astype(f32)

    def mine(row):
        return lax.dynamic_slice_in_dim(small[row], me * CH, CH, axis=0)

    bias_grad = jnp.concatenate([tiny[0, 1, :128], tiny[1, 1, :128]]).reshape(4, 64)[:, :48].reshape(CH)
    grad_b_up = lax.dynamic_index_in_dim(small[:4], me, 0, keepdims=False)
    return (
        layer_out,
        frames_grad,
        grad_kernel,
        bias_grad,
        wq,
        tiny[0, 0, 0:192],
        wk,
        wv,
        tiny[0, 0, 512:704],
        out,
        mine(4),
        mine(5),
        mine(6),
        up,
        grad_b_up,
        down,
        mine(7),
        mine(8),
        mine(9),
    )


def with_halo(x, sides, width):
    for axis, dim in sides:
        count, length = (lax.axis_size(axis), x.shape[dim])
        up = [(i, (i + 1) % count) for i in range(count - 1)]
        down = [(j, i) for i, j in up]
        last = lax.slice_in_dim(x, length - width, length, axis=dim)
        initial = lax.slice_in_dim(x, 0, width, axis=dim)
        before = lax.ppermute(last, axis, up)
        after = lax.ppermute(initial, axis, down)
        x = jnp.concatenate([before, x, after], axis=dim)
    return x


def layer_norm(value, gain, shift):
    center = value - jnp.mean(value, axis=-1, keepdims=True)
    spread = jnp.mean(center * center, axis=-1, keepdims=True)
    return center * lax.rsqrt(spread + eps_norm) * gain + shift


def gelu_exact(value):
    return jax.nn.gelu(value, approximate=False)


def project(rows_in, weight):
    return jnp.einsum("cfd,de->cfe", rows_in, weight, preferred_element_type=jnp.float32)


def project_back(grad_in, weight):
    return jnp.einsum("cfe,de->cfd", grad_in, weight, preferred_element_type=jnp.float32)


def weight_grad(rows_in, grad_in):
    return jnp.einsum("cfd,cfe->de", rows_in, grad_in, preferred_element_type=jnp.float32)


def row_total(grad_in):
    return jnp.sum(grad_in.astype(jnp.float32), axis=(0, 1))


def head_view(rows_in):
    return rows_in.reshape(rows_in.shape[0], rows_in.shape[1], HEADS, rows_in.shape[2] // HEADS)


def conv_apply(padded, weight, frames):
    kernel_span, groups, inner_ch, outer_ch = weight.shape
    taps_weight = jnp.transpose(weight, (0, 2, 1, 3)).reshape(
        kernel_span, inner_ch, groups * outer_ch
    )
    result = lax.conv_general_dilated(
        padded,
        taps_weight,
        (1,),
        "VALID",
        dimension_numbers=("NWC", "WIO", "NWC"),
        feature_group_count=groups,
        preferred_element_type=jnp.float32,
    )
    return result[:, :frames, :]


def conv_weight_grad(padded, grad_in, kernel_shape):
    kernel_span, groups, inner_ch, outer_ch = kernel_shape
    result = lax.conv_general_dilated(
        padded,
        grad_in,
        (1,),
        "VALID",
        dimension_numbers=("CWN", "IWO", "NWC"),
        batch_group_count=groups,
        preferred_element_type=jnp.float32,
    )
    result = result[:, :kernel_span, :].reshape(inner_ch, kernel_span, groups, outer_ch)
    return jnp.transpose(result, (1, 2, 0, 3))


def key_valid_at(lengths, first_row, row_count):
    return (first_row + jnp.arange(row_count, dtype=jnp.int32))[None, :] < lengths[:, None]


def masked_scores(query_h, keys_h, valid_keys, score_scale):
    scores = (
        jnp.einsum("cqhd,ckhd->cqhk", query_h, keys_h, preferred_element_type=jnp.float32)
        * score_scale
    )
    return jnp.where(valid_keys[:, None, None, :], scores, neg_large)


def block_terms(query_h, grad_h, lse_rows, delta_rows, keys_h, values_h, valid_keys, score_scale):
    scores = masked_scores(query_h, keys_h, valid_keys, score_scale)
    probs = jnp.where(valid_keys[:, None, None, :], jnp.exp(scores - lse_rows[..., None]), 0.0)
    grad_probs = jnp.einsum("cqhd,ckhd->cqhk", grad_h, values_h, preferred_element_type=jnp.float32)
    grad_scores = (probs * (grad_probs - delta_rows[..., None])).astype(jnp.bfloat16)
    results = []
    results.append(
        jnp.einsum("cqhk,ckhd->cqhd", grad_scores, keys_h, preferred_element_type=jnp.float32)
        * score_scale
    )
    results.append(
        jnp.einsum("cqhk,cqhd->ckhd", grad_scores, query_h, preferred_element_type=jnp.float32)
        * score_scale
    )
    results.append(
        jnp.einsum(
            "cqhk,cqhd->ckhd",
            probs.astype(jnp.bfloat16),
            grad_h,
            preferred_element_type=jnp.float32,
        )
    )
    return tuple(results)


def on_device_any(
    frames_in,
    lengths,
    kernel,
    conv_bias,
    w_query,
    b_query,
    w_key,
    w_value,
    b_value,
    w_out,
    b_out,
    gain_one,
    shift_one,
    w_up,
    b_up,
    w_down,
    b_down,
    gain_two,
    shift_two,
    out_grad,
):
    clip_count, frames, width = frames_in.shape
    head_dim = width // HEADS
    score_scale = head_dim ** (-0.5)
    half_span = kernel.shape[0] // 2
    wide_size = lax.axis_size("wide")
    positions = lax.axis_index("wide") * frames + jnp.arange(frames, dtype=jnp.int32)
    frame_valid = positions[None, :] < lengths[:, None]
    masked = jnp.where(frame_valid[..., None], frames_in, jnp.zeros((), jnp.bfloat16))
    padded = with_halo(masked, (("wide", 1),), half_span)
    pre_act = conv_apply(padded, kernel, frames) + conv_bias.astype(jnp.float32)
    first_act, pull_first = jax.vjp(gelu_exact, pre_act)
    first_out = masked.astype(jnp.float32) + first_act
    first_low = first_out.astype(jnp.bfloat16)
    query_rows = (project(first_low, w_query) + b_query.astype(jnp.float32)).astype(jnp.bfloat16)
    key_rows = project(first_low, w_key).astype(jnp.bfloat16)
    value_rows = (project(first_low, w_value) + b_value.astype(jnp.float32)).astype(jnp.bfloat16)
    query_h = head_view(query_rows)
    per_step = max(1, min(wide_size, 512 // frames))
    while wide_size % per_step:
        per_step -= 1
    run_max = jnp.full((clip_count, frames, HEADS), neg_large, jnp.float32)
    run_acc = jnp.zeros((clip_count, frames, HEADS, head_dim), jnp.float32)
    keys_p = lax.all_gather(key_rows, "wide", axis=1, tiled=True)
    values_p = lax.all_gather(value_rows, "wide", axis=1, tiled=True)
    row_count = keys_p.shape[1]
    valid_keys = key_valid_at(lengths, jnp.int32(0), row_count)
    scores = masked_scores(query_h, head_view(keys_p), valid_keys, score_scale)
    new_max = jnp.maximum(run_max, jnp.max(scores, axis=-1))
    weights = jnp.where(valid_keys[:, None, None, :], jnp.exp(scores - new_max[..., None]), 0.0)
    factor = jnp.exp(run_max - new_max)
    run_sum = jnp.sum(weights, axis=-1)
    run_acc = run_acc * factor[..., None] + jnp.einsum(
        "cqhk,ckhd->cqhd",
        weights.astype(jnp.bfloat16),
        head_view(values_p),
        preferred_element_type=jnp.float32,
    )
    run_max, run_sum, run_acc = (new_max, run_sum, run_acc)
    lse_rows = run_max + jnp.log(run_sum)
    mixed_heads = run_acc / run_sum[..., None]
    mixed_low = mixed_heads.reshape(clip_count, frames, width).astype(jnp.bfloat16)
    attn_out = project(mixed_low, w_out) + b_out.astype(jnp.float32)
    sum_one = first_out + attn_out
    norm_one, pull_one = jax.vjp(
        layer_norm, sum_one, gain_one.astype(jnp.float32), shift_one.astype(jnp.float32)
    )
    norm_low = norm_one.astype(jnp.bfloat16)
    up_pre = project(norm_low, w_up) + b_up.astype(jnp.float32)
    up_act, pull_up = jax.vjp(gelu_exact, up_pre)
    up_low = up_act.astype(jnp.bfloat16)
    down_out = project(up_low, w_down) + b_down.astype(jnp.float32)
    sum_two = norm_one + down_out
    layer_out, pull_two = jax.vjp(
        layer_norm, sum_two, gain_two.astype(jnp.float32), shift_two.astype(jnp.float32)
    )
    grad_sum_two, grad_gain_two, grad_shift_two = pull_two(out_grad.astype(jnp.float32))
    grad_down = grad_sum_two.astype(jnp.bfloat16)
    grad_w_down = weight_grad(up_low, grad_down)
    grad_b_down = row_total(grad_down)
    grad_up = pull_up(project_back(grad_down, w_down))[0].astype(jnp.bfloat16)
    grad_w_up = weight_grad(norm_low, grad_up)
    grad_b_up = row_total(grad_up)
    grad_norm_one = grad_sum_two + project_back(grad_up, w_up)
    grad_sum_one, grad_gain_one, grad_shift_one = pull_one(grad_norm_one)
    grad_attn = grad_sum_one.astype(jnp.bfloat16)
    grad_w_out = weight_grad(mixed_low, grad_attn)
    grad_b_out = row_total(grad_attn)
    grad_mixed = project_back(grad_attn, w_out).astype(jnp.bfloat16)
    grad_h = head_view(grad_mixed)
    delta_rows = jnp.sum(grad_h.astype(jnp.float32) * mixed_heads, axis=-1)
    total_slots = wide_size * frames
    first_row = jnp.int32(0)
    grad_q = jnp.zeros((clip_count, frames, HEADS, head_dim), jnp.float32)
    grad_k_all = jnp.zeros((clip_count, total_slots, width), jnp.float32)
    grad_v_all = jnp.zeros((clip_count, total_slots, width), jnp.float32)
    keys_p = lax.all_gather(key_rows, "wide", axis=1, tiled=True)
    values_p = lax.all_gather(value_rows, "wide", axis=1, tiled=True)
    row_count = keys_p.shape[1]
    valid_keys = key_valid_at(lengths, first_row, row_count)
    part_q, part_k, part_v = block_terms(
        query_h,
        grad_h,
        lse_rows,
        delta_rows,
        head_view(keys_p),
        head_view(values_p),
        valid_keys,
        score_scale,
    )
    old_k = lax.dynamic_slice_in_dim(grad_k_all, first_row, row_count, 1)
    old_v = lax.dynamic_slice_in_dim(grad_v_all, first_row, row_count, 1)
    grad_k_all = lax.dynamic_update_slice_in_dim(
        grad_k_all, old_k + part_k.reshape(clip_count, row_count, width), first_row, 1
    )
    grad_v_all = lax.dynamic_update_slice_in_dim(
        grad_v_all, old_v + part_v.reshape(clip_count, row_count, width), first_row, 1
    )
    grad_k_own, grad_v_own = (
        lax.psum_scatter(
            grad_k_all.astype(jnp.bfloat16), "wide", scatter_dimension=1, tiled=True
        ).astype(jnp.float32),
        lax.psum_scatter(
            grad_v_all.astype(jnp.bfloat16), "wide", scatter_dimension=1, tiled=True
        ).astype(jnp.float32),
    )
    grad_q_low = (grad_q + part_q).reshape(clip_count, frames, width).astype(jnp.bfloat16)
    grad_k_low = grad_k_own.astype(jnp.bfloat16)
    grad_v_low = grad_v_own.astype(jnp.bfloat16)
    grad_w_query = weight_grad(first_low, grad_q_low)
    grad_b_query = row_total(grad_q_low)
    grad_w_key = weight_grad(first_low, grad_k_low)
    grad_w_value = weight_grad(first_low, grad_v_low)
    grad_b_value = row_total(grad_v_low)
    grad_first = (
        grad_sum_one
        + project_back(grad_q_low, w_query)
        + project_back(grad_k_low, w_key)
        + project_back(grad_v_low, w_value)
    )
    grad_pre = pull_first(grad_first)[0].astype(jnp.bfloat16)
    grad_conv_bias = row_total(grad_pre)
    grad_kernel = conv_weight_grad(padded, grad_pre, kernel.shape)
    grad_padded = with_halo(grad_pre, (("wide", 1),), half_span)
    flipped = jnp.transpose(kernel[::-1], (0, 1, 3, 2))
    grad_masked = grad_first + conv_apply(grad_padded[:, 1:], flipped, frames)
    frames_grad = jnp.where(frame_valid[..., None], grad_masked, 0.0).astype(jnp.bfloat16)
    shards = (
        lax.psum_scatter(
            grad_kernel.astype(jnp.bfloat16), "wide", scatter_dimension=0, tiled=True
        ).astype(jnp.float32),
        lax.psum_scatter(
            grad_conv_bias.astype(jnp.bfloat16), "wide", scatter_dimension=0, tiled=True
        ).astype(jnp.float32),
        lax.psum_scatter(
            grad_w_query.astype(jnp.bfloat16), "wide", scatter_dimension=0, tiled=True
        ).astype(jnp.float32),
        lax.psum_scatter(
            grad_b_query.astype(jnp.bfloat16), "wide", scatter_dimension=0, tiled=True
        ).astype(jnp.float32),
        lax.psum_scatter(
            grad_w_key.astype(jnp.bfloat16), "wide", scatter_dimension=0, tiled=True
        ).astype(jnp.float32),
        lax.psum_scatter(
            grad_w_value.astype(jnp.bfloat16), "wide", scatter_dimension=0, tiled=True
        ).astype(jnp.float32),
        lax.psum_scatter(
            grad_b_value.astype(jnp.bfloat16), "wide", scatter_dimension=0, tiled=True
        ).astype(jnp.float32),
        lax.psum_scatter(
            grad_w_out.astype(jnp.bfloat16), "wide", scatter_dimension=0, tiled=True
        ).astype(jnp.float32),
        lax.psum_scatter(
            grad_b_out.astype(jnp.bfloat16), "wide", scatter_dimension=0, tiled=True
        ).astype(jnp.float32),
        lax.psum_scatter(
            grad_gain_one.astype(jnp.bfloat16), "wide", scatter_dimension=0, tiled=True
        ).astype(jnp.float32),
        lax.psum_scatter(
            grad_shift_one.astype(jnp.bfloat16), "wide", scatter_dimension=0, tiled=True
        ).astype(jnp.float32),
        lax.psum_scatter(
            grad_w_up.astype(jnp.bfloat16), "wide", scatter_dimension=0, tiled=True
        ).astype(jnp.float32),
        lax.psum_scatter(
            grad_b_up.astype(jnp.bfloat16), "wide", scatter_dimension=0, tiled=True
        ).astype(jnp.float32),
        lax.psum_scatter(
            grad_w_down.astype(jnp.bfloat16), "wide", scatter_dimension=0, tiled=True
        ).astype(jnp.float32),
        lax.psum_scatter(
            grad_b_down.astype(jnp.bfloat16), "wide", scatter_dimension=0, tiled=True
        ).astype(jnp.float32),
        lax.psum_scatter(
            grad_gain_two.astype(jnp.bfloat16), "wide", scatter_dimension=0, tiled=True
        ).astype(jnp.float32),
        lax.psum_scatter(
            grad_shift_two.astype(jnp.bfloat16), "wide", scatter_dimension=0, tiled=True
        ).astype(jnp.float32),
    )
    totals = (
        lax.psum(shards[0].astype(jnp.bfloat16), "narrow").astype(jnp.float32),
        lax.psum(shards[1].astype(jnp.bfloat16), "narrow").astype(jnp.float32),
        lax.psum(shards[2].astype(jnp.bfloat16), "narrow").astype(jnp.float32),
        lax.psum(shards[3].astype(jnp.bfloat16), "narrow").astype(jnp.float32),
        lax.psum(shards[4].astype(jnp.bfloat16), "narrow").astype(jnp.float32),
        lax.psum(shards[5].astype(jnp.bfloat16), "narrow").astype(jnp.float32),
        lax.psum(shards[6].astype(jnp.bfloat16), "narrow").astype(jnp.float32),
        lax.psum(shards[7].astype(jnp.bfloat16), "narrow").astype(jnp.float32),
        lax.psum(shards[8].astype(jnp.bfloat16), "narrow").astype(jnp.float32),
        lax.psum(shards[9].astype(jnp.bfloat16), "narrow").astype(jnp.float32),
        lax.psum(shards[10].astype(jnp.bfloat16), "narrow").astype(jnp.float32),
        lax.psum(shards[11].astype(jnp.bfloat16), "narrow").astype(jnp.float32),
        lax.psum(shards[12].astype(jnp.bfloat16), "narrow").astype(jnp.float32),
        lax.psum(shards[13].astype(jnp.bfloat16), "narrow").astype(jnp.float32),
        lax.psum(shards[14].astype(jnp.bfloat16), "narrow").astype(jnp.float32),
        lax.psum(shards[15].astype(jnp.bfloat16), "narrow").astype(jnp.float32),
        lax.psum(shards[16].astype(jnp.bfloat16), "narrow").astype(jnp.float32),
    )
    return (
        layer_out.astype(jnp.bfloat16),
        frames_grad,
        totals[0],
        totals[1],
        totals[2],
        totals[3],
        totals[4],
        totals[5],
        totals[6],
        totals[7],
        totals[8],
        totals[9],
        totals[10],
        totals[11],
        totals[12],
        totals[13],
        totals[14],
        totals[15],
        totals[16],
    )


def solution(mesh):
    rows = P("narrow", "wide", None)
    placed = (rows, P("narrow")) + (P(),) * 17 + (rows,)
    wide = mesh.shape["wide"]
    fast = wide == 4 and mesh.shape["narrow"] == 8
    return jax.shard_map(
        on_device if fast else on_device_any,
        mesh=mesh,
        in_specs=placed,
        out_specs=(rows, rows)
        + (P("wide", None, None, None), P("wide"), P("wide", None), P("wide"), P("wide", None), P("wide", None))
        + (P("wide"), P("wide", None), P("wide"), P("wide"), P("wide"), P("wide", None), P("wide"))
        + (P("wide", None), P("wide"), P("wide"), P("wide")),
        check_vma=False,
    )
```

```python
import functools

import jax
import jax.numpy as jnp
from jax import lax
from jax.experimental import pallas as pl
from jax.experimental.pallas import tpu as pltpu
from jax.sharding import PartitionSpec as P

HEADS = 12
GROUP_CH = 48
SHORT = 102
HALF = 64
UNIQUE = SHORT + HALF
FR = 384
SLOTS = 1536
SROWS = 192
TROWS = 1792
SBASE = 1600
CH = 192
eps_norm = 1e-05
neg_large = -1e30
bf16 = jnp.bfloat16
f32 = jnp.float32
QF = 1536
QB = 768
KB = 512
CB = 1792
VLIM = 60 * 1024 * 1024


def mm(a, b):
    return jnp.dot(a, b, preferred_element_type=f32)


def mm_nt(a, b):
    return lax.dot_general(a, b, (((1,), (1,)), ((), ())), preferred_element_type=f32)


def iota2(shape):
    return lax.broadcasted_iota(jnp.int32, shape, 0), lax.broadcasted_iota(jnp.int32, shape, 1)


def place(shape, rows_from, rows_to, cols_from):
    r, c = iota2(shape)
    hit = (c - cols_from == r - rows_from) & (r >= rows_from) & (r < rows_to)
    return hit.astype(f32).astype(bf16)


def spread(shape, lane0, start):
    r, c = iota2(shape)
    slot, inner = c >> 6, c & 63
    hit = (r == lane0 + start + slot * GROUP_CH + inner) & (inner < GROUP_CH)
    return hit.astype(f32).astype(bf16)


def gather_slots(shape, col0):
    r, c = iota2(shape)
    slot, inner = r >> 6, r & 63
    hit = (c == col0 + slot * GROUP_CH + inner) & (inner < GROUP_CH)
    return hit.astype(f32).astype(bf16)


def full(shape):
    return pl.BlockSpec(shape, lambda *_: (0,) * len(shape))


def smem():
    return pl.BlockSpec(memory_space=pltpu.SMEM)


def vmem():
    return pl.BlockSpec(memory_space=pltpu.VMEM)


def params(**kw):
    return pltpu.CompilerParams(vmem_limit_bytes=VLIM, **kw)


def cost(us):
    return pl.CostEstimate(flops=int(us * 1e9), bytes_accessed=int(us * 3.4e6), transcendentals=0)


def put(keeping, keep, send, rel, row0, data, lane0=0):
    rows, lanes = data.shape

    @pl.when(keeping)
    def _():
        keep[rel, row0 : row0 + rows, lane0 : lane0 + lanes] = data

    @pl.when(jnp.logical_not(keeping))
    def _():
        send[rel, row0 : row0 + rows, lane0 : lane0 + lanes] = data


def xor2(a, b):
    return (a + b) % 2 + 2 * ((a // 2 + b // 2) % 2)


def gelu_parts(v):
    cdf = 0.5 * (1.0 + lax.erf(v * (2.0 ** -0.5)))
    return cdf


def density(v):
    return jnp.exp(-0.5 * v * v) * 0.3989422804014327


def pack_frames_kernel(s_ref, x_ref, *outs):
    me, li = s_ref[0], s_ref[1]
    long, short = x_ref[li], x_ref[1 - li]
    slot = me * FR + lax.broadcasted_iota(jnp.int32, (128, 768), 0)
    short = jnp.where(slot < SHORT, short[:128].astype(f32), 0.0).astype(bf16)
    top = long[:256]
    low = jnp.concatenate([long[256:], short], axis=0)
    for d in range(4):
        first = 192 * d - (64 if d % 2 else 0)
        skip = 64 if d % 2 else 0
        chunk = mm(top[:, first : first + 256], place((256, 384), skip, skip + 192, 0)) + mm(
            low[:, first : first + 256], place((256, 384), skip, skip + 192, 192)
        )
        chunk = chunk.astype(bf16)
        for r in range(4):

            @pl.when((me ^ d) == r)
            def _():
                outs[r][...] = chunk


def pack_frames(scal, frames_in):
    return pl.pallas_call(
        pack_frames_kernel,
        out_shape=[jax.ShapeDtypeStruct((256, 384), bf16)] * 4,
        in_specs=[smem(), vmem()],
        out_specs=[vmem()] * 4,
        compiler_params=params(),
        cost_estimate=cost(3),
        name="pack_frames",
    )(scal, frames_in)


def prep_group(w_ref, wt_ref, wd_ref, z_ref, taps):
    left, right = place((48, 128), 0, 48, 0), place((48, 128), 0, 48, 64)
    wt_ref[...] = jnp.zeros_like(wt_ref)
    for i in range(48):
        taps[pl.ds(i, 128, stride=48), 0:48] = w_ref[i].astype(f32).T

    def rows(k, n):
        return taps[48 * k : 48 * (k + n), 0:48].astype(bf16)

    for k2 in range(8):
        pairs = rows(16 * k2, 16).reshape(8, 2, 48, 48)
        tile = mm(pairs[:, 0].reshape(384, 48), left) + mm(pairs[:, 1].reshape(384, 48), right)
        tile = tile.astype(bf16)
        for p in range(8):
            wt_ref[64 * k2 : 64 * k2 + 48, 128 * p : 128 * p + 128] = tile[48 * p : 48 * p + 48]
    for q in range(4):
        tile = mm(rows(112 - 32 * q, 16), left) + mm(rows(96 - 32 * q, 16), right)
        for b in range(16):
            z_ref[64 * b : 64 * b + 48, :] = tile[48 * (15 - b) : 48 * (15 - b) + 48]
        wd_ref[128 * q : 128 * q + 128, :] = z_ref[...].T.astype(bf16)


def pair_slots(t_ref, rows, groups=(0, 1)):
    wide = jnp.concatenate([t_ref[0:rows, :], t_ref[16 : rows + 16, :]], axis=1)
    r, c = iota2((256, 128))
    out = []
    for j in groups:
        hit = ((r < 128) & (c == r - 64 * j) & (c < 64)) | ((r >= 128) & (c - 64 == r - 128 - 64 * j) & (c >= 64))
        out.append(mm(wide, hit.astype(f32).astype(bf16)).astype(bf16))
    return out


def conv_block(p_refs, w_ref, y_ref, s_ref, shift, n0=0, rows=CB):
    lane = lax.broadcasted_iota(jnp.int32, (rows, 128), 1)
    parts = []
    for j in range(2):
        lhs = jnp.concatenate([p_refs[j][n0 + 32 * q : n0 + 32 * q + rows + 16, :] for q in range(4)], axis=1)
        y_ref[0 : rows + 16] = mm(lhs, w_ref[j])
        total = y_ref[shift : shift + rows + 1, 0:128]
        for p in range(1, 8):
            total += y_ref[shift + 2 * p : shift + 2 * p + rows + 1, 128 * p : 128 * p + 128]
        s_ref[0 : rows + 1, :] = total
        here, after = s_ref[0:rows, :], s_ref[1 : rows + 1, :]
        if j == 0:
            parts.append(here + pltpu.roll(after, 64, 1))
        else:
            parts.append(pltpu.roll(here, 64, 1) + after)
    return jnp.where(lane < 64, parts[0], parts[1])


def front_sync_kernel(
    p0, p1, p2, p3, k_hbm, vec, wq, wk, wv,
    wd_out, pre_out, xp_out, h0_out, h1_out, h2_out, h3_out, qkv_out, ot, lse_ref, rows_ref, w_own, m0, m1, m2, m3,
    wd, pre_ref, xp, h0, h1, h2, h3, qkv, store_s, kg, load_s, wt, taps, zt, rf, slots, y_ref, t_ref, first, wz, vt, o1, o2, o3, frame_s, frame_r, gat_s, gat_r, mix_s, mix_r,
):
    n, me = lax.axis_index("narrow"), lax.axis_index("wide")
    barrier = pltpu.get_barrier_semaphore()

    def device(r):
        return (n, xor2(me, r))

    for r in range(1, 4):
        pl.semaphore_signal(barrier, inc=1, device_id=device(r), device_id_type=pl.DeviceIdType.MESH)
    load = pltpu.make_async_copy(k_hbm.at[pl.ds(4 * me, 4)], kg, load_s)
    load.start()
    pl.semaphore_wait(barrier, 3)

    def copy(r, src, dst, send, recv):
        return pltpu.make_async_remote_copy(
            src_ref=src, dst_ref=dst, send_sem=send, recv_sem=recv, device_id=device(r),
            device_id_type=pl.DeviceIdType.MESH,
        )

    stores = [
        pltpu.make_async_copy(src, dst, store_s.at[i])
        for i, (src, dst) in enumerate(
            ((wd, wd_out), (pre_ref, pre_out), (xp, xp_out), (h0, h0_out), (h1, h1_out), (h2, h2_out), (h3, h3_out),
             (qkv, qkv_out))
        )
    ]
    frames = [copy(r, (p1, p2, p3)[r - 1], rf.at[r - 1], frame_s.at[r - 1], frame_r.at[r - 1]) for r in (3, 1, 2)]
    for c in frames:
        c.start()

    zt[...] = jnp.zeros_like(zt)
    load.wait()

    def prep(g, carry):
        prep_group(kg.at[g], wt.at[g], wd.at[g], zt, taps)
        return carry

    lax.fori_loop(0, 4, prep, 0)
    r_i, c_i = iota2((768, 256))
    pick = ((r_i == 192 * me + c_i) & (c_i < 192)).astype(f32).astype(bf16)
    for k, w in enumerate((wq, wk, wv)):
        w_own[:, 256 * k : 256 * k + 256] = mm(w[...], pick).astype(bf16)
    own_vec = mm(vec[...], pick)
    bias_qkv = jnp.concatenate([own_vec[1:2], jnp.zeros((1, 256), f32), own_vec[2:3]], axis=1)
    bias = [mm(vec[...], spread((768, 128), 0, 192 * me + 96 * c))[0:1] for c in range(2)]
    wz[:, 0:64, :] = jnp.zeros((4, 64, 768), bf16)
    wz[:, 256:320, :] = jnp.zeros((4, 64, 768), bf16)
    for r in range(4):
        wz[r, 64:256, :] = w_own[pl.ds(pl.multiple_of(192 * xor2(me, r), 64), 192), :]

    for c in frames:
        c.wait()
    stores[0].start()
    for c in range(2):
        xp[c, 0:64, :] = jnp.zeros((64, 128), bf16)
        xp[c, 1600:1664, :] = jnp.zeros((64, 128), bf16)
        xp[c, 1792:1936, :] = jnp.zeros((144, 128), bf16)
        top_map, low_map = spread((256, 128), 0, 96 * c), spread((256, 128), 64, 96 * c)
        short = jnp.zeros((128, 128), f32)
        for r in range(4):
            src = xor2(me, r)
            chunk = p0 if r == 0 else rf.at[r - 1]
            low = mm(chunk[:, 128:384], low_map)
            base = pl.multiple_of(64 + FR * src, 64)
            xp[c, pl.ds(base, 256), :] = mm(chunk[:, 0:256], top_map).astype(bf16)
            xp[c, pl.ds(pl.multiple_of(base + 256, 64), 128), :] = low[:128].astype(bf16)
            short += jnp.where(src == 0, low[128:], 0.0)
        xp[c, 1664:1792, :] = short.astype(bf16)
        a, b = pair_slots(xp.at[c], 1920)
        slots[2 * c] = a
        slots[2 * c + 1] = b

    left, right = gather_slots((256, 384), 0), gather_slots((256, 384), 192)

    def rows_of(lo, rows):
        return jnp.concatenate([first[0, lo : lo + rows, :], first[1, lo : lo + rows, :]], axis=1)

    held = (h0, h1, h2, h3)
    spans = [(0, 384), (384, 384), (768, 96)]

    def direct(i, r):
        at = pl.ds(*spans[i])
        return copy(r, h0.at[at], held[r].at[at], gat_s.at[4 * i + r - 1], gat_r.at[4 * i + r - 1])

    def relay(i, r):
        row, rows = spans[i]
        at = pl.ds(row, rows // 2) if r == 1 else pl.ds(row + rows // 2, rows // 2)
        sem = 4 * i + 1 + r
        return copy(3 - r, held[r].at[at], h3.at[at], gat_s.at[sem], gat_r.at[sem])

    def conv(block):
        n0 = 896 * block
        for c in range(2):
            pre = conv_block((slots.at[2 * c], slots.at[2 * c + 1]), wt.at[2 * c : 2 * c + 2], y_ref, t_ref, 0, n0, 896)
            pre = pre + bias[c]
            pre_ref[c, n0 : n0 + 896, :] = pre
            center = xp[c, 64 + n0 : 64 + n0 + 896, :].astype(f32)
            first[c, n0 : n0 + 896, :] = (center + pre * gelu_parts(pre)).astype(bf16)

    def pack(row, lo, rows):
        h0[row : row + rows, :] = (mm(rows_of(lo, rows), left) + mm(rows_of(lo + rows, rows), right)).astype(bf16)

    conv(0)
    pack(0, 0, 384)
    for r in (1, 2):
        direct(0, r).start()
    conv(1)
    pack(384, 768, 384)
    pack(768, SBASE, 96)
    for i in (1, 2):
        for r in (1, 2):
            direct(i, r).start()
    for i in (1, 2, 3):
        stores[i].start()
    for i in range(3):
        for r in (1, 2):
            direct(i, r).wait()
            relay(i, r).start()
    for i in range(3):
        for r in (1, 2):
            relay(i, r).wait()
    for i in (4, 5, 6):
        stores[i].start()

    def project(row, rows, half):
        row0 = 64 * (1 - half)
        total = bias_qkv + jnp.zeros((rows, 768), f32)
        for r in range(4):
            total += mm(held[r][row : row + rows, 128 * half : 128 * half + 256], wz[r, row0 : row0 + 256, :])
        return total.astype(bf16)

    for half in range(2):
        qkv[384 * half : 384 * half + 384, :] = project(0, 384, half)
        qkv[768 + 384 * half : 1152 + 384 * half, :] = project(384, 384, half)
        qkv[SLOTS + 96 * half : SLOTS + 96 * half + 96, :] = project(768, 96, half)
    qkv[SLOTS + SROWS : TROWS, :] = jnp.zeros((TROWS - SLOTS - SROWS, 768), bf16)
    stores[7].start()
    vt[...] = qkv[:, 512:704].astype(f32).T.astype(bf16)

    outs = (m0, o1, o2, o3)
    lse_ref[...] = jnp.zeros_like(lse_ref)
    sent = []
    for h in range(3):
        cols = slice(64 * h, 64 * h + 64)

        def attend(q0, queries, key0, keys, masked):
            query = (qkv[q0 : q0 + queries, 0:256][:, cols].astype(f32) * 0.125).astype(bf16)
            key = qkv[key0 : key0 + keys, 256:512][:, cols]
            scores = mm_nt(key, query)
            if masked:
                slot = lax.broadcasted_iota(jnp.int32, scores.shape, 0)
                scores = jnp.where(slot < SHORT, scores, neg_large)
            top = jnp.max(scores, axis=0, keepdims=True)
            weights = jnp.exp(scores - top)
            total = jnp.sum(weights, axis=0, keepdims=True)
            out = mm(vt[cols, key0 : key0 + keys], weights.astype(bf16))
            ot[cols, q0 : q0 + queries] = out / total
            lse_ref[h : h + 1, q0 : q0 + queries] = top + jnp.log(total)

        for q0 in range(0, SLOTS, QF):
            attend(q0, QF, 0, SLOTS, False)
        attend(SLOTS, 256, SLOTS, 128, True)
        for r in (3, 1, 2, 0):
            src = pl.multiple_of(FR * xor2(me, r), 128)
            outs[r][cols, 0:FR] = ot[cols, pl.ds(src, FR)].astype(bf16)
            outs[r][cols, FR:640] = ot[cols, SLOTS:TROWS].astype(bf16)
            if r:
                at = pl.ds(64 * h, 64)
                sem = 3 * h + r - 1
                c = copy(r, outs[r].at[at], (m1, m2, m3)[r - 1].at[at], mix_s.at[sem], mix_r.at[sem])
                c.start()
                sent.append(c)

    start = pl.multiple_of(FR * (me // 2), 128)
    lane0 = pl.multiple_of(128 * (me % 2), 128)
    r_i, c_i = iota2((256, 768))
    own = jnp.zeros((FR, 768), f32)
    extra0 = jnp.zeros((96, 768), f32)
    extra1 = jnp.zeros((96, 768), f32)
    for r in range(4):
        base = 192 * xor2(me, r)
        inside = (c_i >= base) & (c_i < base + 192)
        sel0 = ((c_i - base == r_i) & inside).astype(f32).astype(bf16)
        sel1 = ((c_i - base == r_i - 64) & inside).astype(f32).astype(bf16)
        own += mm(held[r][pl.ds(start, FR), pl.ds(lane0, 256)], jnp.where(me % 2 == 0, sel0, sel1))
        extra0 += mm(held[r][768:864, 0:256], sel0)
        extra1 += mm(held[r][768:864, 128:384], sel1)
    rows_ref[0:FR, :] = own.astype(bf16)
    rows_ref[FR : FR + 96, :] = extra0.astype(bf16)
    rows_ref[FR + 96 : FR + 192, :] = extra1.astype(bf16)
    for c in sent + stores:
        c.wait()


def front_sync(chunks, kernel, vec, wq, wk, wv):
    sds = jax.ShapeDtypeStruct
    sem = pltpu.SemaphoreType.DMA
    room = lambda *shape: pltpu.VMEM(shape, bf16)
    return pl.pallas_call(
        front_sync_kernel,
        in_specs=[vmem()] * 4 + [pl.BlockSpec(memory_space=pl.ANY)] + [vmem()] * 4,
        out_specs=[pl.BlockSpec(memory_space=pl.ANY)] * 8 + [vmem()] * 8,
        out_shape=[sds((4, 512, 1024), bf16), sds((2, TROWS, 128), f32), sds((2, 1936, 128), bf16)]
        + [sds((864, 384), bf16)] * 4
        + [sds((TROWS, 768), bf16), sds((CH, TROWS), f32), sds((8, TROWS), f32), sds((576, 768), bf16)]
        + [sds((768, 768), bf16)]
        + [sds((CH, 640), bf16)] * 4,
        scratch_shapes=[
            room(4, 512, 1024),
            pltpu.VMEM((2, TROWS, 128), f32),
            room(2, 1936, 128),
            room(864, 384),
            room(864, 384),
            room(864, 384),
            room(864, 384),
            room(TROWS, 768),
            sem((8,)),
            room(4, 48, 48, 128),
            sem,
            room(4, 512, 1024),
            pltpu.VMEM((48 * 128, 128), f32),
            pltpu.VMEM((1024, 128), f32),
            room(3, 256, 384),
            room(4, 1920, 128),
            pltpu.VMEM((912, 1024), f32),
            pltpu.VMEM((904, 128), f32),
            room(2, TROWS, 128),
            room(4, 320, 768),
            room(CH, TROWS),
        ]
        + [room(CH, 640)] * 3
        + [sem((3,)), sem((3,)), sem((12,)), sem((12,)), sem((9,)), sem((9,))],
        compiler_params=params(collective_id=3, has_side_effects=True),
        cost_estimate=cost(65),
        name="front_sync",
    )(*chunks, jnp.transpose(kernel, (1, 2, 3, 0)), vec, wq, wk, wv)


class Line:
    def __init__(self, place, x, e, y, f, o, ss, so, re, rr, sc, rcv, ready=()):
        self.n, self.me = place
        self.ready = ready
        self.z, self.core = self.n // 2, self.n % 2
        self.x, self.e, self.y, self.f, self.o = x, e, y, f, o
        self.ss, self.so, self.re, self.rr, self.sc, self.rcv = ss, so, re, rr, sc, rcv

    def copy(self, src, dst, send, recv, z, core=None):
        return pltpu.make_async_remote_copy(
            src_ref=src, dst_ref=dst, send_sem=send, recv_sem=recv,
            device_id=(2 * z + (self.core if core is None else core), self.me), device_id_type=pl.DeviceIdType.MESH,
        )

    def first(self, k, here):
        return k % 2 == (0 if here == 1 else 1)

    def swap(self, k):
        return self.copy(self.f[k], self.o[k], self.sc.at[k], self.rcv.at[k], self.z, 1 - self.core)

    def inward(self, k, here):
        return self.copy(self.x[k], self.e[k], self.ss.at[k], self.re.at[k], 1 if here == 0 else 2)

    def across(self, k, here):
        src = self.y[k] if self.first(k, here) else self.f[k]
        return self.copy(src, src, self.ss.at[k], self.rr.at[k], 3 - here)

    def outward(self, k, here):
        return self.copy(self.f[k], self.f[k], self.so.at[k], self.rr.at[k], 0 if here == 1 else 3)

    def at_ends(self, do):
        pl.when(self.z == 0)(lambda: do(0))
        pl.when(self.z == 3)(lambda: do(3))

    def at_inner(self, do):
        pl.when(self.z == 1)(lambda: do(1))
        pl.when(self.z == 2)(lambda: do(2))

    def begin(self, ks):
        def do(here):
            for k in ks:
                self.inward(k, here).start()

        self.at_ends(do)

    def part(self, k):
        own = self.x[k][...].astype(f32)
        return own if k in self.ready else own + self.e[k][...].astype(f32)

    def meet(self, ks, here):
        for k in ks:
            if k not in self.ready:
                self.inward(k, here).wait_recv()
            if self.first(k, here):
                self.y[k][...] = self.part(k).astype(bf16)
                self.across(k, here).start()

    def close(self, ks, here):
        for k in ks:
            if not self.first(k, here):
                self.across(k, here).wait_recv()
                self.f[k][...] = (self.part(k) + self.y[k][...].astype(f32)).astype(bf16)
                self.across(k, here).start()
                self.outward(k, here).start()
                self.swap(k).start()

    def pass_on(self, ks, here):
        for k in ks:
            if self.first(k, here):
                self.across(k, here).wait_recv()
                self.outward(k, here).start()
                self.swap(k).start()

    def settle(self, here):
        for k in range(len(self.x)):
            self.across(k, here).wait_send()
            self.outward(k, here).wait_send()
            self.swap(k).wait()

    def receive(self, here):
        count = len(self.x)
        for k in range(count):
            self.copy(self.f[k], self.f[k], self.so.at[k], self.rr.at[k], self.z).wait_recv()
            self.swap(k).start()
        for k in range(count):
            if k not in self.ready:
                self.inward(k, here).wait_send()
            self.swap(k).wait()

    def greet(self, barrier, peers):
        self.signal_all(barrier, peers)
        self.wait_all(barrier, len(peers))

    def signal_all(self, barrier, peers):
        def signal(device):
            pl.semaphore_signal(barrier, inc=1, device_id=device, device_id_type=pl.DeviceIdType.MESH)

        for peer in peers + [(2 * self.z + 1 - self.core, self.me)]:
            signal(peer)

        @pl.when(self.z > 0)
        def _():
            signal((2 * self.z - 2 + self.core, self.me))

        @pl.when(self.z < 3)
        def _():
            signal((2 * self.z + 2 + self.core, self.me))

    def wait_all(self, barrier, peers):
        pl.semaphore_wait(barrier, peers + 1 + jnp.minimum(self.z, 1) + jnp.minimum(3 - self.z, 1))


def attn_sync_kernel(
    qkv_hbm, ot_hbm, lse_ref, d0, d1, d2, d3, gst, w_hbm, h0, h1, h2, h3,
    nl, gd, ul_hbm, gu_hbm, m0, m1, m2, m3, gac, sums,
    a1_out, a2_out, b_out, g_out, qsums,
    ring, load_s, dot_, do_, kt, delta, dqt, dk, dv, dqkv, keep1, send1, got1, keep2, send2, got2,
    bkeep, bsend, bgot, ra, rd, g0, g1, g2, g3, rg, core_s, core_r, wide_s, wide_r, qkv_ref, ot_ref, w_ref, held,
    xu, eu, z_s, z_r,
):
    n, me = lax.axis_index("narrow"), lax.axis_index("wide")
    core = n % 2
    other = n + 1 - 2 * core
    MESH = pl.DeviceIdType.MESH

    barrier = pltpu.get_barrier_semaphore()
    line = Line((n, me), *[[]] * 5, *[None] * 6)
    line.signal_all(barrier, [(n, xor2(me, r)) for r in range(1, 4)])

    def inward(here):
        return line.copy(xu, eu, z_s, z_r, 1 if here in (0, 1) else 2)

    def load(i):
        if i < 4:
            j = 2 * (1 - core) + i if i < 2 else 2 * core + i - 2
            src = gu_hbm.at[:, pl.ds(pl.multiple_of(768 * j, 128), 768)]
        else:
            src = ul_hbm.at[:, 768 * (i - 4) : 768 * (i - 3)]
        return pltpu.make_async_copy(src, ring.at[i % 2], load_s.at[i])

    load(0).start()
    load(1).start()
    late = [
        pltpu.make_async_copy(src, dst, load_s.at[8 + i])
        for i, (src, dst) in enumerate(
            ((qkv_hbm, qkv_ref), (ot_hbm, ot_ref), (w_hbm, w_ref), (h0, held.at[0]), (h1, held.at[1]),
             (h2, held.at[2]), (h3, held.at[3]))
        )
    ]
    for c in late:
        c.start()
    line.wait_all(barrier, 3)

    def to_wide(i, r, src, dst):
        return pltpu.make_async_remote_copy(
            src_ref=src, dst_ref=dst, send_sem=wide_s.at[i], recv_sem=wide_r.at[i],
            device_id=(n, xor2(me, r)), device_id_type=MESH,
        )

    def to_core(i, src, dst):
        return pltpu.make_async_remote_copy(
            src_ref=src, dst_ref=dst, send_sem=core_s.at[i], recv_sem=core_r.at[i],
            device_id=(other, me), device_id_type=MESH,
        )

    send_d = [to_wide(r - 1, r, (d1, d2, d3)[r - 1], rd.at[r - 1]) for r in (3, 1, 2)]
    for c in send_d:
        c.start()

    core1, core2, coreb = to_core(0, send1, got1), to_core(1, send2, got2), to_core(2, bsend, bgot)
    for i in range(4):
        load(i).wait()
        up = tn(nl[...], ring[i % 2]).astype(bf16)
        to = send1 if i < 2 else keep1
        row = 192 * (i % 2)
        for e in range(4):
            to[xor2(me, e), row : row + 192, :] = up[192 * e : 192 * e + 192]
        load(i + 2).start()
        if i == 1:
            core1.start()
    for c in send_d:
        c.wait()
    for c in late:
        c.wait()
    short = d0[:, FR : FR + 256].astype(f32)
    dot_[:, pl.ds(pl.multiple_of(FR * me, 128), FR)] = d0[:, 0:FR]
    for r in range(1, 4):
        dot_[:, pl.ds(pl.multiple_of(FR * xor2(me, r), 128), FR)] = rd[r - 1, :, 0:FR]
        short += rd[r - 1, :, FR : FR + 256].astype(f32)
    dot_[:, SLOTS:TROWS] = short.astype(bf16)
    whole = dot_[...].astype(f32)
    do_[...] = whole.T.astype(bf16)
    prod = whole * ot_ref[...]
    for h in range(3):
        delta[h : h + 1, :] = jnp.sum(prod[64 * h : 64 * h + 64], axis=0, keepdims=True)
    kt[...] = qkv_ref[:, 256:448].astype(f32).T.astype(bf16)
    core1.wait()
    for r in range(4):
        keep1[r] = (keep1[r].astype(f32) + got1[r].astype(f32)).astype(bf16)
    send_a = [to_wide(2 + r, r, keep1.at[r], ra.at[r - 1]) for r in (3, 1, 2)]
    for c in send_a:
        c.start()

    keep_k, keep_v = [], []
    for h in range(3):
        cols = slice(64 * h, 64 * h + 64)
        dk[...] = jnp.zeros_like(dk)
        dv[...] = jnp.zeros_like(dv)

        def step(q0, queries, key0, keys, masked):
            at_q = pl.ds(q0, queries)
            query = qkv_ref[at_q, 0:256][:, cols]
            scaled = (query.astype(f32) * 0.125).astype(bf16)
            grad = do_[at_q, :][:, cols]
            grad_t = dot_[cols, at_q]
            lse = lse_ref[h : h + 1, at_q]
            dl = delta[h : h + 1, at_q]
            grad_q = jnp.zeros((64, queries), f32)
            piece = min(keys, KB)
            for at in range(key0, key0 + keys, piece):
                key = qkv_ref[at : at + piece, 256:512][:, cols]
                val = qkv_ref[at : at + piece, 512:768][:, cols]
                probs = jnp.exp(mm_nt(key, scaled) - lse)
                if masked:
                    slot = lax.broadcasted_iota(jnp.int32, probs.shape, 0)
                    probs = jnp.where(slot < SHORT, probs, 0.0)
                grad_p = mm(val, grad_t)
                grad_s = (probs * (grad_p - dl)).astype(bf16)
                dv[at : at + piece, :] += mm(probs.astype(bf16), grad)
                dk[at : at + piece, :] += mm(grad_s, query)
                grad_q += mm(kt[cols, at : at + piece], grad_s)
            dqt[cols, at_q] = grad_q * 0.125

        for q0 in range(0, SLOTS, QB):
            step(q0, QB, 0, SLOTS, False)
        step(SLOTS, 256, SLOTS, 128, True)
        keep_k.append((dk[...] * 0.125).astype(bf16))
        keep_v.append(dv[...].astype(bf16))
    zeros = jnp.zeros((TROWS, 64), bf16)
    dqkv[:, 0:192] = dqt[...].T.astype(bf16)
    dqkv[:, 192:256] = zeros
    dqkv[:, 256:512] = jnp.concatenate(keep_k + [zeros], axis=1)
    dqkv[:, 512:768] = jnp.concatenate(keep_v + [zeros], axis=1)

    parts = (g0, g1, g2, g3)
    lanes = pl.multiple_of(FR * me, 128)
    near, far = slice(0, 896), slice(896, TROWS)

    def project(r):
        rows = pl.ds(pl.multiple_of(192 * xor2(me, r), 64), 192)
        part = mm_nt(w_ref[rows, :], dqkv[...])
        parts[r][...] = part.astype(bf16)
        own = gst[rows, 0:FR].astype(f32)
        parts[r][:, pl.ds(lanes, FR)] = (parts[r][:, pl.ds(lanes, FR)].astype(f32) + own).astype(bf16)
        parts[r][:, SLOTS:TROWS] = (part[:, SLOTS:TROWS] + gst[rows, FR : FR + 256].astype(f32)).astype(bf16)

    def hop(i, r, src, half):
        return to_wide(6 + i, r, src.at[:, half], rg.at[i])

    first = [hop(0, 1, g3, near), hop(1, 2, g3, far), hop(2, 1, g1, near), hop(3, 2, g2, far)]
    second = [hop(4, 2, g2, near), hop(5, 1, g1, far)]
    project(3)
    first[0].start()
    first[1].start()
    project(1)
    first[2].start()
    project(2)
    first[3].start()
    for c in send_a:
        c.wait()
    total = keep1[0].astype(f32) + ra[0].astype(f32) + ra[1].astype(f32) + ra[2].astype(f32)
    xu[...] = total.astype(bf16)
    line.at_ends(lambda here: inward(here).start())
    project(0)
    qsums[...] = jnp.sum(dqkv[...].astype(f32), axis=0, keepdims=True)

    extra = jnp.concatenate([sums[...], jnp.zeros((16, 768), f32)], axis=0).astype(bf16)
    for j in range(4):
        load(4 + j).wait()
        down = tn(ring[j % 2], gd[...]).astype(bf16)
        rel = xor2(me, j)
        put(core == 0, keep2, send2, rel, 0, down[0:496])
        put(core == 1, keep2, send2, rel, 0, down[496:768])
        if j < 2:
            load(6 + j).start()
    for r, m in enumerate((m0, m1, m2, m3)):
        put(core == 1, keep2, send2, r, 272, mm(m[...], gac[...]).astype(bf16))
        put(core == 1, keep2, send2, r, 464, extra)
    core2.start()

    def join(part, half, i):
        part[:, half] = (part[:, half].astype(f32) + rg[i].astype(f32)).astype(bf16)

    r_i, c_i = iota2((768, 640))
    squeeze = ((r_i - 64 * (r_i >> 8) == c_i) & ((r_i & 255) < 192)).astype(f32).astype(bf16)

    def chunk_grad(chunk, r):
        turned = chunk.astype(f32).T.astype(bf16)
        value = (
            mm(turned[0:192, 0:384], dqkv[0:384, :])
            + mm(turned[192:384, 0:384], dqkv[384:768, :])
            + mm(turned[0:192, 384:768], dqkv[768:1152, :])
            + mm(turned[192:384, 384:768], dqkv[1152:1536, :])
            + mm(turned[0:192, 768:864], dqkv[SLOTS : SLOTS + 96, :])
            + mm(turned[192:384, 768:864], dqkv[SLOTS + 96 : SLOTS + 192, :])
        ).astype(bf16)
        value = mm(value, squeeze).astype(bf16)
        put(core == 0, bkeep, bsend, r, 0, value[0:96])
        put(core == 1, bkeep, bsend, r, 0, value[96:192])

    first[0].wait()
    join(g2, near, 0)
    second[0].start()
    first[1].wait()
    join(g1, far, 1)
    second[1].start()
    for r in range(4):
        chunk_grad(held[r], r)
    coreb.start()
    core2.wait()
    for r in range(4):
        a2_out[r] = (keep2[r].astype(f32) + got2[r].astype(f32)).astype(bf16)
    coreb.wait()
    for r in range(4):
        b_out[r] = (bkeep[r].astype(f32) + bgot[r].astype(f32)).astype(bf16)
    first[2].wait()
    first[3].wait()
    second[0].wait()
    g_out[:, near] = g0[:, near].astype(f32) + rg[2].astype(f32) + rg[4].astype(f32)
    second[1].wait()
    g_out[:, far] = g0[:, far].astype(f32) + rg[3].astype(f32) + rg[5].astype(f32)

    def at_end(here):
        inward(here).wait_send()
        a1_out[...] = xu[...]

    def at_middle(here):
        inward(here).wait_recv()
        a1_out[...] = (xu[...].astype(f32) + eu[...].astype(f32)).astype(bf16)

    line.at_ends(at_end)
    line.at_inner(at_middle)


def attn_sync(qkv, ot, lse, dparts, gst, wqkv, first, nl, gd, ul, gu, mix, gac, sums):
    sds = jax.ShapeDtypeStruct
    hbm = pl.BlockSpec(memory_space=pl.ANY)
    sem = pltpu.SemaphoreType.DMA
    room = lambda *shape: pltpu.VMEM(shape, bf16)
    return pl.pallas_call(
        attn_sync_kernel,
        in_specs=[hbm] * 2 + [vmem()] * 6 + [hbm] * 5 + [vmem()] * 2 + [hbm] * 2 + [vmem()] * 6,
        out_specs=[vmem()] * 5,
        out_shape=[
            sds((384, 768), bf16), sds((4, 496, 768), bf16), sds((4, 96, 640), bf16), sds((CH, TROWS), f32),
            sds((1, 768), f32),
        ],
        scratch_shapes=[
            room(2, 768, 768),
            sem((15,)),
            room(CH, TROWS),
            room(TROWS, CH),
            room(CH, TROWS),
            pltpu.VMEM((8, TROWS), f32),
            pltpu.VMEM((CH, TROWS), f32),
            pltpu.VMEM((TROWS, 64), f32),
            pltpu.VMEM((TROWS, 64), f32),
            room(TROWS, 768),
        ]
        + [room(4, 384, 768)] * 3
        + [room(4, 496, 768)] * 3
        + [room(4, 96, 640)] * 3
        + [room(3, 384, 768), room(3, CH, 640)]
        + [room(CH, TROWS)] * 4
        + [room(6, CH, 896), sem((3,)), sem((3,)), sem((12,)), sem((12,))]
        + [room(TROWS, 768), pltpu.VMEM((CH, TROWS), f32), room(768, 768), room(4, 864, 384)]
        + [room(384, 768), room(384, 768), sem, sem],
        compiler_params=params(collective_id=2, has_side_effects=True),
        cost_estimate=cost(90),
        name="attn_sync",
    )(qkv, ot, lse, *dparts, gst, wqkv, *first, nl, gd, ul, gu, *mix, gac, sums)


def wgrad_front(pair, gsum, pre_ref, sums_ref, half, gf, g_ref, gp):
    at = pl.ds(pl.multiple_of(96 * pair, 32), 96)
    total = gsum[at, :]
    pad = jnp.zeros((16, TROWS), f32)
    rows = jnp.concatenate([total[0:48], pad, total[48:96], pad], axis=0)
    gf[0:SLOTS, :] = rows[:, 0:SLOTS].T
    gf[SLOTS:SBASE, :] = jnp.zeros((SBASE - SLOTS, 128), f32)
    gf[SBASE:TROWS, :] = rows[:, SLOTS:TROWS].T[0 : TROWS - SBASE]
    g_ref[0:64, :] = jnp.zeros((64, 128), bf16)
    g_ref[1856:1936, :] = jnp.zeros((80, 128), bf16)
    gp[0:16, :] = jnp.zeros((16, 128), f32)
    pre = pre_ref[pair]
    slope = gelu_parts(pre) + pre * density(pre)
    wide = (gf[...] * slope).astype(bf16).astype(f32)
    bias_sum = jnp.sum(wide, axis=0, keepdims=True)
    row = lax.broadcasted_iota(jnp.int32, (TROWS, 128), 0)
    wide = jnp.where(row < SBASE + UNIQUE, wide, 0.0)
    gp[16 : 16 + TROWS, :] = wide
    g_ref[64 : 64 + TROWS, :] = wide.astype(bf16)
    extra = jnp.concatenate(
        [sums_ref[...], jnp.concatenate([bias_sum, jnp.zeros((1, 640), f32)], axis=1), jnp.zeros((14, 768), f32)], axis=0
    )
    half[0, 192:208, :] = extra.astype(bf16)


def wgrad_group(pair, j, me, x_ref, half, gp, p0, bb, g2, xt):
    lane = lax.broadcasted_iota(jnp.int32, (TROWS, 128), 1)
    here, before = gp[16 : 16 + TROWS, :], gp[15 : 15 + TROWS, :]
    p0[...] = pair_slots(x_ref.at[pair], 1920, (j,))[0]
    pack0, pack1 = gather_slots((256, 384), 0), gather_slots((256, 384), 192)
    bb[0:16, :] = jnp.zeros((16, 128), f32)
    if j == 0:
        bb[16 : 16 + TROWS, :] = jnp.where(lane < 64, here, pltpu.roll(before, 64, 1))
    else:
        bb[16 : 16 + TROWS, :] = jnp.where(lane < 64, pltpu.roll(here, 64, 1), before)
    for p in range(8):
        g2[:, 128 * p : 128 * p + 128] = bb[16 - 2 * p : 16 - 2 * p + TROWS, :].astype(bf16)
    for q in range(4):
        xt[128 * q : 128 * q + 128, :] = p0[32 * q : 32 * q + TROWS, :].astype(f32).T.astype(bf16)
    for side in range(2):
        base = 512 * side
        left = mm(xt[...], g2[:, base : base + 256]).astype(bf16)
        right = mm(xt[...], g2[:, base + 256 : base + 512]).astype(bf16)
        packed = (mm(left, pack0) + mm(right, pack1)).astype(bf16)
        for m in range(4):
            tile = jnp.concatenate([packed[128 * m : 128 * m + 48], packed[128 * m + 64 : 128 * m + 112]], axis=0)
            half[xor2(me, m), 96 * j : 96 * j + 96, 384 * side : 384 * side + 384] = tile


def conv_sync_kernel(
    gsum, pre_ref, x_ref, sums_ref, xu, wd_hbm, a_hbm, b_ref,
    fu, fa, fb, fc, ou, oa, ob, oc, f0, f1, f2, f3,
    gp, p0, p1, bb, g2, xt, y_ref, t_ref, gf, g, fg, s1, s2, s3,
    csend, ckeep, cgot, ra, rb, rc, xa, xb, eu, ea, eb, ec, yu, ya, yb, yc, next1, next2,
    z0, z1, z2, z3, z4, z5, wide_s, wide_r, core_s, core_r, wd_ref, load_s,
):
    n, me = lax.axis_index("narrow"), lax.axis_index("wide")
    core = n % 2

    pieces = [(3, None, 96 * r, 96) for r in range(4)]
    pieces += [(0, r, 0, 96) for r in range(4)] + [(2, r, 0, 96) for r in range(4)]
    pieces += [(1, None, 0, 128), (1, None, 128, 128), (1, None, 256, 128), (1, None, 384, 112)]
    pieces += [(2, 0, 96, 112), (2, 1, 96, 96), (2, 2, 96, 48), (2, 2, 144, 48), (2, 3, 96, 48), (2, 3, 144, 48)]
    set_u, set_b, set_c, set_a, set_d = range(0, 4), range(4, 8), range(8, 12), range(12, 16), range(16, 22)

    def views(refs):
        out = []
        for which, r, row, rows in pieces:
            ref = refs[which]
            out.append(ref.at[row : row + rows] if r is None else ref.at[r, row : row + rows])
        return out

    sets = ((xb, xa, csend, xu), (eb, ea, ec, eu), (yb, ya, yc, yu), (fb, fa, fc, fu), (ob, oa, oc, ou))
    line = Line((n, me), *(views(refs) for refs in sets), z0, z1, z2, z3, z4, z5, set_u)
    loads = [
        pltpu.make_async_copy(wd_hbm, wd_ref, load_s.at[0]),
        pltpu.make_async_copy(a_hbm.at[0], xa, load_s.at[1]),
        pltpu.make_async_copy(a_hbm.at[2, 0:256], next1, load_s.at[2]),
        pltpu.make_async_copy(a_hbm.at[1, 256:496], next2, load_s.at[3]),
    ]
    for c in loads:
        c.start()
    line.greet(pltpu.get_barrier_semaphore(), [(n, xor2(me, r)) for r in range(1, 4)])

    def to_wide(sem, r, src, dst):
        return pltpu.make_async_remote_copy(
            src_ref=src, dst_ref=dst, send_sem=wide_s.at[sem], recv_sem=wide_r.at[sem],
            device_id=(n, xor2(me, r)), device_id_type=pl.DeviceIdType.MESH,
        )

    def over_wide(which, src, dst):
        return [to_wide(3 * which + r - 1, r, src(r), dst(r)) for r in (3, 1, 2)]

    def start(copies):
        for c in copies:
            c.start()

    def wait(copies):
        for c in copies:
            c.wait()

    halves = (slice(0, 256), slice(256, 496))
    send_b = over_wide(0, lambda r: b_ref.at[r], lambda r: rb.at[r - 1])
    near, far = halves
    send_a = [
        to_wide(3, 1, a_hbm.at[3, near], ra.at[0, near]), to_wide(4, 2, a_hbm.at[3, far], ra.at[0, far]),
        to_wide(5, 1, a_hbm.at[1, near], ra.at[1, near]), to_wide(6, 2, a_hbm.at[2, far], ra.at[1, far]),
        to_wide(7, 2, next1, ra.at[2, near]), to_wide(8, 1, next2, ra.at[2, far]),
    ]
    groups = (slice(0, 96), slice(96, 192))
    send_c = [
        over_wide(3 + i, lambda r, at=at: ckeep.at[r, at], lambda r, at=at: rc.at[r - 1, at])
        for i, at in enumerate(groups)
    ]
    send_f = over_wide(5, lambda r: (s1, s2, s3)[r - 1], lambda r: (f1, f2, f3)[r - 1])
    crossing = (slice(0, 96), slice(96, 208))
    to_core = [
        line.copy(csend.at[:, at], cgot.at[:, at], core_s.at[i], core_r.at[i], line.z, 1 - core)
        for i, at in enumerate(crossing)
    ]
    start(send_b)
    start(send_a[:4])
    line.at_inner(lambda here: line.meet(set_u, here))

    def group(pair, j, half, slot):
        wgrad_group(pair, j, me, x_ref, half, gp.at[slot], p0, bb, g2, xt)

    def dgrad(pair, slot):
        a, b = pair_slots(g.at[slot], 1920)
        p0[...] = a
        p1[...] = b
        value = conv_block((p0, p1), wd_ref.at[pl.ds(2 * pair, 2)], y_ref, t_ref, 1) + gf[slot]
        fg[pair] = value.astype(bf16)

    def add_a(i):
        wait([send_a[2 + i], send_a[4 + i]])
        at = halves[i]
        xa[at] = (xa[at].astype(f32) + ra[1, at].astype(f32) + ra[2, at].astype(f32)).astype(bf16)
        line.begin(set_a[2 * i : 2 * i + 2])

    def add_core(i):
        to_core[i].wait()
        at = crossing[i]
        for r in range(4):
            ckeep[r, at] = (ckeep[r, at].astype(f32) + cgot[r, at].astype(f32)).astype(bf16)
        start(send_c[i])

    def take_c(i):
        wait(send_c[i])
        csend[0, crossing[i]] = ckeep[0, crossing[i]]
        for r in range(1, 4):
            csend[r, groups[i]] = rc[r - 1, groups[i]]
        line.begin((set_c, set_d)[i])

    def inner(*does):
        def do(here):
            for act, ks in does:
                act(ks, here)

        line.at_inner(do)

    meet, close, pass_on = line.meet, line.close, line.pass_on
    wgrad_front(1 - core, gsum, pre_ref, sums_ref, csend, gf.at[0], g.at[0], gp.at[0])
    group(1 - core, 0, csend, 0)
    to_core[0].start()
    inner((close, set_u))
    wait(send_b)
    xb[0] = b_ref[0]
    for r in range(1, 4):
        xb[r] = rb[r - 1]
    line.begin(set_b)
    wgrad_front(core, gsum, pre_ref, sums_ref, ckeep, gf.at[1], g.at[1], gp.at[1])
    group(core, 0, ckeep, 1)
    inner((pass_on, set_u), (meet, set_b[0:2]))
    add_core(0)
    group(1 - core, 1, csend, 0)
    to_core[1].start()
    inner((meet, set_b[2:4]), (close, set_b[0:2]))
    wait(loads)
    wait(send_a[0:2])
    next1[...] = (next1[...].astype(f32) + ra[0, near].astype(f32)).astype(bf16)
    next2[...] = (next2[...].astype(f32) + ra[0, far].astype(f32)).astype(bf16)
    start(send_a[4:6])
    take_c(0)
    group(core, 1, ckeep, 1)
    inner((close, set_b[2:4]), (pass_on, set_b[0:2]))
    add_core(1)
    inner((meet, set_c[0:2]))
    add_a(0)
    dgrad(1 - core, 0)
    inner((pass_on, set_b[2:4]), (close, set_c[0:2]), (meet, set_c[2:4]))
    add_a(1)
    take_c(1)
    dgrad(core, 1)
    inner((pass_on, set_c[0:2]), (meet, set_a[0:2]), (close, set_c[2:4]))
    pack0, pack1 = gather_slots((256, 384), 0), gather_slots((256, 384), 192)

    def rows_of(lo, rows):
        return jnp.concatenate([fg[0, lo : lo + rows, :], fg[1, lo : lo + rows, :]], axis=1)

    outs = (f0, s1, s2, s3)
    for d in range(4):
        low = jnp.concatenate([rows_of(FR * d + 256, 128), rows_of(SBASE, 128)], axis=0)
        chunk = (mm(rows_of(FR * d, 256), pack0) + mm(low, pack1)).astype(bf16)
        for r in range(4):

            @pl.when(xor2(me, d) == r)
            def _():
                outs[r][...] = chunk

    start(send_f)

    rest = [set_a[0:2], set_a[2:4], set_d[0:2], set_d[2:4], set_d[4:6]]
    does = []
    for i, pair in enumerate(rest):
        if i + 1 < len(rest):
            does.append((meet, rest[i + 1]))
        does.append((close, pair))
        does.append((pass_on, rest[i - 1] if i else set_c[2:4]))
    inner(*does, (pass_on, rest[-1]), (lambda ks, here: line.settle(here), None))
    line.at_ends(line.receive)
    wait(send_f)


def conv_sync(gsum, pre, xp, sums, up_sum, wd, ffn_halves, qkv_halves):
    sds = jax.ShapeDtypeStruct
    shapes = [(384, 768), (496, 768), (4, 96, 640), (4, 208, 768)]
    hbm = pl.BlockSpec(memory_space=pl.ANY)
    sem = pltpu.SemaphoreType.DMA
    room = lambda *shape: pltpu.VMEM(shape, bf16)
    return pl.pallas_call(
        conv_sync_kernel,
        in_specs=[vmem()] * 5 + [hbm] * 2 + [vmem()],
        out_specs=[vmem()] * 12,
        out_shape=[sds(v, bf16) for v in shapes * 2] + [sds((256, 384), bf16)] * 4,
        scratch_shapes=[
            pltpu.VMEM((2, 16 + TROWS, 128), f32),
            room(1920, 128),
            room(1920, 128),
            pltpu.VMEM((16 + TROWS, 128), f32),
            room(TROWS, 1024),
            room(512, TROWS),
            pltpu.VMEM((CB + 16, 1024), f32),
            pltpu.VMEM((CB + 8, 128), f32),
            pltpu.VMEM((2, TROWS, 128), f32),
            room(2, 1936, 128),
            room(2, TROWS, 128),
        ]
        + [room(256, 384)] * 3
        + [room(4, 208, 768)] * 3
        + [room(3, 496, 768), room(3, 96, 640), room(3, 192, 768), room(496, 768), room(4, 96, 640)]
        + [room(*v) for v in shapes * 2]
        + [room(256, 768), room(240, 768)]
        + [sem((22,))] * 6
        + [sem((18,)), sem((18,)), sem((2,)), sem((2,)), room(4, 512, 1024), sem((4,))],
        compiler_params=params(collective_id=1, has_side_effects=True),
        cost_estimate=cost(100),
        name="conv_sync",
    )(gsum, pre, xp, sums, up_sum, wd, ffn_halves, qkv_halves)


def results_kernel(
    s_ref, c0, c1, c2, c3, own1, other1, own2, other2, ownb, otherb, ownc, otherc,
    frames, up, down, out, wq, wk, wv, small, gk_hbm, tiny,
    gk, sems,
):
    me, li, core = s_ref[0], s_ref[1], s_ref[2]

    def half(h, own, other):
        return jnp.where(core == h, own, other)

    stores = []
    for g in range(16):
        slot = g % 8
        if g >= 8:
            stores[g - 8].wait()
        rel = me ^ (g // 4)
        h, row = (g // 2) % 2, 96 * (g % 2)
        x = half(h, ownc[rel, row : row + 96], otherc[rel, row : row + 96]).astype(f32)
        for k2 in range(2):
            for b in range(16):
                gk[slot, 16 * k2 + b] = x[48 * k2 : 48 * k2 + 48, 48 * b : 48 * b + 48]
        stores.append(pltpu.make_async_copy(gk.at[slot], gk_hbm.at[:, g], sems.at[g]))
        stores[g].start()
    for h in range(2):
        tiny[h] = half(h, ownc[0, 192:208], otherc[0, 192:208])

    r_i, c_i = iota2((256, 768))
    top = jnp.zeros((256, 768), f32)
    low = jnp.zeros((256, 768), f32)
    totals = [jnp.zeros((CH, 768), f32)] * 3
    qkv = jnp.concatenate(
        [jnp.concatenate([half(h, ownb[r], otherb[r]) for h in range(2)], axis=0) for r in range(4)], axis=0
    )
    for r, chunk in enumerate((c0, c1, c2, c3)):
        base = 192 * (me ^ r)
        inside = (c_i >= base) & (c_i < base + 192)
        at0, at64 = (((c_i - base == r_i - skip) & inside).astype(f32).astype(bf16) for skip in (0, 64))
        top += mm(chunk[:, 0:256], at0)
        low += mm(chunk[:, 128:384], at64)
        for k, (lane0, move) in enumerate(((0, at0), (128, at64), (384, at0))):
            totals[k] = totals[k] + mm(qkv[192 * r : 192 * r + 192, lane0 : lane0 + 256], move)
    wq[...], wk[...], wv[...] = totals
    frames[li, 0:256, :] = top.astype(bf16)
    frames[li, 256:384, :] = low[0:128].astype(bf16)
    slot = me * FR + lax.broadcasted_iota(jnp.int32, (128, 768), 0)
    frames[1 - li, 0:128, :] = jnp.where(slot < SHORT, low[128:], 0.0).astype(bf16)
    frames[1 - li, 128:384, :] = jnp.zeros((256, 768), bf16)

    for j in range(4):
        at = slice(192 * (j % 2), 192 * (j % 2) + 192)
        up[:, 768 * j : 768 * j + 768] = half(j // 2, own1[at, :], other1[at, :]).astype(f32)
    down[0:496, :] = half(0, own2[...], other2[...]).astype(f32)
    low_half = half(1, own2[...], other2[...]).astype(f32)
    down[496:768, :] = low_half[0:272]
    out[...] = low_half[272:464]
    small[...] = low_half[464:480]
    for store in stores[8:]:
        store.wait()


def results(scal, *parts):
    sds = jax.ShapeDtypeStruct
    return pl.pallas_call(
        results_kernel,
        in_specs=[smem()] + [vmem()] * 12,
        out_specs=[vmem()] * 8 + [pl.BlockSpec(memory_space=pl.ANY), vmem()],
        out_shape=[sds((2, FR, 768), bf16), sds((CH, 3072), f32), sds((768, 768), f32)]
        + [sds((CH, 768), f32)] * 4
        + [sds((16, 768), f32), sds((32, 16, 48, 48), f32), sds((2, 16, 768), bf16)],
        scratch_shapes=[pltpu.VMEM((8, 32, 48, 48), f32), pltpu.SemaphoreType.DMA((16,))],
        compiler_params=params(),
        cost_estimate=cost(12),
        name="results",
    )(scal, *parts)


def norm(v):
    center = v - jnp.mean(v, axis=-1, keepdims=True)
    scale = lax.rsqrt(jnp.mean(center * center, axis=-1, keepdims=True) + eps_norm)
    return center * scale, scale


def norm_back(e, n, scale):
    return (e - jnp.mean(e, axis=-1, keepdims=True) - n * jnp.mean(e * n, axis=-1, keepdims=True)) * scale


def ffn_kernel(
    s_ref, rows_ref, m0, m1, m2, m3, wo, wu_hbm, bu, wd_hbm, vecs, og,
    lo, ul_hbm, gu_hbm, nl, gd, gac, x0, x1, x2, x3, gst, sums,
    wu, wd, ul, gu, slope, v, gsc, mix, sems,
):
    me, li = s_ref[0], s_ref[1]
    const = FR + UNIQUE
    bo, g1, s1, bd, g2, s2 = (vecs[k : k + 1, :] for k in range(6))
    loads = [
        pltpu.make_async_copy(wu_hbm, wu, sems.at[0]),
        pltpu.make_async_copy(wd_hbm, wd, sems.at[1]),
    ]
    for load in loads:
        load.start()

    def total(x):
        return jnp.sum(x, axis=0, keepdims=True)

    for r, m in enumerate((m0, m1, m2, m3)):
        mix[pl.ds(pl.multiple_of(192 * (me ^ r), 64), 192), :] = m[...]
    out = tn(mix[...], wo[...])
    gsc[0:576, :] = rows_ref[...].astype(f32) + out[0:576] + bo
    last = gsc[const : const + 1, :]
    v[0:FR, :] = gsc[0:FR, :]
    v[FR : FR + 128, :] = jnp.where(me == 0, gsc[FR : FR + 128, :], last)
    mine = jnp.where(me == 0, 1.0, 0.0)
    keep_low = (lax.broadcasted_iota(jnp.int32, (64, 768), 0) < UNIQUE - 128).astype(f32) * mine
    v[FR + 128 : FR + 192, :] = jnp.where(keep_low > 0.5, gsc[FR + 128 : FR + 192, :], last)
    v[FR + 192 :, :] = jnp.broadcast_to(last, (192, 768))

    n1, scale1 = norm(v[...])
    v[...] = n1
    norm_one = n1 * g1 + s1
    low = norm_one.astype(bf16)
    nl[...] = low
    down = norm_one + bd
    stores = []
    loads[0].wait()
    for j in range(4):
        cols = slice(768 * j, 768 * j + 768)
        up = mm(low, wu[:, cols]) + bu[:, cols]
        cdf = gelu_parts(up)
        slope[:, cols] = cdf + up * density(up)
        act = (up * cdf).astype(bf16)
        ul[:, cols] = act
        stores.append(pltpu.make_async_copy(ul.at[:, cols], ul_hbm.at[:, cols], sems.at[2 + j]))
        stores[-1].start()
        if j == 0:
            loads[1].wait()
        down += mm(act, wd[cols, :])
    n2, scale2 = norm(down)
    result = (n2 * g2 + s2).astype(bf16)
    lo[li] = result[0:FR]
    lo[1 - li] = result[FR:]
    given = jnp.concatenate([og[li], og[1 - li]], axis=0).astype(f32)
    sums[8:9, :] = total(given * n2)
    sums[9:10, :] = total(given)
    sums[10:16, :] = jnp.zeros((6, 768), f32)
    grad_two = norm_back(given * g2, n2, scale2)
    grad_down = grad_two.astype(bf16)
    gd[...] = grad_down
    sums[7:8, :] = total(grad_down.astype(f32))
    grad_n = grad_two
    for j in range(4):
        cols = slice(768 * j, 768 * j + 768)
        grad_up = (mm_nt(grad_down, wd[cols, :]) * slope[:, cols]).astype(bf16)
        gu[:, cols] = grad_up
        stores.append(pltpu.make_async_copy(gu.at[:, cols], gu_hbm.at[:, cols], sems.at[6 + j]))
        stores[-1].start()
        sums[j : j + 1, :] = total(grad_up.astype(f32))
        grad_n += mm_nt(grad_up, wu[:, cols])
    n1 = v[...]
    sums[5:6, :] = total(grad_n * n1)
    sums[6:7, :] = total(grad_n)
    grad_one = norm_back(grad_n * g1, n1, scale1)
    grad_attn = grad_one.astype(bf16).astype(f32)
    sums[4:5, :] = total(grad_attn)

    at = lax.broadcasted_iota(jnp.int32, (64, 768), 0) == UNIQUE - 128

    def collapsed(g):
        upper = g[FR : FR + 128] * mine
        lower = g[FR + 128 : FR + 192] * keep_low
        rest = total(g[FR:]) - total(upper) - total(lower)
        return jnp.concatenate(
            [g[0:FR], upper, jnp.where(at, rest, lower), jnp.zeros((64, 768), f32)], axis=0
        )

    gac[...] = collapsed(grad_attn).astype(bf16)
    for r, out in enumerate((x0, x1, x2, x3)):
        at_r = pl.ds(pl.multiple_of(192 * (me ^ r), 64), 192)
        out[...] = mm_nt(wo[at_r, :], gac[...]).astype(bf16)
    gsc[...] = collapsed(grad_one)
    gst[...] = gsc[...].T.astype(bf16)
    for store in stores:
        store.wait()


def ffn(scal, rows, mix, wo, wu, bu, wd, vecs, og):
    sds = jax.ShapeDtypeStruct
    hbm = pl.BlockSpec(memory_space=pl.ANY)
    return pl.pallas_call(
        ffn_kernel,
        in_specs=[smem()] + [vmem()] * 6 + [hbm, vmem(), hbm, vmem(), vmem()],
        out_specs=[vmem(), hbm, hbm] + [vmem()] * 9,
        out_shape=[
            sds((2, FR, 768), bf16), sds((768, 3072), bf16), sds((768, 3072), bf16), sds((768, 768), bf16),
            sds((768, 768), bf16), sds((640, 768), bf16),
        ]
        + [sds((CH, 640), bf16)] * 4
        + [sds((768, 640), bf16), sds((16, 768), f32)],
        scratch_shapes=[
            pltpu.VMEM((768, 3072), bf16),
            pltpu.VMEM((3072, 768), bf16),
            pltpu.VMEM((768, 3072), bf16),
            pltpu.VMEM((768, 3072), bf16),
            pltpu.VMEM((768, 3072), f32),
            pltpu.VMEM((768, 768), f32),
            pltpu.VMEM((640, 768), f32),
            pltpu.VMEM((768, 640), bf16),
            pltpu.SemaphoreType.DMA((10,)),
        ],
        compiler_params=params(),
        cost_estimate=cost(28),
        name="ffn",
    )(scal, rows, *mix, wo, wu, bu, wd, vecs, og)


def tn(a, b):
    return lax.dot_general(a, b, (((0,), (0,)), ((), ())), preferred_element_type=f32)


def on_device(
    frames_in, lengths, kernel, conv_bias, w_query, b_query, w_key, w_value, b_value, w_out, b_out,
    gain_one, shift_one, w_up, b_up, w_down, b_down, gain_two, shift_two, out_grad,
):
    me = lax.axis_index("wide").astype(jnp.int32)
    place_n = lax.axis_index("narrow").astype(jnp.int32)
    core, z = place_n & 1, place_n >> 1
    li = jnp.where(lengths[0] >= lengths[1], 0, 1).astype(jnp.int32)
    scal = jnp.stack([me, li, core, z])
    chunks = pack_frames(scal, frames_in)
    vec = jnp.concatenate([jnp.stack([conv_bias, b_query, b_value]), jnp.zeros((13, conv_bias.shape[0]), bf16)], axis=0)
    vecs = jnp.stack([b_out, gain_one, shift_one, b_down, gain_two, shift_two]).astype(f32)
    bu = b_up.astype(f32)[None]

    wd, pre, xp, h0, h1, h2, h3, qkv, mixed_t, lse, rows, wqkv, *mix = front_sync(
        chunks, kernel, vec, w_query, w_key, w_value
    )
    first = [h0, h1, h2, h3]
    layer_out, ul, gu, nl, gd, gac, x0, x1, x2, x3, gst, sums = ffn(
        scal, rows, mix, w_out, w_up, bu, w_down, vecs, out_grad
    )
    up_sum, ffn_halves, qkv_halves, gsum, qkv_sums = attn_sync(
        qkv, mixed_t, lse, [x0, x1, x2, x3], gst, wqkv, first, nl, gd, ul, gu, mix, gac, sums
    )
    own1, own2, ownb, ownc, other1, other2, otherb, otherc, *fchunks = conv_sync(
        gsum, pre, xp, qkv_sums, up_sum, wd, ffn_halves, qkv_halves
    )
    frames_grad, up, down, out, wq, wk, wv, small, grad_kernel, tiny = results(
        scal, *fchunks, own1, other1, own2, other2, ownb, otherb, ownc, otherc
    )
    tiny = tiny.astype(f32)

    def mine(row):
        return lax.dynamic_slice_in_dim(small[row], me * CH, CH, axis=0)

    bias_grad = jnp.concatenate([tiny[0, 1, :128], tiny[1, 1, :128]]).reshape(4, 64)[:, :48].reshape(CH)
    grad_b_up = lax.dynamic_index_in_dim(small[:4], me, 0, keepdims=False)
    return (
        layer_out,
        frames_grad,
        grad_kernel,
        bias_grad,
        wq,
        tiny[0, 0, 0:192],
        wk,
        wv,
        tiny[0, 0, 512:704],
        out,
        mine(4),
        mine(5),
        mine(6),
        up,
        grad_b_up,
        down,
        mine(7),
        mine(8),
        mine(9),
    )


def with_halo(x, sides, width):
    for axis, dim in sides:
        count, length = (lax.axis_size(axis), x.shape[dim])
        up = [(i, (i + 1) % count) for i in range(count - 1)]
        down = [(j, i) for i, j in up]
        last = lax.slice_in_dim(x, length - width, length, axis=dim)
        initial = lax.slice_in_dim(x, 0, width, axis=dim)
        before = lax.ppermute(last, axis, up)
        after = lax.ppermute(initial, axis, down)
        x = jnp.concatenate([before, x, after], axis=dim)
    return x


def layer_norm(value, gain, shift):
    center = value - jnp.mean(value, axis=-1, keepdims=True)
    spread = jnp.mean(center * center, axis=-1, keepdims=True)
    return center * lax.rsqrt(spread + eps_norm) * gain + shift


def gelu_exact(value):
    return jax.nn.gelu(value, approximate=False)


def project(rows_in, weight):
    return jnp.einsum("cfd,de->cfe", rows_in, weight, preferred_element_type=jnp.float32)


def project_back(grad_in, weight):
    return jnp.einsum("cfe,de->cfd", grad_in, weight, preferred_element_type=jnp.float32)


def weight_grad(rows_in, grad_in):
    return jnp.einsum("cfd,cfe->de", rows_in, grad_in, preferred_element_type=jnp.float32)


def row_total(grad_in):
    return jnp.sum(grad_in.astype(jnp.float32), axis=(0, 1))


def head_view(rows_in):
    return rows_in.reshape(rows_in.shape[0], rows_in.shape[1], HEADS, rows_in.shape[2] // HEADS)


def conv_apply(padded, weight, frames):
    kernel_span, groups, inner_ch, outer_ch = weight.shape
    taps_weight = jnp.transpose(weight, (0, 2, 1, 3)).reshape(
        kernel_span, inner_ch, groups * outer_ch
    )
    result = lax.conv_general_dilated(
        padded,
        taps_weight,
        (1,),
        "VALID",
        dimension_numbers=("NWC", "WIO", "NWC"),
        feature_group_count=groups,
        preferred_element_type=jnp.float32,
    )
    return result[:, :frames, :]


def conv_weight_grad(padded, grad_in, kernel_shape):
    kernel_span, groups, inner_ch, outer_ch = kernel_shape
    result = lax.conv_general_dilated(
        padded,
        grad_in,
        (1,),
        "VALID",
        dimension_numbers=("CWN", "IWO", "NWC"),
        batch_group_count=groups,
        preferred_element_type=jnp.float32,
    )
    result = result[:, :kernel_span, :].reshape(inner_ch, kernel_span, groups, outer_ch)
    return jnp.transpose(result, (1, 2, 0, 3))


def key_valid_at(lengths, first_row, row_count):
    return (first_row + jnp.arange(row_count, dtype=jnp.int32))[None, :] < lengths[:, None]


def masked_scores(query_h, keys_h, valid_keys, score_scale):
    scores = (
        jnp.einsum("cqhd,ckhd->cqhk", query_h, keys_h, preferred_element_type=jnp.float32)
        * score_scale
    )
    return jnp.where(valid_keys[:, None, None, :], scores, neg_large)


def block_terms(query_h, grad_h, lse_rows, delta_rows, keys_h, values_h, valid_keys, score_scale):
    scores = masked_scores(query_h, keys_h, valid_keys, score_scale)
    probs = jnp.where(valid_keys[:, None, None, :], jnp.exp(scores - lse_rows[..., None]), 0.0)
    grad_probs = jnp.einsum("cqhd,ckhd->cqhk", grad_h, values_h, preferred_element_type=jnp.float32)
    grad_scores = (probs * (grad_probs - delta_rows[..., None])).astype(jnp.bfloat16)
    results = []
    results.append(
        jnp.einsum("cqhk,ckhd->cqhd", grad_scores, keys_h, preferred_element_type=jnp.float32)
        * score_scale
    )
    results.append(
        jnp.einsum("cqhk,cqhd->ckhd", grad_scores, query_h, preferred_element_type=jnp.float32)
        * score_scale
    )
    results.append(
        jnp.einsum(
            "cqhk,cqhd->ckhd",
            probs.astype(jnp.bfloat16),
            grad_h,
            preferred_element_type=jnp.float32,
        )
    )
    return tuple(results)


def on_device_any(
    frames_in,
    lengths,
    kernel,
    conv_bias,
    w_query,
    b_query,
    w_key,
    w_value,
    b_value,
    w_out,
    b_out,
    gain_one,
    shift_one,
    w_up,
    b_up,
    w_down,
    b_down,
    gain_two,
    shift_two,
    out_grad,
):
    clip_count, frames, width = frames_in.shape
    head_dim = width // HEADS
    score_scale = head_dim ** (-0.5)
    half_span = kernel.shape[0] // 2
    wide_size = lax.axis_size("wide")
    positions = lax.axis_index("wide") * frames + jnp.arange(frames, dtype=jnp.int32)
    frame_valid = positions[None, :] < lengths[:, None]
    masked = jnp.where(frame_valid[..., None], frames_in, jnp.zeros((), jnp.bfloat16))
    padded = with_halo(masked, (("wide", 1),), half_span)
    pre_act = conv_apply(padded, kernel, frames) + conv_bias.astype(jnp.float32)
    first_act, pull_first = jax.vjp(gelu_exact, pre_act)
    first_out = masked.astype(jnp.float32) + first_act
    first_low = first_out.astype(jnp.bfloat16)
    query_rows = (project(first_low, w_query) + b_query.astype(jnp.float32)).astype(jnp.bfloat16)
    key_rows = project(first_low, w_key).astype(jnp.bfloat16)
    value_rows = (project(first_low, w_value) + b_value.astype(jnp.float32)).astype(jnp.bfloat16)
    query_h = head_view(query_rows)
    per_step = max(1, min(wide_size, 512 // frames))
    while wide_size % per_step:
        per_step -= 1
    run_max = jnp.full((clip_count, frames, HEADS), neg_large, jnp.float32)
    run_acc = jnp.zeros((clip_count, frames, HEADS, head_dim), jnp.float32)
    keys_p = lax.all_gather(key_rows, "wide", axis=1, tiled=True)
    values_p = lax.all_gather(value_rows, "wide", axis=1, tiled=True)
    row_count = keys_p.shape[1]
    valid_keys = key_valid_at(lengths, jnp.int32(0), row_count)
    scores = masked_scores(query_h, head_view(keys_p), valid_keys, score_scale)
    new_max = jnp.maximum(run_max, jnp.max(scores, axis=-1))
    weights = jnp.where(valid_keys[:, None, None, :], jnp.exp(scores - new_max[..., None]), 0.0)
    factor = jnp.exp(run_max - new_max)
    run_sum = jnp.sum(weights, axis=-1)
    run_acc = run_acc * factor[..., None] + jnp.einsum(
        "cqhk,ckhd->cqhd",
        weights.astype(jnp.bfloat16),
        head_view(values_p),
        preferred_element_type=jnp.float32,
    )
    run_max, run_sum, run_acc = (new_max, run_sum, run_acc)
    lse_rows = run_max + jnp.log(run_sum)
    mixed_heads = run_acc / run_sum[..., None]
    mixed_low = mixed_heads.reshape(clip_count, frames, width).astype(jnp.bfloat16)
    attn_out = project(mixed_low, w_out) + b_out.astype(jnp.float32)
    sum_one = first_out + attn_out
    norm_one, pull_one = jax.vjp(
        layer_norm, sum_one, gain_one.astype(jnp.float32), shift_one.astype(jnp.float32)
    )
    norm_low = norm_one.astype(jnp.bfloat16)
    up_pre = project(norm_low, w_up) + b_up.astype(jnp.float32)
    up_act, pull_up = jax.vjp(gelu_exact, up_pre)
    up_low = up_act.astype(jnp.bfloat16)
    down_out = project(up_low, w_down) + b_down.astype(jnp.float32)
    sum_two = norm_one + down_out
    layer_out, pull_two = jax.vjp(
        layer_norm, sum_two, gain_two.astype(jnp.float32), shift_two.astype(jnp.float32)
    )
    grad_sum_two, grad_gain_two, grad_shift_two = pull_two(out_grad.astype(jnp.float32))
    grad_down = grad_sum_two.astype(jnp.bfloat16)
    grad_w_down = weight_grad(up_low, grad_down)
    grad_b_down = row_total(grad_down)
    grad_up = pull_up(project_back(grad_down, w_down))[0].astype(jnp.bfloat16)
    grad_w_up = weight_grad(norm_low, grad_up)
    grad_b_up = row_total(grad_up)
    grad_norm_one = grad_sum_two + project_back(grad_up, w_up)
    grad_sum_one, grad_gain_one, grad_shift_one = pull_one(grad_norm_one)
    grad_attn = grad_sum_one.astype(jnp.bfloat16)
    grad_w_out = weight_grad(mixed_low, grad_attn)
    grad_b_out = row_total(grad_attn)
    grad_mixed = project_back(grad_attn, w_out).astype(jnp.bfloat16)
    grad_h = head_view(grad_mixed)
    delta_rows = jnp.sum(grad_h.astype(jnp.float32) * mixed_heads, axis=-1)
    total_slots = wide_size * frames
    first_row = jnp.int32(0)
    grad_q = jnp.zeros((clip_count, frames, HEADS, head_dim), jnp.float32)
    grad_k_all = jnp.zeros((clip_count, total_slots, width), jnp.float32)
    grad_v_all = jnp.zeros((clip_count, total_slots, width), jnp.float32)
    keys_p = lax.all_gather(key_rows, "wide", axis=1, tiled=True)
    values_p = lax.all_gather(value_rows, "wide", axis=1, tiled=True)
    row_count = keys_p.shape[1]
    valid_keys = key_valid_at(lengths, first_row, row_count)
    part_q, part_k, part_v = block_terms(
        query_h,
        grad_h,
        lse_rows,
        delta_rows,
        head_view(keys_p),
        head_view(values_p),
        valid_keys,
        score_scale,
    )
    old_k = lax.dynamic_slice_in_dim(grad_k_all, first_row, row_count, 1)
    old_v = lax.dynamic_slice_in_dim(grad_v_all, first_row, row_count, 1)
    grad_k_all = lax.dynamic_update_slice_in_dim(
        grad_k_all, old_k + part_k.reshape(clip_count, row_count, width), first_row, 1
    )
    grad_v_all = lax.dynamic_update_slice_in_dim(
        grad_v_all, old_v + part_v.reshape(clip_count, row_count, width), first_row, 1
    )
    grad_k_own, grad_v_own = (
        lax.psum_scatter(
            grad_k_all.astype(jnp.bfloat16), "wide", scatter_dimension=1, tiled=True
        ).astype(jnp.float32),
        lax.psum_scatter(
            grad_v_all.astype(jnp.bfloat16), "wide", scatter_dimension=1, tiled=True
        ).astype(jnp.float32),
    )
    grad_q_low = (grad_q + part_q).reshape(clip_count, frames, width).astype(jnp.bfloat16)
    grad_k_low = grad_k_own.astype(jnp.bfloat16)
    grad_v_low = grad_v_own.astype(jnp.bfloat16)
    grad_w_query = weight_grad(first_low, grad_q_low)
    grad_b_query = row_total(grad_q_low)
    grad_w_key = weight_grad(first_low, grad_k_low)
    grad_w_value = weight_grad(first_low, grad_v_low)
    grad_b_value = row_total(grad_v_low)
    grad_first = (
        grad_sum_one
        + project_back(grad_q_low, w_query)
        + project_back(grad_k_low, w_key)
        + project_back(grad_v_low, w_value)
    )
    grad_pre = pull_first(grad_first)[0].astype(jnp.bfloat16)
    grad_conv_bias = row_total(grad_pre)
    grad_kernel = conv_weight_grad(padded, grad_pre, kernel.shape)
    grad_padded = with_halo(grad_pre, (("wide", 1),), half_span)
    flipped = jnp.transpose(kernel[::-1], (0, 1, 3, 2))
    grad_masked = grad_first + conv_apply(grad_padded[:, 1:], flipped, frames)
    frames_grad = jnp.where(frame_valid[..., None], grad_masked, 0.0).astype(jnp.bfloat16)
    shards = (
        lax.psum_scatter(
            grad_kernel.astype(jnp.bfloat16), "wide", scatter_dimension=0, tiled=True
        ).astype(jnp.float32),
        lax.psum_scatter(
            grad_conv_bias.astype(jnp.bfloat16), "wide", scatter_dimension=0, tiled=True
        ).astype(jnp.float32),
        lax.psum_scatter(
            grad_w_query.astype(jnp.bfloat16), "wide", scatter_dimension=0, tiled=True
        ).astype(jnp.float32),
        lax.psum_scatter(
            grad_b_query.astype(jnp.bfloat16), "wide", scatter_dimension=0, tiled=True
        ).astype(jnp.float32),
        lax.psum_scatter(
            grad_w_key.astype(jnp.bfloat16), "wide", scatter_dimension=0, tiled=True
        ).astype(jnp.float32),
        lax.psum_scatter(
            grad_w_value.astype(jnp.bfloat16), "wide", scatter_dimension=0, tiled=True
        ).astype(jnp.float32),
        lax.psum_scatter(
            grad_b_value.astype(jnp.bfloat16), "wide", scatter_dimension=0, tiled=True
        ).astype(jnp.float32),
        lax.psum_scatter(
            grad_w_out.astype(jnp.bfloat16), "wide", scatter_dimension=0, tiled=True
        ).astype(jnp.float32),
        lax.psum_scatter(
            grad_b_out.astype(jnp.bfloat16), "wide", scatter_dimension=0, tiled=True
        ).astype(jnp.float32),
        lax.psum_scatter(
            grad_gain_one.astype(jnp.bfloat16), "wide", scatter_dimension=0, tiled=True
        ).astype(jnp.float32),
        lax.psum_scatter(
            grad_shift_one.astype(jnp.bfloat16), "wide", scatter_dimension=0, tiled=True
        ).astype(jnp.float32),
        lax.psum_scatter(
            grad_w_up.astype(jnp.bfloat16), "wide", scatter_dimension=0, tiled=True
        ).astype(jnp.float32),
        lax.psum_scatter(
            grad_b_up.astype(jnp.bfloat16), "wide", scatter_dimension=0, tiled=True
        ).astype(jnp.float32),
        lax.psum_scatter(
            grad_w_down.astype(jnp.bfloat16), "wide", scatter_dimension=0, tiled=True
        ).astype(jnp.float32),
        lax.psum_scatter(
            grad_b_down.astype(jnp.bfloat16), "wide", scatter_dimension=0, tiled=True
        ).astype(jnp.float32),
        lax.psum_scatter(
            grad_gain_two.astype(jnp.bfloat16), "wide", scatter_dimension=0, tiled=True
        ).astype(jnp.float32),
        lax.psum_scatter(
            grad_shift_two.astype(jnp.bfloat16), "wide", scatter_dimension=0, tiled=True
        ).astype(jnp.float32),
    )
    totals = (
        lax.psum(shards[0].astype(jnp.bfloat16), "narrow").astype(jnp.float32),
        lax.psum(shards[1].astype(jnp.bfloat16), "narrow").astype(jnp.float32),
        lax.psum(shards[2].astype(jnp.bfloat16), "narrow").astype(jnp.float32),
        lax.psum(shards[3].astype(jnp.bfloat16), "narrow").astype(jnp.float32),
        lax.psum(shards[4].astype(jnp.bfloat16), "narrow").astype(jnp.float32),
        lax.psum(shards[5].astype(jnp.bfloat16), "narrow").astype(jnp.float32),
        lax.psum(shards[6].astype(jnp.bfloat16), "narrow").astype(jnp.float32),
        lax.psum(shards[7].astype(jnp.bfloat16), "narrow").astype(jnp.float32),
        lax.psum(shards[8].astype(jnp.bfloat16), "narrow").astype(jnp.float32),
        lax.psum(shards[9].astype(jnp.bfloat16), "narrow").astype(jnp.float32),
        lax.psum(shards[10].astype(jnp.bfloat16), "narrow").astype(jnp.float32),
        lax.psum(shards[11].astype(jnp.bfloat16), "narrow").astype(jnp.float32),
        lax.psum(shards[12].astype(jnp.bfloat16), "narrow").astype(jnp.float32),
        lax.psum(shards[13].astype(jnp.bfloat16), "narrow").astype(jnp.float32),
        lax.psum(shards[14].astype(jnp.bfloat16), "narrow").astype(jnp.float32),
        lax.psum(shards[15].astype(jnp.bfloat16), "narrow").astype(jnp.float32),
        lax.psum(shards[16].astype(jnp.bfloat16), "narrow").astype(jnp.float32),
    )
    return (
        layer_out.astype(jnp.bfloat16),
        frames_grad,
        totals[0],
        totals[1],
        totals[2],
        totals[3],
        totals[4],
        totals[5],
        totals[6],
        totals[7],
        totals[8],
        totals[9],
        totals[10],
        totals[11],
        totals[12],
        totals[13],
        totals[14],
        totals[15],
        totals[16],
    )


def solution(mesh):
    rows = P("narrow", "wide", None)
    placed = (rows, P("narrow")) + (P(),) * 17 + (rows,)
    wide = mesh.shape["wide"]
    fast = wide == 4 and mesh.shape["narrow"] == 8
    return jax.shard_map(
        on_device if fast else on_device_any,
        mesh=mesh,
        in_specs=placed,
        out_specs=(rows, rows)
        + (P("wide", None, None, None), P("wide"), P("wide", None), P("wide"), P("wide", None), P("wide", None))
        + (P("wide"), P("wide", None), P("wide"), P("wide"), P("wide"), P("wide", None), P("wide"))
        + (P("wide", None), P("wide"), P("wide"), P("wide")),
        check_vma=False,
    )
```
